32 devices in a mesh: blk: 4 (over y, core), head: 4 (over z), dp: 2 (over x).
Axes of the slice: x: 2, y: 2, z: 4, core: 2. Of those that a mesh axis runs over, the one named last changes fastest.
Arguments:
- atoms: float32 [2, 1024, 512], P('dp', 'blk'), may hold values from -6 to 6
- pair: float32 [2, 64, 1024, 1024], P('dp', 'head', 'blk'), may hold values from -6 to 6
- mol_ids: int32 [2, 1024], P('dp', 'blk'), may hold values from 0 to 1023, as said below
- ln1_gain: float32 [512], replicated, may hold values from 0.25 to 1.75
- ln1_bias: float32 [512], replicated, may hold values from -3 to 3
- w_query: float32 [512, 512], P(None, 'head'), may hold values from -0.25 to 0.25
- b_query: float32 [512], P('head'), may hold values from -3 to 3
- w_key: float32 [512, 512], P(None, 'head'), may hold values from -0.25 to 0.25
- w_value: float32 [512, 512], P(None, 'head'), may hold values from -0.25 to 0.25
- b_value: float32 [512], P('head'), may hold values from -3 to 3
- w_out: float32 [512, 512], P('head'), may hold values from -2 to 2
- b_out: float32 [512], replicated, may hold values from -3 to 3
- ln2_gain: float32 [512], replicated, may hold values from 0.25 to 1.75
- ln2_bias: float32 [512], replicated, may hold values from -3 to 3
- w_up: float32 [512, 2048], P(None, 'head'), may hold values from -0.25 to 0.25
- b_up: float32 [2048], P('head'), may hold values from -3 to 3
- w_down: float32 [2048, 512], P('head'), may hold values from -0.125 to 0.125
- b_down: float32 [512], replicated, may hold values from -3 to 3
- cot_atoms: float32 [2, 1024, 512], P('dp', 'blk'), may hold values from -6 to 6
- cot_pair: float32 [2, 64, 1024, 1024], P('dp', 'head', 'blk'), may hold values from -6 to 6
Outputs:
- out_atoms: float32 [2, 1024, 512], P('dp', 'blk')
- out_pair: float32 [2, 64, 1024, 1024], P('dp', 'head', 'blk')
- aux_penalty: float32 [], replicated
- grad_atoms: float32 [2, 1024, 512], P('dp', 'blk')
- grad_pair: float32 [2, 64, 1024, 1024], P('dp', 'head', 'blk')
- grad_ln1_gain: float32 [512], replicated
- grad_ln1_bias: float32 [512], replicated
- grad_w_query: float32 [512, 512], P(None, 'head')
- grad_b_query: float32 [512], P('head')
- grad_w_key: float32 [512, 512], P(None, 'head')
- grad_w_value: float32 [512, 512], P(None, 'head')
- grad_b_value: float32 [512], P('head')
- grad_w_out: float32 [512, 512], P('head')
- grad_b_out: float32 [512], replicated
- grad_ln2_gain: float32 [512], replicated
- grad_ln2_bias: float32 [512], replicated
- grad_w_up: float32 [512, 2048], P(None, 'head')
- grad_b_up: float32 [2048], P('head')
- grad_w_down: float32 [2048, 512], P('head')
- grad_b_down: float32 [512], replicated
The draws below stay inside these ranges and needn't reach their ends.
Inputs may be any that keep to these rules, and one draw needn't show every extreme that they name: `mol_ids`: non-decreasing by steps of one along the atoms of a group, the last atom numbered 1024 - 1; atoms with equal numbers form one molecule of consecutive atoms; every molecule has at most 768 atoms, and in every group one molecule has exactly 768.
All inputs are finite; a program needn't handle non-finite values.
Results may differ from the reference program's by a relative error of at most 0.0003.
Values sent between devices are 32-bit elements; how exact they have to be, the bound alone decides.
A program may use at most 192 MiB of HBM per device.

```python
import math
import jax
import jax.numpy as jnp
from jax import lax

D = 512
H = 64
DH = 8
FF = 2048
SEQ = 1024
ROWS = 256
MOL_MAX = 768
HD = 512
N_DP = 2


def draw_mol_ids(key, part):
    key = jax.random.fold_in(key, 11)
    key_start, key_cuts = jax.random.split(key, 2)
    opening = jax.random.randint(key_start, (N_DP, 1), 1, ROWS).astype(jnp.int32)
    cuts = jax.random.randint(key_cuts, (N_DP, SEQ), 0, 2).astype(jnp.int32)
    place = jnp.arange(SEQ, dtype=jnp.int32)[None, :]
    closing = opening + MOL_MAX
    inside = jnp.logical_and(place >= opening, place < closing)
    begins = jnp.logical_or(jnp.logical_or(place == 0, place == opening), place == closing)
    begins = jnp.logical_or(begins, jnp.logical_and(jnp.logical_not(inside), cuts == 1))
    labels = (jnp.cumsum(begins.astype(jnp.int32), axis=1) - 1).astype(jnp.int32)
    return (labels + (SEQ - 1 - labels[:, -1:])).astype(jnp.int32)


def block_scale(key, extent, pieces, smallest, high):
    loudness, own = 1.0, jax.random.fold_in(key, 6)
    for dim, blocks in pieces:
        steps = jnp.exp(jax.random.uniform(jax.random.fold_in(own, dim), (blocks,), jnp.float32, smallest / len(pieces), high / len(pieces)))
        loudness = loudness * jnp.repeat(steps, extent[dim] // blocks).reshape([-1 if axis == dim else 1 for axis in range(len(extent))])
    return loudness


def gaussian(rng, dims, width, limit, cuts=(), kind=jnp.bfloat16):
    entries = width * jax.random.normal(rng, dims, jnp.float32)
    if cuts:
        entries = entries * block_scale(rng, dims, cuts, -0.22, 0.18)
    return jnp.clip(entries, -limit, limit).astype(kind)


def setup_inputs(seed: int = 0) -> dict:
    streams_of = jax.random.split(jax.random.key(seed), 21)
    return {
        "atoms": gaussian(streams_of[0], (N_DP, SEQ, D), 1.0, 6.0, ((0, 2), (1, 4)), jnp.float32),
        "pair": gaussian(streams_of[1], (N_DP, H, SEQ, SEQ), 1.0, 6.0, ((0, 2), (1, 4), (2, 4)), jnp.float32),
        "mol_ids": draw_mol_ids(jax.random.fold_in(streams_of[20], 71), 0),
        "ln1_gain": jnp.clip(1.0 + 0.15 * jax.random.normal(streams_of[3], (D,), jnp.float32), 0.25, 1.75),
        "ln1_bias": gaussian(streams_of[4], (D,), 0.3, 3.0, (), jnp.float32),
        "w_query": gaussian(streams_of[5], (D, HD), D ** -0.5, 0.25, ((1, 4),), jnp.float32),
        "b_query": gaussian(streams_of[6], (HD,), 0.3, 3.0, ((0, 4),), jnp.float32),
        "w_key": gaussian(streams_of[7], (D, HD), D ** -0.5, 0.25, ((1, 4),), jnp.float32),
        "w_value": gaussian(streams_of[8], (D, HD), D ** -0.5, 0.25, ((1, 4),), jnp.float32),
        "b_value": gaussian(streams_of[9], (HD,), 0.3, 3.0, ((0, 4),), jnp.float32),
        "w_out": gaussian(streams_of[10], (HD, D), (max(2, HD * 16 // SEQ)) ** -0.5, 2.0, ((0, 4),), jnp.float32),
        "b_out": gaussian(streams_of[11], (D,), 0.5, 3.0, (), jnp.float32),
        "ln2_gain": jnp.clip(1.0 + 0.15 * jax.random.normal(streams_of[12], (D,), jnp.float32), 0.25, 1.75),
        "ln2_bias": gaussian(streams_of[13], (D,), 0.3, 3.0, (), jnp.float32),
        "w_up": gaussian(streams_of[14], (D, FF), D ** -0.5, 0.25, ((1, 4),), jnp.float32),
        "b_up": gaussian(streams_of[15], (FF,), 0.5, 3.0, ((0, 4),), jnp.float32),
        "w_down": gaussian(streams_of[16], (FF, D), FF ** -0.5, 0.125, ((0, 4),), jnp.float32),
        "b_down": gaussian(streams_of[17], (D,), 0.5, 3.0, (), jnp.float32),
        "cot_atoms": gaussian(streams_of[18], (N_DP, SEQ, D), 1.0, 6.0, ((0, 2), (1, 4)), jnp.float32),
        "cot_pair": gaussian(streams_of[19], (N_DP, H, SEQ, SEQ), 1.0, 6.0, ((0, 2), (1, 4), (2, 4)), jnp.float32),
    }


NORM_EPS = 1e-05
MASK_FILL = -1e+30
FULL_PRECISION = lax.Precision.HIGHEST

@jax.custom_vjp
def low(v):
    return lax.optimization_barrier(v.astype(jnp.bfloat16)).astype(jnp.float32)

@jax.custom_vjp
def low_back(v):
    return v

def low_keep(v):
    return (low(v), None)

def low_pass(kept, grad):
    return (grad,)

def back_keep(v):
    return (v, None)

def back_low(kept, grad):
    return (low(grad),)
low.defvjp(low_keep, low_pass)
low_back.defvjp(back_keep, back_low)

def layer_norm(inputs, scale_gain, shift_bias):
    average = lax.optimization_barrier(jnp.mean(inputs, -1, keepdims=True))
    centred = inputs - average
    variance = lax.optimization_barrier(jnp.mean(centred * centred, -1, keepdims=True))
    return centred * lax.rsqrt(variance + NORM_EPS) * scale_gain + shift_bias

def matmul_full(left, right):
    return jnp.dot(left, right, precision=FULL_PRECISION)

def attend_group(queries, key_rows, value_rows, pair_group, group_ids):
    block_rows = math.gcd(SEQ, 512)
    block_total = SEQ // block_rows
    query_blocks = queries.reshape(block_total, block_rows, H, DH)
    pair_blocks = pair_group.reshape(H, block_total, block_rows, SEQ).transpose(1, 0, 2, 3)
    id_blocks = group_ids.reshape(block_total, block_rows)

    @jax.checkpoint
    def one_block(operands):
        query_block, pair_block, id_block = operands
        scores = jnp.einsum('qhd,khd->hqk', query_block, key_rows, precision=FULL_PRECISION)
        logits = scores + pair_block
        same_mol = id_block[:, None] == group_ids[None, :]
        masked = jnp.where(same_mol[None], logits, MASK_FILL)
        row_max = lax.optimization_barrier(jnp.max(masked, -1, keepdims=True))
        expos = jnp.where(same_mol[None], jnp.exp(masked - row_max), 0.0)
        weights = expos / lax.optimization_barrier(jnp.sum(expos, -1, keepdims=True))
        mixed = jnp.einsum('hqk,khd->qhd', weights, value_rows, precision=FULL_PRECISION)
        squares = lax.optimization_barrier(jnp.sum(scores * scores, 0))
        valid = same_mol.astype(jnp.float32)
        numer = jnp.sum(valid * jnp.log1p(jnp.exp(jnp.sqrt(squares + 1.0) - math.sqrt(H))))
        return (mixed.reshape(block_rows, H * DH), logits, numer, jnp.sum(valid))
    mixed, logits, numer, count = lax.map(one_block, (query_blocks, pair_blocks, id_blocks))
    logits = logits.transpose(1, 0, 2, 3).reshape(H, SEQ, SEQ)
    return (mixed.reshape(SEQ, H * DH), logits, jnp.sum(numer), jnp.sum(count))

def forward(atoms, pair, ln1_gain, ln1_bias, w_query, b_query, w_key, w_value, b_value, w_out, b_out, ln2_gain, ln2_bias, w_up, b_up, w_down, b_down, mol_ids):
    atom_outs = []
    pair_outs = []
    numer_total = jnp.zeros((), jnp.float32)
    count_total = jnp.zeros((), jnp.float32)
    for group_index in range(N_DP):
        inputs = atoms[group_index]
        normed = layer_norm(inputs, ln1_gain, ln1_bias)
        queries = ((matmul_full(normed, w_query) + b_query) * DH ** (-0.5)).reshape(SEQ, H, DH)
        key_rows = matmul_full(normed, w_key).reshape(SEQ, H, DH)
        value_rows = (matmul_full(normed, w_value) + b_value).reshape(SEQ, H, DH)
        mixed, logits, numer, count = attend_group(queries, key_rows, value_rows, pair[group_index], mol_ids[group_index])
        hidden = inputs + (matmul_full(mixed, w_out) + b_out)
        normed_two = layer_norm(hidden, ln2_gain, ln2_bias)
        activated = jax.nn.gelu(matmul_full(normed_two, w_up) + b_up, approximate=False)
        atom_outs.append(hidden + (matmul_full(activated, w_down) + b_down))
        pair_outs.append(logits)
        numer_total = numer_total + numer
        count_total = count_total + count
    return ((jnp.stack(atom_outs), jnp.stack(pair_outs)), (numer_total, count_total))

def reference(atoms, pair, mol_ids, ln1_gain, ln1_bias, w_query, b_query, w_key, w_value, b_value, w_out, b_out, ln2_gain, ln2_bias, w_up, b_up, w_down, b_down, cot_atoms, cot_pair):

    def wrapped(*params):
        return forward(*params, mol_ids)
    primal, pullback, totals = jax.vjp(wrapped, atoms, pair, ln1_gain, ln1_bias, w_query, b_query, w_key, w_value, b_value, w_out, b_out, ln2_gain, ln2_bias, w_up, b_up, w_down, b_down, has_aux=True)
    g_atoms, g_pair, g_ln1_gain, g_ln1_bias, g_w_query, g_b_query, g_w_key, g_w_value, g_b_value, g_w_out, g_b_out, g_ln2_gain, g_ln2_bias, g_w_up, g_b_up, g_w_down, g_b_down = pullback((cot_atoms, cot_pair))
    penalty = totals[0] / totals[1]
    return (primal[0], primal[1], penalty, g_atoms, g_pair, g_ln1_gain, g_ln1_bias, g_w_query, g_b_query, g_w_key, g_w_value, g_b_value, g_w_out, g_b_out, g_ln2_gain, g_ln2_bias, g_w_up, g_b_up, g_w_down, g_b_down)
```

```python
import functools
import math

import jax
import jax.numpy as jnp
from jax import lax
from jax.experimental import pallas as pl
from jax.experimental.pallas import tpu as pltpu
from jax.sharding import PartitionSpec as P

DH = 8
LANES = 128
STRIP = 16
CHUNK = 256
GROUP = 2
NORM_EPS = 1e-05
MASK_FILL = -1e30
F32 = jnp.float32
BF16 = jnp.bfloat16
MESH = pl.DeviceIdType.MESH
NN = (((1,), (0,)), ((), ()))
NT = (((1,), (1,)), ((), ()))
TN = (((0,), (0,)), ((), ()))
VMEM = pl.BlockSpec(memory_space=pltpu.VMEM)


def dot(left, right, dims=NN):
    return lax.dot_general(left, right, dims, preferred_element_type=F32)


def halves(value):
    high = value.astype(BF16)
    return high, (value - high.astype(F32)).astype(BF16)


def dot_halves(left, right, dims=NN):
    return dot(left[0], right[0], dims) + (
        dot(left[0], right[1], dims) + dot(left[1], right[0], dims)
    )


def dot_full(left, right, dims=NN):
    return dot_halves(halves(left), halves(right), dims)


def normalize(inputs):
    centred = inputs - jnp.mean(inputs, -1, keepdims=True)
    rate = lax.rsqrt(jnp.mean(centred * centred, -1, keepdims=True) + NORM_EPS)
    return centred * rate, rate


def normalize_back(grad, gain, normal, rate):
    scaled = grad * gain
    return rate * (
        scaled
        - jnp.mean(scaled, -1, keepdims=True)
        - normal * jnp.mean(scaled * normal, -1, keepdims=True)
    )


def column_sum(value):
    return jnp.sum(value, 0, keepdims=True)


def send(src, dst, send_sem, recv_sem, target):
    copy = pltpu.make_async_remote_copy(
        src_ref=src,
        dst_ref=dst,
        send_sem=send_sem,
        recv_sem=recv_sem,
        device_id=target,
        device_id_type=MESH,
    )
    copy.start()
    return copy


def arrived(ref, sem):
    pltpu.make_async_remote_copy(
        src_ref=ref, dst_ref=ref, send_sem=sem, recv_sem=sem, device_id={}, device_id_type=MESH
    ).wait_recv()


def meet(targets):
    barrier = pltpu.get_barrier_semaphore()
    for target in targets:
        pl.semaphore_signal(barrier, inc=1, device_id=target, device_id_type=MESH)
    pl.semaphore_wait(barrier, len(targets))


def others(index, count):
    return [lax.rem(index + step, count) for step in range(1, count)]


def project_kernel(
    atoms, ids, gain, bias, w_query, b_query, w_key, w_value, b_value,
    queries, kept, id_column, send_sem, recv_sem,
):
    blocks, feats = kept.shape[0], w_query.shape[1]
    rows = atoms.shape[0]
    chips = blocks // 2
    blk = lax.axis_index("blk")
    core, chip = lax.rem(blk, 2), lax.div(blk, 2)
    sibling = blk + 1 - 2 * core
    far = [step * 2 + core for step in others(chip, chips)]
    meet([{"blk": peer} for peer in [sibling] + far])
    normal, _ = normalize(atoms[...])
    normed = halves(normal * gain[...] + bias[...])
    kept[blk, 0:feats, :] = dot_halves(normed, halves(w_key[...])).T
    kept[blk, feats : 2 * feats, :] = (dot_halves(normed, halves(w_value[...])) + b_value[...]).T
    id_row = ids[...].astype(F32)
    kept[blk, 2 * feats : 2 * feats + 8, :] = jnp.broadcast_to(id_row, (8, rows))
    copies = [
        send(kept.at[blk], kept.at[blk], send_sem.at[place], recv_sem.at[blk], {"blk": peer})
        for place, peer in enumerate([sibling] + far)
    ]
    id_column[...] = jnp.broadcast_to(id_row, (LANES, rows)).T
    queries[...] = (
        (dot_halves(normed, halves(w_query[...])) + b_query[...]) * (DH ** (-0.5))
    ).T
    for place, source in enumerate(far):
        arrived(kept.at[source], recv_sem.at[source])
        copies.append(
            send(
                kept.at[source], kept.at[source], send_sem.at[chips + place], recv_sem.at[source],
                {"blk": sibling},
            )
        )
    for source in [sibling] + [peer + 1 - 2 * core for peer in far]:
        arrived(kept.at[source], recv_sem.at[source])
    for copy in copies:
        copy.wait_send()


def project(blocks, atoms, ids, gain, bias, w_query, b_query, w_key, w_value, b_value):
    rows, feats = atoms.shape[0], w_query.shape[1]
    return pl.pallas_call(
        project_kernel,
        out_shape=[
            jax.ShapeDtypeStruct((feats, rows), F32),
            jax.ShapeDtypeStruct((blocks, 2 * feats + 8, rows), F32),
            jax.ShapeDtypeStruct((rows, LANES), F32),
        ],
        in_specs=[VMEM] * 9,
        out_specs=[VMEM] * 3,
        scratch_shapes=[
            pltpu.SemaphoreType.DMA((blocks,)),
            pltpu.SemaphoreType.DMA((blocks,)),
        ],
        compiler_params=pltpu.CompilerParams(
            collective_id=0, has_side_effects=True, vmem_limit_bytes=32 << 20
        ),
        name="project",
    )(atoms, ids, gain, bias, w_query, b_query, w_key, w_value, b_value)


def whole_row(ref, low, count):
    return jnp.concatenate([ref[n, low : low + count, :] for n in range(ref.shape[0])], axis=1)


def stacked(parts):
    return jnp.concatenate(parts, axis=0).astype(BF16)


def wide_halves(value):
    high = value.astype(BF16).astype(F32)
    return high, value - high


def attend_kernel(
    pair, queries, keys, values, ids, id_column,
    mixed, log_sums, squares, id_row, score, high, low,
):
    group, rows, cols = score.shape
    strips = rows // STRIP
    chunk = min(CHUNK, cols)

    @pl.when(pl.program_id(0) == 0)
    def _():
        squares[...] = jnp.zeros_like(squares)
        one = whole_row(ids, 0, 8)
        id_row[...] = jnp.concatenate([one, one], axis=0)

    for g in range(group):
        head = slice(8 * g, 8 * g + 8)
        q_high, q_low = wide_halves(queries[head, :])
        k_high, k_low = wide_halves(whole_row(keys, 8 * g, 8))
        v_high, v_low = wide_halves(whole_row(values, 8 * g, 8))
        ones = jnp.ones_like(v_high)
        q_pack = stacked([q_high, q_high, q_low, q_low])
        k_pack = stacked([k_high, k_low, k_high, k_low])
        v_pack = stacked([v_high, v_low, ones, jnp.zeros_like(ones)])
        tops = [None] * strips
        for start in range(0, cols, chunk):
            part = slice(start, start + chunk)
            score[g, :, part] = dot(q_pack, k_pack[:, part], TN)
            for s in range(strips):
                line = pl.ds(s * STRIP, STRIP)
                own = id_column[line, :]
                for j in range(start, start + chunk, LANES):
                    tile = pl.ds(j, LANES)
                    value = score[g, line, tile]
                    squares[line, tile] += value * value
                    value = jnp.where(own == id_row[:, tile], pair[0, g, line, tile] + value, MASK_FILL)
                    score[g, line, tile] = value
                    tops[s] = value if tops[s] is None else jnp.maximum(tops[s], value)
        tops = [
            jnp.broadcast_to(jnp.max(top, axis=1, keepdims=True), (STRIP, LANES)) for top in tops
        ]
        totals = [None] * strips
        gathered = None
        for start in range(0, cols, chunk):
            part = slice(start, start + chunk)
            for s in range(strips):
                line = pl.ds(s * STRIP, STRIP)
                for j in range(start, start + chunk, LANES):
                    tile = pl.ds(j, LANES)
                    weight = jnp.exp(score[g, line, tile] - tops[s])
                    high[g, line, tile], low[g, line, tile] = halves(weight)
                    totals[s] = weight if totals[s] is None else totals[s] + weight
            term = dot(v_pack[:, part], high[g, :, part], NT) + dot(
                v_pack[:, part], low[g, :, part], NT
            )
            gathered = term if gathered is None else gathered + term
        for s in range(strips):
            total = jnp.sum(totals[s], axis=1, keepdims=True)
            log_sums[g, pl.ds(s * STRIP, STRIP), :] = tops[s] + jnp.log(total)
        mixed[head, :] = (gathered[0:8] + gathered[8:16]) / gathered[16:17]


def head_specs(kept_shape, feats, group):
    blocks, _, rows = kept_shape
    first = feats // (8 * group)
    return (
        pl.BlockSpec((blocks, 8 * group, rows), lambda h: (0, h, 0)),
        pl.BlockSpec((blocks, 8 * group, rows), lambda h: (0, first + h, 0)),
        pl.BlockSpec((blocks, 8, rows), lambda h: (0, 2 * feats // 8, 0)),
    )


def attend(pair, queries, kept, id_column):
    _, heads, rows, cols = pair.shape
    group = GROUP
    feats = heads * DH
    keys, values, ids = head_specs(kept.shape, feats, group)
    return pl.pallas_call(
        attend_kernel,
        grid=(heads // group,),
        in_specs=[
            pl.BlockSpec((1, group, rows, cols), lambda h: (0, h, 0, 0)),
            pl.BlockSpec((8 * group, rows), lambda h: (h, 0)),
            keys,
            values,
            ids,
            pl.BlockSpec((rows, LANES), lambda h: (0, 0)),
        ],
        out_specs=[
            pl.BlockSpec((8 * group, rows), lambda h: (h, 0)),
            pl.BlockSpec((group, rows, LANES), lambda h: (h, 0, 0)),
            pl.BlockSpec((rows, cols), lambda h: (0, 0)),
            pl.BlockSpec((STRIP, cols), lambda h: (0, 0)),
        ],
        out_shape=[
            jax.ShapeDtypeStruct((feats, rows), F32),
            jax.ShapeDtypeStruct((heads, rows, LANES), F32),
            jax.ShapeDtypeStruct((rows, cols), F32),
            jax.ShapeDtypeStruct((STRIP, cols), F32),
        ],
        scratch_shapes=[
            pltpu.VMEM((group, rows, cols), F32),
            pltpu.VMEM((group, rows, cols), BF16),
            pltpu.VMEM((group, rows, cols), BF16),
        ],
        compiler_params=pltpu.CompilerParams(vmem_limit_bytes=48 << 20),
        cost_estimate=pl.CostEstimate(
            flops=2 * 200 * heads * rows * cols,
            bytes_accessed=4 * heads * rows * cols,
            transcendentals=heads * rows * cols,
        ),
        name="attend",
    )(pair, queries, kept, kept, kept, id_column)


def attend_back_kernel(
    pair, cot, queries, keys, values, mixed, d_mixed, log_sums, id_column, id_row,
    out_pair, grad_pair, d_queries, d_keys, d_values, score, d_prob, p_high, p_low, g_high, g_low,
):
    group, rows, cols = score.shape
    blocks = d_keys.shape[0] * 2
    chunk = min(CHUNK, cols)
    place = lax.broadcasted_iota(jnp.int32, (8, rows), 0)

    def both(left, high, low, dims):
        value = dot(left, high, dims) + dot(left, low, dims)
        return value[0:8] + value[8:16]

    for g in range(group):
        head = slice(8 * g, 8 * g + 8)
        q_high, q_low = wide_halves(queries[head, :])
        k_high, k_low = wide_halves(whole_row(keys, 8 * g, 8))
        v_high, v_low = wide_halves(whole_row(values, 8 * g, 8))
        m_high, m_low = wide_halves(d_mixed[head, :])
        first = -column_sum(mixed[head, :] * d_mixed[head, :])
        delta_high, second = wide_halves(first)
        delta_mid, delta_low = wide_halves(second)
        deltas = jnp.where(
            place == 0, delta_high, jnp.where(place == 1, delta_mid, jnp.where(place == 2, delta_low, 0.0))
        )
        q_pack = stacked([q_high, q_high, q_low, q_low])
        k_pack = stacked([k_high, k_low, k_high, k_low])
        m_pack = stacked([m_high, m_high, m_low, deltas])
        v_pack = stacked([v_high, v_low, v_high, jnp.ones_like(v_high)])
        q_pair = stacked([q_high, q_low])
        k_pair = stacked([k_high, k_low])
        m_pair = stacked([m_high, m_low])
        d_query = None
        for start in range(0, cols, chunk):
            part = slice(start, start + chunk)
            score[g, :, part] = dot(q_pack, k_pack[:, part], TN)
            d_prob[g, :, part] = dot(m_pack, v_pack[:, part], TN)
            for s in range(rows // STRIP):
                line = pl.ds(s * STRIP, STRIP)
                own = id_column[line, :]
                log_sum = log_sums[g, line, :]
                for j in range(start, start + chunk, LANES):
                    tile = pl.ds(j, LANES)
                    value = pair[0, g, line, tile] + score[g, line, tile]
                    out_pair[0, g, line, tile] = value
                    prob = jnp.exp(jnp.where(own == id_row[:, tile], value - log_sum, MASK_FILL))
                    p_high[g, line, tile], p_low[g, line, tile] = halves(prob)
                    grad = prob * d_prob[g, line, tile] + cot[0, g, line, tile]
                    grad_pair[0, g, line, tile] = grad
                    g_high[g, line, tile], g_low[g, line, tile] = halves(grad)
            d_value = both(m_pair, p_high[g, :, part], p_low[g, :, part], NN)
            d_key = both(q_pair, g_high[g, :, part], g_low[g, :, part], NN)
            for n in range(start // rows, (start + chunk) // rows):
                span = slice(n * rows - start, (n + 1) * rows - start)
                d_keys[n // 2, n % 2, head, :] = d_key[:, span]
                d_values[n // 2, n % 2, head, :] = d_value[:, span]
            term = both(k_pair[:, part], g_high[g, :, part], g_low[g, :, part], NT)
            d_query = term if d_query is None else d_query + term
        d_queries[head, :] = d_query * (DH ** (-0.5))


def attend_back(pair, cot, queries, kept, mixed, d_mixed, log_sums, id_column, id_row):
    _, heads, rows, cols = pair.shape
    group = GROUP
    feats = heads * DH
    blocks = kept.shape[0]
    keys, values, _ = head_specs(kept.shape, feats, group)
    big = pl.BlockSpec((1, group, rows, cols), lambda h: (0, h, 0, 0))
    flat = pl.BlockSpec((8 * group, rows), lambda h: (h, 0))
    split = pl.BlockSpec((blocks // 2, 2, 8 * group, rows), lambda h: (0, 0, h, 0))
    return pl.pallas_call(
        attend_back_kernel,
        grid=(heads // group,),
        in_specs=[
            big, big, flat, keys, values, flat, flat,
            pl.BlockSpec((group, rows, LANES), lambda h: (h, 0, 0)),
            pl.BlockSpec((rows, LANES), lambda h: (0, 0)),
            pl.BlockSpec((STRIP, cols), lambda h: (0, 0)),
        ],
        out_specs=[big, big, flat, split, split],
        out_shape=[
            jax.ShapeDtypeStruct(pair.shape, F32),
            jax.ShapeDtypeStruct(pair.shape, F32),
            jax.ShapeDtypeStruct((feats, rows), F32),
            jax.ShapeDtypeStruct((blocks // 2, 2, feats, rows), F32),
            jax.ShapeDtypeStruct((blocks // 2, 2, feats, rows), F32),
        ],
        scratch_shapes=[pltpu.VMEM((group, rows, cols), F32)] * 2
        + [pltpu.VMEM((group, rows, cols), BF16)] * 4,
        compiler_params=pltpu.CompilerParams(vmem_limit_bytes=56 << 20),
        cost_estimate=pl.CostEstimate(
            flops=2 * 400 * heads * rows * cols,
            bytes_accessed=16 * heads * rows * cols,
            transcendentals=heads * rows * cols,
        ),
        name="attend_back",
    )(pair, cot, queries, kept, kept, mixed, d_mixed, log_sums, id_column, id_row)


SMALL_LN1_GAIN, SMALL_LN1_BIAS, SMALL_LN2_GAIN, SMALL_LN2_BIAS = 0, 1, 2, 3
SMALL_B_OUT, SMALL_B_DOWN, SMALL_PENALTY = 4, 5, 6
SMALL_B_QUERY, SMALL_B_VALUE, SMALL_B_UP = 8, 9, 10
SMALL_ROWS = 16


def feed_kernel(
    mixed, atoms, w_out, b_out, gain, bias, w_up, b_up, w_down, cot,
    d_mixed, hidden, down, d_hidden, grad_up, grad_down, small,
    mixed_all, normal_two, rate_two, part, landed, back, back_landed,
    mix_send, mix_recv, part_send, part_recv, back_send, back_recv,
):
    zs, feats, rows = mixed_all.shape
    piece = rows // zs
    width = atoms.shape[1]
    z = lax.axis_index("head")
    peers = others(z, zs)
    meet([{"head": peer} for peer in peers])
    mixed_all[z] = mixed[...]
    copies = [
        send(mixed_all.at[z], mixed_all.at[z], mix_send.at[n], mix_recv.at[z], {"head": peer})
        for n, peer in enumerate(peers)
    ]
    mine = pl.ds(pl.multiple_of(z * piece, 8), piece)
    small[...] = jnp.zeros_like(small)
    small[SMALL_B_DOWN : SMALL_B_DOWN + 1, :] = column_sum(cot[mine, :])
    cots = halves(cot[...])
    downs = halves(w_down[...])
    d_act = dot_halves(cots, downs, NT)
    ups = halves(w_up[...])
    outs = halves(w_out[...])
    for peer in peers:
        arrived(mixed_all.at[peer], mix_recv.at[peer])
    mixed_rows = mixed_all[...].reshape(zs * feats, rows).T
    hidden_rows = atoms[...] + dot_halves(halves(mixed_rows), outs) + b_out[...]
    hidden[...] = hidden_rows
    normal, rate = normalize(hidden_rows)
    normal_two[...] = normal
    rate_two[...] = jnp.broadcast_to(rate, rate_two.shape)
    normed = normal * gain[...] + bias[...]
    pre = dot_halves(halves(normed), ups) + b_up[...]
    phi = 0.5 * (1.0 + lax.erf(pre * math.sqrt(0.5)))
    act = pre * phi
    d_pre = d_act * (phi + pre * jnp.exp(-0.5 * pre * pre) * (1.0 / math.sqrt(2.0 * math.pi)))
    d_pres = halves(d_pre)
    part[...] = dot_halves(d_pres, ups, NT).reshape(zs, piece, width)
    copies += [
        send(part.at[peer], landed.at[z], part_send.at[n], part_recv.at[z], {"head": peer})
        for n, peer in enumerate(peers)
    ]
    landed[z] = part[z]
    down[...] = dot_halves(halves(act), downs)
    grad_up[...] = dot_halves(halves(normed.T), d_pres)
    grad_down[...] = dot_halves(halves(act.T), cots)
    small[SMALL_B_UP : SMALL_B_UP + 1, 0 : d_pre.shape[1]] = column_sum(d_pre)
    for peer in peers:
        arrived(landed.at[peer], part_recv.at[peer])
    d_normed = functools.reduce(jnp.add, [landed[n] for n in range(zs)])
    normal = normal_two[mine, :]
    small[SMALL_LN2_GAIN : SMALL_LN2_GAIN + 1, :] = column_sum(d_normed * normal)
    small[SMALL_LN2_BIAS : SMALL_LN2_BIAS + 1, :] = column_sum(d_normed)
    d_rows = cot[mine, :] + normalize_back(d_normed, gain[...], normal, rate_two[mine, 0:1])
    d_hidden[...] = d_rows
    small[SMALL_B_OUT : SMALL_B_OUT + 1, :] = column_sum(d_rows)
    d_halves = halves(d_rows)
    for n in range(zs):
        some = slice(n * feats, (n + 1) * feats)
        back[n] = dot_halves(d_halves, (outs[0][some], outs[1][some]), NT)
    copies += [
        send(back.at[peer], back_landed.at[z], back_send.at[n], back_recv.at[z], {"head": peer})
        for n, peer in enumerate(peers)
    ]
    back_landed[z] = back[z]
    for peer in peers:
        arrived(back_landed.at[peer], back_recv.at[peer])
    d_mixed[...] = back_landed[...].reshape(rows, feats).T
    for copy in copies:
        copy.wait_send()


def feed(zs, mixed, atoms, w_out, b_out, gain, bias, w_up, b_up, w_down, cot):
    feats, rows = mixed.shape
    width = atoms.shape[1]
    units = w_up.shape[1]
    piece = rows // zs
    return pl.pallas_call(
        feed_kernel,
        out_shape=[
            jax.ShapeDtypeStruct((feats, rows), F32),
            jax.ShapeDtypeStruct((rows, width), F32),
            jax.ShapeDtypeStruct((rows, width), F32),
            jax.ShapeDtypeStruct((piece, width), F32),
            jax.ShapeDtypeStruct((width, units), F32),
            jax.ShapeDtypeStruct((units, width), F32),
            jax.ShapeDtypeStruct((SMALL_ROWS, width), F32),
        ],
        in_specs=[VMEM] * 10,
        out_specs=[VMEM] * 7,
        scratch_shapes=[
            pltpu.VMEM((zs, feats, rows), F32),
            pltpu.VMEM((rows, width), F32),
            pltpu.VMEM((rows, LANES), F32),
            pltpu.VMEM((zs, piece, width), F32),
            pltpu.VMEM((zs, piece, width), F32),
            pltpu.VMEM((zs, piece, feats), F32),
            pltpu.VMEM((zs, piece, feats), F32),
        ]
        + [pltpu.SemaphoreType.DMA((zs,))] * 6,
        compiler_params=pltpu.CompilerParams(
            collective_id=1, has_side_effects=True, vmem_limit_bytes=48 << 20
        ),
        name="feed",
    )(mixed, atoms, w_out, b_out, gain, bias, w_up, b_up, w_down, cot)


def finish_kernel(
    d_queries, d_keys, d_values, mixed, atoms, d_hidden, d_hidden_all, w_query, w_key, w_value,
    gain, bias, squares, id_column, id_row, small_in,
    grad_atoms, grad_query, grad_key, grad_value, grad_out, small, penalty,
    sib_keys, sib_values, go_keys, go_values, got_keys, got_values,
    part, landed, grads, sib_grads, go_grads, got_grads, total_grads, small_z, small_all,
    sib_send, sib_recv, kv_send, kv_recv, part_send, part_recv, back_send, back_recv,
    g_send, g_recv, t_send, t_recv, f_send, small_z_send, small_z_recv, small_send, small_recv,
):
    chips, _, feats, rows = d_keys.shape
    zs, piece, width = part.shape
    teams, _, share, _ = grads.shape
    blk, z, dp = lax.axis_index("blk"), lax.axis_index("head"), lax.axis_index("dp")
    core, chip = lax.rem(blk, 2), lax.div(blk, 2)
    other_core = 1 - core
    sibling = {"blk": blk + 1 - 2 * core}
    peers = others(z, zs)
    team = dp * chips + chip
    far_teams = others(team, teams)
    far_chips = others(chip, chips)
    place = team * 2 + core
    far_places = others(place, teams * 2)

    def of_team(value, kind):
        return {"dp": lax.div(value, chips), "blk": lax.rem(value, chips) * 2 + kind}

    plane = [of_team(lax.div(value, 2), lax.rem(value, 2)) for value in far_places]
    meet([{"head": peer} for peer in peers] + plane)
    copies = [
        send(d_keys.at[:, other_core], sib_keys, sib_send.at[0], sib_recv.at[0], sibling),
        send(d_values.at[:, other_core], sib_values, sib_send.at[1], sib_recv.at[1], sibling),
    ]
    normal, rate = normalize(atoms[...])
    normed = halves(normal * gain[...] + bias[...])
    dq_rows = d_queries[...].T
    d_normed = dot_full(dq_rows, w_query[...], NT)
    grad_q = dot_halves(halves(d_queries[...]), normed)
    grad_o = dot_full(mixed[...], d_hidden_all[...])
    mine = pl.ds(pl.multiple_of(z * piece, 8), piece)
    own = id_column[mine, 0:1]
    same = own == id_row[0:1, :]
    norms = jnp.sqrt(squares[...] + 1.0)
    terms = jnp.where(same, jnp.log1p(jnp.exp(norms - math.sqrt(zs * feats // DH))), 0.0)
    number = jnp.where(same, 1.0, 0.0)

    def total(value):
        return jnp.sum(jnp.sum(value, axis=1, keepdims=True), axis=0, keepdims=True)

    lane = lax.broadcasted_iota(jnp.int32, (1, width), 1)
    small_z[z] = small_in[0:8, :]
    small_z[z, SMALL_PENALTY : SMALL_PENALTY + 1, :] = jnp.where(
        lane == 0, total(terms), jnp.where(lane == 1, total(number), 0.0)
    )
    arrived(sib_keys, sib_recv.at[0])
    arrived(sib_values, sib_recv.at[1])
    go_keys[...] = sib_keys[...] + d_keys[:, core]
    go_values[...] = sib_values[...] + d_values[:, core]
    for n, peer in enumerate(far_chips):
        target = {"blk": peer * 2 + core}
        copies.append(send(go_keys.at[peer], got_keys.at[chip], kv_send.at[0, n], kv_recv.at[0, chip], target))
        copies.append(
            send(go_values.at[peer], got_values.at[chip], kv_send.at[1, n], kv_recv.at[1, chip], target)
        )
    got_keys[chip] = go_keys[chip]
    got_values[chip] = go_values[chip]
    for peer in far_chips:
        arrived(got_keys.at[peer], kv_recv.at[0, peer])
        arrived(got_values.at[peer], kv_recv.at[1, peer])
    dk = functools.reduce(jnp.add, [got_keys[n] for n in range(chips)])
    dv = functools.reduce(jnp.add, [got_values[n] for n in range(chips)])
    dv_rows = dv.T
    d_normed = (
        d_normed + dot_full(dk.T, w_key[...], NT) + dot_full(dv_rows, w_value[...], NT)
    )
    part[...] = d_normed.reshape(zs, piece, width)
    copies += [
        send(part.at[peer], landed.at[z], part_send.at[n], part_recv.at[z], {"head": peer})
        for n, peer in enumerate(peers)
    ]
    landed[z] = part[z]
    grad_k = dot_halves(halves(dk), normed)
    grad_v = dot_halves(halves(dv), normed)
    grads[...] = jnp.concatenate([grad_q, grad_k, grad_v, grad_o], axis=0).reshape(grads.shape)
    copies.append(send(grads.at[:, other_core], sib_grads, sib_send.at[2], sib_recv.at[2], sibling))
    arrived(sib_grads, sib_recv.at[2])
    go_grads[...] = sib_grads[...] + grads[:, core]
    copies += [
        send(go_grads.at[peer], got_grads.at[team], g_send.at[n], g_recv.at[team], of_team(peer, core))
        for n, peer in enumerate(far_teams)
    ]
    got_grads[team] = go_grads[team]
    for peer in peers:
        arrived(landed.at[peer], part_recv.at[peer])
    d_normed = functools.reduce(jnp.add, [landed[n] for n in range(zs)])
    normal, rate = normalize(atoms[mine, :])
    small_z[z, SMALL_LN1_GAIN : SMALL_LN1_GAIN + 1, :] = column_sum(d_normed * normal)
    small_z[z, SMALL_LN1_BIAS : SMALL_LN1_BIAS + 1, :] = column_sum(d_normed)
    grad_atoms[mine, :] = d_hidden[...] + normalize_back(d_normed, gain[...], normal, rate)
    copies += [
        send(small_z.at[z], small_z.at[z], small_z_send.at[n], small_z_recv.at[z], {"head": peer})
        for n, peer in enumerate(peers)
    ]
    copies += [
        send(grad_atoms.at[mine], grad_atoms.at[mine], back_send.at[n], back_recv.at[z], {"head": peer})
        for n, peer in enumerate(peers)
    ]
    for peer in far_teams:
        arrived(got_grads.at[peer], g_recv.at[peer])
    total_grads[team, core] = functools.reduce(jnp.add, [got_grads[n] for n in range(teams)])
    ready = total_grads.at[team, core]
    copies.append(send(ready, ready, t_send.at[0], t_recv.at[team, core], sibling))
    copies += [
        send(ready, ready, t_send.at[n + 1], t_recv.at[team, core], of_team(peer, core))
        for n, peer in enumerate(far_teams)
    ]
    for peer in peers:
        arrived(small_z.at[peer], small_z_recv.at[peer])
    small_all[place, 0:8, :] = functools.reduce(jnp.add, [small_z[n] for n in range(zs)])
    small_all[place, 8:16, :] = small_in[8:16, :]
    small_all[place, SMALL_B_QUERY : SMALL_B_QUERY + 1, 0:feats] = column_sum(dq_rows)
    small_all[place, SMALL_B_VALUE : SMALL_B_VALUE + 1, 0:feats] = column_sum(dv_rows)
    copies += [
        send(small_all.at[place], small_all.at[place], small_send.at[n], small_recv.at[place], target)
        for n, target in enumerate(plane)
    ]
    for n, peer in enumerate(far_teams):
        ready = total_grads.at[peer, core]
        arrived(ready, t_recv.at[peer, core])
        copies.append(send(ready, ready, f_send.at[n], t_recv.at[peer, core], sibling))
    for source in far_places:
        arrived(small_all.at[source], small_recv.at[source])
    summed = functools.reduce(jnp.add, [small_all[n] for n in range(2 * teams)])
    small[...] = summed
    ends = summed[SMALL_PENALTY : SMALL_PENALTY + 1, :]
    penalty[...] = ends[:, 0:1] / ends[:, 1:2]
    for peer in [team] + far_teams:
        ready = total_grads.at[peer, other_core]
        arrived(ready, t_recv.at[peer, other_core])
    done = total_grads[...].reshape(4 * feats, width)
    grad_query[...] = done[0:feats].T
    grad_key[...] = done[feats : 2 * feats].T
    grad_value[...] = done[2 * feats : 3 * feats].T
    grad_out[...] = done[3 * feats :]
    for peer in peers:
        there = pl.ds(pl.multiple_of(peer * piece, 8), piece)
        arrived(grad_atoms.at[there], back_recv.at[peer])
    for copy in copies:
        copy.wait_send()


def finish(zs, dps, *operands):
    d_queries, d_keys, atoms = operands[0], operands[1], operands[4]
    chips, _, feats, rows = d_keys.shape
    width = atoms.shape[1]
    piece = rows // zs
    teams = dps * chips
    share = 4 * feats // (2 * teams)
    some = pltpu.VMEM((chips, feats, rows), F32)
    slab = pltpu.VMEM((zs, piece, width), F32)
    both = pltpu.VMEM((teams, 2, share, width), F32)
    one = pltpu.VMEM((teams, share, width), F32)
    dma = pltpu.SemaphoreType.DMA
    return pl.pallas_call(
        finish_kernel,
        out_shape=[
            jax.ShapeDtypeStruct((rows, width), F32),
            jax.ShapeDtypeStruct((width, feats), F32),
            jax.ShapeDtypeStruct((width, feats), F32),
            jax.ShapeDtypeStruct((width, feats), F32),
            jax.ShapeDtypeStruct((feats, width), F32),
            jax.ShapeDtypeStruct((SMALL_ROWS, width), F32),
            jax.ShapeDtypeStruct((1, 1), F32),
        ],
        in_specs=[VMEM] * len(operands),
        out_specs=[VMEM] * 7,
        scratch_shapes=[some] * 6
        + [slab, slab, both, one, one, one, both]
        + [
            pltpu.VMEM((zs, 8, width), F32),
            pltpu.VMEM((2 * teams, SMALL_ROWS, width), F32),
            dma((3,)), dma((3,)),
            dma((2, chips)), dma((2, chips)),
            dma((zs,)), dma((zs,)),
            dma((zs,)), dma((zs,)),
            dma((teams,)), dma((teams,)),
            dma((teams,)), dma((teams, 2)), dma((teams,)),
            dma((zs,)), dma((zs,)),
            dma((2 * teams,)), dma((2 * teams,)),
        ],
        compiler_params=pltpu.CompilerParams(
            collective_id=2, has_side_effects=True, vmem_limit_bytes=56 << 20
        ),
        name="finish",
    )(*operands)


def local(
    zs, dps,
    atoms, pair, mol_ids, ln1_gain, ln1_bias, w_query, b_query, w_key, w_value, b_value, w_out, b_out,
    ln2_gain, ln2_bias, w_up, b_up, w_down, b_down, cot_atoms, cot_pair,
):
    blocks = pair.shape[3] // pair.shape[2]
    inputs, cot = atoms[0], cot_atoms[0]

    def line(value):
        return value.reshape(1, -1)

    queries, kept, id_column = project(
        blocks, inputs, mol_ids, line(ln1_gain), line(ln1_bias), w_query, line(b_query), w_key, w_value,
        line(b_value),
    )
    w_out_all = lax.all_gather(w_out, "head", axis=0, tiled=True)
    mixed, log_sums, squares, id_row = attend(pair, queries, kept, id_column)
    squares = lax.psum_scatter(squares, "head", scatter_dimension=0, tiled=True)
    d_mixed, hidden, down, d_hidden, grad_up, grad_down, small = feed(
        zs, mixed, inputs, w_out_all, line(b_out), line(ln2_gain), line(ln2_bias), w_up, line(b_up), w_down, cot
    )
    down = lax.psum(down, "head")
    out_atoms = hidden + down + b_down
    d_hidden_all = lax.all_gather(d_hidden, "head", axis=0, tiled=True)
    grad_up, grad_down = lax.psum((grad_up, grad_down), ("blk", "dp"))
    out_pair, grad_pair, d_queries, d_keys, d_values = attend_back(
        pair, cot_pair, queries, kept, mixed, d_mixed, log_sums, id_column, id_row
    )
    grad_atoms, grad_query, grad_key, grad_value, grad_out, small, penalty = finish(
        zs, dps,
        d_queries, d_keys, d_values, mixed, inputs, d_hidden, d_hidden_all, w_query, w_key, w_value,
        line(ln1_gain), line(ln1_bias), squares, id_column, id_row, small,
    )
    feats, units = w_query.shape[1], w_up.shape[1]
    return (
        out_atoms[None],
        out_pair,
        penalty[0, 0],
        grad_atoms[None],
        grad_pair,
        small[SMALL_LN1_GAIN],
        small[SMALL_LN1_BIAS],
        grad_query,
        small[SMALL_B_QUERY, :feats],
        grad_key,
        grad_value,
        small[SMALL_B_VALUE, :feats],
        grad_out,
        small[SMALL_B_OUT],
        small[SMALL_LN2_GAIN],
        small[SMALL_LN2_BIAS],
        grad_up,
        small[SMALL_B_UP, :units],
        grad_down,
        small[SMALL_B_DOWN],
    )


def solution(mesh):
    rows, pairs = P("dp", "blk", None), P("dp", "head", "blk", None)
    columns = P(None, "head")
    return jax.shard_map(
        functools.partial(local, mesh.shape["head"], mesh.shape["dp"]),
        mesh=mesh,
        in_specs=(
            rows, pairs, P("dp", "blk"), P(), P(), columns, P("head"), columns, columns, P("head"),
            P("head", None), P(), P(), P(), columns, P("head"), P("head", None), P(), rows, pairs,
        ),
        out_specs=(
            rows, pairs, P(), rows, pairs, P(), P(), columns, P("head"), columns, columns, P("head"),
            P("head", None), P(), P(), P(), columns, P("head"), P("head", None), P(),
        ),
        check_vma=False,
    )
```

```python
import functools
import math

import jax
import jax.numpy as jnp
from jax import lax
from jax.experimental import pallas as pl
from jax.experimental.pallas import tpu as pltpu
from jax.sharding import PartitionSpec as P

DH = 8
LANES = 128
STRIP = 16
CHUNK = 256
GROUP = 2
NORM_EPS = 1e-05
MASK_FILL = -1e30
F32 = jnp.float32
BF16 = jnp.bfloat16
MESH = pl.DeviceIdType.MESH
NN = (((1,), (0,)), ((), ()))
NT = (((1,), (1,)), ((), ()))
TN = (((0,), (0,)), ((), ()))
VMEM = pl.BlockSpec(memory_space=pltpu.VMEM)


def dot(left, right, dims=NN):
    return lax.dot_general(left, right, dims, preferred_element_type=F32)


def halves(value):
    high = value.astype(BF16)
    return high, (value - high.astype(F32)).astype(BF16)


def dot_halves(left, right, dims=NN):
    return dot(left[0], right[0], dims) + (
        dot(left[0], right[1], dims) + dot(left[1], right[0], dims)
    )


def dot_full(left, right, dims=NN):
    return dot_halves(halves(left), halves(right), dims)


def normalize(inputs):
    centred = inputs - jnp.mean(inputs, -1, keepdims=True)
    rate = lax.rsqrt(jnp.mean(centred * centred, -1, keepdims=True) + NORM_EPS)
    return centred * rate, rate


def normalize_back(grad, gain, normal, rate):
    scaled = grad * gain
    return rate * (
        scaled
        - jnp.mean(scaled, -1, keepdims=True)
        - normal * jnp.mean(scaled * normal, -1, keepdims=True)
    )


def column_sum(value):
    return jnp.sum(value, 0, keepdims=True)


def send(src, dst, send_sem, recv_sem, target):
    copy = pltpu.make_async_remote_copy(
        src_ref=src,
        dst_ref=dst,
        send_sem=send_sem,
        recv_sem=recv_sem,
        device_id=target,
        device_id_type=MESH,
    )
    copy.start()
    return copy


def arrived(ref, sem):
    pltpu.make_async_remote_copy(
        src_ref=ref, dst_ref=ref, send_sem=sem, recv_sem=sem, device_id={}, device_id_type=MESH
    ).wait_recv()


def meet(targets):
    barrier = pltpu.get_barrier_semaphore()
    for target in targets:
        pl.semaphore_signal(barrier, inc=1, device_id=target, device_id_type=MESH)
    pl.semaphore_wait(barrier, len(targets))


def others(index, count):
    return [lax.rem(index + step, count) for step in range(1, count)]


class Operand:
    def __init__(self, source, slot, sem):
        self.source, self.slot, self.shape = source, slot, slot.shape
        self.copy = pltpu.make_async_copy(source, slot, sem)
        self.copy.start()

    @property
    def ref(self):
        if self.copy is not None:
            self.copy.wait()
            self.copy = None
        return self.slot

    def __getitem__(self, index):
        return self.ref[index]


class Result:
    def __init__(self, target, slot, sem):
        self.slot, self.shape, self.at = slot, slot.shape, slot.at
        self.copy = pltpu.make_async_copy(slot, target, sem)
        self.begun = False

    def __setitem__(self, index, value):
        self.slot[index] = value

    def __getitem__(self, index):
        return self.slot[index]

    def flush(self):
        if not self.begun:
            self.copy.start()
            self.begun = True


def staged_call(kernel, name, operands, results, scratch, megabytes, remote=None):
    n_in, n_out = len(operands), len(results)

    def body(*refs):
        sources, targets, refs = refs[:n_in], refs[n_in : n_in + n_out], refs[n_in + n_out :]
        slots, made, refs = refs[:n_in], refs[n_in : n_in + n_out], refs[n_in + n_out :]
        in_sem, out_sem, refs = refs[0], refs[1], refs[2:]
        ins = [Operand(sources[n], slots[n], in_sem.at[n]) for n in range(n_in)]
        outs = [Result(targets[n], made[n], out_sem.at[n]) for n in range(n_out)]
        kernel(ins, outs, refs)
        for operand in ins:
            operand.ref
        for result in outs:
            result.flush()
        for result in outs:
            result.copy.wait()

    anywhere = pl.BlockSpec(memory_space=pl.ANY)
    extra = {} if remote is None else {"collective_id": remote, "has_side_effects": True}
    return pl.pallas_call(
        body,
        out_shape=[jax.ShapeDtypeStruct(shape, F32) for shape in results],
        in_specs=[anywhere] * n_in,
        out_specs=[anywhere] * n_out,
        scratch_shapes=[pltpu.VMEM(value.shape, value.dtype) for value in operands]
        + [pltpu.VMEM(shape, F32) for shape in results]
        + [pltpu.SemaphoreType.DMA((n_in,)), pltpu.SemaphoreType.DMA((n_out,))]
        + list(scratch),
        compiler_params=pltpu.CompilerParams(vmem_limit_bytes=megabytes << 20, **extra),
        name=name,
    )(*operands)


def project_kernel(operands, results, scratch):
    atoms, ids, gain, bias, w_key, w_value, b_value, w_query, b_query = operands
    queries, kept, id_column = results
    send_sem, recv_sem = scratch
    blocks, feats = kept.shape[0], w_query.shape[1]
    rows = atoms.shape[0]
    chips = blocks // 2
    blk = lax.axis_index("blk")
    core, chip = lax.rem(blk, 2), lax.div(blk, 2)
    sibling = blk + 1 - 2 * core
    far = [step * 2 + core for step in others(chip, chips)]
    meet([{"blk": peer} for peer in [sibling] + far])
    normal, _ = normalize(atoms[...])
    normed = halves(normal * gain[...] + bias[...])
    kept[blk, 0:feats, :] = dot_halves(normed, halves(w_key[...])).T
    kept[blk, feats : 2 * feats, :] = (dot_halves(normed, halves(w_value[...])) + b_value[...]).T
    id_row = ids[...].astype(F32)
    kept[blk, 2 * feats : 2 * feats + 8, :] = jnp.broadcast_to(id_row, (8, rows))
    copies = [
        send(kept.at[blk], kept.at[blk], send_sem.at[place], recv_sem.at[blk], {"blk": peer})
        for place, peer in enumerate([sibling] + far)
    ]
    id_column[...] = jnp.broadcast_to(id_row, (LANES, rows)).T
    queries[...] = (
        (dot_halves(normed, halves(w_query[...])) + b_query[...]) * (DH ** (-0.5))
    ).T
    for place, source in enumerate(far):
        arrived(kept.at[source], recv_sem.at[source])
        copies.append(
            send(
                kept.at[source], kept.at[source], send_sem.at[chips + place], recv_sem.at[source],
                {"blk": sibling},
            )
        )
    for source in [sibling] + [peer + 1 - 2 * core for peer in far]:
        arrived(kept.at[source], recv_sem.at[source])
    for copy in copies:
        copy.wait_send()


def project(blocks, *operands):
    rows, feats = operands[0].shape[0], operands[4].shape[1]
    return staged_call(
        project_kernel,
        "project",
        operands,
        [(feats, rows), (blocks, 2 * feats + 8, rows), (rows, LANES)],
        [pltpu.SemaphoreType.DMA((blocks,)), pltpu.SemaphoreType.DMA((blocks,))],
        32,
        remote=0,
    )


def whole_row(ref, low, count):
    return jnp.concatenate([ref[n, low : low + count, :] for n in range(ref.shape[0])], axis=1)


def stacked(parts):
    return jnp.concatenate(parts, axis=0).astype(BF16)


def wide_halves(value):
    high = value.astype(BF16).astype(F32)
    return high, value - high


def attend_kernel(
    pair, queries, keys, values, ids, id_column,
    mixed, log_sums, squares, id_row, score, high, low,
):
    group, rows, cols = score.shape
    strips = rows // STRIP
    chunk = min(CHUNK, cols)

    @pl.when(pl.program_id(0) == 0)
    def _():
        squares[...] = jnp.zeros_like(squares)
        one = whole_row(ids, 0, 8)
        id_row[...] = jnp.concatenate([one, one], axis=0)

    for g in range(group):
        head = slice(8 * g, 8 * g + 8)
        q_high, q_low = wide_halves(queries[head, :])
        k_high, k_low = wide_halves(whole_row(keys, 8 * g, 8))
        v_high, v_low = wide_halves(whole_row(values, 8 * g, 8))
        ones = jnp.ones_like(v_high)
        q_pack = stacked([q_high, q_high, q_low, q_low])
        k_pack = stacked([k_high, k_low, k_high, k_low])
        v_pack = stacked([v_high, v_low, ones, jnp.zeros_like(ones)])
        tops = [None] * strips
        for start in range(0, cols, chunk):
            part = slice(start, start + chunk)
            score[g, :, part] = dot(q_pack, k_pack[:, part], TN)
            for s in range(strips):
                line = pl.ds(s * STRIP, STRIP)
                own = id_column[line, :]
                for j in range(start, start + chunk, LANES):
                    tile = pl.ds(j, LANES)
                    value = score[g, line, tile]
                    squares[line, tile] += value * value
                    value = jnp.where(own == id_row[:, tile], pair[0, g, line, tile] + value, MASK_FILL)
                    score[g, line, tile] = value
                    tops[s] = value if tops[s] is None else jnp.maximum(tops[s], value)
        tops = [
            jnp.broadcast_to(jnp.max(top, axis=1, keepdims=True), (STRIP, LANES)) for top in tops
        ]
        totals = [None] * strips
        gathered = None
        for start in range(0, cols, chunk):
            part = slice(start, start + chunk)
            for s in range(strips):
                line = pl.ds(s * STRIP, STRIP)
                for j in range(start, start + chunk, LANES):
                    tile = pl.ds(j, LANES)
                    weight = jnp.exp(score[g, line, tile] - tops[s])
                    high[g, line, tile], low[g, line, tile] = halves(weight)
                    totals[s] = weight if totals[s] is None else totals[s] + weight
            term = dot(v_pack[:, part], high[g, :, part], NT) + dot(
                v_pack[:, part], low[g, :, part], NT
            )
            gathered = term if gathered is None else gathered + term
        for s in range(strips):
            total = jnp.sum(totals[s], axis=1, keepdims=True)
            log_sums[g, pl.ds(s * STRIP, STRIP), :] = tops[s] + jnp.log(total)
        mixed[head, :] = (gathered[0:8] + gathered[8:16]) / gathered[16:17]


def head_specs(kept_shape, feats, group):
    blocks, _, rows = kept_shape
    first = feats // (8 * group)
    return (
        pl.BlockSpec((blocks, 8 * group, rows), lambda h: (0, h, 0)),
        pl.BlockSpec((blocks, 8 * group, rows), lambda h: (0, first + h, 0)),
        pl.BlockSpec((blocks, 8, rows), lambda h: (0, 2 * feats // 8, 0)),
    )


def attend(pair, queries, kept, id_column):
    _, heads, rows, cols = pair.shape
    group = GROUP
    feats = heads * DH
    keys, values, ids = head_specs(kept.shape, feats, group)
    return pl.pallas_call(
        attend_kernel,
        grid=(heads // group,),
        in_specs=[
            pl.BlockSpec((1, group, rows, cols), lambda h: (0, h, 0, 0)),
            pl.BlockSpec((8 * group, rows), lambda h: (h, 0)),
            keys,
            values,
            ids,
            pl.BlockSpec((rows, LANES), lambda h: (0, 0)),
        ],
        out_specs=[
            pl.BlockSpec((8 * group, rows), lambda h: (h, 0)),
            pl.BlockSpec((group, rows, LANES), lambda h: (h, 0, 0)),
            pl.BlockSpec((rows, cols), lambda h: (0, 0)),
            pl.BlockSpec((STRIP, cols), lambda h: (0, 0)),
        ],
        out_shape=[
            jax.ShapeDtypeStruct((feats, rows), F32),
            jax.ShapeDtypeStruct((heads, rows, LANES), F32),
            jax.ShapeDtypeStruct((rows, cols), F32),
            jax.ShapeDtypeStruct((STRIP, cols), F32),
        ],
        scratch_shapes=[
            pltpu.VMEM((group, rows, cols), F32),
            pltpu.VMEM((group, rows, cols), BF16),
            pltpu.VMEM((group, rows, cols), BF16),
        ],
        compiler_params=pltpu.CompilerParams(vmem_limit_bytes=48 << 20),
        cost_estimate=pl.CostEstimate(
            flops=2 * 200 * heads * rows * cols,
            bytes_accessed=4 * heads * rows * cols,
            transcendentals=heads * rows * cols,
        ),
        name="attend",
    )(pair, queries, kept, kept, kept, id_column)


def attend_back_kernel(
    pair, cot, queries, keys, values, mixed, d_mixed, log_sums, id_column, id_row,
    out_pair, grad_pair, d_queries, d_keys, d_values, score, d_prob, p_high, p_low, g_high, g_low,
):
    group, rows, cols = score.shape
    blocks = d_keys.shape[0] * 2
    chunk = min(CHUNK, cols)
    place = lax.broadcasted_iota(jnp.int32, (8, rows), 0)

    def both(left, high, low, dims):
        value = dot(left, high, dims) + dot(left, low, dims)
        return value[0:8] + value[8:16]

    for g in range(group):
        head = slice(8 * g, 8 * g + 8)
        q_high, q_low = wide_halves(queries[head, :])
        k_high, k_low = wide_halves(whole_row(keys, 8 * g, 8))
        v_high, v_low = wide_halves(whole_row(values, 8 * g, 8))
        m_high, m_low = wide_halves(d_mixed[head, :])
        first = -column_sum(mixed[head, :] * d_mixed[head, :])
        delta_high, second = wide_halves(first)
        delta_mid, delta_low = wide_halves(second)
        deltas = jnp.where(
            place == 0, delta_high, jnp.where(place == 1, delta_mid, jnp.where(place == 2, delta_low, 0.0))
        )
        q_pack = stacked([q_high, q_high, q_low, q_low])
        k_pack = stacked([k_high, k_low, k_high, k_low])
        m_pack = stacked([m_high, m_high, m_low, deltas])
        v_pack = stacked([v_high, v_low, v_high, jnp.ones_like(v_high)])
        q_pair = stacked([q_high, q_low])
        k_pair = stacked([k_high, k_low])
        m_pair = stacked([m_high, m_low])
        d_query = None
        for start in range(0, cols, chunk):
            part = slice(start, start + chunk)
            score[g, :, part] = dot(q_pack, k_pack[:, part], TN)
            d_prob[g, :, part] = dot(m_pack, v_pack[:, part], TN)
            for s in range(rows // STRIP):
                line = pl.ds(s * STRIP, STRIP)
                own = id_column[line, :]
                log_sum = log_sums[g, line, :]
                for j in range(start, start + chunk, LANES):
                    tile = pl.ds(j, LANES)
                    value = pair[0, g, line, tile] + score[g, line, tile]
                    out_pair[0, g, line, tile] = value
                    prob = jnp.exp(jnp.where(own == id_row[:, tile], value - log_sum, MASK_FILL))
                    p_high[g, line, tile], p_low[g, line, tile] = halves(prob)
                    grad = prob * d_prob[g, line, tile] + cot[0, g, line, tile]
                    grad_pair[0, g, line, tile] = grad
                    g_high[g, line, tile], g_low[g, line, tile] = halves(grad)
            d_value = both(m_pair, p_high[g, :, part], p_low[g, :, part], NN)
            d_key = both(q_pair, g_high[g, :, part], g_low[g, :, part], NN)
            for n in range(start // rows, (start + chunk) // rows):
                span = slice(n * rows - start, (n + 1) * rows - start)
                d_keys[n // 2, n % 2, head, :] = d_key[:, span]
                d_values[n // 2, n % 2, head, :] = d_value[:, span]
            term = both(k_pair[:, part], g_high[g, :, part], g_low[g, :, part], NT)
            d_query = term if d_query is None else d_query + term
        d_queries[head, :] = d_query * (DH ** (-0.5))


def attend_back(pair, cot, queries, kept, mixed, d_mixed, log_sums, id_column, id_row):
    _, heads, rows, cols = pair.shape
    group = GROUP
    feats = heads * DH
    blocks = kept.shape[0]
    keys, values, _ = head_specs(kept.shape, feats, group)
    big = pl.BlockSpec((1, group, rows, cols), lambda h: (0, h, 0, 0))
    flat = pl.BlockSpec((8 * group, rows), lambda h: (h, 0))
    split = pl.BlockSpec((blocks // 2, 2, 8 * group, rows), lambda h: (0, 0, h, 0))
    return pl.pallas_call(
        attend_back_kernel,
        grid=(heads // group,),
        in_specs=[
            big, big, flat, keys, values, flat, flat,
            pl.BlockSpec((group, rows, LANES), lambda h: (h, 0, 0)),
            pl.BlockSpec((rows, LANES), lambda h: (0, 0)),
            pl.BlockSpec((STRIP, cols), lambda h: (0, 0)),
        ],
        out_specs=[big, big, flat, split, split],
        out_shape=[
            jax.ShapeDtypeStruct(pair.shape, F32),
            jax.ShapeDtypeStruct(pair.shape, F32),
            jax.ShapeDtypeStruct((feats, rows), F32),
            jax.ShapeDtypeStruct((blocks // 2, 2, feats, rows), F32),
            jax.ShapeDtypeStruct((blocks // 2, 2, feats, rows), F32),
        ],
        scratch_shapes=[pltpu.VMEM((group, rows, cols), F32)] * 2
        + [pltpu.VMEM((group, rows, cols), BF16)] * 4,
        compiler_params=pltpu.CompilerParams(vmem_limit_bytes=56 << 20),
        cost_estimate=pl.CostEstimate(
            flops=2 * 400 * heads * rows * cols,
            bytes_accessed=16 * heads * rows * cols,
            transcendentals=heads * rows * cols,
        ),
        name="attend_back",
    )(pair, cot, queries, kept, kept, mixed, d_mixed, log_sums, id_column, id_row)


SMALL_LN1_GAIN, SMALL_LN1_BIAS, SMALL_LN2_GAIN, SMALL_LN2_BIAS = 0, 1, 2, 3
SMALL_B_OUT, SMALL_B_DOWN, SMALL_PENALTY = 4, 5, 6
SMALL_B_QUERY, SMALL_B_VALUE, SMALL_B_UP = 8, 9, 10
SMALL_ROWS = 16


def team_device(team, core, chips):
    return {"dp": lax.div(team, chips), "blk": lax.rem(team, chips) * 2 + core}


def feed_kernel(operands, results, scratch):
    mixed, cot, w_down, atoms, w_up, w_out, b_out, gain, bias, b_up = operands
    d_mixed, hidden, down, d_hidden, grad_share, small = results
    (
        mixed_all, normal_two, rate_two, part, landed, back, back_landed, grads, sib_grads, go_grads, got_grads,
        mix_send, mix_recv, part_send, part_recv, back_send, back_recv, sib_send, sib_recv, g_send, g_recv,
    ) = scratch
    zs, feats, rows = mixed_all.shape
    teams, _, share, width = grads.shape
    chips = teams // lax.axis_size("dp")
    piece = rows // zs
    z, blk = lax.axis_index("head"), lax.axis_index("blk")
    core, chip = lax.rem(blk, 2), lax.div(blk, 2)
    team = lax.axis_index("dp") * chips + chip
    sibling = {"blk": blk + 1 - 2 * core}
    peers, far_teams = others(z, zs), others(team, teams)
    meet([{"head": peer} for peer in peers] + [sibling] + [team_device(peer, core, chips) for peer in far_teams])
    copies = [
        send(mixed.source, mixed_all.at[z], mix_send.at[n], mix_recv.at[z], {"head": peer})
        for n, peer in enumerate(peers)
    ]
    mine = pl.ds(pl.multiple_of(z * piece, 8), piece)
    small[...] = jnp.zeros(small.shape, F32)
    small[SMALL_B_DOWN : SMALL_B_DOWN + 1, :] = column_sum(cot[mine, :])
    cots = halves(cot[...])
    downs = halves(w_down[...])
    d_act = dot_halves(cots, downs, NT)
    ups = halves(w_up[...])
    outs = halves(w_out[...])
    mixed_all[z] = mixed[...]
    for peer in peers:
        arrived(mixed_all.at[peer], mix_recv.at[peer])
    mixed_rows = mixed_all[...].reshape(zs * feats, rows).T
    hidden_rows = atoms[...] + dot_halves(halves(mixed_rows), outs) + b_out[...]
    hidden[...] = hidden_rows
    hidden.flush()
    normal, rate = normalize(hidden_rows)
    normal_two[...] = normal
    rate_two[...] = jnp.broadcast_to(rate, rate_two.shape)
    normed = normal * gain[...] + bias[...]
    pre = dot_halves(halves(normed), ups) + b_up[...]
    phi = 0.5 * (1.0 + lax.erf(pre * math.sqrt(0.5)))
    act = pre * phi
    d_pre = d_act * (phi + pre * jnp.exp(-0.5 * pre * pre) * (1.0 / math.sqrt(2.0 * math.pi)))
    d_pres = halves(d_pre)
    part[...] = dot_halves(d_pres, ups, NT).reshape(zs, piece, width)
    copies += [
        send(part.at[peer], landed.at[z], part_send.at[n], part_recv.at[z], {"head": peer})
        for n, peer in enumerate(peers)
    ]
    landed[z] = part[z]
    grad_up = dot_halves(halves(d_pre.T), halves(normed))
    grad_down = dot_halves(halves(act.T), cots)
    grads[...] = jnp.concatenate([grad_up, grad_down], axis=0).reshape(grads.shape)
    copies.append(send(grads.at[:, 1 - core], sib_grads, sib_send.at[0], sib_recv.at[0], sibling))
    down[...] = dot_halves(halves(act), downs)
    down.flush()
    small[SMALL_B_UP : SMALL_B_UP + 1, 0 : d_pre.shape[1]] = column_sum(d_pre)
    arrived(sib_grads, sib_recv.at[0])
    go_grads[...] = sib_grads[...] + grads[:, core]
    copies += [
        send(
            go_grads.at[peer], got_grads.at[team], g_send.at[n], g_recv.at[team], team_device(peer, core, chips)
        )
        for n, peer in enumerate(far_teams)
    ]
    got_grads[team] = go_grads[team]
    for peer in peers:
        arrived(landed.at[peer], part_recv.at[peer])
    d_normed = functools.reduce(jnp.add, [landed[n] for n in range(zs)])
    normal = normal_two[mine, :]
    d_rows = cot[mine, :] + normalize_back(d_normed, gain[...], normal, rate_two[mine, 0:1])
    d_halves = halves(d_rows)
    for n in range(zs):
        some = slice(n * feats, (n + 1) * feats)
        back[n] = dot_halves(d_halves, (outs[0][some], outs[1][some]), NT)
    copies += [
        send(back.at[peer], back_landed.at[z], back_send.at[n], back_recv.at[z], {"head": peer})
        for n, peer in enumerate(peers)
    ]
    back_landed[z] = back[z]
    d_hidden[...] = d_rows
    d_hidden.flush()
    small[SMALL_LN2_GAIN : SMALL_LN2_GAIN + 1, :] = column_sum(d_normed * normal)
    small[SMALL_LN2_BIAS : SMALL_LN2_BIAS + 1, :] = column_sum(d_normed)
    small[SMALL_B_OUT : SMALL_B_OUT + 1, :] = column_sum(d_rows)
    small.flush()
    for peer in peers:
        arrived(back_landed.at[peer], back_recv.at[peer])
    d_mixed[...] = back_landed[...].reshape(rows, feats).T
    d_mixed.flush()
    for peer in far_teams:
        arrived(got_grads.at[peer], g_recv.at[peer])
    grad_share[...] = functools.reduce(jnp.add, [got_grads[n] for n in range(teams)])
    for copy in copies:
        copy.wait_send()


def feed(zs, teams, *operands):
    feats, rows = operands[0].shape
    width, units = operands[4].shape
    piece = rows // zs
    share = units // teams
    slab = pltpu.VMEM((zs, piece, width), F32)
    narrow = pltpu.VMEM((zs, piece, feats), F32)
    one = pltpu.VMEM((teams, share, width), F32)
    dma = pltpu.SemaphoreType.DMA
    return staged_call(
        feed_kernel,
        "feed",
        operands,
        [(feats, rows), (rows, width), (rows, width), (piece, width), (share, width), (SMALL_ROWS, width)],
        [
            pltpu.VMEM((zs, feats, rows), F32),
            pltpu.VMEM((rows, width), F32),
            pltpu.VMEM((rows, LANES), F32),
            slab, slab, narrow, narrow,
            pltpu.VMEM((teams, 2, share, width), F32),
            one, one, one,
        ]
        + [dma((zs,))] * 6
        + [dma((1,)), dma((1,)), dma((teams,)), dma((teams,))],
        56,
        remote=1,
    )


def finish_kernel(operands, results, scratch):
    (
        d_keys, d_values, d_hidden, share_in, d_queries, atoms, gain, bias, w_query, mixed, squares, id_column,
        id_row, small_in, w_key, w_value,
    ) = operands
    grad_atoms, total_grads, total_big, small, penalty = results
    (
        sib_keys, sib_values, go_keys, go_values, got_keys, got_values,
        part, landed, grads, sib_grads, go_grads, got_grads, hidden_all, small_z, small_all,
        sib_send, sib_recv, kv_send, kv_recv, part_send, part_recv, back_send, back_recv,
        g_send, g_recv, t_send, t_recv, f_send, b_send, b_recv, bf_send, h_send, h_recv,
        small_z_send, small_z_recv, small_send, small_recv,
    ) = scratch
    chips, _, feats, rows = d_keys.shape
    zs, piece, width = part.shape
    teams, _, share, _ = grads.shape
    blk, z, dp = lax.axis_index("blk"), lax.axis_index("head"), lax.axis_index("dp")
    core, chip = lax.rem(blk, 2), lax.div(blk, 2)
    other_core = 1 - core
    sibling = {"blk": blk + 1 - 2 * core}
    peers = others(z, zs)
    team = dp * chips + chip
    far_teams = others(team, teams)
    far_chips = others(chip, chips)
    place = team * 2 + core
    far_places = others(place, teams * 2)
    plane = [team_device(lax.div(value, 2), lax.rem(value, 2), chips) for value in far_places]
    meet([{"head": peer} for peer in peers] + plane)
    copies = [
        send(d_keys.source.at[:, other_core], sib_keys, sib_send.at[0], sib_recv.at[0], sibling),
        send(d_values.source.at[:, other_core], sib_values, sib_send.at[1], sib_recv.at[1], sibling),
    ]
    copies += [
        send(d_hidden.source, hidden_all.at[z], h_send.at[n], h_recv.at[z], {"head": peer})
        for n, peer in enumerate(peers)
    ]
    own_keys, own_values = d_keys.ref, d_values.ref
    arrived(sib_keys, sib_recv.at[0])
    arrived(sib_values, sib_recv.at[1])
    go_keys[...] = sib_keys[...] + own_keys[:, core]
    go_values[...] = sib_values[...] + own_values[:, core]
    for n, peer in enumerate(far_chips):
        target = {"blk": peer * 2 + core}
        copies.append(send(go_keys.at[peer], got_keys.at[chip], kv_send.at[0, n], kv_recv.at[0, chip], target))
        copies.append(
            send(go_values.at[peer], got_values.at[chip], kv_send.at[1, n], kv_recv.at[1, chip], target)
        )
    got_keys[chip] = go_keys[chip]
    got_values[chip] = go_values[chip]
    total_big[team, core] = share_in[...]
    ready = total_big.at[team, core]
    copies.append(send(ready, ready, b_send.at[0], b_recv.at[team, core], sibling))
    copies += [
        send(ready, ready, b_send.at[n + 1], b_recv.at[team, core], team_device(peer, core, chips))
        for n, peer in enumerate(far_teams)
    ]
    normal, rate = normalize(atoms[...])
    normed = halves(normal * gain[...] + bias[...])
    dq_rows = d_queries[...].T
    d_normed = dot_full(dq_rows, w_query[...], NT)
    grad_q = dot_halves(halves(d_queries[...]), normed)
    mine = pl.ds(pl.multiple_of(z * piece, 8), piece)
    own = id_column[mine, 0:1]
    same = own == id_row[0:1, :]
    norms = jnp.sqrt(squares[...] + 1.0)
    terms = jnp.where(same, jnp.log1p(jnp.exp(norms - math.sqrt(zs * feats // DH))), 0.0)
    number = jnp.where(same, 1.0, 0.0)

    def total(value):
        return jnp.sum(jnp.sum(value, axis=1, keepdims=True), axis=0, keepdims=True)

    lane = lax.broadcasted_iota(jnp.int32, (1, width), 1)
    small_z[z] = small_in[0:8, :]
    small_z[z, SMALL_PENALTY : SMALL_PENALTY + 1, :] = jnp.where(
        lane == 0, total(terms), jnp.where(lane == 1, total(number), 0.0)
    )
    hidden_all[z] = d_hidden[...]
    for peer in far_chips:
        arrived(got_keys.at[peer], kv_recv.at[0, peer])
        arrived(got_values.at[peer], kv_recv.at[1, peer])
    dk = functools.reduce(jnp.add, [got_keys[n] for n in range(chips)])
    dv = functools.reduce(jnp.add, [got_values[n] for n in range(chips)])
    dv_rows = dv.T
    d_normed = (
        d_normed + dot_full(dk.T, w_key[...], NT) + dot_full(dv_rows, w_value[...], NT)
    )
    part[...] = d_normed.reshape(zs, piece, width)
    copies += [
        send(part.at[peer], landed.at[z], part_send.at[n], part_recv.at[z], {"head": peer})
        for n, peer in enumerate(peers)
    ]
    landed[z] = part[z]
    grad_k = dot_halves(halves(dk), normed)
    grad_v = dot_halves(halves(dv), normed)
    for peer in peers:
        arrived(hidden_all.at[peer], h_recv.at[peer])
    grad_o = dot_full(mixed[...], hidden_all[...].reshape(rows, width))
    grads[...] = jnp.concatenate([grad_q, grad_k, grad_v, grad_o], axis=0).reshape(grads.shape)
    copies.append(send(grads.at[:, other_core], sib_grads, sib_send.at[2], sib_recv.at[2], sibling))
    arrived(sib_grads, sib_recv.at[2])
    go_grads[...] = sib_grads[...] + grads[:, core]
    copies += [
        send(
            go_grads.at[peer], got_grads.at[team], g_send.at[n], g_recv.at[team], team_device(peer, core, chips)
        )
        for n, peer in enumerate(far_teams)
    ]
    got_grads[team] = go_grads[team]
    for peer in peers:
        arrived(landed.at[peer], part_recv.at[peer])
    d_normed = functools.reduce(jnp.add, [landed[n] for n in range(zs)])
    normal, rate = normalize(atoms[mine, :])
    grad_atoms[mine, :] = d_hidden[...] + normalize_back(d_normed, gain[...], normal, rate)
    small_z[z, SMALL_LN1_GAIN : SMALL_LN1_GAIN + 1, :] = column_sum(d_normed * normal)
    small_z[z, SMALL_LN1_BIAS : SMALL_LN1_BIAS + 1, :] = column_sum(d_normed)
    copies += [
        send(small_z.at[z], small_z.at[z], small_z_send.at[n], small_z_recv.at[z], {"head": peer})
        for n, peer in enumerate(peers)
    ]
    copies += [
        send(grad_atoms.at[mine], grad_atoms.at[mine], back_send.at[n], back_recv.at[z], {"head": peer})
        for n, peer in enumerate(peers)
    ]
    for peer in far_teams:
        arrived(got_grads.at[peer], g_recv.at[peer])
    total_grads[team, core] = functools.reduce(jnp.add, [got_grads[n] for n in range(teams)])
    ready = total_grads.at[team, core]
    copies.append(send(ready, ready, t_send.at[0], t_recv.at[team, core], sibling))
    copies += [
        send(ready, ready, t_send.at[n + 1], t_recv.at[team, core], team_device(peer, core, chips))
        for n, peer in enumerate(far_teams)
    ]
    for peer in peers:
        arrived(small_z.at[peer], small_z_recv.at[peer])
    small_all[place, 0:8, :] = functools.reduce(jnp.add, [small_z[n] for n in range(zs)])
    small_all[place, 8:16, :] = small_in[8:16, :]
    small_all[place, SMALL_B_QUERY : SMALL_B_QUERY + 1, 0:feats] = column_sum(dq_rows)
    small_all[place, SMALL_B_VALUE : SMALL_B_VALUE + 1, 0:feats] = column_sum(dv_rows)
    copies += [
        send(small_all.at[place], small_all.at[place], small_send.at[n], small_recv.at[place], target)
        for n, target in enumerate(plane)
    ]
    for n, peer in enumerate(far_teams):
        ready = total_big.at[peer, core]
        arrived(ready, b_recv.at[peer, core])
        copies.append(send(ready, ready, bf_send.at[n], b_recv.at[peer, core], sibling))
    for n, peer in enumerate(far_teams):
        ready = total_grads.at[peer, core]
        arrived(ready, t_recv.at[peer, core])
        copies.append(send(ready, ready, f_send.at[n], t_recv.at[peer, core], sibling))
    for source in far_places:
        arrived(small_all.at[source], small_recv.at[source])
    summed = functools.reduce(jnp.add, [small_all[n] for n in range(2 * teams)])
    small[...] = summed
    ends = summed[SMALL_PENALTY : SMALL_PENALTY + 1, :]
    penalty[...] = ends[:, 0:1] / ends[:, 1:2]
    for peer in [team] + far_teams:
        arrived(total_big.at[peer, other_core], b_recv.at[peer, other_core])
    total_big.flush()
    for peer in [team] + far_teams:
        arrived(total_grads.at[peer, other_core], t_recv.at[peer, other_core])
    total_grads.flush()
    for peer in peers:
        there = pl.ds(pl.multiple_of(peer * piece, 8), piece)
        arrived(grad_atoms.at[there], back_recv.at[peer])
    for copy in copies:
        copy.wait_send()


def finish(zs, dps, *operands):
    d_keys, share_in, atoms = operands[0], operands[3], operands[5]
    chips, _, feats, rows = d_keys.shape
    width = atoms.shape[1]
    piece = rows // zs
    teams = dps * chips
    share = 4 * feats // (2 * teams)
    some = pltpu.VMEM((chips, feats, rows), F32)
    slab = pltpu.VMEM((zs, piece, width), F32)
    one = pltpu.VMEM((teams, share, width), F32)
    dma = pltpu.SemaphoreType.DMA
    return staged_call(
        finish_kernel,
        "finish",
        operands,
        [
            (rows, width),
            (teams, 2, share, width),
            (teams, 2) + share_in.shape,
            (SMALL_ROWS, width),
            (1, 1),
        ],
        [some] * 6
        + [slab, slab, pltpu.VMEM((teams, 2, share, width), F32), one, one, one, slab]
        + [
            pltpu.VMEM((zs, 8, width), F32),
            pltpu.VMEM((2 * teams, SMALL_ROWS, width), F32),
            dma((3,)), dma((3,)),
            dma((2, chips)), dma((2, chips)),
            dma((zs,)), dma((zs,)),
            dma((zs,)), dma((zs,)),
            dma((teams,)), dma((teams,)),
            dma((teams,)), dma((teams, 2)), dma((teams,)),
            dma((teams,)), dma((teams, 2)), dma((teams,)),
            dma((zs,)), dma((zs,)),
            dma((zs,)), dma((zs,)),
            dma((2 * teams,)), dma((2 * teams,)),
        ],
        58,
        remote=2,
    )


def place_kernel(operands, results, scratch):
    total_grads, total_big, small, hidden, down, b_down, rows_in = operands
    grad_query, grad_key, grad_value, grad_out, grad_up, grad_down, out_atoms, grad_atoms = results[:8]
    feats, units = grad_out.shape[0], grad_down.shape[0]
    width = grad_out.shape[1]
    grad_atoms[...] = rows_in[...]
    grad_atoms.flush()
    done = total_grads[...].reshape(4 * feats, width)
    grad_query[...] = done[0:feats].T
    grad_query.flush()
    grad_key[...] = done[feats : 2 * feats].T
    grad_key.flush()
    grad_value[...] = done[2 * feats : 3 * feats].T
    grad_value.flush()
    grad_out[...] = done[3 * feats :]
    grad_out.flush()
    done = total_big[...].reshape(2 * units, width)
    grad_up[...] = done[0:units].T
    grad_up.flush()
    grad_down[...] = done[units:]
    grad_down.flush()
    out_atoms[...] = hidden[...] + down[...] + b_down[...]
    out_atoms.flush()
    for result, row in zip(results[8:], SMALL_OUTPUTS, strict=True):
        result[...] = small[row : row + 1, 0 : result.shape[1]]


SMALL_OUTPUTS = (
    SMALL_LN1_GAIN, SMALL_LN1_BIAS, SMALL_B_QUERY, SMALL_B_VALUE, SMALL_B_OUT, SMALL_LN2_GAIN, SMALL_LN2_BIAS,
    SMALL_B_UP, SMALL_B_DOWN,
)


def place(feats, units, *operands):
    rows, width = operands[3].shape
    lengths = {SMALL_B_QUERY: feats, SMALL_B_VALUE: feats, SMALL_B_UP: units}
    return staged_call(
        place_kernel,
        "place",
        operands,
        [(width, feats)] * 3
        + [(feats, width), (width, units), (units, width), (rows, width), (rows, width)]
        + [(1, lengths.get(row, width)) for row in SMALL_OUTPUTS],
        [],
        32,
    )


def local(
    zs, dps,
    atoms, pair, mol_ids, ln1_gain, ln1_bias, w_query, b_query, w_key, w_value, b_value, w_out, b_out,
    ln2_gain, ln2_bias, w_up, b_up, w_down, b_down, cot_atoms, cot_pair,
):
    blocks = pair.shape[3] // pair.shape[2]
    inputs, cot = atoms[0], cot_atoms[0]

    def line(value):
        return value.reshape(1, -1)

    queries, kept, id_column = project(
        blocks, inputs, mol_ids, line(ln1_gain), line(ln1_bias), w_key, w_value, line(b_value), w_query,
        line(b_query),
    )
    w_out_all = lax.all_gather(w_out, "head", axis=0, tiled=True)
    mixed, log_sums, squares, id_row = attend(pair, queries, kept, id_column)
    d_mixed, hidden, down, d_hidden, grad_share, small = feed(
        zs, dps * blocks // 2,
        mixed, cot, w_down, inputs, w_up, w_out_all, line(b_out), line(ln2_gain), line(ln2_bias), line(b_up),
    )
    squares, d_mixed = lax.optimization_barrier((squares, d_mixed))
    squares = lax.psum_scatter(squares, "head", scatter_dimension=0, tiled=True)
    down = lax.psum(down, "head")
    out_pair, grad_pair, d_queries, d_keys, d_values = attend_back(
        pair, cot_pair, queries, kept, mixed, d_mixed, log_sums, id_column, id_row
    )
    grad_atoms, total_grads, total_big, small, penalty = finish(
        zs, dps,
        d_keys, d_values, d_hidden, grad_share, d_queries, inputs, line(ln1_gain), line(ln1_bias), w_query, mixed,
        squares, id_column, id_row, small, w_key, w_value,
    )
    placed = place(
        w_query.shape[1], w_up.shape[1],
        total_grads, total_big, small, hidden, down, line(b_down), grad_atoms,
    )
    grad_query, grad_key, grad_value, grad_out, grad_up, grad_down, out_atoms, grad_atoms = placed[:8]
    (
        grad_ln1_gain, grad_ln1_bias, grad_b_query, grad_b_value, grad_b_out, grad_ln2_gain, grad_ln2_bias,
        grad_b_up, grad_b_down,
    ) = [value.reshape(-1) for value in placed[8:]]
    return (
        out_atoms[None],
        out_pair,
        penalty[0, 0],
        grad_atoms[None],
        grad_pair,
        grad_ln1_gain,
        grad_ln1_bias,
        grad_query,
        grad_b_query,
        grad_key,
        grad_value,
        grad_b_value,
        grad_out,
        grad_b_out,
        grad_ln2_gain,
        grad_ln2_bias,
        grad_up,
        grad_b_up,
        grad_down,
        grad_b_down,
    )


def solution(mesh):
    rows, pairs = P("dp", "blk", None), P("dp", "head", "blk", None)
    columns = P(None, "head")
    return jax.shard_map(
        functools.partial(local, mesh.shape["head"], mesh.shape["dp"]),
        mesh=mesh,
        in_specs=(
            rows, pairs, P("dp", "blk"), P(), P(), columns, P("head"), columns, columns, P("head"),
            P("head", None), P(), P(), P(), columns, P("head"), P("head", None), P(), rows, pairs,
        ),
        out_specs=(
            rows, pairs, P(), rows, pairs, P(), P(), columns, P("head"), columns, columns, P("head"),
            P("head", None), P(), P(), P(), columns, P("head"), P("head", None), P(),
        ),
        check_vma=False,
    )
```

```python
import functools
import math

import jax
import jax.numpy as jnp
from jax import lax
from jax.experimental import pallas as pl
from jax.experimental.pallas import tpu as pltpu
from jax.sharding import PartitionSpec as P

DH = 8
LANES = 128
STRIP = 16
CHUNK = 256
GROUP = 2
NORM_EPS = 1e-05
MASK_FILL = -1e30
F32 = jnp.float32
BF16 = jnp.bfloat16
MESH = pl.DeviceIdType.MESH
NN = (((1,), (0,)), ((), ()))
NT = (((1,), (1,)), ((), ()))
TN = (((0,), (0,)), ((), ()))
VMEM = pl.BlockSpec(memory_space=pltpu.VMEM)


def dot(left, right, dims=NN):
    return lax.dot_general(left, right, dims, preferred_element_type=F32)


def halves(value):
    high = value.astype(BF16)
    return high, (value - high.astype(F32)).astype(BF16)


def dot_halves(left, right, dims=NN):
    return dot(left[0], right[0], dims) + (
        dot(left[0], right[1], dims) + dot(left[1], right[0], dims)
    )


def dot_full(left, right, dims=NN):
    return dot_halves(halves(left), halves(right), dims)


def normalize(inputs):
    centred = inputs - jnp.mean(inputs, -1, keepdims=True)
    rate = lax.rsqrt(jnp.mean(centred * centred, -1, keepdims=True) + NORM_EPS)
    return centred * rate, rate


def normalize_back(grad, gain, normal, rate):
    scaled = grad * gain
    return rate * (
        scaled
        - jnp.mean(scaled, -1, keepdims=True)
        - normal * jnp.mean(scaled * normal, -1, keepdims=True)
    )


def column_sum(value):
    return jnp.sum(value, 0, keepdims=True)


def send(src, dst, send_sem, recv_sem, target):
    copy = pltpu.make_async_remote_copy(
        src_ref=src,
        dst_ref=dst,
        send_sem=send_sem,
        recv_sem=recv_sem,
        device_id=target,
        device_id_type=MESH,
    )
    copy.start()
    return copy


def arrived(ref, sem):
    pltpu.make_async_remote_copy(
        src_ref=ref, dst_ref=ref, send_sem=sem, recv_sem=sem, device_id={}, device_id_type=MESH
    ).wait_recv()


def greet(targets):
    for target in targets:
        pl.semaphore_signal(pltpu.get_barrier_semaphore(), inc=1, device_id=target, device_id_type=MESH)


def meet(targets):
    pl.semaphore_wait(pltpu.get_barrier_semaphore(), len(targets))


def others(index, count):
    return [lax.rem(index + step, count) for step in range(1, count)]


class Operand:
    def __init__(self, source, slot, sem):
        self.source, self.slot, self.shape = source, slot, slot.shape
        self.copy = pltpu.make_async_copy(source, slot, sem)
        self.copy.start()

    @property
    def ref(self):
        if self.copy is not None:
            self.copy.wait()
            self.copy = None
        return self.slot

    def __getitem__(self, index):
        return self.ref[index]


class Result:
    def __init__(self, target, slot, sem):
        self.slot, self.shape, self.at = slot, slot.shape, slot.at
        self.copy = pltpu.make_async_copy(slot, target, sem)
        self.begun = False

    def __setitem__(self, index, value):
        self.slot[index] = value

    def __getitem__(self, index):
        return self.slot[index]

    def flush(self):
        if not self.begun:
            self.copy.start()
            self.begun = True


def staged_call(kernel, name, operands, results, scratch, megabytes, remote=None, raw=()):
    n_in, n_out, n_raw = len(operands), len(results), len(raw)

    def body(*refs):
        sources, left, refs = refs[:n_in], refs[n_in : n_in + n_raw], refs[n_in + n_raw :]
        targets, refs = refs[:n_out], refs[n_out:]
        slots, made, refs = refs[:n_in], refs[n_in : n_in + n_out], refs[n_in + n_out :]
        in_sem, out_sem, refs = refs[0], refs[1], refs[2:]
        ins = [Operand(sources[n], slots[n], in_sem.at[n]) for n in range(n_in)]
        outs = [Result(targets[n], made[n], out_sem.at[n]) for n in range(n_out)]
        kernel(ins, outs, refs, left)
        for operand in ins:
            operand.ref
        for result in outs:
            result.flush()
        for result in outs:
            result.copy.wait()

    anywhere = pl.BlockSpec(memory_space=pltpu.HBM)
    extra = {} if remote is None else {"collective_id": remote, "has_side_effects": True}
    return pl.pallas_call(
        body,
        out_shape=[jax.ShapeDtypeStruct(shape, F32) for shape in results],
        in_specs=[anywhere] * (n_in + n_raw),
        out_specs=[anywhere] * n_out,
        scratch_shapes=[pltpu.VMEM(value.shape, value.dtype) for value in operands]
        + [pltpu.VMEM(shape, F32) for shape in results]
        + [pltpu.SemaphoreType.DMA((n_in,)), pltpu.SemaphoreType.DMA((n_out,))]
        + list(scratch),
        compiler_params=pltpu.CompilerParams(vmem_limit_bytes=megabytes << 20, **extra),
        name=name,
    )(*operands, *raw)


def whole_row(ref, low, count):
    return jnp.concatenate([ref[n, low : low + count, :] for n in range(ref.shape[0])], axis=1)


def joined(pieces):
    return jnp.concatenate(list(pieces), axis=1)


def stacked(parts):
    return jnp.concatenate(parts, axis=0).astype(BF16)


def wide_halves(value):
    high = value.astype(BF16).astype(F32)
    return high, value - high


def attend_group(pair, queries, keys, values, id_column, id_row, log_sums, first, score, high, low):
    group, rows, cols = score.shape
    strips = rows // STRIP
    chunk = min(CHUNK, cols)
    mixed = []
    for g in range(group):
        head = slice(8 * g, 8 * g + 8)
        q_high, q_low = wide_halves(queries[head, :])
        k_high, k_low = wide_halves(keys[head, :])
        v_high, v_low = wide_halves(values[head, :])
        ones = jnp.ones_like(v_high)
        q_pack = stacked([q_high, q_high, q_low, q_low])
        k_pack = stacked([k_high, k_low, k_high, k_low])
        v_pack = stacked([v_high, v_low, ones, jnp.zeros_like(ones)])
        tops = [None] * strips
        for start in range(0, cols, chunk):
            part = slice(start, start + chunk)
            score[g, :, part] = dot(q_pack, k_pack[:, part], TN)
            for s in range(strips):
                line = pl.ds(s * STRIP, STRIP)
                own = id_column[line, :]
                for j in range(start, start + chunk, LANES):
                    tile = pl.ds(j, LANES)
                    value = pair[g, line, tile] + score[g, line, tile]
                    value = jnp.where(own == id_row[:, tile], value, MASK_FILL)
                    score[g, line, tile] = value
                    tops[s] = value if tops[s] is None else jnp.maximum(tops[s], value)
        tops = [
            jnp.broadcast_to(jnp.max(top, axis=1, keepdims=True), (STRIP, LANES)) for top in tops
        ]
        totals = [None] * strips
        gathered = None
        for start in range(0, cols, chunk):
            part = slice(start, start + chunk)
            for s in range(strips):
                line = pl.ds(s * STRIP, STRIP)
                for j in range(start, start + chunk, LANES):
                    tile = pl.ds(j, LANES)
                    weight = jnp.exp(score[g, line, tile] - tops[s])
                    high[g, line, tile], low[g, line, tile] = halves(weight)
                    totals[s] = weight if totals[s] is None else totals[s] + weight
            term = dot(v_pack[:, part], high[g, :, part], NT) + dot(
                v_pack[:, part], low[g, :, part], NT
            )
            gathered = term if gathered is None else gathered + term
        for s in range(strips):
            total = jnp.sum(totals[s], axis=1, keepdims=True)
            log_sums[first + g, pl.ds(s * STRIP, STRIP), :] = tops[s] + jnp.log(total)
        mixed.append((gathered[0:8] + gathered[8:16]) / gathered[16:17])
    return jnp.concatenate(mixed, axis=0)


def head_specs(kept_shape, feats, group):
    blocks, _, rows = kept_shape
    first = feats // (8 * group)
    return (
        pl.BlockSpec((blocks, 8 * group, rows), lambda h: (0, h, 0)),
        pl.BlockSpec((blocks, 8 * group, rows), lambda h: (0, first + h, 0)),
        pl.BlockSpec((blocks, 8, rows), lambda h: (0, 2 * feats // 8, 0)),
    )


def attend_back_kernel(
    pair, cot, queries, keys, values, mixed, d_mixed, log_sums, id_column, id_row,
    out_pair, grad_pair, d_queries, d_keys, d_values, score, d_prob, p_high, p_low, g_high, g_low,
):
    group, rows, cols = score.shape
    blocks = d_keys.shape[0] * 2
    chunk = min(CHUNK, cols)
    place = lax.broadcasted_iota(jnp.int32, (8, rows), 0)

    def both(left, high, low, dims):
        value = dot(left, high, dims) + dot(left, low, dims)
        return value[0:8] + value[8:16]

    for g in range(group):
        head = slice(8 * g, 8 * g + 8)
        q_high, q_low = wide_halves(queries[head, :])
        k_high, k_low = wide_halves(whole_row(keys, 8 * g, 8))
        v_high, v_low = wide_halves(whole_row(values, 8 * g, 8))
        m_high, m_low = wide_halves(d_mixed[head, :])
        first = -column_sum(mixed[head, :] * d_mixed[head, :])
        delta_high, second = wide_halves(first)
        delta_mid, delta_low = wide_halves(second)
        deltas = jnp.where(
            place == 0, delta_high, jnp.where(place == 1, delta_mid, jnp.where(place == 2, delta_low, 0.0))
        )
        q_pack = stacked([q_high, q_high, q_low, q_low])
        k_pack = stacked([k_high, k_low, k_high, k_low])
        m_pack = stacked([m_high, m_high, m_low, deltas])
        v_pack = stacked([v_high, v_low, v_high, jnp.ones_like(v_high)])
        q_pair = stacked([q_high, q_low])
        k_pair = stacked([k_high, k_low])
        m_pair = stacked([m_high, m_low])
        d_query = None
        for start in range(0, cols, chunk):
            part = slice(start, start + chunk)
            score[g, :, part] = dot(q_pack, k_pack[:, part], TN)
            d_prob[g, :, part] = dot(m_pack, v_pack[:, part], TN)
            for s in range(rows // STRIP):
                line = pl.ds(s * STRIP, STRIP)
                own = id_column[line, :]
                log_sum = log_sums[g, line, :]
                for j in range(start, start + chunk, LANES):
                    tile = pl.ds(j, LANES)
                    value = pair[0, g, line, tile] + score[g, line, tile]
                    out_pair[0, g, line, tile] = value
                    prob = jnp.exp(jnp.where(own == id_row[:, tile], value - log_sum, MASK_FILL))
                    p_high[g, line, tile], p_low[g, line, tile] = halves(prob)
                    grad = prob * d_prob[g, line, tile] + cot[0, g, line, tile]
                    grad_pair[0, g, line, tile] = grad
                    g_high[g, line, tile], g_low[g, line, tile] = halves(grad)
            d_value = both(m_pair, p_high[g, :, part], p_low[g, :, part], NN)
            d_key = both(q_pair, g_high[g, :, part], g_low[g, :, part], NN)
            for n in range(start // rows, (start + chunk) // rows):
                span = slice(n * rows - start, (n + 1) * rows - start)
                d_keys[n // 2, n % 2, head, :] = d_key[:, span]
                d_values[n // 2, n % 2, head, :] = d_value[:, span]
            term = both(k_pair[:, part], g_high[g, :, part], g_low[g, :, part], NT)
            d_query = term if d_query is None else d_query + term
        d_queries[head, :] = d_query * (DH ** (-0.5))


def attend_back(pair, cot, queries, kept, mixed, d_mixed, log_sums, id_column, id_row):
    _, heads, rows, cols = pair.shape
    group = GROUP
    feats = heads * DH
    blocks = kept.shape[0]
    keys, values, _ = head_specs(kept.shape, feats, group)
    big = pl.BlockSpec((1, group, rows, cols), lambda h: (0, h, 0, 0))
    flat = pl.BlockSpec((8 * group, rows), lambda h: (h, 0))
    split = pl.BlockSpec((blocks // 2, 2, 8 * group, rows), lambda h: (0, 0, h, 0))
    return pl.pallas_call(
        attend_back_kernel,
        grid=(heads // group,),
        in_specs=[
            big, big, flat, keys, values, flat, flat,
            pl.BlockSpec((group, rows, LANES), lambda h: (h, 0, 0)),
            pl.BlockSpec((rows, LANES), lambda h: (0, 0)),
            pl.BlockSpec((STRIP, cols), lambda h: (0, 0)),
        ],
        out_specs=[big, big, flat, split, split],
        out_shape=[
            jax.ShapeDtypeStruct(pair.shape, F32),
            jax.ShapeDtypeStruct(pair.shape, F32),
            jax.ShapeDtypeStruct((feats, rows), F32),
            jax.ShapeDtypeStruct((blocks // 2, 2, feats, rows), F32),
            jax.ShapeDtypeStruct((blocks // 2, 2, feats, rows), F32),
        ],
        scratch_shapes=[pltpu.VMEM((group, rows, cols), F32)] * 2
        + [pltpu.VMEM((group, rows, cols), BF16)] * 4,
        compiler_params=pltpu.CompilerParams(vmem_limit_bytes=56 << 20),
        cost_estimate=pl.CostEstimate(
            flops=2 * 400 * heads * rows * cols,
            bytes_accessed=16 * heads * rows * cols,
            transcendentals=heads * rows * cols,
        ),
        name="attend_back",
    )(pair, cot, queries, kept, kept, mixed, d_mixed, log_sums, id_column, id_row)


SMALL_LN1_GAIN, SMALL_LN1_BIAS, SMALL_LN2_GAIN, SMALL_LN2_BIAS = 0, 1, 2, 3
SMALL_B_OUT, SMALL_B_DOWN, SMALL_PENALTY = 4, 5, 6
SMALL_B_QUERY, SMALL_B_VALUE, SMALL_B_UP = 8, 9, 10
SMALL_ROWS = 16


def team_device(team, core, chips):
    return {"dp": lax.div(team, chips), "blk": lax.rem(team, chips) * 2 + core}


def front_kernel(operands, results, scratch, raw):
    (
        atoms, ids, gain_one, bias_one, w_key, w_value, b_value, w_query, b_query, w_out, cot, w_down, w_up, b_out,
        gain, bias, b_up,
    ) = operands
    (pair,) = raw
    (
        queries, kept, id_column, log_sums, mixed, id_row, d_mixed, hidden, down, d_hidden, grad_share, small,
    ) = results
    (
        pair_buf, score, high, low, q_part, q_land, q_all, k_all, w_all, squares, mixed_all, normal_two, rate_two,
        part, landed, back, back_landed, grads, sib_grads, go_grads, got_grads,
        pair_sem, kept_send, kept_recv, kz_send, kf_send, ks_send, k_recv, q_send, q_recv, w_send, wf_send, w_recv,
        mix_send, mix_recv, part_send, part_recv, back_send, back_recv, sib_send, sib_recv, g_send, g_recv,
    ) = scratch
    zs, feats, rows = mixed_all.shape
    blocks = kept.shape[0]
    chips = blocks // 2
    teams, _, share, width = grads.shape
    _, group, _, cols = pair_buf.shape
    heads = feats // DH
    groups = heads // group
    piece = rows // zs
    z, blk = lax.axis_index("head"), lax.axis_index("blk")
    core, chip = lax.rem(blk, 2), lax.div(blk, 2)
    team = lax.axis_index("dp") * chips + chip
    other_core = 1 - core
    sib_blk = blk + 1 - 2 * core
    sibling = {"blk": sib_blk}
    peers, far_teams = others(z, zs), others(team, teams)
    far = [step * 2 + core for step in others(chip, chips)]
    far_siblings = [step * 2 + other_core for step in others(chip, chips)]
    mine = pl.ds(pl.multiple_of(z * piece, 8), piece)

    def pair_copy(index, slot):
        return pltpu.make_async_copy(
            pair.at[0, pl.ds(index * group, group)], pair_buf.at[slot], pair_sem.at[slot]
        )

    meeting = [{"head": peer} for peer in peers] + [sibling]
    meeting += [team_device(peer, core, chips) for peer in far_teams]
    greet(meeting)
    for n in range(2):
        pair_copy(n, n).start()

    normal, _ = normalize(atoms[...])
    normed = halves(normal * gain_one[...] + bias_one[...])
    kept[blk, 0:feats, :] = dot_halves(normed, halves(w_key[...])).T
    kept[blk, feats : 2 * feats, :] = (dot_halves(normed, halves(w_value[...])) + b_value[...]).T
    id_line = ids[...].astype(F32)
    kept[blk, 2 * feats : 2 * feats + 8, :] = jnp.broadcast_to(id_line, (8, rows))
    meet(meeting)
    copies = [
        send(kept.at[blk], kept.at[blk], kept_send.at[n], kept_recv.at[blk], {"blk": peer})
        for n, peer in enumerate([sib_blk] + far)
    ]
    copies += [
        send(kept.at[blk, 0:feats], k_all.at[blk, z], kz_send.at[n], k_recv.at[blk, z], {"head": peer})
        for n, peer in enumerate(peers)
    ]
    q_rows = (dot_halves(normed, halves(w_query[...])) + b_query[...]) * (DH ** (-0.5))
    q_part[...] = q_rows.reshape(zs, piece, feats)
    copies += [
        send(q_part.at[peer], q_land.at[z], q_send.at[n], q_recv.at[z], {"head": peer})
        for n, peer in enumerate(peers)
    ]
    half = feats // 2
    w_mine = w_out.source.at[pl.ds(pl.multiple_of(core * half, 8), half)]
    copies += [
        send(w_mine, w_all.at[z, core], w_send.at[n], w_recv.at[z, core], {"head": peer})
        for n, peer in enumerate(peers)
    ]
    queries[...] = q_rows.T
    queries.flush()
    q_land[z] = q_part[z]
    w_all[z] = w_out[...].reshape(2, half, width)
    id_column[...] = jnp.broadcast_to(id_line, (LANES, rows)).T
    id_column.flush()
    small[...] = jnp.zeros(small.shape, F32)
    for n, source in enumerate(far):
        arrived(kept.at[source], kept_recv.at[source])
        copies.append(
            send(kept.at[source], kept.at[source], kept_send.at[chips + n], kept_recv.at[source], sibling)
        )
    for source in [sib_blk] + far_siblings:
        arrived(kept.at[source], kept_recv.at[source])
    kept.flush()
    one = joined(kept[n, 2 * feats : 2 * feats + 8, :] for n in range(blocks))
    id_row[...] = jnp.concatenate([one, one], axis=0)
    id_row.flush()

    def mix_copies(index):
        some = pl.ds(pl.multiple_of(index * (8 * group), 8 * group), 8 * group)
        return [
            pltpu.make_async_remote_copy(
                src_ref=mixed.at[some],
                dst_ref=mixed_all.at[z, some],
                send_sem=mix_send.at[n, index],
                recv_sem=mix_recv.at[z, index],
                device_id={"head": peer},
                device_id_type=MESH,
            )
            for n, peer in enumerate(peers)
        ]

    def step(index, carry):
        slot = lax.rem(index, 2)
        pair_copy(index, slot).wait()
        low_row = pl.multiple_of(index * (8 * group), 8 * group)
        some = pl.ds(low_row, 8 * group)
        values = pl.ds(pl.multiple_of(feats + low_row, 8), 8 * group)
        mixed[some, :] = attend_group(
            pair_buf.at[slot],
            queries[some, :],
            joined(kept[n, some, :] for n in range(blocks)),
            joined(kept[n, values, :] for n in range(blocks)),
            id_column, id_row, log_sums, index * group, score, high, low,
        )
        for copy in mix_copies(index):
            copy.start()

        @pl.when(index + 2 < groups)
        def _():
            pair_copy(index + 2, slot).start()

        return carry

    lax.fori_loop(0, groups, step, 0)
    mixed.flush()
    log_sums.flush()
    for n, peer in enumerate(peers):
        ready = w_all.at[peer, core]
        arrived(ready, w_recv.at[peer, core])
        copies.append(send(ready, ready, wf_send.at[n], w_recv.at[peer, core], sibling))
    for n, peer in enumerate(peers):
        ready = k_all.at[blk, peer]
        arrived(ready, k_recv.at[blk, peer])
        copies += [
            send(ready, ready, kf_send.at[n, m], k_recv.at[blk, peer], {"blk": target})
            for m, target in enumerate([sib_blk] + far)
        ]

    small[SMALL_B_DOWN : SMALL_B_DOWN + 1, :] = column_sum(cot[mine, :])
    cots = halves(cot[...])
    downs = halves(w_down[...])
    d_act = dot_halves(cots, downs, NT)
    ups = halves(w_up[...])
    for peer in peers:
        arrived(w_all.at[peer, other_core], w_recv.at[peer, other_core])
    outs = halves(w_all[...].reshape(zs * feats, width))
    mixed_all[z] = mixed[...]
    for peer in peers:
        for index in range(groups):
            some = pl.ds(index * (8 * group), 8 * group)
            arrived(mixed_all.at[peer, some], mix_recv.at[peer, index])
    mixed_rows = mixed_all[...].reshape(zs * feats, rows).T
    hidden_rows = atoms[...] + dot_halves(halves(mixed_rows), outs) + b_out[...]
    hidden[...] = hidden_rows
    hidden.flush()
    normal, rate = normalize(hidden_rows)
    normal_two[...] = normal
    rate_two[...] = jnp.broadcast_to(rate, rate_two.shape)
    normed = normal * gain[...] + bias[...]
    pre = dot_halves(halves(normed), ups) + b_up[...]
    phi = 0.5 * (1.0 + lax.erf(pre * math.sqrt(0.5)))
    act = pre * phi
    d_pre = d_act * (phi + pre * jnp.exp(-0.5 * pre * pre) * (1.0 / math.sqrt(2.0 * math.pi)))
    d_pres = halves(d_pre)
    part[...] = dot_halves(d_pres, ups, NT).reshape(zs, piece, width)
    copies += [
        send(part.at[peer], landed.at[z], part_send.at[n], part_recv.at[z], {"head": peer})
        for n, peer in enumerate(peers)
    ]
    landed[z] = part[z]
    grad_up = dot_halves(halves(d_pre.T), halves(normed))
    grad_down = dot_halves(halves(act.T), cots)
    grads[...] = jnp.concatenate([grad_up, grad_down], axis=0).reshape(grads.shape)
    copies.append(send(grads.at[:, other_core], sib_grads, sib_send.at[0], sib_recv.at[0], sibling))
    for n, source in enumerate(far):
        for m, peer in enumerate(peers):
            ready = k_all.at[source, peer]
            arrived(ready, k_recv.at[source, peer])
            copies.append(send(ready, ready, ks_send.at[n, m], k_recv.at[source, peer], sibling))
    down[...] = dot_halves(halves(act), downs)
    down.flush()
    small[SMALL_B_UP : SMALL_B_UP + 1, 0 : d_pre.shape[1]] = column_sum(d_pre)
    arrived(sib_grads, sib_recv.at[0])
    go_grads[...] = sib_grads[...] + grads[:, core]
    copies += [
        send(
            go_grads.at[peer], got_grads.at[team], g_send.at[n], g_recv.at[team], team_device(peer, core, chips)
        )
        for n, peer in enumerate(far_teams)
    ]
    got_grads[team] = go_grads[team]
    for peer in peers:
        arrived(q_land.at[peer], q_recv.at[peer])
    for n in range(zs):
        q_all[n] = q_land[n].T
    for n in range(blocks):
        k_all[n, z] = kept[n, 0:feats, :]
    for source in [sib_blk] + far_siblings:
        for peer in peers:
            arrived(k_all.at[source, peer], k_recv.at[source, peer])
    squares[...] = jnp.zeros(squares.shape, F32)
    at_once = 4
    rounds = heads // at_once

    def square_step(index, carry):
        there = lax.div(index, rounds)
        some = pl.ds(pl.multiple_of(lax.rem(index, rounds) * (8 * at_once), 8 * at_once), 8 * at_once)
        q_some = q_all[there, some, :]
        k_some = joined(k_all[n, there, some, :] for n in range(blocks))
        added = None
        for h in range(at_once):
            head = slice(8 * h, 8 * h + 8)
            q_high, q_low = wide_halves(q_some[head])
            k_high, k_low = wide_halves(k_some[head])
            value = dot(
                stacked([q_high, q_high, q_low, q_low]), stacked([k_high, k_low, k_high, k_low]), TN
            )
            added = value * value if added is None else added + value * value
        squares[...] += added
        return carry

    lax.fori_loop(0, zs * rounds, square_step, 0)
    same = id_column[mine, 0:1] == id_row[0:1, :]
    norms = jnp.sqrt(squares[...] + 1.0)
    terms = jnp.where(same, jnp.log1p(jnp.exp(norms - math.sqrt(zs * heads))), 0.0)
    number = jnp.where(same, 1.0, 0.0)

    def total(value):
        return jnp.sum(jnp.sum(value, axis=1, keepdims=True), axis=0, keepdims=True)

    lane = lax.broadcasted_iota(jnp.int32, (1, width), 1)
    small[SMALL_PENALTY : SMALL_PENALTY + 1, :] = jnp.where(
        lane == 0, total(terms), jnp.where(lane == 1, total(number), 0.0)
    )
    for peer in peers:
        arrived(landed.at[peer], part_recv.at[peer])
    d_normed = functools.reduce(jnp.add, [landed[n] for n in range(zs)])
    normal = normal_two[mine, :]
    d_rows = cot[mine, :] + normalize_back(d_normed, gain[...], normal, rate_two[mine, 0:1])
    d_halves = halves(d_rows)
    for n in range(zs):
        some = slice(n * feats, (n + 1) * feats)
        back[n] = dot_halves(d_halves, (outs[0][some], outs[1][some]), NT)
    copies += [
        send(back.at[peer], back_landed.at[z], back_send.at[n], back_recv.at[z], {"head": peer})
        for n, peer in enumerate(peers)
    ]
    back_landed[z] = back[z]
    d_hidden[...] = d_rows
    d_hidden.flush()
    small[SMALL_LN2_GAIN : SMALL_LN2_GAIN + 1, :] = column_sum(d_normed * normal)
    small[SMALL_LN2_BIAS : SMALL_LN2_BIAS + 1, :] = column_sum(d_normed)
    small[SMALL_B_OUT : SMALL_B_OUT + 1, :] = column_sum(d_rows)
    small.flush()
    for peer in peers:
        arrived(back_landed.at[peer], back_recv.at[peer])
    d_mixed[...] = back_landed[...].reshape(rows, feats).T
    d_mixed.flush()
    for peer in far_teams:
        arrived(got_grads.at[peer], g_recv.at[peer])
    grad_share[...] = functools.reduce(jnp.add, [got_grads[n] for n in range(teams)])
    for copy in copies:
        copy.wait_send()

    def drain(index, carry):
        for copy in mix_copies(index):
            copy.wait_send()
        return carry

    lax.fori_loop(0, groups, drain, 0)


def front(zs, teams, pair, *operands):
    _, heads, rows, cols = pair.shape
    feats, blocks = heads * DH, cols // rows
    width, units = operands[0].shape[1], operands[12].shape[1]
    piece, share, group = rows // zs, units // teams, GROUP
    groups = heads // group
    slab = pltpu.VMEM((zs, piece, width), F32)
    narrow = pltpu.VMEM((zs, piece, feats), F32)
    one = pltpu.VMEM((teams, share, width), F32)
    dma = pltpu.SemaphoreType.DMA
    return staged_call(
        front_kernel,
        "front",
        operands,
        [
            (feats, rows), (blocks, 2 * feats + 8, rows), (rows, LANES), (heads, rows, LANES), (feats, rows),
            (STRIP, cols), (feats, rows), (rows, width), (rows, width), (piece, width), (share, width),
            (SMALL_ROWS, width),
        ],
        [
            pltpu.VMEM((2, group, rows, cols), F32),
            pltpu.VMEM((group, rows, cols), F32),
            pltpu.VMEM((group, rows, cols), BF16),
            pltpu.VMEM((group, rows, cols), BF16),
            narrow, narrow,
            pltpu.VMEM((zs, feats, piece), F32),
            pltpu.VMEM((blocks, zs, feats, rows), F32),
            pltpu.VMEM((zs, 2, feats // 2, width), F32),
            pltpu.VMEM((piece, cols), F32),
            pltpu.VMEM((zs, feats, rows), F32),
            pltpu.VMEM((rows, width), F32),
            pltpu.VMEM((rows, LANES), F32),
            slab, slab, narrow, narrow,
            pltpu.VMEM((teams, 2, share, width), F32),
            one, one, one,
            dma((2,)),
            dma((blocks,)), dma((blocks,)),
            dma((zs,)), dma((zs, blocks // 2)), dma((blocks // 2, zs)), dma((blocks, zs)),
            dma((zs,)), dma((zs,)),
            dma((zs,)), dma((zs,)), dma((zs, 2)),
            dma((zs, groups)), dma((zs, groups)),
            dma((zs,)), dma((zs,)),
            dma((zs,)), dma((zs,)),
            dma((1,)), dma((1,)),
            dma((teams,)), dma((teams,)),
        ],
        58,
        remote=0,
        raw=(pair,),
    )


def finish_kernel(operands, results, scratch, raw):
    (
        d_keys, d_values, d_hidden, share_in, d_queries, atoms, gain, bias, w_query, mixed, small_in, w_key, w_value,
    ) = operands
    grad_atoms, total_grads, total_big, small, penalty = results
    (
        sib_keys, sib_values, go_keys, go_values, got_keys, got_values,
        part, landed, grads, sib_grads, go_grads, got_grads, hidden_all, small_z, small_all,
        sib_send, sib_recv, kv_send, kv_recv, part_send, part_recv, back_send, back_recv,
        g_send, g_recv, t_send, t_recv, f_send, b_send, b_recv, bf_send, h_send, h_recv,
        small_z_send, small_z_recv, small_send, small_recv,
    ) = scratch
    chips, _, feats, rows = d_keys.shape
    zs, piece, width = part.shape
    teams, _, share, _ = grads.shape
    blk, z, dp = lax.axis_index("blk"), lax.axis_index("head"), lax.axis_index("dp")
    core, chip = lax.rem(blk, 2), lax.div(blk, 2)
    other_core = 1 - core
    sibling = {"blk": blk + 1 - 2 * core}
    peers = others(z, zs)
    team = dp * chips + chip
    far_teams = others(team, teams)
    far_chips = others(chip, chips)
    place = team * 2 + core
    far_places = others(place, teams * 2)
    plane = [team_device(lax.div(value, 2), lax.rem(value, 2), chips) for value in far_places]
    meeting = [{"head": peer} for peer in peers] + plane
    greet(meeting)
    meet(meeting)
    copies = [
        send(d_keys.source.at[:, other_core], sib_keys, sib_send.at[0], sib_recv.at[0], sibling),
        send(d_values.source.at[:, other_core], sib_values, sib_send.at[1], sib_recv.at[1], sibling),
    ]
    copies += [
        send(d_hidden.source, hidden_all.at[z], h_send.at[n], h_recv.at[z], {"head": peer})
        for n, peer in enumerate(peers)
    ]
    own_keys, own_values = d_keys.ref, d_values.ref
    arrived(sib_keys, sib_recv.at[0])
    arrived(sib_values, sib_recv.at[1])
    go_keys[...] = sib_keys[...] + own_keys[:, core]
    go_values[...] = sib_values[...] + own_values[:, core]
    for n, peer in enumerate(far_chips):
        target = {"blk": peer * 2 + core}
        copies.append(send(go_keys.at[peer], got_keys.at[chip], kv_send.at[0, n], kv_recv.at[0, chip], target))
        copies.append(
            send(go_values.at[peer], got_values.at[chip], kv_send.at[1, n], kv_recv.at[1, chip], target)
        )
    got_keys[chip] = go_keys[chip]
    got_values[chip] = go_values[chip]
    total_big[team, core] = share_in[...]
    ready = total_big.at[team, core]
    copies.append(send(ready, ready, b_send.at[0], b_recv.at[team, core], sibling))
    copies += [
        send(ready, ready, b_send.at[n + 1], b_recv.at[team, core], team_device(peer, core, chips))
        for n, peer in enumerate(far_teams)
    ]
    normal, rate = normalize(atoms[...])
    normed = halves(normal * gain[...] + bias[...])
    dq_rows = d_queries[...].T
    d_normed = dot_full(dq_rows, w_query[...], NT)
    grad_q = dot_halves(halves(d_queries[...]), normed)
    mine = pl.ds(pl.multiple_of(z * piece, 8), piece)
    small_z[z] = small_in[0:8, :]
    hidden_all[z] = d_hidden[...]
    for peer in far_chips:
        arrived(got_keys.at[peer], kv_recv.at[0, peer])
        arrived(got_values.at[peer], kv_recv.at[1, peer])
    dk = functools.reduce(jnp.add, [got_keys[n] for n in range(chips)])
    dv = functools.reduce(jnp.add, [got_values[n] for n in range(chips)])
    dv_rows = dv.T
    d_normed = (
        d_normed + dot_full(dk.T, w_key[...], NT) + dot_full(dv_rows, w_value[...], NT)
    )
    part[...] = d_normed.reshape(zs, piece, width)
    copies += [
        send(part.at[peer], landed.at[z], part_send.at[n], part_recv.at[z], {"head": peer})
        for n, peer in enumerate(peers)
    ]
    landed[z] = part[z]
    grad_k = dot_halves(halves(dk), normed)
    grad_v = dot_halves(halves(dv), normed)
    for peer in peers:
        arrived(hidden_all.at[peer], h_recv.at[peer])
    grad_o = dot_full(mixed[...], hidden_all[...].reshape(rows, width))
    grads[...] = jnp.concatenate([grad_q, grad_k, grad_v, grad_o], axis=0).reshape(grads.shape)
    copies.append(send(grads.at[:, other_core], sib_grads, sib_send.at[2], sib_recv.at[2], sibling))
    arrived(sib_grads, sib_recv.at[2])
    go_grads[...] = sib_grads[...] + grads[:, core]
    copies += [
        send(
            go_grads.at[peer], got_grads.at[team], g_send.at[n], g_recv.at[team], team_device(peer, core, chips)
        )
        for n, peer in enumerate(far_teams)
    ]
    got_grads[team] = go_grads[team]
    for peer in peers:
        arrived(landed.at[peer], part_recv.at[peer])
    d_normed = functools.reduce(jnp.add, [landed[n] for n in range(zs)])
    normal, rate = normalize(atoms[mine, :])
    grad_atoms[mine, :] = d_hidden[...] + normalize_back(d_normed, gain[...], normal, rate)
    small_z[z, SMALL_LN1_GAIN : SMALL_LN1_GAIN + 1, :] = column_sum(d_normed * normal)
    small_z[z, SMALL_LN1_BIAS : SMALL_LN1_BIAS + 1, :] = column_sum(d_normed)
    copies += [
        send(small_z.at[z], small_z.at[z], small_z_send.at[n], small_z_recv.at[z], {"head": peer})
        for n, peer in enumerate(peers)
    ]
    copies += [
        send(grad_atoms.at[mine], grad_atoms.at[mine], back_send.at[n], back_recv.at[z], {"head": peer})
        for n, peer in enumerate(peers)
    ]
    for peer in far_teams:
        arrived(got_grads.at[peer], g_recv.at[peer])
    total_grads[team, core] = functools.reduce(jnp.add, [got_grads[n] for n in range(teams)])
    ready = total_grads.at[team, core]
    copies.append(send(ready, ready, t_send.at[0], t_recv.at[team, core], sibling))
    copies += [
        send(ready, ready, t_send.at[n + 1], t_recv.at[team, core], team_device(peer, core, chips))
        for n, peer in enumerate(far_teams)
    ]
    for peer in peers:
        arrived(small_z.at[peer], small_z_recv.at[peer])
    small_all[place, 0:8, :] = functools.reduce(jnp.add, [small_z[n] for n in range(zs)])
    small_all[place, 8:16, :] = small_in[8:16, :]
    small_all[place, SMALL_B_QUERY : SMALL_B_QUERY + 1, 0:feats] = column_sum(dq_rows)
    small_all[place, SMALL_B_VALUE : SMALL_B_VALUE + 1, 0:feats] = column_sum(dv_rows)
    copies += [
        send(small_all.at[place], small_all.at[place], small_send.at[n], small_recv.at[place], target)
        for n, target in enumerate(plane)
    ]
    for n, peer in enumerate(far_teams):
        ready = total_big.at[peer, core]
        arrived(ready, b_recv.at[peer, core])
        copies.append(send(ready, ready, bf_send.at[n], b_recv.at[peer, core], sibling))
    for n, peer in enumerate(far_teams):
        ready = total_grads.at[peer, core]
        arrived(ready, t_recv.at[peer, core])
        copies.append(send(ready, ready, f_send.at[n], t_recv.at[peer, core], sibling))
    for source in far_places:
        arrived(small_all.at[source], small_recv.at[source])
    summed = functools.reduce(jnp.add, [small_all[n] for n in range(2 * teams)])
    small[...] = summed
    ends = summed[SMALL_PENALTY : SMALL_PENALTY + 1, :]
    penalty[...] = ends[:, 0:1] / ends[:, 1:2]
    for peer in [team] + far_teams:
        arrived(total_big.at[peer, other_core], b_recv.at[peer, other_core])
    total_big.flush()
    for peer in [team] + far_teams:
        arrived(total_grads.at[peer, other_core], t_recv.at[peer, other_core])
    total_grads.flush()
    for peer in peers:
        there = pl.ds(pl.multiple_of(peer * piece, 8), piece)
        arrived(grad_atoms.at[there], back_recv.at[peer])
    for copy in copies:
        copy.wait_send()


def finish(zs, dps, *operands):
    d_keys, share_in, atoms = operands[0], operands[3], operands[5]
    chips, _, feats, rows = d_keys.shape
    width = atoms.shape[1]
    piece = rows // zs
    teams = dps * chips
    share = 4 * feats // (2 * teams)
    some = pltpu.VMEM((chips, feats, rows), F32)
    slab = pltpu.VMEM((zs, piece, width), F32)
    one = pltpu.VMEM((teams, share, width), F32)
    dma = pltpu.SemaphoreType.DMA
    return staged_call(
        finish_kernel,
        "finish",
        operands,
        [
            (rows, width),
            (teams, 2, share, width),
            (teams, 2) + share_in.shape,
            (SMALL_ROWS, width),
            (1, 1),
        ],
        [some] * 6
        + [slab, slab, pltpu.VMEM((teams, 2, share, width), F32), one, one, one, slab]
        + [
            pltpu.VMEM((zs, 8, width), F32),
            pltpu.VMEM((2 * teams, SMALL_ROWS, width), F32),
            dma((3,)), dma((3,)),
            dma((2, chips)), dma((2, chips)),
            dma((zs,)), dma((zs,)),
            dma((zs,)), dma((zs,)),
            dma((teams,)), dma((teams,)),
            dma((teams,)), dma((teams, 2)), dma((teams,)),
            dma((teams,)), dma((teams, 2)), dma((teams,)),
            dma((zs,)), dma((zs,)),
            dma((zs,)), dma((zs,)),
            dma((2 * teams,)), dma((2 * teams,)),
        ],
        58,
        remote=2,
    )


def place_kernel(operands, results, scratch, raw):
    total_grads, total_big, small, hidden, down, b_down, rows_in = operands
    grad_query, grad_key, grad_value, grad_out, grad_up, grad_down, out_atoms, grad_atoms = results[:8]
    feats, units = grad_out.shape[0], grad_down.shape[0]
    width = grad_out.shape[1]
    grad_atoms[...] = rows_in[...]
    grad_atoms.flush()
    done = total_grads[...].reshape(4 * feats, width)
    grad_query[...] = done[0:feats].T
    grad_query.flush()
    grad_key[...] = done[feats : 2 * feats].T
    grad_key.flush()
    grad_value[...] = done[2 * feats : 3 * feats].T
    grad_value.flush()
    grad_out[...] = done[3 * feats :]
    grad_out.flush()
    done = total_big[...].reshape(2 * units, width)
    grad_up[...] = done[0:units].T
    grad_up.flush()
    grad_down[...] = done[units:]
    grad_down.flush()
    out_atoms[...] = hidden[...] + down[...] + b_down[...]
    out_atoms.flush()
    for result, row in zip(results[8:], SMALL_OUTPUTS, strict=True):
        result[...] = small[row : row + 1, 0 : result.shape[1]]


SMALL_OUTPUTS = (
    SMALL_LN1_GAIN, SMALL_LN1_BIAS, SMALL_B_QUERY, SMALL_B_VALUE, SMALL_B_OUT, SMALL_LN2_GAIN, SMALL_LN2_BIAS,
    SMALL_B_UP, SMALL_B_DOWN,
)


def place(feats, units, *operands):
    rows, width = operands[3].shape
    lengths = {SMALL_B_QUERY: feats, SMALL_B_VALUE: feats, SMALL_B_UP: units}
    return staged_call(
        place_kernel,
        "place",
        operands,
        [(width, feats)] * 3
        + [(feats, width), (width, units), (units, width), (rows, width), (rows, width)]
        + [(1, lengths.get(row, width)) for row in SMALL_OUTPUTS],
        [],
        32,
    )


def local(
    zs, dps,
    atoms, pair, mol_ids, ln1_gain, ln1_bias, w_query, b_query, w_key, w_value, b_value, w_out, b_out,
    ln2_gain, ln2_bias, w_up, b_up, w_down, b_down, cot_atoms, cot_pair,
):
    blocks = pair.shape[3] // pair.shape[2]
    inputs, cot = atoms[0], cot_atoms[0]

    def line(value):
        return value.reshape(1, -1)

    (
        queries, kept, id_column, log_sums, mixed, id_row, d_mixed, hidden, down, d_hidden, grad_share, small,
    ) = front(
        zs, dps * blocks // 2, pair,
        inputs, mol_ids, line(ln1_gain), line(ln1_bias), w_key, w_value, line(b_value), w_query, line(b_query),
        w_out, cot, w_down, w_up, line(b_out), line(ln2_gain), line(ln2_bias), line(b_up),
    )
    down = lax.psum(down, "head")
    out_pair, grad_pair, d_queries, d_keys, d_values = attend_back(
        pair, cot_pair, queries, kept, mixed, d_mixed, log_sums, id_column, id_row
    )
    grad_atoms, total_grads, total_big, small, penalty = finish(
        zs, dps,
        d_keys, d_values, d_hidden, grad_share, d_queries, inputs, line(ln1_gain), line(ln1_bias), w_query, mixed,
        small, w_key, w_value,
    )
    placed = place(
        w_query.shape[1], w_up.shape[1],
        total_grads, total_big, small, hidden, down, line(b_down), grad_atoms,
    )
    grad_query, grad_key, grad_value, grad_out, grad_up, grad_down, out_atoms, grad_atoms = placed[:8]
    (
        grad_ln1_gain, grad_ln1_bias, grad_b_query, grad_b_value, grad_b_out, grad_ln2_gain, grad_ln2_bias,
        grad_b_up, grad_b_down,
    ) = [value.reshape(-1) for value in placed[8:]]
    return (
        out_atoms[None],
        out_pair,
        penalty[0, 0],
        grad_atoms[None],
        grad_pair,
        grad_ln1_gain,
        grad_ln1_bias,
        grad_query,
        grad_b_query,
        grad_key,
        grad_value,
        grad_b_value,
        grad_out,
        grad_b_out,
        grad_ln2_gain,
        grad_ln2_bias,
        grad_up,
        grad_b_up,
        grad_down,
        grad_b_down,
    )


def solution(mesh):
    rows, pairs = P("dp", "blk", None), P("dp", "head", "blk", None)
    columns = P(None, "head")
    return jax.shard_map(
        functools.partial(local, mesh.shape["head"], mesh.shape["dp"]),
        mesh=mesh,
        in_specs=(
            rows, pairs, P("dp", "blk"), P(), P(), columns, P("head"), columns, columns, P("head"),
            P("head", None), P(), P(), P(), columns, P("head"), P("head", None), P(), rows, pairs,
        ),
        out_specs=(
            rows, pairs, P(), rows, pairs, P(), P(), columns, P("head"), columns, columns, P("head"),
            P("head", None), P(), P(), P(), columns, P("head"), P("head", None), P(),
        ),
        check_vma=False,
    )
```

```python
import functools
import math

import jax
import jax.numpy as jnp
from jax import lax
from jax.experimental import pallas as pl
from jax.experimental.pallas import tpu as pltpu
from jax.sharding import PartitionSpec as P

DH = 8
LANES = 128
STRIP = 16
CHUNK = 256
GROUP = 2
NORM_EPS = 1e-05
MASK_FILL = -1e30
F32 = jnp.float32
BF16 = jnp.bfloat16
MESH = pl.DeviceIdType.MESH
NN = (((1,), (0,)), ((), ()))
NT = (((1,), (1,)), ((), ()))
TN = (((0,), (0,)), ((), ()))
VMEM = pl.BlockSpec(memory_space=pltpu.VMEM)


def dot(left, right, dims=NN):
    return lax.dot_general(left, right, dims, preferred_element_type=F32)


def halves(value):
    high = value.astype(BF16)
    return high, (value - high.astype(F32)).astype(BF16)


def dot_halves(left, right, dims=NN):
    return dot(left[0], right[0], dims) + (
        dot(left[0], right[1], dims) + dot(left[1], right[0], dims)
    )


def dot_full(left, right, dims=NN):
    return dot_halves(halves(left), halves(right), dims)


def normalize(inputs):
    centred = inputs - jnp.mean(inputs, -1, keepdims=True)
    rate = lax.rsqrt(jnp.mean(centred * centred, -1, keepdims=True) + NORM_EPS)
    return centred * rate, rate


def normalize_back(grad, gain, normal, rate):
    scaled = grad * gain
    return rate * (
        scaled
        - jnp.mean(scaled, -1, keepdims=True)
        - normal * jnp.mean(scaled * normal, -1, keepdims=True)
    )


def column_sum(value):
    return jnp.sum(value, 0, keepdims=True)


def send(src, dst, send_sem, recv_sem, target):
    copy = pltpu.make_async_remote_copy(
        src_ref=src,
        dst_ref=dst,
        send_sem=send_sem,
        recv_sem=recv_sem,
        device_id=target,
        device_id_type=MESH,
    )
    copy.start()
    return copy


def arrived(ref, sem):
    pltpu.make_async_remote_copy(
        src_ref=ref, dst_ref=ref, send_sem=sem, recv_sem=sem, device_id={}, device_id_type=MESH
    ).wait_recv()


def greet(targets):
    for target in targets:
        pl.semaphore_signal(pltpu.get_barrier_semaphore(), inc=1, device_id=target, device_id_type=MESH)


def meet(targets):
    pl.semaphore_wait(pltpu.get_barrier_semaphore(), len(targets))


def others(index, count):
    return [lax.rem(index + step, count) for step in range(1, count)]


class Operand:
    def __init__(self, source, slot, sem):
        self.source, self.slot, self.shape = source, slot, slot.shape
        self.copy = pltpu.make_async_copy(source, slot, sem)
        self.copy.start()

    @property
    def ref(self):
        if self.copy is not None:
            self.copy.wait()
            self.copy = None
        return self.slot

    def __getitem__(self, index):
        return self.ref[index]


class Result:
    def __init__(self, target, slot, sem):
        self.slot, self.shape, self.at = slot, slot.shape, slot.at
        self.copy = pltpu.make_async_copy(slot, target, sem)
        self.begun = False

    def __setitem__(self, index, value):
        self.slot[index] = value

    def __getitem__(self, index):
        return self.slot[index]

    def flush(self):
        if not self.begun:
            self.copy.start()
            self.begun = True


def staged_call(kernel, name, operands, results, scratch, megabytes, remote=None, raw=(), straight=()):
    n_in, n_out, n_raw, n_straight = len(operands), len(results), len(raw), len(straight)

    def body(*refs):
        sources, left, refs = refs[:n_in], refs[n_in : n_in + n_raw], refs[n_in + n_raw :]
        moved, refs = refs[:n_straight], refs[n_straight:]
        arrays, refs = refs[:n_straight], refs[n_straight:]
        targets, refs = refs[:n_out], refs[n_out:]
        slots, made, refs = refs[:n_in], refs[n_in : n_in + n_out], refs[n_in + n_out :]
        in_sem, out_sem, move_sem, refs = refs[0], refs[1], refs[2], refs[3:]
        through, refs = refs[:n_straight], refs[n_straight:]
        loads = [pltpu.make_async_copy(moved[n], through[n], move_sem.at[n]) for n in range(n_straight)]
        moves = [pltpu.make_async_copy(through[n], arrays[n], move_sem.at[n]) for n in range(n_straight)]
        for load in loads:
            load.start()
        ins = [Operand(sources[n], slots[n], in_sem.at[n]) for n in range(n_in)]
        outs = [Result(targets[n], made[n], out_sem.at[n]) for n in range(n_out)]
        for load, move in zip(loads, moves, strict=True):
            load.wait()
            move.start()
        kernel(ins, outs, refs, left)
        for operand in ins:
            operand.ref
        for result in outs:
            result.flush()
        for copy in moves + [result.copy for result in outs]:
            copy.wait()

    anywhere = pl.BlockSpec(memory_space=pltpu.HBM)
    extra = {} if remote is None else {"collective_id": remote, "has_side_effects": True}
    return pl.pallas_call(
        body,
        out_shape=[jax.ShapeDtypeStruct(value.shape, value.dtype) for value in straight]
        + [jax.ShapeDtypeStruct(shape, F32) for shape in results],
        in_specs=[anywhere] * (n_in + n_raw + n_straight),
        out_specs=[anywhere] * (n_straight + n_out),
        scratch_shapes=[pltpu.VMEM(value.shape, value.dtype) for value in operands]
        + [pltpu.VMEM(shape, F32) for shape in results]
        + [pltpu.SemaphoreType.DMA((n,)) for n in (n_in, n_out, max(1, n_straight))]
        + [pltpu.VMEM(value.shape, value.dtype) for value in straight]
        + list(scratch),
        compiler_params=pltpu.CompilerParams(vmem_limit_bytes=megabytes << 20, **extra),
        name=name,
    )(*operands, *raw, *straight)


def joined(pieces):
    return jnp.concatenate(list(pieces), axis=1)


def stacked(parts):
    return jnp.concatenate(parts, axis=0).astype(BF16)


def wide_halves(value):
    high = value.astype(BF16).astype(F32)
    return high, value - high


def attend_group(pair, queries, keys, values, id_column, id_row, log_sums, first, score, high, low):
    group, rows, cols = score.shape
    strips = rows // STRIP
    chunk = min(CHUNK, cols)
    mixed = []
    for g in range(group):
        head = slice(8 * g, 8 * g + 8)
        q_high, q_low = wide_halves(queries[head, :])
        k_high, k_low = wide_halves(keys[head, :])
        v_high, v_low = wide_halves(values[head, :])
        ones = jnp.ones_like(v_high)
        q_pack = stacked([q_high, q_high, q_low, q_low])
        k_pack = stacked([k_high, k_low, k_high, k_low])
        v_pack = stacked([v_high, v_low, ones, jnp.zeros_like(ones)])
        tops = [None] * strips
        for start in range(0, cols, chunk):
            part = slice(start, start + chunk)
            score[g, :, part] = dot(q_pack, k_pack[:, part], TN)
            for s in range(strips):
                line = pl.ds(s * STRIP, STRIP)
                own = id_column[line, :]
                for j in range(start, start + chunk, LANES):
                    tile = pl.ds(j, LANES)
                    value = pair[g, line, tile] + score[g, line, tile]
                    value = jnp.where(own == id_row[:, tile], value, MASK_FILL)
                    score[g, line, tile] = value
                    tops[s] = value if tops[s] is None else jnp.maximum(tops[s], value)
        tops = [
            jnp.broadcast_to(jnp.max(top, axis=1, keepdims=True), (STRIP, LANES)) for top in tops
        ]
        totals = [None] * strips
        gathered = None
        for start in range(0, cols, chunk):
            part = slice(start, start + chunk)
            for s in range(strips):
                line = pl.ds(s * STRIP, STRIP)
                for j in range(start, start + chunk, LANES):
                    tile = pl.ds(j, LANES)
                    weight = jnp.exp(score[g, line, tile] - tops[s])
                    high[g, line, tile], low[g, line, tile] = halves(weight)
                    totals[s] = weight if totals[s] is None else totals[s] + weight
            term = dot(v_pack[:, part], high[g, :, part], NT) + dot(
                v_pack[:, part], low[g, :, part], NT
            )
            gathered = term if gathered is None else gathered + term
        for s in range(strips):
            total = jnp.sum(totals[s], axis=1, keepdims=True)
            log_sums[first + g, pl.ds(s * STRIP, STRIP), :] = tops[s] + jnp.log(total)
        mixed.append((gathered[0:8] + gathered[8:16]) / gathered[16:17])
    return jnp.concatenate(mixed, axis=0)


def attend_back_kernel(
    pair, cot, queries, keys, values, mixed, d_mixed, log_sums, id_column, id_row,
    out_pair, grad_pair, d_queries, d_keys, d_values,
    pair_buf, cot_buf, out_buf, grad_buf, score, d_prob, p_high, p_low, g_high, g_low, in_sem, out_sem,
):
    heads = pair.shape[1]
    rows, cols = score.shape
    depth = pair_buf.shape[0]
    chunk = min(CHUNK, cols)
    place = lax.broadcasted_iota(jnp.int32, (8, rows), 0)

    def moves(index, sources, targets, sem, outward):
        slot = lax.rem(index, depth)
        return [
            pltpu.make_async_copy(buf.at[slot], array.at[0, index], sem.at[n, slot])
            if outward
            else pltpu.make_async_copy(array.at[0, index], buf.at[slot], sem.at[n, slot])
            for n, (array, buf) in enumerate(zip(sources, targets, strict=True))
        ]

    def inward(index):
        return moves(index, (pair, cot), (pair_buf, cot_buf), in_sem, False)

    def outward(index):
        return moves(index, (out_pair, grad_pair), (out_buf, grad_buf), out_sem, True)

    def both(left, high, low, dims):
        value = dot(left, high, dims) + dot(left, low, dims)
        return value[0:8] + value[8:16]

    for n in range(min(depth, heads)):
        for copy in inward(n):
            copy.start()

    def step(index, carry):
        slot = lax.rem(index, depth)
        head = pl.ds(pl.multiple_of(index * 8, 8), 8)
        q_high, q_low = wide_halves(queries[head, :])
        k_high, k_low = wide_halves(joined(keys[n, head, :] for n in range(keys.shape[0])))
        v_high, v_low = wide_halves(joined(values[n, head, :] for n in range(keys.shape[0])))
        m_high, m_low = wide_halves(d_mixed[head, :])
        delta_high, rest = wide_halves(-column_sum(mixed[head, :] * d_mixed[head, :]))
        delta_mid, delta_low = wide_halves(rest)
        deltas = jnp.where(
            place == 0, delta_high, jnp.where(place == 1, delta_mid, jnp.where(place == 2, delta_low, 0.0))
        )
        q_pack = stacked([q_high, q_high, q_low, q_low])
        k_pack = stacked([k_high, k_low, k_high, k_low])
        m_pack = stacked([m_high, m_high, m_low, deltas])
        v_pack = stacked([v_high, v_low, v_high, jnp.ones_like(v_high)])
        q_pair = stacked([q_high, q_low])
        k_pair = stacked([k_high, k_low])
        m_pair = stacked([m_high, m_low])
        for copy in inward(index):
            copy.wait()

        @pl.when(index >= depth)
        def _():
            for copy in outward(index - depth):
                copy.wait()

        d_query = [None]

        def before(part):
            score[:, part] = dot(q_pack, k_pack[:, part], TN)
            d_prob[:, part] = dot(m_pack, v_pack[:, part], TN)

        def middle(part):
            for s in range(rows // STRIP):
                line = pl.ds(s * STRIP, STRIP)
                own = id_column[line, :]
                log_sum = log_sums[index, line, :]
                for j in range(part.start, part.stop, LANES):
                    tile = pl.ds(j, LANES)
                    value = pair_buf[slot, line, tile] + score[line, tile]
                    out_buf[slot, line, tile] = value
                    prob = jnp.exp(jnp.where(own == id_row[:, tile], value - log_sum, MASK_FILL))
                    p_high[line, tile], p_low[line, tile] = halves(prob)
                    grad = prob * d_prob[line, tile] + cot_buf[slot, line, tile]
                    grad_buf[slot, line, tile] = grad
                    g_high[line, tile], g_low[line, tile] = halves(grad)

        def after(part):
            d_value = both(m_pair, p_high[:, part], p_low[:, part], NN)
            d_key = both(q_pair, g_high[:, part], g_low[:, part], NN)
            for n in range(part.start // rows, part.stop // rows):
                span = slice(n * rows - part.start, (n + 1) * rows - part.start)
                d_keys[n // 2, n % 2, head, :] = d_key[:, span]
                d_values[n // 2, n % 2, head, :] = d_value[:, span]
            term = both(k_pair[:, part], g_high[:, part], g_low[:, part], NT)
            d_query[0] = term if d_query[0] is None else d_query[0] + term

        parts = [slice(start, start + chunk) for start in range(0, cols, chunk)]
        before(parts[0])
        for n, part in enumerate(parts):
            if n + 1 < len(parts):
                before(parts[n + 1])
            middle(part)
            if n >= 1:
                after(parts[n - 1])
        after(parts[-1])
        d_queries[head, :] = d_query[0] * (DH ** (-0.5))
        for copy in outward(index):
            copy.start()

        @pl.when(index + depth < heads)
        def _():
            for copy in inward(index + depth):
                copy.start()

        return carry

    lax.fori_loop(0, heads, step, 0)
    for n in range(max(0, heads - depth), heads):
        for copy in outward(n):
            copy.wait()


def attend_back(pair, cot, queries, kept, mixed, d_mixed, log_sums, id_column, id_row):
    _, heads, rows, cols = pair.shape
    feats = heads * DH
    blocks = kept.shape[0]
    depth = 4
    big = pl.BlockSpec(memory_space=pltpu.HBM)
    flat = pl.BlockSpec((feats, rows), lambda n: (0, 0))
    split = pl.BlockSpec((blocks // 2, 2, feats, rows), lambda n: (0, 0, 0, 0))
    return pl.pallas_call(
        attend_back_kernel,
        grid=(1,),
        in_specs=[
            big, big, flat,
            pl.BlockSpec((blocks, feats, rows), lambda n: (0, 0, 0)),
            pl.BlockSpec((blocks, feats, rows), lambda n: (0, 1, 0)),
            flat, flat,
            pl.BlockSpec((heads, rows, LANES), lambda n: (0, 0, 0)),
            pl.BlockSpec((rows, LANES), lambda n: (0, 0)),
            pl.BlockSpec((STRIP, cols), lambda n: (0, 0)),
        ],
        out_specs=[big, big, flat, split, split],
        out_shape=[
            jax.ShapeDtypeStruct(pair.shape, F32),
            jax.ShapeDtypeStruct(pair.shape, F32),
            jax.ShapeDtypeStruct((feats, rows), F32),
            jax.ShapeDtypeStruct((blocks // 2, 2, feats, rows), F32),
            jax.ShapeDtypeStruct((blocks // 2, 2, feats, rows), F32),
        ],
        scratch_shapes=[pltpu.VMEM((depth, rows, cols), F32)] * 4
        + [pltpu.VMEM((rows, cols), F32)] * 2
        + [pltpu.VMEM((rows, cols), BF16)] * 4
        + [pltpu.SemaphoreType.DMA((2, depth))] * 2,
        compiler_params=pltpu.CompilerParams(vmem_limit_bytes=60 << 20),
        cost_estimate=pl.CostEstimate(
            flops=2 * 400 * heads * rows * cols,
            bytes_accessed=16 * heads * rows * cols,
            transcendentals=heads * rows * cols,
        ),
        name="attend_back",
    )(pair, cot, queries, kept, kept, mixed, d_mixed, log_sums, id_column, id_row)


SMALL_LN1_GAIN, SMALL_LN1_BIAS, SMALL_LN2_GAIN, SMALL_LN2_BIAS = 0, 1, 2, 3
SMALL_B_OUT, SMALL_B_DOWN, SMALL_PENALTY = 4, 5, 6
SMALL_B_QUERY, SMALL_B_VALUE, SMALL_B_UP = 8, 9, 10
SMALL_ROWS = 16


def team_device(team, core, chips):
    return {"dp": lax.div(team, chips), "blk": lax.rem(team, chips) * 2 + core}


def front_kernel(operands, results, scratch, raw):
    (
        atoms, ids, gain_one, bias_one, w_key, w_value, b_value, w_query, b_query, w_out, cot, w_down, w_up, b_out,
        gain, bias, b_up,
    ) = operands
    (pair,) = raw
    (
        queries, kept, id_column, log_sums, mixed, id_row, d_mixed, hidden, down, d_hidden, up_share, down_share, small,
    ) = results
    (
        pair_buf, score, high, low, q_part, q_land, q_all, k_all, w_all, squares, mixed_all, normal_two, rate_two,
        part, landed, back, back_landed, ups_part, ups_sib, ups_go, ups_got, downs_part, downs_sib, downs_go, downs_got,
        pair_sem, kept_send, kept_recv, kz_send, kf_send, ks_send, k_recv, q_send, q_recv, w_send, wx_send, wf_send, w_recv,
        mix_send, mix_recv, part_send, part_recv, back_send, back_recv, sib_send, sib_recv, g_send, g_recv,
    ) = scratch
    zs, feats, rows = mixed_all.shape
    blocks = kept.shape[0]
    chips = blocks // 2
    teams, width = ups_part.shape[0], atoms.shape[1]
    _, group, _, cols = pair_buf.shape
    heads = feats // DH
    groups = heads // group
    piece = rows // zs
    z, blk = lax.axis_index("head"), lax.axis_index("blk")
    core, chip = lax.rem(blk, 2), lax.div(blk, 2)
    dp, dps = lax.axis_index("dp"), lax.axis_size("dp")
    partners = others(dp, dps)
    team = dp * chips + chip
    other_core = 1 - core
    sib_blk = blk + 1 - 2 * core
    sibling = {"blk": sib_blk}
    peers, far_teams = others(z, zs), others(team, teams)
    far = [step * 2 + core for step in others(chip, chips)]
    far_siblings = [step * 2 + other_core for step in others(chip, chips)]
    mine = pl.ds(pl.multiple_of(z * piece, 8), piece)

    def pair_copy(index, slot):
        return pltpu.make_async_copy(
            pair.at[0, pl.ds(index * group, group)], pair_buf.at[slot], pair_sem.at[slot]
        )

    meeting = [{"head": peer} for peer in peers] + [sibling]
    meeting += [team_device(peer, core, chips) for peer in far_teams]
    greet(meeting)
    for n in range(2):
        pair_copy(n, n).start()

    normal, _ = normalize(atoms[...])
    normed = halves(normal * gain_one[...] + bias_one[...])
    meet(meeting)
    copies = []
    fewer = feats // (2 * dps)
    w_mine = w_out.source.at[pl.ds(pl.multiple_of((dp * 2 + core) * fewer, 8), fewer)]
    copies += [
        send(w_mine, w_all.at[z, dp, core], w_send.at[n], w_recv.at[z, dp, core], {"head": peer})
        for n, peer in enumerate(peers)
    ]
    kept[blk, 0:feats, :] = dot_halves(normed, halves(w_key[...])).T
    copies += [
        send(kept.at[blk, 0:feats], k_all.at[blk, z], kz_send.at[n], k_recv.at[blk, z], {"head": peer})
        for n, peer in enumerate(peers)
    ]
    kept[blk, feats : 2 * feats, :] = (dot_halves(normed, halves(w_value[...])) + b_value[...]).T
    id_line = ids[...].astype(F32)
    kept[blk, 2 * feats : 2 * feats + 8, :] = jnp.broadcast_to(id_line, (8, rows))
    copies += [
        send(kept.at[blk], kept.at[blk], kept_send.at[n], kept_recv.at[blk], {"blk": peer})
        for n, peer in enumerate([sib_blk] + far)
    ]
    q_rows = (dot_halves(normed, halves(w_query[...])) + b_query[...]) * (DH ** (-0.5))
    q_part[...] = q_rows.reshape(zs, piece, feats)
    queries[...] = q_rows.T
    queries.flush()
    q_land[z] = q_part[z]
    w_all[z] = w_out[...].reshape(dps, 2, fewer, width)
    id_column[...] = jnp.broadcast_to(id_line, (LANES, rows)).T
    id_column.flush()
    small[...] = jnp.zeros(small.shape, F32)
    for n, peer in enumerate(peers):
        ready = w_all.at[peer, dp, core]
        arrived(ready, w_recv.at[peer, dp, core])
        copies += [
            send(ready, ready, wx_send.at[n, m], w_recv.at[peer, dp, core], {"dp": partner})
            for m, partner in enumerate(partners)
        ]
    for n, source in enumerate(far):
        arrived(kept.at[source], kept_recv.at[source])
        copies.append(
            send(kept.at[source], kept.at[source], kept_send.at[chips + n], kept_recv.at[source], sibling)
        )
    for source in [sib_blk] + far_siblings:
        arrived(kept.at[source], kept_recv.at[source])
    kept.flush()
    one = joined(kept[n, 2 * feats : 2 * feats + 8, :] for n in range(blocks))
    id_row[...] = jnp.concatenate([one, one], axis=0)
    id_row.flush()

    def mix_copies(index):
        some = pl.ds(pl.multiple_of(index * (8 * group), 8 * group), 8 * group)
        return [
            pltpu.make_async_remote_copy(
                src_ref=mixed.at[some],
                dst_ref=mixed_all.at[z, some],
                send_sem=mix_send.at[n, index],
                recv_sem=mix_recv.at[z, index],
                device_id={"head": peer},
                device_id_type=MESH,
            )
            for n, peer in enumerate(peers)
        ]

    def step(index, carry):
        slot = lax.rem(index, 2)
        pair_copy(index, slot).wait()
        low_row = pl.multiple_of(index * (8 * group), 8 * group)
        some = pl.ds(low_row, 8 * group)
        values = pl.ds(pl.multiple_of(feats + low_row, 8), 8 * group)
        mixed[some, :] = attend_group(
            pair_buf.at[slot],
            queries[some, :],
            joined(kept[n, some, :] for n in range(blocks)),
            joined(kept[n, values, :] for n in range(blocks)),
            id_column, id_row, log_sums, index * group, score, high, low,
        )
        for copy in mix_copies(index):
            copy.start()

        @pl.when(index + 2 < groups)
        def _():
            pair_copy(index + 2, slot).start()

        return carry

    lax.fori_loop(0, groups, step, 0)
    mixed.flush()
    log_sums.flush()
    for n, peer in enumerate(peers):
        for kind in range(dps):
            ready = w_all.at[peer, kind, core]

            @pl.when(dp != kind)
            def _(ready=ready, sem=w_recv.at[peer, kind, core]):
                arrived(ready, sem)

            copies.append(send(ready, ready, wf_send.at[n, kind], w_recv.at[peer, kind, core], sibling))
    for n, peer in enumerate(peers):
        ready = k_all.at[blk, peer]
        arrived(ready, k_recv.at[blk, peer])
        copies += [
            send(ready, ready, kf_send.at[n, m], k_recv.at[blk, peer], {"blk": target})
            for m, target in enumerate([sib_blk] + far)
        ]

    small[SMALL_B_DOWN : SMALL_B_DOWN + 1, :] = column_sum(cot[mine, :])
    cots = halves(cot[...])
    downs = halves(w_down[...])
    d_act = dot_halves(cots, downs, NT)
    ups = halves(w_up[...])
    for peer in peers:
        for kind in range(dps):
            arrived(w_all.at[peer, kind, other_core], w_recv.at[peer, kind, other_core])
    outs = halves(w_all[...].reshape(zs * feats, width))
    mixed_all[z] = mixed[...]
    for peer in peers:
        for index in range(groups):
            some = pl.ds(index * (8 * group), 8 * group)
            arrived(mixed_all.at[peer, some], mix_recv.at[peer, index])
    copies += [
        send(q_part.at[peer], q_land.at[z], q_send.at[n], q_recv.at[z], {"head": peer})
        for n, peer in enumerate(peers)
    ]
    mixed_rows = mixed_all[...].reshape(zs * feats, rows).T
    hidden_rows = atoms[...] + dot_halves(halves(mixed_rows), outs) + b_out[...]
    hidden[...] = hidden_rows
    hidden.flush()
    normal, rate = normalize(hidden_rows)
    normal_two[...] = normal
    rate_two[...] = jnp.broadcast_to(rate, rate_two.shape)
    normed = normal * gain[...] + bias[...]
    pre = dot_halves(halves(normed), ups) + b_up[...]
    phi = 0.5 * (1.0 + lax.erf(pre * math.sqrt(0.5)))
    act = pre * phi
    d_pre = d_act * (phi + pre * jnp.exp(-0.5 * pre * pre) * (1.0 / math.sqrt(2.0 * math.pi)))
    d_pres = halves(d_pre)
    part[...] = dot_halves(d_pres, ups, NT).reshape(zs, piece, width)
    copies += [
        send(part.at[peer], landed.at[z], part_send.at[n], part_recv.at[z], {"head": peer})
        for n, peer in enumerate(peers)
    ]
    landed[z] = part[z]
    ups_part[...] = dot_halves(halves(normed.T), d_pres).reshape(ups_part.shape)
    copies.append(send(ups_part.at[:, other_core], ups_sib, sib_send.at[0], sib_recv.at[0], sibling))
    downs_part[...] = dot_halves(halves(act.T), cots).reshape(downs_part.shape)
    copies.append(send(downs_part.at[:, other_core], downs_sib, sib_send.at[1], sib_recv.at[1], sibling))
    for n, source in enumerate(far):
        for m, peer in enumerate(peers):
            ready = k_all.at[source, peer]
            arrived(ready, k_recv.at[source, peer])
            copies.append(send(ready, ready, ks_send.at[n, m], k_recv.at[source, peer], sibling))
    down[...] = dot_halves(halves(act), downs)
    down.flush()
    small[SMALL_B_UP : SMALL_B_UP + 1, 0 : d_pre.shape[1]] = column_sum(d_pre)
    for kind, (parts, sib, go, got) in enumerate(
        [(ups_part, ups_sib, ups_go, ups_got), (downs_part, downs_sib, downs_go, downs_got)]
    ):
        arrived(sib, sib_recv.at[kind])
        go[...] = sib[...] + parts[:, core]
        copies += [
            send(
                go.at[peer], got.at[team], g_send.at[kind, n], g_recv.at[kind, team],
                team_device(peer, core, chips),
            )
            for n, peer in enumerate(far_teams)
        ]
        got[team] = go[team]
    for peer in peers:
        arrived(q_land.at[peer], q_recv.at[peer])
    for n in range(zs):
        q_all[n] = q_land[n].T
    for n in range(blocks):
        k_all[n, z] = kept[n, 0:feats, :]
    for source in [sib_blk] + far_siblings:
        for peer in peers:
            arrived(k_all.at[source, peer], k_recv.at[source, peer])
    squares[...] = jnp.zeros(squares.shape, F32)
    at_once = 4
    rounds = heads // at_once

    def square_step(index, carry):
        there = lax.div(index, rounds)
        some = pl.ds(pl.multiple_of(lax.rem(index, rounds) * (8 * at_once), 8 * at_once), 8 * at_once)
        q_some = q_all[there, some, :]
        k_some = joined(k_all[n, there, some, :] for n in range(blocks))
        added = None
        for h in range(at_once):
            head = slice(8 * h, 8 * h + 8)
            q_high, q_low = wide_halves(q_some[head])
            k_high, k_low = wide_halves(k_some[head])
            value = dot(
                stacked([q_high, q_high, q_low, q_low]), stacked([k_high, k_low, k_high, k_low]), TN
            )
            added = value * value if added is None else added + value * value
        squares[...] += added
        return carry

    lax.fori_loop(0, zs * rounds, square_step, 0)
    same = id_column[mine, 0:1] == id_row[0:1, :]
    norms = jnp.sqrt(squares[...] + 1.0)
    terms = jnp.where(same, jnp.log1p(jnp.exp(norms - math.sqrt(zs * heads))), 0.0)
    number = jnp.where(same, 1.0, 0.0)

    def total(value):
        return jnp.sum(jnp.sum(value, axis=1, keepdims=True), axis=0, keepdims=True)

    lane = lax.broadcasted_iota(jnp.int32, (1, width), 1)
    small[SMALL_PENALTY : SMALL_PENALTY + 1, :] = jnp.where(
        lane == 0, total(terms), jnp.where(lane == 1, total(number), 0.0)
    )
    for peer in peers:
        arrived(landed.at[peer], part_recv.at[peer])
    d_normed = functools.reduce(jnp.add, [landed[n] for n in range(zs)])
    normal = normal_two[mine, :]
    d_rows = cot[mine, :] + normalize_back(d_normed, gain[...], normal, rate_two[mine, 0:1])
    d_halves = halves(d_rows)
    for n in range(zs):
        some = slice(n * feats, (n + 1) * feats)
        back[n] = dot_halves(d_halves, (outs[0][some], outs[1][some]), NT)
    copies += [
        send(back.at[peer], back_landed.at[z], back_send.at[n], back_recv.at[z], {"head": peer})
        for n, peer in enumerate(peers)
    ]
    back_landed[z] = back[z]
    d_hidden[...] = d_rows
    d_hidden.flush()
    small[SMALL_LN2_GAIN : SMALL_LN2_GAIN + 1, :] = column_sum(d_normed * normal)
    small[SMALL_LN2_BIAS : SMALL_LN2_BIAS + 1, :] = column_sum(d_normed)
    small[SMALL_B_OUT : SMALL_B_OUT + 1, :] = column_sum(d_rows)
    small.flush()
    for peer in peers:
        arrived(back_landed.at[peer], back_recv.at[peer])
    d_mixed[...] = back_landed[...].reshape(rows, feats).T
    d_mixed.flush()
    for kind, (got, result) in enumerate([(ups_got, up_share), (downs_got, down_share)]):
        for peer in far_teams:
            arrived(got.at[peer], g_recv.at[kind, peer])
        result[...] = functools.reduce(jnp.add, [got[n] for n in range(teams)])
        result.flush()
    for copy in copies:
        copy.wait_send()

    def drain(index, carry):
        for copy in mix_copies(index):
            copy.wait_send()
        return carry

    lax.fori_loop(0, groups, drain, 0)


def front(zs, dps, teams, pair, *operands):
    _, heads, rows, cols = pair.shape
    feats, blocks = heads * DH, cols // rows
    width, units = operands[0].shape[1], operands[12].shape[1]
    piece, group = rows // zs, GROUP
    up_rows, down_rows = width // (2 * teams), units // (2 * teams)
    groups = heads // group
    slab = pltpu.VMEM((zs, piece, width), F32)
    narrow = pltpu.VMEM((zs, piece, feats), F32)
    one_up, one_down = pltpu.VMEM((teams, up_rows, units), F32), pltpu.VMEM((teams, down_rows, width), F32)
    dma = pltpu.SemaphoreType.DMA
    return staged_call(
        front_kernel,
        "front",
        operands,
        [
            (feats, rows), (blocks, 2 * feats + 8, rows), (rows, LANES), (heads, rows, LANES), (feats, rows),
            (STRIP, cols), (feats, rows), (rows, width), (rows, width), (piece, width),
            (up_rows, units), (down_rows, width), (SMALL_ROWS, width),
        ],
        [
            pltpu.VMEM((2, group, rows, cols), F32),
            pltpu.VMEM((group, rows, cols), F32),
            pltpu.VMEM((group, rows, cols), BF16),
            pltpu.VMEM((group, rows, cols), BF16),
            narrow, narrow,
            pltpu.VMEM((zs, feats, piece), F32),
            pltpu.VMEM((blocks, zs, feats, rows), F32),
            pltpu.VMEM((zs, dps, 2, feats // (2 * dps), width), F32),
            pltpu.VMEM((piece, cols), F32),
            pltpu.VMEM((zs, feats, rows), F32),
            pltpu.VMEM((rows, width), F32),
            pltpu.VMEM((rows, LANES), F32),
            slab, slab, narrow, narrow,
            pltpu.VMEM((teams, 2, up_rows, units), F32),
            one_up, one_up, one_up,
            pltpu.VMEM((teams, 2, down_rows, width), F32),
            one_down, one_down, one_down,
            dma((2,)),
            dma((blocks,)), dma((blocks,)),
            dma((zs,)), dma((zs, blocks // 2)), dma((blocks // 2, zs)), dma((blocks, zs)),
            dma((zs,)), dma((zs,)),
            dma((zs,)), dma((zs, dps)), dma((zs, dps)), dma((zs, dps, 2)),
            dma((zs, groups)), dma((zs, groups)),
            dma((zs,)), dma((zs,)),
            dma((zs,)), dma((zs,)),
            dma((2,)), dma((2,)),
            dma((2, teams)), dma((2, teams)),
        ],
        58,
        remote=0,
        raw=(pair,),
    )


def finish_kernel(operands, results, scratch, raw):
    (
        d_keys, d_values, d_hidden, d_queries, atoms, gain, bias, w_query, mixed, small_in, w_key, w_value,
    ) = operands
    grad_atoms, total_grads, small, penalty = results
    (
        sib_keys, sib_values, go_keys, go_values, got_keys, got_values,
        part, landed, grads, sib_grads, go_grads, got_grads, hidden_all, small_z, small_all,
        sib_send, sib_recv, kv_send, kv_recv, part_send, part_recv, back_send, back_recv,
        g_send, g_recv, t_send, t_recv, f_send, h_send, h_recv,
        small_z_send, small_z_recv, small_send, small_recv,
    ) = scratch
    chips, _, feats, rows = d_keys.shape
    zs, piece, width = part.shape
    teams, _, share, _ = grads.shape
    blk, z, dp = lax.axis_index("blk"), lax.axis_index("head"), lax.axis_index("dp")
    core, chip = lax.rem(blk, 2), lax.div(blk, 2)
    other_core = 1 - core
    sibling = {"blk": blk + 1 - 2 * core}
    peers = others(z, zs)
    team = dp * chips + chip
    far_teams = others(team, teams)
    far_chips = others(chip, chips)
    place = team * 2 + core
    far_places = others(place, teams * 2)
    plane = [team_device(lax.div(value, 2), lax.rem(value, 2), chips) for value in far_places]
    meeting = [{"head": peer} for peer in peers] + plane
    greet(meeting)
    meet(meeting)
    copies = [
        send(d_keys.source.at[:, other_core], sib_keys, sib_send.at[0], sib_recv.at[0], sibling),
        send(d_values.source.at[:, other_core], sib_values, sib_send.at[1], sib_recv.at[1], sibling),
    ]
    copies += [
        send(d_hidden.source, hidden_all.at[z], h_send.at[n], h_recv.at[z], {"head": peer})
        for n, peer in enumerate(peers)
    ]
    own_keys, own_values = d_keys.ref, d_values.ref
    for kind, (sib, mine_too, go, got) in enumerate(
        [(sib_keys, own_keys, go_keys, got_keys), (sib_values, own_values, go_values, got_values)]
    ):
        arrived(sib, sib_recv.at[kind])
        go[...] = sib[...] + mine_too[:, core]
        copies += [
            send(
                go.at[peer], got.at[chip], kv_send.at[kind, n], kv_recv.at[kind, chip],
                {"blk": peer * 2 + core},
            )
            for n, peer in enumerate(far_chips)
        ]
    got_keys[chip] = go_keys[chip]
    got_values[chip] = go_values[chip]
    normal, rate = normalize(atoms[...])
    normed = halves(normal * gain[...] + bias[...])
    dq_rows = d_queries[...].T
    d_normed = dot_full(dq_rows, w_query[...], NT)
    grad_q = dot_halves(halves(d_queries[...]), normed)
    mine = pl.ds(pl.multiple_of(z * piece, 8), piece)
    small_z[z] = small_in[0:8, :]
    hidden_all[z] = d_hidden[...]
    for peer in far_chips:
        arrived(got_keys.at[peer], kv_recv.at[0, peer])
        arrived(got_values.at[peer], kv_recv.at[1, peer])
    dk = functools.reduce(jnp.add, [got_keys[n] for n in range(chips)])
    dv = functools.reduce(jnp.add, [got_values[n] for n in range(chips)])
    dv_rows = dv.T
    d_normed = (
        d_normed + dot_full(dk.T, w_key[...], NT) + dot_full(dv_rows, w_value[...], NT)
    )
    part[...] = d_normed.reshape(zs, piece, width)
    copies += [
        send(part.at[peer], landed.at[z], part_send.at[n], part_recv.at[z], {"head": peer})
        for n, peer in enumerate(peers)
    ]
    landed[z] = part[z]
    grad_k = dot_halves(halves(dk), normed)
    grad_v = dot_halves(halves(dv), normed)
    for peer in peers:
        arrived(hidden_all.at[peer], h_recv.at[peer])
    grad_o = dot_full(mixed[...], hidden_all[...].reshape(rows, width))
    grads[...] = jnp.concatenate([grad_q, grad_k, grad_v, grad_o], axis=0).reshape(grads.shape)
    copies.append(send(grads.at[:, other_core], sib_grads, sib_send.at[2], sib_recv.at[2], sibling))
    arrived(sib_grads, sib_recv.at[2])
    go_grads[...] = sib_grads[...] + grads[:, core]
    copies += [
        send(
            go_grads.at[peer], got_grads.at[team], g_send.at[n], g_recv.at[team], team_device(peer, core, chips)
        )
        for n, peer in enumerate(far_teams)
    ]
    got_grads[team] = go_grads[team]
    for peer in peers:
        arrived(landed.at[peer], part_recv.at[peer])
    d_normed = functools.reduce(jnp.add, [landed[n] for n in range(zs)])
    normal, rate = normalize(atoms[mine, :])
    grad_atoms[mine, :] = d_hidden[...] + normalize_back(d_normed, gain[...], normal, rate)
    small_z[z, SMALL_LN1_GAIN : SMALL_LN1_GAIN + 1, :] = column_sum(d_normed * normal)
    small_z[z, SMALL_LN1_BIAS : SMALL_LN1_BIAS + 1, :] = column_sum(d_normed)
    copies += [
        send(small_z.at[z], small_z.at[z], small_z_send.at[n], small_z_recv.at[z], {"head": peer})
        for n, peer in enumerate(peers)
    ]
    copies += [
        send(grad_atoms.at[mine], grad_atoms.at[mine], back_send.at[n], back_recv.at[z], {"head": peer})
        for n, peer in enumerate(peers)
    ]
    for peer in far_teams:
        arrived(got_grads.at[peer], g_recv.at[peer])
    total_grads[team, core] = functools.reduce(jnp.add, [got_grads[n] for n in range(teams)])
    ready = total_grads.at[team, core]
    copies.append(send(ready, ready, t_send.at[0], t_recv.at[team, core], sibling))
    copies += [
        send(ready, ready, t_send.at[n + 1], t_recv.at[team, core], team_device(peer, core, chips))
        for n, peer in enumerate(far_teams)
    ]
    for peer in peers:
        arrived(small_z.at[peer], small_z_recv.at[peer])
    small_all[place, 0:8, :] = functools.reduce(jnp.add, [small_z[n] for n in range(zs)])
    small_all[place, 8:16, :] = small_in[8:16, :]
    small_all[place, SMALL_B_QUERY : SMALL_B_QUERY + 1, 0:feats] = column_sum(dq_rows)
    small_all[place, SMALL_B_VALUE : SMALL_B_VALUE + 1, 0:feats] = column_sum(dv_rows)
    copies += [
        send(small_all.at[place], small_all.at[place], small_send.at[n], small_recv.at[place], target)
        for n, target in enumerate(plane)
    ]
    for n, peer in enumerate(far_teams):
        ready = total_grads.at[peer, core]
        arrived(ready, t_recv.at[peer, core])
        copies.append(send(ready, ready, f_send.at[n], t_recv.at[peer, core], sibling))
    for source in far_places:
        arrived(small_all.at[source], small_recv.at[source])
    summed = functools.reduce(jnp.add, [small_all[n] for n in range(2 * teams)])
    small[...] = summed
    ends = summed[SMALL_PENALTY : SMALL_PENALTY + 1, :]
    penalty[...] = ends[:, 0:1] / ends[:, 1:2]
    for peer in [team] + far_teams:
        arrived(total_grads.at[peer, other_core], t_recv.at[peer, other_core])
    total_grads.flush()
    for peer in peers:
        there = pl.ds(pl.multiple_of(peer * piece, 8), piece)
        arrived(grad_atoms.at[there], back_recv.at[peer])
    for copy in copies:
        copy.wait_send()


def finish(zs, dps, *operands):
    d_keys, atoms = operands[0], operands[4]
    chips, _, feats, rows = d_keys.shape
    width = atoms.shape[1]
    piece = rows // zs
    teams = dps * chips
    share = 4 * feats // (2 * teams)
    some = pltpu.VMEM((chips, feats, rows), F32)
    slab = pltpu.VMEM((zs, piece, width), F32)
    one = pltpu.VMEM((teams, share, width), F32)
    dma = pltpu.SemaphoreType.DMA
    return staged_call(
        finish_kernel,
        "finish",
        operands,
        [
            (rows, width),
            (teams, 2, share, width),
            (SMALL_ROWS, width),
            (1, 1),
        ],
        [some] * 6
        + [slab, slab, pltpu.VMEM((teams, 2, share, width), F32), one, one, one, slab]
        + [
            pltpu.VMEM((zs, 8, width), F32),
            pltpu.VMEM((2 * teams, SMALL_ROWS, width), F32),
            dma((3,)), dma((3,)),
            dma((2, chips)), dma((2, chips)),
            dma((zs,)), dma((zs,)),
            dma((zs,)), dma((zs,)),
            dma((teams,)), dma((teams,)),
            dma((teams,)), dma((teams, 2)), dma((teams,)),
            dma((zs,)), dma((zs,)),
            dma((zs,)), dma((zs,)),
            dma((2 * teams,)), dma((2 * teams,)),
        ],
        58,
        remote=2,
    )


def place_kernel(operands, results, scratch, raw):
    total_grads, hidden, down, b_down, small = operands
    grad_query, grad_key, grad_value, grad_out, out_atoms = results[:5]
    feats, width = grad_out.shape
    done = total_grads[...].reshape(4 * feats, width)
    grad_query[...] = done[0:feats].T
    grad_query.flush()
    grad_key[...] = done[feats : 2 * feats].T
    grad_key.flush()
    grad_value[...] = done[2 * feats : 3 * feats].T
    grad_value.flush()
    grad_out[...] = done[3 * feats :]
    grad_out.flush()
    out_atoms[...] = hidden[...] + down[...] + b_down[...]
    out_atoms.flush()
    for result, row in zip(results[5:], SMALL_OUTPUTS, strict=True):
        result[...] = small[row : row + 1, 0 : result.shape[1]]


SMALL_OUTPUTS = (
    SMALL_LN1_GAIN, SMALL_LN1_BIAS, SMALL_B_QUERY, SMALL_B_VALUE, SMALL_B_OUT, SMALL_LN2_GAIN, SMALL_LN2_BIAS,
    SMALL_B_UP, SMALL_B_DOWN,
)


def place(feats, units, straight, *operands):
    rows, width = operands[1].shape
    lengths = {SMALL_B_QUERY: feats, SMALL_B_VALUE: feats, SMALL_B_UP: units}
    return staged_call(
        place_kernel,
        "place",
        operands,
        [(width, feats)] * 3
        + [(feats, width), (rows, width)]
        + [(1, lengths.get(row, width)) for row in SMALL_OUTPUTS],
        [],
        58,
        straight=straight,
    )


def local(
    zs, dps,
    atoms, pair, mol_ids, ln1_gain, ln1_bias, w_query, b_query, w_key, w_value, b_value, w_out, b_out,
    ln2_gain, ln2_bias, w_up, b_up, w_down, b_down, cot_atoms, cot_pair,
):
    blocks = pair.shape[3] // pair.shape[2]
    inputs, cot = atoms[0], cot_atoms[0]

    def line(value):
        return value.reshape(1, -1)

    (
        queries, kept, id_column, log_sums, mixed, id_row, d_mixed, hidden, down, d_hidden, up_share, down_share, small,
    ) = front(
        zs, dps, dps * blocks // 2, pair,
        inputs, mol_ids, line(ln1_gain), line(ln1_bias), w_key, w_value, line(b_value), w_query, line(b_query),
        w_out, cot, w_down, w_up, line(b_out), line(ln2_gain), line(ln2_bias), line(b_up),
    )
    down = lax.psum(down, "head")
    grad_up = lax.all_gather(up_share, ("dp", "blk"), axis=0, tiled=True)
    grad_down = lax.all_gather(down_share, ("dp", "blk"), axis=0, tiled=True)
    out_pair, grad_pair, d_queries, d_keys, d_values = attend_back(
        pair, cot_pair, queries, kept, mixed, d_mixed, log_sums, id_column, id_row
    )
    grad_atoms, total_grads, small, penalty = finish(
        zs, dps,
        d_keys, d_values, d_hidden, d_queries, inputs, line(ln1_gain), line(ln1_bias), w_query, mixed,
        small, w_key, w_value,
    )
    placed = place(
        w_query.shape[1], w_up.shape[1],
        [grad_atoms, grad_up, grad_down],
        total_grads, hidden, down, line(b_down), small,
    )
    grad_atoms, grad_up, grad_down, grad_query, grad_key, grad_value, grad_out, out_atoms = placed[:8]
    (
        grad_ln1_gain, grad_ln1_bias, grad_b_query, grad_b_value, grad_b_out, grad_ln2_gain, grad_ln2_bias,
        grad_b_up, grad_b_down,
    ) = [value.reshape(-1) for value in placed[8:]]
    return (
        out_atoms[None],
        out_pair,
        penalty[0, 0],
        grad_atoms[None],
        grad_pair,
        grad_ln1_gain,
        grad_ln1_bias,
        grad_query,
        grad_b_query,
        grad_key,
        grad_value,
        grad_b_value,
        grad_out,
        grad_b_out,
        grad_ln2_gain,
        grad_ln2_bias,
        grad_up,
        grad_b_up,
        grad_down,
        grad_b_down,
    )


def solution(mesh):
    rows, pairs = P("dp", "blk", None), P("dp", "head", "blk", None)
    columns = P(None, "head")
    return jax.shard_map(
        functools.partial(local, mesh.shape["head"], mesh.shape["dp"]),
        mesh=mesh,
        in_specs=(
            rows, pairs, P("dp", "blk"), P(), P(), columns, P("head"), columns, columns, P("head"),
            P("head", None), P(), P(), P(), columns, P("head"), P("head", None), P(), rows, pairs,
        ),
        out_specs=(
            rows, pairs, P(), rows, pairs, P(), P(), columns, P("head"), columns, columns, P("head"),
            P("head", None), P(), P(), P(), columns, P("head"), P("head", None), P(),
        ),
        check_vma=False,
    )
```

```python
import functools
import math

import jax
import jax.numpy as jnp
from jax import lax
from jax.experimental import pallas as pl
from jax.experimental.pallas import tpu as pltpu
from jax.sharding import PartitionSpec as P

DH = 8
LANES = 128
STRIP = 16
CHUNK = 256
GROUP = 2
NORM_EPS = 1e-05
MASK_FILL = -1e30
F32 = jnp.float32
BF16 = jnp.bfloat16
MESH = pl.DeviceIdType.MESH
NN = (((1,), (0,)), ((), ()))
NT = (((1,), (1,)), ((), ()))
TN = (((0,), (0,)), ((), ()))
VMEM = pl.BlockSpec(memory_space=pltpu.VMEM)


def dot(left, right, dims=NN):
    return lax.dot_general(left, right, dims, preferred_element_type=F32)


def halves(value):
    high = value.astype(BF16)
    return high, (value - high.astype(F32)).astype(BF16)


def dot_halves(left, right, dims=NN):
    return dot(left[0], right[0], dims) + (
        dot(left[0], right[1], dims) + dot(left[1], right[0], dims)
    )


def dot_full(left, right, dims=NN):
    return dot_halves(halves(left), halves(right), dims)


def normalize(inputs):
    centred = inputs - jnp.mean(inputs, -1, keepdims=True)
    rate = lax.rsqrt(jnp.mean(centred * centred, -1, keepdims=True) + NORM_EPS)
    return centred * rate, rate


def normalize_back(grad, gain, normal, rate):
    scaled = grad * gain
    return rate * (
        scaled
        - jnp.mean(scaled, -1, keepdims=True)
        - normal * jnp.mean(scaled * normal, -1, keepdims=True)
    )


def column_sum(value):
    return jnp.sum(value, 0, keepdims=True)


def send(src, dst, send_sem, recv_sem, target):
    copy = pltpu.make_async_remote_copy(
        src_ref=src,
        dst_ref=dst,
        send_sem=send_sem,
        recv_sem=recv_sem,
        device_id=target,
        device_id_type=MESH,
    )
    copy.start()
    return copy


def arrived(ref, sem):
    pltpu.make_async_remote_copy(
        src_ref=ref, dst_ref=ref, send_sem=sem, recv_sem=sem, device_id={}, device_id_type=MESH
    ).wait_recv()


def greet(targets):
    for target in targets:
        pl.semaphore_signal(pltpu.get_barrier_semaphore(), inc=1, device_id=target, device_id_type=MESH)


def meet(targets):
    pl.semaphore_wait(pltpu.get_barrier_semaphore(), len(targets))


def others(index, count):
    return [lax.rem(index + step, count) for step in range(1, count)]


class Operand:
    def __init__(self, source, slot, sem):
        self.source, self.slot, self.shape = source, slot, slot.shape
        self.copy = pltpu.make_async_copy(source, slot, sem)
        self.copy.start()

    @property
    def ref(self):
        if self.copy is not None:
            self.copy.wait()
            self.copy = None
        return self.slot

    def __getitem__(self, index):
        return self.ref[index]


class Result:
    def __init__(self, target, slot, sem):
        self.slot, self.shape, self.at = slot, slot.shape, slot.at
        self.copy = pltpu.make_async_copy(slot, target, sem)
        self.begun = False

    def __setitem__(self, index, value):
        self.slot[index] = value

    def __getitem__(self, index):
        return self.slot[index]

    def flush(self):
        if not self.begun:
            self.copy.start()
            self.begun = True


def staged_call(kernel, name, operands, results, scratch, megabytes, remote=None, raw=(), straight=()):
    n_in, n_out, n_raw, n_straight = len(operands), len(results), len(raw), len(straight)

    def body(*refs):
        sources, left, refs = refs[:n_in], refs[n_in : n_in + n_raw], refs[n_in + n_raw :]
        moved, refs = refs[:n_straight], refs[n_straight:]
        arrays, refs = refs[:n_straight], refs[n_straight:]
        targets, refs = refs[:n_out], refs[n_out:]
        slots, made, refs = refs[:n_in], refs[n_in : n_in + n_out], refs[n_in + n_out :]
        in_sem, out_sem, move_sem, refs = refs[0], refs[1], refs[2], refs[3:]
        through, refs = refs[:n_straight], refs[n_straight:]
        loads = [pltpu.make_async_copy(moved[n], through[n], move_sem.at[n]) for n in range(n_straight)]
        moves = [pltpu.make_async_copy(through[n], arrays[n], move_sem.at[n]) for n in range(n_straight)]
        for load in loads:
            load.start()
        ins = [Operand(sources[n], slots[n], in_sem.at[n]) for n in range(n_in)]
        outs = [Result(targets[n], made[n], out_sem.at[n]) for n in range(n_out)]
        for load, move in zip(loads, moves, strict=True):
            load.wait()
            move.start()
        kernel(ins, outs, refs, left)
        for operand in ins:
            operand.ref
        for result in outs:
            result.flush()
        for copy in moves + [result.copy for result in outs]:
            copy.wait()

    anywhere = pl.BlockSpec(memory_space=pltpu.HBM)
    extra = {} if remote is None else {"collective_id": remote, "has_side_effects": True}
    return pl.pallas_call(
        body,
        out_shape=[jax.ShapeDtypeStruct(value.shape, value.dtype) for value in straight]
        + [jax.ShapeDtypeStruct(shape, F32) for shape in results],
        in_specs=[anywhere] * (n_in + n_raw + n_straight),
        out_specs=[anywhere] * (n_straight + n_out),
        scratch_shapes=[pltpu.VMEM(value.shape, value.dtype) for value in operands]
        + [pltpu.VMEM(shape, F32) for shape in results]
        + [pltpu.SemaphoreType.DMA((n,)) for n in (n_in, n_out, max(1, n_straight))]
        + [pltpu.VMEM(value.shape, value.dtype) for value in straight]
        + list(scratch),
        compiler_params=pltpu.CompilerParams(vmem_limit_bytes=megabytes << 20, **extra),
        name=name,
    )(*operands, *raw, *straight)


def joined(pieces):
    return jnp.concatenate(list(pieces), axis=1)


def stacked(parts):
    return jnp.concatenate(parts, axis=0).astype(BF16)


def wide_halves(value):
    high = value.astype(BF16).astype(F32)
    return high, value - high


def attend_group(pair, queries, keys, values, id_column, id_row, log_sums, first, score, high, low):
    group, rows, cols = score.shape
    strips = rows // STRIP
    chunk = min(CHUNK, cols)
    mixed = []
    for g in range(group):
        head = slice(8 * g, 8 * g + 8)
        q_high, q_low = wide_halves(queries[head, :])
        k_high, k_low = wide_halves(keys[head, :])
        v_high, v_low = wide_halves(values[head, :])
        ones = jnp.ones_like(v_high)
        q_pack = stacked([q_high, q_high, q_low, q_low])
        k_pack = stacked([k_high, k_low, k_high, k_low])
        v_pack = stacked([v_high, v_low, ones, jnp.zeros_like(ones)])
        tops = [None] * strips
        for start in range(0, cols, chunk):
            part = slice(start, start + chunk)
            score[g, :, part] = dot(q_pack, k_pack[:, part], TN)
            for s in range(strips):
                line = pl.ds(s * STRIP, STRIP)
                own = id_column[line, :]
                for j in range(start, start + chunk, LANES):
                    tile = pl.ds(j, LANES)
                    value = pair[g, line, tile] + score[g, line, tile]
                    value = jnp.where(own == id_row[:, tile], value, MASK_FILL)
                    score[g, line, tile] = value
                    tops[s] = value if tops[s] is None else jnp.maximum(tops[s], value)
        tops = [
            jnp.broadcast_to(jnp.max(top, axis=1, keepdims=True), (STRIP, LANES)) for top in tops
        ]
        totals = [None] * strips
        gathered = None
        for start in range(0, cols, chunk):
            part = slice(start, start + chunk)
            for s in range(strips):
                line = pl.ds(s * STRIP, STRIP)
                for j in range(start, start + chunk, LANES):
                    tile = pl.ds(j, LANES)
                    weight = jnp.exp(score[g, line, tile] - tops[s])
                    high[g, line, tile], low[g, line, tile] = halves(weight)
                    totals[s] = weight if totals[s] is None else totals[s] + weight
            term = dot(v_pack[:, part], high[g, :, part], NT) + dot(
                v_pack[:, part], low[g, :, part], NT
            )
            gathered = term if gathered is None else gathered + term
        for s in range(strips):
            total = jnp.sum(totals[s], axis=1, keepdims=True)
            log_sums[first + g, pl.ds(s * STRIP, STRIP), :] = tops[s] + jnp.log(total)
        mixed.append((gathered[0:8] + gathered[8:16]) / gathered[16:17])
    return jnp.concatenate(mixed, axis=0)


def attend_back_kernel(
    pair, cot, queries, keys, values, mixed, d_mixed, log_sums, id_column, id_row,
    out_pair, grad_pair, d_queries, d_keys, d_values,
    pair_buf, cot_buf, out_buf, grad_buf, score, d_prob, p_high, p_low, g_high, g_low, in_sem, out_sem,
):
    heads = pair.shape[1]
    rows, cols = score.shape
    depth = pair_buf.shape[0]
    chunk = min(CHUNK, cols)
    place = lax.broadcasted_iota(jnp.int32, (8, rows), 0)

    def moves(index, sources, targets, sem, outward):
        slot = lax.rem(index, depth)
        return [
            pltpu.make_async_copy(buf.at[slot], array.at[0, index], sem.at[n, slot])
            if outward
            else pltpu.make_async_copy(array.at[0, index], buf.at[slot], sem.at[n, slot])
            for n, (array, buf) in enumerate(zip(sources, targets, strict=True))
        ]

    def inward(index):
        return moves(index, (pair, cot), (pair_buf, cot_buf), in_sem, False)

    def outward(index):
        return moves(index, (out_pair, grad_pair), (out_buf, grad_buf), out_sem, True)

    def both(left, high, low, dims):
        value = dot(left, high, dims) + dot(left, low, dims)
        return value[0:8] + value[8:16]

    for n in range(min(depth, heads)):
        for copy in inward(n):
            copy.start()

    def step(index, carry):
        slot = lax.rem(index, depth)
        head = pl.ds(pl.multiple_of(index * 8, 8), 8)
        q_high, q_low = wide_halves(queries[head, :])
        k_high, k_low = wide_halves(joined(keys[n, head, :] for n in range(keys.shape[0])))
        v_high, v_low = wide_halves(joined(values[n, head, :] for n in range(keys.shape[0])))
        m_high, m_low = wide_halves(d_mixed[head, :])
        delta_high, rest = wide_halves(-column_sum(mixed[head, :] * d_mixed[head, :]))
        delta_mid, delta_low = wide_halves(rest)
        deltas = jnp.where(
            place == 0, delta_high, jnp.where(place == 1, delta_mid, jnp.where(place == 2, delta_low, 0.0))
        )
        q_pack = stacked([q_high, q_high, q_low, q_low])
        k_pack = stacked([k_high, k_low, k_high, k_low])
        m_pack = stacked([m_high, m_high, m_low, deltas])
        v_pack = stacked([v_high, v_low, v_high, jnp.ones_like(v_high)])
        q_pair = stacked([q_high, q_low])
        k_pair = stacked([k_high, k_low])
        m_pair = stacked([m_high, m_low])
        for copy in inward(index):
            copy.wait()

        @pl.when(index >= depth)
        def _():
            for copy in outward(index - depth):
                copy.wait()

        d_query = [None]

        def before(part):
            score[:, part] = dot(q_pack, k_pack[:, part], TN)
            d_prob[:, part] = dot(m_pack, v_pack[:, part], TN)

        def middle(part):
            for s in range(rows // STRIP):
                line = pl.ds(s * STRIP, STRIP)
                own = id_column[line, :]
                log_sum = log_sums[index, line, :]
                for j in range(part.start, part.stop, LANES):
                    tile = pl.ds(j, LANES)
                    value = pair_buf[slot, line, tile] + score[line, tile]
                    out_buf[slot, line, tile] = value
                    prob = jnp.exp(jnp.where(own == id_row[:, tile], value - log_sum, MASK_FILL))
                    p_high[line, tile], p_low[line, tile] = halves(prob)
                    grad = prob * d_prob[line, tile] + cot_buf[slot, line, tile]
                    grad_buf[slot, line, tile] = grad
                    g_high[line, tile], g_low[line, tile] = halves(grad)

        def after(part):
            d_value = both(m_pair, p_high[:, part], p_low[:, part], NN)
            d_key = both(q_pair, g_high[:, part], g_low[:, part], NN)
            for n in range(part.start // rows, part.stop // rows):
                span = slice(n * rows - part.start, (n + 1) * rows - part.start)
                d_keys[n // 2, n % 2, head, :] = d_key[:, span]
                d_values[n // 2, n % 2, head, :] = d_value[:, span]
            term = both(k_pair[:, part], g_high[:, part], g_low[:, part], NT)
            d_query[0] = term if d_query[0] is None else d_query[0] + term

        parts = [slice(start, start + chunk) for start in range(0, cols, chunk)]
        before(parts[0])
        for n, part in enumerate(parts):
            if n + 1 < len(parts):
                before(parts[n + 1])
            middle(part)
            if n >= 1:
                after(parts[n - 1])
        after(parts[-1])
        d_queries[head, :] = d_query[0] * (DH ** (-0.5))
        for copy in outward(index):
            copy.start()

        @pl.when(index + depth < heads)
        def _():
            for copy in inward(index + depth):
                copy.start()

        return carry

    lax.fori_loop(0, heads, step, 0)
    for n in range(max(0, heads - depth), heads):
        for copy in outward(n):
            copy.wait()


def attend_back(pair, cot, queries, kept, mixed, d_mixed, log_sums, id_column, id_row):
    _, heads, rows, cols = pair.shape
    feats = heads * DH
    blocks = kept.shape[0]
    depth = 4
    big = pl.BlockSpec(memory_space=pltpu.HBM)
    flat = pl.BlockSpec((feats, rows), lambda n: (0, 0))
    split = pl.BlockSpec((blocks // 2, 2, feats, rows), lambda n: (0, 0, 0, 0))
    return pl.pallas_call(
        attend_back_kernel,
        grid=(1,),
        in_specs=[
            big, big, flat,
            pl.BlockSpec((blocks, feats, rows), lambda n: (0, 0, 0)),
            pl.BlockSpec((blocks, feats, rows), lambda n: (0, 1, 0)),
            flat, flat,
            pl.BlockSpec((heads, rows, LANES), lambda n: (0, 0, 0)),
            pl.BlockSpec((rows, LANES), lambda n: (0, 0)),
            pl.BlockSpec((STRIP, cols), lambda n: (0, 0)),
        ],
        out_specs=[big, big, flat, split, split],
        out_shape=[
            jax.ShapeDtypeStruct(pair.shape, F32),
            jax.ShapeDtypeStruct(pair.shape, F32),
            jax.ShapeDtypeStruct((feats, rows), F32),
            jax.ShapeDtypeStruct((blocks // 2, 2, feats, rows), F32),
            jax.ShapeDtypeStruct((blocks // 2, 2, feats, rows), F32),
        ],
        scratch_shapes=[pltpu.VMEM((depth, rows, cols), F32)] * 4
        + [pltpu.VMEM((rows, cols), F32)] * 2
        + [pltpu.VMEM((rows, cols), BF16)] * 4
        + [pltpu.SemaphoreType.DMA((2, depth))] * 2,
        compiler_params=pltpu.CompilerParams(vmem_limit_bytes=60 << 20),
        cost_estimate=pl.CostEstimate(
            flops=2 * 400 * heads * rows * cols,
            bytes_accessed=16 * heads * rows * cols,
            transcendentals=heads * rows * cols,
        ),
        name="attend_back",
    )(pair, cot, queries, kept, kept, mixed, d_mixed, log_sums, id_column, id_row)


SMALL_LN1_GAIN, SMALL_LN1_BIAS, SMALL_LN2_GAIN, SMALL_LN2_BIAS = 0, 1, 2, 3
SMALL_B_OUT, SMALL_B_DOWN, SMALL_PENALTY = 4, 5, 6
SMALL_B_QUERY, SMALL_B_VALUE, SMALL_B_UP = 8, 9, 10
SMALL_ROWS = 16


def team_device(team, core, chips):
    return {"dp": lax.div(team, chips), "blk": lax.rem(team, chips) * 2 + core}


def front_kernel(operands, results, scratch, raw):
    (
        atoms, ids, gain_one, bias_one, w_key, w_value, b_value, w_query, b_query, w_out, cot, w_down, w_up, b_out,
        gain, bias, b_up, b_down,
    ) = operands
    (pair,) = raw
    (
        queries, kept, id_column, log_sums, mixed, id_row, d_mixed, out_mine, d_hidden, up_share, down_share, small,
    ) = results[:12]
    parcels = results[12:]
    (
        pair_buf, score, high, low, q_part, q_land, q_all, k_all, w_all, squares, mixed_all, hidden_two, down, normal_two, rate_two,
        part, landed, back, back_landed, ups_part, ups_sib, ups_go, ups_got, downs_part, downs_sib, downs_go, downs_got,
        pair_sem, kept_send, kept_recv, kz_send, kf_send, ks_send, k_recv, q_send, q_recv, w_send, wx_send, wf_send, w_recv,
        mix_send, mix_recv, part_send, part_recv, back_send, back_recv, sib_send, sib_recv, g_send, g_recv,
    ) = scratch
    zs, feats, rows = mixed_all.shape
    blocks = kept.shape[0]
    chips = blocks // 2
    teams, width = ups_part.shape[0], atoms.shape[1]
    _, group, _, cols = pair_buf.shape
    heads = feats // DH
    groups = heads // group
    piece = rows // zs
    z, blk = lax.axis_index("head"), lax.axis_index("blk")
    core, chip = lax.rem(blk, 2), lax.div(blk, 2)
    dp, dps = lax.axis_index("dp"), lax.axis_size("dp")
    partners = others(dp, dps)
    team = dp * chips + chip
    other_core = 1 - core
    sib_blk = blk + 1 - 2 * core
    sibling = {"blk": sib_blk}
    peers, far_teams = others(z, zs), others(team, teams)
    far = [step * 2 + core for step in others(chip, chips)]
    far_siblings = [step * 2 + other_core for step in others(chip, chips)]
    mine = pl.ds(pl.multiple_of(z * piece, 8), piece)

    def pair_copy(index, slot):
        return pltpu.make_async_copy(
            pair.at[0, pl.ds(index * group, group)], pair_buf.at[slot], pair_sem.at[slot]
        )

    meeting = [{"head": peer} for peer in peers] + [sibling]
    meeting += [team_device(peer, core, chips) for peer in far_teams]
    greet(meeting)
    for n in range(2):
        pair_copy(n, n).start()

    normal, _ = normalize(atoms[...])
    normed = halves(normal * gain_one[...] + bias_one[...])
    meet(meeting)
    copies = []
    fewer = feats // (2 * dps)
    w_mine = w_out.source.at[pl.ds(pl.multiple_of((dp * 2 + core) * fewer, 8), fewer)]
    copies += [
        send(w_mine, w_all.at[z, dp, core], w_send.at[n], w_recv.at[z, dp, core], {"head": peer})
        for n, peer in enumerate(peers)
    ]
    kept[blk, 0:feats, :] = dot_halves(normed, halves(w_key[...])).T
    copies += [
        send(kept.at[blk, 0:feats], k_all.at[blk, z], kz_send.at[n], k_recv.at[blk, z], {"head": peer})
        for n, peer in enumerate(peers)
    ]
    kept[blk, feats : 2 * feats, :] = (dot_halves(normed, halves(w_value[...])) + b_value[...]).T
    id_line = ids[...].astype(F32)
    kept[blk, 2 * feats : 2 * feats + 8, :] = jnp.broadcast_to(id_line, (8, rows))
    copies += [
        send(kept.at[blk], kept.at[blk], kept_send.at[n], kept_recv.at[blk], {"blk": peer})
        for n, peer in enumerate([sib_blk] + far)
    ]
    q_rows = (dot_halves(normed, halves(w_query[...])) + b_query[...]) * (DH ** (-0.5))
    q_part[...] = q_rows.reshape(zs, piece, feats)
    queries[...] = q_rows.T
    queries.flush()
    q_land[z] = q_part[z]
    w_all[z] = w_out[...].reshape(dps, 2, fewer, width)
    id_column[...] = jnp.broadcast_to(id_line, (LANES, rows)).T
    id_column.flush()
    small[...] = jnp.zeros(small.shape, F32)
    for n, peer in enumerate(peers):
        ready = w_all.at[peer, dp, core]
        arrived(ready, w_recv.at[peer, dp, core])
        copies += [
            send(ready, ready, wx_send.at[n, m], w_recv.at[peer, dp, core], {"dp": partner})
            for m, partner in enumerate(partners)
        ]
    for n, source in enumerate(far):
        arrived(kept.at[source], kept_recv.at[source])
        copies.append(
            send(kept.at[source], kept.at[source], kept_send.at[chips + n], kept_recv.at[source], sibling)
        )
    for source in [sib_blk] + far_siblings:
        arrived(kept.at[source], kept_recv.at[source])
    kept.flush()
    one = joined(kept[n, 2 * feats : 2 * feats + 8, :] for n in range(blocks))
    id_row[...] = jnp.concatenate([one, one], axis=0)
    id_row.flush()

    def mix_copies(index):
        some = pl.ds(pl.multiple_of(index * (8 * group), 8 * group), 8 * group)
        return [
            pltpu.make_async_remote_copy(
                src_ref=mixed.at[some],
                dst_ref=mixed_all.at[z, some],
                send_sem=mix_send.at[n, index],
                recv_sem=mix_recv.at[z, index],
                device_id={"head": peer},
                device_id_type=MESH,
            )
            for n, peer in enumerate(peers)
        ]

    def step(index, carry):
        slot = lax.rem(index, 2)
        pair_copy(index, slot).wait()
        low_row = pl.multiple_of(index * (8 * group), 8 * group)
        some = pl.ds(low_row, 8 * group)
        values = pl.ds(pl.multiple_of(feats + low_row, 8), 8 * group)
        mixed[some, :] = attend_group(
            pair_buf.at[slot],
            queries[some, :],
            joined(kept[n, some, :] for n in range(blocks)),
            joined(kept[n, values, :] for n in range(blocks)),
            id_column, id_row, log_sums, index * group, score, high, low,
        )
        for copy in mix_copies(index):
            copy.start()

        @pl.when(index + 2 < groups)
        def _():
            pair_copy(index + 2, slot).start()

        return carry

    lax.fori_loop(0, groups, step, 0)
    mixed.flush()
    log_sums.flush()
    for n, peer in enumerate(peers):
        for kind in range(dps):
            ready = w_all.at[peer, kind, core]

            @pl.when(dp != kind)
            def _(ready=ready, sem=w_recv.at[peer, kind, core]):
                arrived(ready, sem)

            copies.append(send(ready, ready, wf_send.at[n, kind], w_recv.at[peer, kind, core], sibling))
    for n, peer in enumerate(peers):
        ready = k_all.at[blk, peer]
        arrived(ready, k_recv.at[blk, peer])
        copies += [
            send(ready, ready, kf_send.at[n, m], k_recv.at[blk, peer], {"blk": target})
            for m, target in enumerate([sib_blk] + far)
        ]

    small[SMALL_B_DOWN : SMALL_B_DOWN + 1, :] = column_sum(cot[mine, :])
    cots = halves(cot[...])
    downs = halves(w_down[...])
    d_act = dot_halves(cots, downs, NT)
    ups = halves(w_up[...])
    for peer in peers:
        for kind in range(dps):
            arrived(w_all.at[peer, kind, other_core], w_recv.at[peer, kind, other_core])
    outs = halves(w_all[...].reshape(zs * feats, width))
    mixed_all[z] = mixed[...]
    for peer in peers:
        for index in range(groups):
            some = pl.ds(index * (8 * group), 8 * group)
            arrived(mixed_all.at[peer, some], mix_recv.at[peer, index])
    copies += [
        send(q_part.at[peer], q_land.at[z], q_send.at[n], q_recv.at[z], {"head": peer})
        for n, peer in enumerate(peers)
    ]
    mixed_rows = mixed_all[...].reshape(zs * feats, rows).T
    hidden_rows = atoms[...] + dot_halves(halves(mixed_rows), outs) + b_out[...]
    hidden_two[...] = hidden_rows
    normal, rate = normalize(hidden_rows)
    normal_two[...] = normal
    rate_two[...] = jnp.broadcast_to(rate, rate_two.shape)
    normed = normal * gain[...] + bias[...]
    pre = dot_halves(halves(normed), ups) + b_up[...]
    phi = 0.5 * (1.0 + lax.erf(pre * math.sqrt(0.5)))
    act = pre * phi
    d_pre = d_act * (phi + pre * jnp.exp(-0.5 * pre * pre) * (1.0 / math.sqrt(2.0 * math.pi)))
    d_pres = halves(d_pre)
    part[...] = dot_halves(d_pres, ups, NT).reshape(zs, piece, width)
    copies += [
        send(part.at[peer], landed.at[z], part_send.at[n], part_recv.at[z], {"head": peer})
        for n, peer in enumerate(peers)
    ]
    landed[z] = part[z]
    ups_part[...] = dot_halves(halves(normed.T), d_pres).reshape(ups_part.shape)
    copies.append(send(ups_part.at[:, other_core], ups_sib, sib_send.at[0], sib_recv.at[0], sibling))
    downs_part[...] = dot_halves(halves(act.T), cots).reshape(downs_part.shape)
    copies.append(send(downs_part.at[:, other_core], downs_sib, sib_send.at[1], sib_recv.at[1], sibling))
    for n, source in enumerate(far):
        for m, peer in enumerate(peers):
            ready = k_all.at[source, peer]
            arrived(ready, k_recv.at[source, peer])
            copies.append(send(ready, ready, ks_send.at[n, m], k_recv.at[source, peer], sibling))
    down[...] = dot_halves(halves(act), downs)
    out_mine[...] = hidden_two[mine, :] + down[mine, :] + b_down[...]
    out_mine.flush()
    small[SMALL_B_UP : SMALL_B_UP + 1, 0 : d_pre.shape[1]] = column_sum(d_pre)
    for kind, (parts, sib, go, got) in enumerate(
        [(ups_part, ups_sib, ups_go, ups_got), (downs_part, downs_sib, downs_go, downs_got)]
    ):
        arrived(sib, sib_recv.at[kind])
        go[...] = sib[...] + parts[:, core]
        copies += [
            send(
                go.at[peer], got.at[team], g_send.at[kind, n], g_recv.at[kind, team],
                team_device(peer, core, chips),
            )
            for n, peer in enumerate(far_teams)
        ]
        got[team] = go[team]
    for peer in peers:
        arrived(q_land.at[peer], q_recv.at[peer])
    for n in range(zs):
        q_all[n] = q_land[n].T
    for n in range(blocks):
        k_all[n, z] = kept[n, 0:feats, :]
    for source in [sib_blk] + far_siblings:
        for peer in peers:
            arrived(k_all.at[source, peer], k_recv.at[source, peer])
    squares[...] = jnp.zeros(squares.shape, F32)
    at_once = 4
    rounds = heads // at_once

    def square_step(index, carry):
        there = lax.div(index, rounds)
        some = pl.ds(pl.multiple_of(lax.rem(index, rounds) * (8 * at_once), 8 * at_once), 8 * at_once)
        q_some = q_all[there, some, :]
        k_some = joined(k_all[n, there, some, :] for n in range(blocks))
        added = None
        for h in range(at_once):
            head = slice(8 * h, 8 * h + 8)
            q_high, q_low = wide_halves(q_some[head])
            k_high, k_low = wide_halves(k_some[head])
            value = dot(
                stacked([q_high, q_high, q_low, q_low]), stacked([k_high, k_low, k_high, k_low]), TN
            )
            added = value * value if added is None else added + value * value
        squares[...] += added
        return carry

    lax.fori_loop(0, zs * rounds, square_step, 0)
    same = id_column[mine, 0:1] == id_row[0:1, :]
    norms = jnp.sqrt(squares[...] + 1.0)
    terms = jnp.where(same, jnp.log1p(jnp.exp(norms - math.sqrt(zs * heads))), 0.0)
    number = jnp.where(same, 1.0, 0.0)

    def total(value):
        return jnp.sum(jnp.sum(value, axis=1, keepdims=True), axis=0, keepdims=True)

    lane = lax.broadcasted_iota(jnp.int32, (1, width), 1)
    small[SMALL_PENALTY : SMALL_PENALTY + 1, :] = jnp.where(
        lane == 0, total(terms), jnp.where(lane == 1, total(number), 0.0)
    )
    for peer in peers:
        arrived(landed.at[peer], part_recv.at[peer])
    d_normed = functools.reduce(jnp.add, [landed[n] for n in range(zs)])
    normal = normal_two[mine, :]
    d_rows = cot[mine, :] + normalize_back(d_normed, gain[...], normal, rate_two[mine, 0:1])
    d_halves = halves(d_rows)
    for n in range(zs):
        some = slice(n * feats, (n + 1) * feats)
        back[n] = dot_halves(d_halves, (outs[0][some], outs[1][some]), NT)
    copies += [
        send(back.at[peer], back_landed.at[z], back_send.at[n], back_recv.at[z], {"head": peer})
        for n, peer in enumerate(peers)
    ]
    back_landed[z] = back[z]
    d_hidden[...] = d_rows
    d_hidden.flush()
    for peer, parcel in zip(peers, parcels, strict=True):
        parcel[0:piece, :] = down[pl.ds(pl.multiple_of(peer * piece, 8), piece), :]
        parcel[piece : 2 * piece, :] = d_rows
        parcel.flush()
    small[SMALL_LN2_GAIN : SMALL_LN2_GAIN + 1, :] = column_sum(d_normed * normal)
    small[SMALL_LN2_BIAS : SMALL_LN2_BIAS + 1, :] = column_sum(d_normed)
    small[SMALL_B_OUT : SMALL_B_OUT + 1, :] = column_sum(d_rows)
    small.flush()
    for peer in peers:
        arrived(back_landed.at[peer], back_recv.at[peer])
    d_mixed[...] = back_landed[...].reshape(rows, feats).T
    d_mixed.flush()
    for kind, (got, result) in enumerate([(ups_got, up_share), (downs_got, down_share)]):
        for peer in far_teams:
            arrived(got.at[peer], g_recv.at[kind, peer])
        result[...] = functools.reduce(jnp.add, [got[n] for n in range(teams)])
        result.flush()
    for copy in copies:
        copy.wait_send()

    def drain(index, carry):
        for copy in mix_copies(index):
            copy.wait_send()
        return carry

    lax.fori_loop(0, groups, drain, 0)


def front(zs, dps, teams, pair, *operands):
    _, heads, rows, cols = pair.shape
    feats, blocks = heads * DH, cols // rows
    width, units = operands[0].shape[1], operands[12].shape[1]
    piece, group = rows // zs, GROUP
    up_rows, down_rows = width // (2 * teams), units // (2 * teams)
    groups = heads // group
    slab = pltpu.VMEM((zs, piece, width), F32)
    narrow = pltpu.VMEM((zs, piece, feats), F32)
    one_up, one_down = pltpu.VMEM((teams, up_rows, units), F32), pltpu.VMEM((teams, down_rows, width), F32)
    dma = pltpu.SemaphoreType.DMA
    return staged_call(
        front_kernel,
        "front",
        operands,
        [
            (feats, rows), (blocks, 2 * feats + 8, rows), (rows, LANES), (heads, rows, LANES), (feats, rows),
            (STRIP, cols), (feats, rows), (piece, width), (piece, width),
            (up_rows, units), (down_rows, width), (SMALL_ROWS, width),
        ]
        + [(2 * piece, width)] * (zs - 1),
        [
            pltpu.VMEM((2, group, rows, cols), F32),
            pltpu.VMEM((group, rows, cols), F32),
            pltpu.VMEM((group, rows, cols), BF16),
            pltpu.VMEM((group, rows, cols), BF16),
            narrow, narrow,
            pltpu.VMEM((zs, feats, piece), F32),
            pltpu.VMEM((blocks, zs, feats, rows), F32),
            pltpu.VMEM((zs, dps, 2, feats // (2 * dps), width), F32),
            pltpu.VMEM((piece, cols), F32),
            pltpu.VMEM((zs, feats, rows), F32),
            pltpu.VMEM((rows, width), F32),
            pltpu.VMEM((rows, width), F32),
            pltpu.VMEM((rows, width), F32),
            pltpu.VMEM((rows, LANES), F32),
            slab, slab, narrow, narrow,
            pltpu.VMEM((teams, 2, up_rows, units), F32),
            one_up, one_up, one_up,
            pltpu.VMEM((teams, 2, down_rows, width), F32),
            one_down, one_down, one_down,
            dma((2,)),
            dma((blocks,)), dma((blocks,)),
            dma((zs,)), dma((zs, blocks // 2)), dma((blocks // 2, zs)), dma((blocks, zs)),
            dma((zs,)), dma((zs,)),
            dma((zs,)), dma((zs, dps)), dma((zs, dps)), dma((zs, dps, 2)),
            dma((zs, groups)), dma((zs, groups)),
            dma((zs,)), dma((zs,)),
            dma((zs,)), dma((zs,)),
            dma((2,)), dma((2,)),
            dma((2, teams)), dma((2, teams)),
        ],
        58,
        remote=0,
        raw=(pair,),
    )


def finish_kernel(operands, results, scratch, raw):
    (
        d_keys, d_values, out_mine, d_hidden, d_queries, atoms, gain, bias, w_query, mixed, small_in, w_key, w_value,
        up_share, down_share,
    ) = operands[:15]
    parcels = operands[15:]
    grad_atoms, out_atoms, total_grads, grad_up, grad_down, small, penalty = results
    (
        sib_keys, sib_values, go_keys, go_values, got_keys, got_values,
        part, landed, grads, sib_grads, go_grads, got_grads, hidden_all, small_z, small_all,
        sib_send, sib_recv, kv_send, kv_recv, part_send, part_recv, back_send, back_recv,
        g_send, g_recv, t_send, t_recv, f_send, b_send, b_recv, bf_send, out_send, out_recv,
        small_z_send, small_z_recv, small_send, small_recv,
    ) = scratch
    chips, _, feats, rows = d_keys.shape
    zs, piece, width = part.shape
    teams, _, share, _ = grads.shape
    blk, z, dp = lax.axis_index("blk"), lax.axis_index("head"), lax.axis_index("dp")
    core, chip = lax.rem(blk, 2), lax.div(blk, 2)
    other_core = 1 - core
    sibling = {"blk": blk + 1 - 2 * core}
    peers = others(z, zs)
    team = dp * chips + chip
    far_teams = others(team, teams)
    far_chips = others(chip, chips)
    place = team * 2 + core
    far_places = others(place, teams * 2)
    plane = [team_device(lax.div(value, 2), lax.rem(value, 2), chips) for value in far_places]
    meeting = [{"head": peer} for peer in peers] + plane
    greet(meeting)
    meet(meeting)
    copies = [
        send(d_keys.source.at[:, other_core], sib_keys, sib_send.at[0], sib_recv.at[0], sibling),
        send(d_values.source.at[:, other_core], sib_values, sib_send.at[1], sib_recv.at[1], sibling),
    ]
    mine = pl.ds(pl.multiple_of(z * piece, 8), piece)
    out_atoms[mine, :] = functools.reduce(jnp.add, [parcel[0:piece, :] for parcel in parcels], out_mine[...])
    copies += [
        send(out_atoms.at[mine], out_atoms.at[mine], out_send.at[n], out_recv.at[z], {"head": peer})
        for n, peer in enumerate(peers)
    ]
    own_keys, own_values = d_keys.ref, d_values.ref
    for kind, (sib, mine_too, go, got) in enumerate(
        [(sib_keys, own_keys, go_keys, got_keys), (sib_values, own_values, go_values, got_values)]
    ):
        arrived(sib, sib_recv.at[kind])
        go[...] = sib[...] + mine_too[:, core]
        copies += [
            send(
                go.at[peer], got.at[chip], kv_send.at[kind, n], kv_recv.at[kind, chip],
                {"blk": peer * 2 + core},
            )
            for n, peer in enumerate(far_chips)
        ]
    got_keys[chip] = go_keys[chip]
    got_values[chip] = go_values[chip]
    normal, rate = normalize(atoms[...])
    normed = halves(normal * gain[...] + bias[...])
    dq_rows = d_queries[...].T
    d_normed = dot_full(dq_rows, w_query[...], NT)
    grad_q = dot_halves(halves(d_queries[...]), normed)
    small_z[z] = small_in[0:8, :]
    hidden_all[z] = d_hidden[...]
    for n, parcel in enumerate(parcels):
        hidden_all[lax.rem(z + zs - 1 - n, zs)] = parcel[piece : 2 * piece, :]
    grad_o = dot_full(mixed[...], hidden_all[...].reshape(rows, width))
    for peer in far_chips:
        arrived(got_keys.at[peer], kv_recv.at[0, peer])
        arrived(got_values.at[peer], kv_recv.at[1, peer])
    dk = functools.reduce(jnp.add, [got_keys[n] for n in range(chips)])
    dv = functools.reduce(jnp.add, [got_values[n] for n in range(chips)])
    dv_rows = dv.T
    d_normed = (
        d_normed + dot_full(dk.T, w_key[...], NT) + dot_full(dv_rows, w_value[...], NT)
    )
    part[...] = d_normed.reshape(zs, piece, width)
    copies += [
        send(part.at[peer], landed.at[z], part_send.at[n], part_recv.at[z], {"head": peer})
        for n, peer in enumerate(peers)
    ]
    landed[z] = part[z]
    grad_k = dot_halves(halves(dk), normed)
    grad_v = dot_halves(halves(dv), normed)
    grads[...] = jnp.concatenate([grad_q, grad_k, grad_v, grad_o], axis=0).reshape(grads.shape)
    copies.append(send(grads.at[:, other_core], sib_grads, sib_send.at[2], sib_recv.at[2], sibling))
    arrived(sib_grads, sib_recv.at[2])
    go_grads[...] = sib_grads[...] + grads[:, core]
    copies += [
        send(
            go_grads.at[peer], got_grads.at[team], g_send.at[n], g_recv.at[team], team_device(peer, core, chips)
        )
        for n, peer in enumerate(far_teams)
    ]
    got_grads[team] = go_grads[team]
    bigs = [(up_share, grad_up), (down_share, grad_down)]

    def big_rows(result, source, kind):
        count = result.shape[0] // (2 * teams)
        return result.at[pl.ds(pl.multiple_of((source * 2 + kind) * count, 8), count)]

    for kind, (share_in, result) in enumerate(bigs):
        ready = big_rows(result, team, core)
        ready[...] = share_in[...]
        copies.append(send(ready, ready, b_send.at[kind, 0], b_recv.at[kind, team, core], sibling))
        copies += [
            send(
                ready, ready, b_send.at[kind, n + 1], b_recv.at[kind, team, core],
                team_device(peer, core, chips),
            )
            for n, peer in enumerate(far_teams)
        ]
    for peer in peers:
        arrived(landed.at[peer], part_recv.at[peer])
    d_normed = functools.reduce(jnp.add, [landed[n] for n in range(zs)])
    normal, rate = normalize(atoms[mine, :])
    grad_atoms[mine, :] = d_hidden[...] + normalize_back(d_normed, gain[...], normal, rate)
    small_z[z, SMALL_LN1_GAIN : SMALL_LN1_GAIN + 1, :] = column_sum(d_normed * normal)
    small_z[z, SMALL_LN1_BIAS : SMALL_LN1_BIAS + 1, :] = column_sum(d_normed)
    copies += [
        send(small_z.at[z], small_z.at[z], small_z_send.at[n], small_z_recv.at[z], {"head": peer})
        for n, peer in enumerate(peers)
    ]
    copies += [
        send(grad_atoms.at[mine], grad_atoms.at[mine], back_send.at[n], back_recv.at[z], {"head": peer})
        for n, peer in enumerate(peers)
    ]
    for peer in far_teams:
        arrived(got_grads.at[peer], g_recv.at[peer])
    total_grads[team, core] = functools.reduce(jnp.add, [got_grads[n] for n in range(teams)])
    ready = total_grads.at[team, core]
    copies.append(send(ready, ready, t_send.at[0], t_recv.at[team, core], sibling))
    copies += [
        send(ready, ready, t_send.at[n + 1], t_recv.at[team, core], team_device(peer, core, chips))
        for n, peer in enumerate(far_teams)
    ]
    for peer in peers:
        arrived(small_z.at[peer], small_z_recv.at[peer])
    small_all[place, 0:8, :] = functools.reduce(jnp.add, [small_z[n] for n in range(zs)])
    small_all[place, 8:16, :] = small_in[8:16, :]
    small_all[place, SMALL_B_QUERY : SMALL_B_QUERY + 1, 0:feats] = column_sum(dq_rows)
    small_all[place, SMALL_B_VALUE : SMALL_B_VALUE + 1, 0:feats] = column_sum(dv_rows)
    copies += [
        send(small_all.at[place], small_all.at[place], small_send.at[n], small_recv.at[place], target)
        for n, target in enumerate(plane)
    ]
    for n, peer in enumerate(far_teams):
        ready = total_grads.at[peer, core]
        arrived(ready, t_recv.at[peer, core])
        copies.append(send(ready, ready, f_send.at[n], t_recv.at[peer, core], sibling))
    for kind, (_, result) in enumerate(bigs):
        for n, peer in enumerate(far_teams):
            ready = big_rows(result, peer, core)
            arrived(ready, b_recv.at[kind, peer, core])
            copies.append(send(ready, ready, bf_send.at[kind, n], b_recv.at[kind, peer, core], sibling))
    for source in far_places:
        arrived(small_all.at[source], small_recv.at[source])
    summed = functools.reduce(jnp.add, [small_all[n] for n in range(2 * teams)])
    small[...] = summed
    ends = summed[SMALL_PENALTY : SMALL_PENALTY + 1, :]
    penalty[...] = ends[:, 0:1] / ends[:, 1:2]
    for peer in [team] + far_teams:
        arrived(total_grads.at[peer, other_core], t_recv.at[peer, other_core])
    total_grads.flush()
    for kind, (_, result) in enumerate(bigs):
        for peer in [team] + far_teams:
            arrived(big_rows(result, peer, other_core), b_recv.at[kind, peer, other_core])
        result.flush()
    for peer in peers:
        there = pl.ds(pl.multiple_of(peer * piece, 8), piece)
        arrived(out_atoms.at[there], out_recv.at[peer])
    out_atoms.flush()
    for peer in peers:
        there = pl.ds(pl.multiple_of(peer * piece, 8), piece)
        arrived(grad_atoms.at[there], back_recv.at[peer])
    for copy in copies:
        copy.wait_send()


def finish(zs, dps, *operands):
    d_keys, atoms = operands[0], operands[5]
    units = operands[14].shape[0] * 2 * dps * d_keys.shape[0]
    chips, _, feats, rows = d_keys.shape
    width = atoms.shape[1]
    piece = rows // zs
    teams = dps * chips
    share = 4 * feats // (2 * teams)
    some = pltpu.VMEM((chips, feats, rows), F32)
    slab = pltpu.VMEM((zs, piece, width), F32)
    one = pltpu.VMEM((teams, share, width), F32)
    dma = pltpu.SemaphoreType.DMA
    return staged_call(
        finish_kernel,
        "finish",
        operands,
        [
            (rows, width),
            (rows, width),
            (teams, 2, share, width),
            (width, units),
            (units, width),
            (SMALL_ROWS, width),
            (1, 1),
        ],
        [some] * 6
        + [slab, slab, pltpu.VMEM((teams, 2, share, width), F32), one, one, one, slab]
        + [
            pltpu.VMEM((zs, 8, width), F32),
            pltpu.VMEM((2 * teams, SMALL_ROWS, width), F32),
            dma((3,)), dma((3,)),
            dma((2, chips)), dma((2, chips)),
            dma((zs,)), dma((zs,)),
            dma((zs,)), dma((zs,)),
            dma((teams,)), dma((teams,)),
            dma((teams,)), dma((teams, 2)), dma((teams,)),
            dma((2, teams)), dma((2, teams, 2)), dma((2, teams)),
            dma((zs,)), dma((zs,)),
            dma((zs,)), dma((zs,)),
            dma((2 * teams,)), dma((2 * teams,)),
        ],
        58,
        remote=2,
    )


def place_kernel(operands, results, scratch, raw):
    total_grads, small = operands
    grad_query, grad_key, grad_value, grad_out = results[:4]
    feats, width = grad_out.shape
    done = total_grads[...].reshape(4 * feats, width)
    grad_query[...] = done[0:feats].T
    grad_query.flush()
    grad_key[...] = done[feats : 2 * feats].T
    grad_key.flush()
    grad_value[...] = done[2 * feats : 3 * feats].T
    grad_value.flush()
    grad_out[...] = done[3 * feats :]
    grad_out.flush()
    for result, row in zip(results[4:], SMALL_OUTPUTS, strict=True):
        result[...] = small[row : row + 1, 0 : result.shape[1]]


SMALL_OUTPUTS = (
    SMALL_LN1_GAIN, SMALL_LN1_BIAS, SMALL_B_QUERY, SMALL_B_VALUE, SMALL_B_OUT, SMALL_LN2_GAIN, SMALL_LN2_BIAS,
    SMALL_B_UP, SMALL_B_DOWN,
)


def place(feats, units, straight, *operands):
    width = operands[1].shape[1]
    lengths = {SMALL_B_QUERY: feats, SMALL_B_VALUE: feats, SMALL_B_UP: units}
    return staged_call(
        place_kernel,
        "place",
        operands,
        [(width, feats)] * 3
        + [(feats, width)]
        + [(1, lengths.get(row, width)) for row in SMALL_OUTPUTS],
        [],
        58,
        straight=straight,
    )


def local(
    zs, dps,
    atoms, pair, mol_ids, ln1_gain, ln1_bias, w_query, b_query, w_key, w_value, b_value, w_out, b_out,
    ln2_gain, ln2_bias, w_up, b_up, w_down, b_down, cot_atoms, cot_pair,
):
    blocks = pair.shape[3] // pair.shape[2]
    inputs, cot = atoms[0], cot_atoms[0]

    def line(value):
        return value.reshape(1, -1)

    (
        queries, kept, id_column, log_sums, mixed, id_row, d_mixed, out_mine, d_hidden, up_share, down_share, small,
        *parcels,
    ) = front(
        zs, dps, dps * blocks // 2, pair,
        inputs, mol_ids, line(ln1_gain), line(ln1_bias), w_key, w_value, line(b_value), w_query, line(b_query),
        w_out, cot, w_down, w_up, line(b_out), line(ln2_gain), line(ln2_bias), line(b_up),
        line(b_down),
    )
    parcels = [
        lax.ppermute(parcel, "head", [(source, (source + n + 1) % zs) for source in range(zs)])
        for n, parcel in enumerate(parcels)
    ]
    out_pair, grad_pair, d_queries, d_keys, d_values = attend_back(
        pair, cot_pair, queries, kept, mixed, d_mixed, log_sums, id_column, id_row
    )
    grad_atoms, out_atoms, total_grads, grad_up, grad_down, small, penalty = finish(
        zs, dps,
        d_keys, d_values, out_mine, d_hidden, d_queries, inputs, line(ln1_gain), line(ln1_bias), w_query, mixed,
        small, w_key, w_value, up_share, down_share, *parcels,
    )
    placed = place(
        w_query.shape[1], w_up.shape[1],
        [grad_atoms, out_atoms, grad_up, grad_down],
        total_grads, small,
    )
    grad_atoms, out_atoms, grad_up, grad_down, grad_query, grad_key, grad_value, grad_out = placed[:8]
    (
        grad_ln1_gain, grad_ln1_bias, grad_b_query, grad_b_value, grad_b_out, grad_ln2_gain, grad_ln2_bias,
        grad_b_up, grad_b_down,
    ) = [value.reshape(-1) for value in placed[8:]]
    return (
        out_atoms[None],
        out_pair,
        penalty[0, 0],
        grad_atoms[None],
        grad_pair,
        grad_ln1_gain,
        grad_ln1_bias,
        grad_query,
        grad_b_query,
        grad_key,
        grad_value,
        grad_b_value,
        grad_out,
        grad_b_out,
        grad_ln2_gain,
        grad_ln2_bias,
        grad_up,
        grad_b_up,
        grad_down,
        grad_b_down,
    )


def solution(mesh):
    rows, pairs = P("dp", "blk", None), P("dp", "head", "blk", None)
    columns = P(None, "head")
    return jax.shard_map(
        functools.partial(local, mesh.shape["head"], mesh.shape["dp"]),
        mesh=mesh,
        in_specs=(
            rows, pairs, P("dp", "blk"), P(), P(), columns, P("head"), columns, columns, P("head"),
            P("head", None), P(), P(), P(), columns, P("head"), P("head", None), P(), rows, pairs,
        ),
        out_specs=(
            rows, pairs, P(), rows, pairs, P(), P(), columns, P("head"), columns, columns, P("head"),
            P("head", None), P(), P(), P(), columns, P("head"), P("head", None), P(),
        ),
        check_vma=False,
    )
```

```python
import functools
import math

import jax
import jax.numpy as jnp
from jax import lax
from jax.experimental import pallas as pl
from jax.experimental.pallas import tpu as pltpu
from jax.sharding import PartitionSpec as P

DH = 8
LANES = 128
STRIP = 16
CHUNK = 256
GROUP = 2
NORM_EPS = 1e-05
MASK_FILL = -1e30
F32 = jnp.float32
BF16 = jnp.bfloat16
MESH = pl.DeviceIdType.MESH
NN = (((1,), (0,)), ((), ()))
NT = (((1,), (1,)), ((), ()))
TN = (((0,), (0,)), ((), ()))
VMEM = pl.BlockSpec(memory_space=pltpu.VMEM)


def dot(left, right, dims=NN):
    return lax.dot_general(left, right, dims, preferred_element_type=F32)


def halves(value):
    high = value.astype(BF16)
    return high, (value - high.astype(F32)).astype(BF16)


def dot_halves(left, right, dims=NN):
    return dot(left[0], right[0], dims) + (
        dot(left[0], right[1], dims) + dot(left[1], right[0], dims)
    )


def dot_full(left, right, dims=NN):
    return dot_halves(halves(left), halves(right), dims)


def normalize(inputs):
    centred = inputs - jnp.mean(inputs, -1, keepdims=True)
    rate = lax.rsqrt(jnp.mean(centred * centred, -1, keepdims=True) + NORM_EPS)
    return centred * rate, rate


def normalize_back(grad, gain, normal, rate):
    scaled = grad * gain
    return rate * (
        scaled
        - jnp.mean(scaled, -1, keepdims=True)
        - normal * jnp.mean(scaled * normal, -1, keepdims=True)
    )


def column_sum(value):
    return jnp.sum(value, 0, keepdims=True)


def send(src, dst, send_sem, recv_sem, target):
    copy = pltpu.make_async_remote_copy(
        src_ref=src,
        dst_ref=dst,
        send_sem=send_sem,
        recv_sem=recv_sem,
        device_id=target,
        device_id_type=MESH,
    )
    copy.start()
    return copy


def arrived(ref, sem):
    pltpu.make_async_remote_copy(
        src_ref=ref, dst_ref=ref, send_sem=sem, recv_sem=sem, device_id={}, device_id_type=MESH
    ).wait_recv()


def greet(targets):
    for target in targets:
        pl.semaphore_signal(pltpu.get_barrier_semaphore(), inc=1, device_id=target, device_id_type=MESH)


def meet(targets):
    pl.semaphore_wait(pltpu.get_barrier_semaphore(), len(targets))


def others(index, count):
    return [lax.rem(index + step, count) for step in range(1, count)]


class Operand:
    def __init__(self, source, slot, sem):
        self.source, self.slot, self.shape = source, slot, slot.shape
        self.copy = pltpu.make_async_copy(source, slot, sem)
        self.copy.start()

    @property
    def ref(self):
        if self.copy is not None:
            self.copy.wait()
            self.copy = None
        return self.slot

    def __getitem__(self, index):
        return self.ref[index]


class Result:
    def __init__(self, target, slot, sem):
        self.slot, self.shape, self.at = slot, slot.shape, slot.at
        self.copy = pltpu.make_async_copy(slot, target, sem)
        self.begun = False

    def __setitem__(self, index, value):
        self.slot[index] = value

    def __getitem__(self, index):
        return self.slot[index]

    def flush(self):
        if not self.begun:
            self.copy.start()
            self.begun = True


def staged_call(kernel, name, operands, results, scratch, megabytes, remote=None, raw=(), straight=(), raw_results=(), cost=None):
    n_in, n_out, n_raw, n_straight = len(operands), len(results), len(raw), len(straight)
    n_left = len(raw_results)

    def body(*refs):
        sources, left, refs = refs[:n_in], refs[n_in : n_in + n_raw], refs[n_in + n_raw :]
        moved, refs = refs[:n_straight], refs[n_straight:]
        arrays, refs = refs[:n_straight], refs[n_straight:]
        left, refs = left + refs[:n_left], refs[n_left:]
        targets, refs = refs[:n_out], refs[n_out:]
        slots, made, refs = refs[:n_in], refs[n_in : n_in + n_out], refs[n_in + n_out :]
        in_sem, out_sem, move_sem, refs = refs[0], refs[1], refs[2], refs[3:]
        through, refs = refs[:n_straight], refs[n_straight:]
        loads = [pltpu.make_async_copy(moved[n], through[n], move_sem.at[n]) for n in range(n_straight)]
        moves = [pltpu.make_async_copy(through[n], arrays[n], move_sem.at[n]) for n in range(n_straight)]
        for load in loads:
            load.start()
        ins = [Operand(sources[n], slots[n], in_sem.at[n]) for n in range(n_in)]
        outs = [Result(targets[n], made[n], out_sem.at[n]) for n in range(n_out)]
        for load, move in zip(loads, moves, strict=True):
            load.wait()
            move.start()
        kernel(ins, outs, refs, left)
        for operand in ins:
            operand.ref
        for result in outs:
            result.flush()
        for copy in moves + [result.copy for result in outs]:
            copy.wait()

    anywhere = pl.BlockSpec(memory_space=pltpu.HBM)
    extra = {} if remote is None else {"collective_id": remote, "has_side_effects": True}
    return pl.pallas_call(
        body,
        out_shape=[jax.ShapeDtypeStruct(value.shape, value.dtype) for value in straight]
        + [jax.ShapeDtypeStruct(shape, F32) for shape in raw_results]
        + [jax.ShapeDtypeStruct(shape, F32) for shape in results],
        in_specs=[anywhere] * (n_in + n_raw + n_straight),
        out_specs=[anywhere] * (n_straight + n_left + n_out),
        scratch_shapes=[pltpu.VMEM(value.shape, value.dtype) for value in operands]
        + [pltpu.VMEM(shape, F32) for shape in results]
        + [pltpu.SemaphoreType.DMA((n,)) for n in (n_in, n_out, max(1, n_straight))]
        + [pltpu.VMEM(value.shape, value.dtype) for value in straight]
        + list(scratch),
        compiler_params=pltpu.CompilerParams(vmem_limit_bytes=megabytes << 20, **extra),
        cost_estimate=cost,
        name=name,
    )(*operands, *raw, *straight)


def joined(pieces):
    return jnp.concatenate(list(pieces), axis=1)


def stacked(parts):
    return jnp.concatenate(parts, axis=0).astype(BF16)


def wide_halves(value):
    high = value.astype(BF16).astype(F32)
    return high, value - high


def attend_group(pair, queries, keys, values, id_column, id_row, log_sums, first, score, high, low):
    group, rows, cols = score.shape
    strips = rows // STRIP
    chunk = min(CHUNK, cols)
    mixed = []
    for g in range(group):
        head = slice(8 * g, 8 * g + 8)
        q_high, q_low = wide_halves(queries[head, :])
        k_high, k_low = wide_halves(keys[head, :])
        v_high, v_low = wide_halves(values[head, :])
        ones = jnp.ones_like(v_high)
        q_pack = stacked([q_high, q_high, q_low, q_low])
        k_pack = stacked([k_high, k_low, k_high, k_low])
        v_pack = stacked([v_high, v_low, ones, jnp.zeros_like(ones)])
        tops = [None] * strips
        for start in range(0, cols, chunk):
            part = slice(start, start + chunk)
            score[g, :, part] = dot(q_pack, k_pack[:, part], TN)
            for s in range(strips):
                line = pl.ds(s * STRIP, STRIP)
                own = id_column[line, :]
                for j in range(start, start + chunk, LANES):
                    tile = pl.ds(j, LANES)
                    value = pair[g, line, tile] + score[g, line, tile]
                    value = jnp.where(own == id_row[:, tile], value, MASK_FILL)
                    score[g, line, tile] = value
                    tops[s] = value if tops[s] is None else jnp.maximum(tops[s], value)
        tops = [
            jnp.broadcast_to(jnp.max(top, axis=1, keepdims=True), (STRIP, LANES)) for top in tops
        ]
        totals = [None] * strips
        gathered = None
        for start in range(0, cols, chunk):
            part = slice(start, start + chunk)
            for s in range(strips):
                line = pl.ds(s * STRIP, STRIP)
                for j in range(start, start + chunk, LANES):
                    tile = pl.ds(j, LANES)
                    weight = jnp.exp(score[g, line, tile] - tops[s])
                    high[g, line, tile], low[g, line, tile] = halves(weight)
                    totals[s] = weight if totals[s] is None else totals[s] + weight
            term = dot(v_pack[:, part], high[g, :, part], NT) + dot(
                v_pack[:, part], low[g, :, part], NT
            )
            gathered = term if gathered is None else gathered + term
        for s in range(strips):
            total = jnp.sum(totals[s], axis=1, keepdims=True)
            log_sums[first + g, pl.ds(s * STRIP, STRIP), :] = tops[s] + jnp.log(total)
        mixed.append((gathered[0:8] + gathered[8:16]) / gathered[16:17])
    return jnp.concatenate(mixed, axis=0)


def chunks_of(cols):
    chunk = min(CHUNK, cols)
    return [slice(start, start + chunk) for start in range(0, cols, chunk)]


def score_packs(queries, keys):
    q_high, q_low = wide_halves(queries)
    k_high, k_low = wide_halves(keys)
    return stacked([q_high, q_high, q_low, q_low]), stacked([k_high, k_low, k_high, k_low])


def attend_back_kernel(operands, results, scratch, raw):
    queries, kept, d_mixed, mixed, id_column, id_row = operands
    d_queries, d_keys, d_values = results
    pair, cot, log_sums, out_pair, grad_pair = raw
    pair_buf, cot_buf, log_buf, out_buf, grad_buf = scratch[:5]
    here = scratch[5:11]
    in_sem, out_sem = scratch[11:]
    heads = pair.shape[1]
    feats = heads * DH
    depth, rows, cols = pair_buf.shape
    blocks = kept.shape[0]
    parts = chunks_of(cols)
    place = lax.broadcasted_iota(jnp.int32, (8, rows), 0)

    def inward(index):
        slot = lax.rem(index, depth)
        sources = (pair.at[0, index], cot.at[0, index], log_sums.at[index])
        return [
            pltpu.make_async_copy(source, buf.at[slot], in_sem.at[n, slot])
            for n, (source, buf) in enumerate(zip(sources, (pair_buf, cot_buf, log_buf), strict=True))
        ]

    def outward(index):
        slot = lax.rem(index, depth)
        return [
            pltpu.make_async_copy(buf.at[slot], array.at[0, index], out_sem.at[n, slot])
            for n, (array, buf) in enumerate([(out_pair, out_buf), (grad_pair, grad_buf)])
        ]

    for n in range(2):
        for copy in inward(n):
            copy.start()
    for operand in operands:
        operand.ref

    def rows_of(index):
        return pl.ds(pl.multiple_of(index * 8, 8), 8)

    def key_rows(index):
        return joined(kept[n, rows_of(index), :] for n in range(blocks))

    def value_rows(index):
        some = pl.ds(pl.multiple_of(feats + index * 8, 8), 8)
        return joined(kept[n, some, :] for n in range(blocks))

    def packs(index):
        head = rows_of(index)
        q_pack, k_pack = score_packs(queries[head, :], key_rows(index))
        v_high, v_low = wide_halves(value_rows(index))
        m_high, m_low = wide_halves(d_mixed[head, :])
        delta_high, rest = wide_halves(-column_sum(mixed[head, :] * d_mixed[head, :]))
        delta_mid, delta_low = wide_halves(rest)
        deltas = jnp.where(
            place == 0, delta_high, jnp.where(place == 1, delta_mid, jnp.where(place == 2, delta_low, 0.0))
        )
        m_pack = stacked([m_high, m_high, m_low, deltas])
        v_pack = stacked([v_high, v_low, v_high, jnp.ones_like(v_high)])
        return q_pack, k_pack, m_pack, v_pack

    def pairs(index):
        head = rows_of(index)
        return [stacked(wide_halves(value)) for value in (queries[head, :], key_rows(index), d_mixed[head, :])]

    def before(pack, part, there):
        q_pack, k_pack, m_pack, v_pack = pack
        there[0][:, part] = dot(q_pack, k_pack[:, part], TN)
        there[1][:, part] = dot(m_pack, v_pack[:, part], TN)

    def middle(index, slot, part, here):
        score, d_prob, p_high, p_low, g_high, g_low = here
        for s in range(rows // STRIP):
            line = pl.ds(s * STRIP, STRIP)
            own = id_column[line, :]
            log_sum = log_buf[slot, line, :]
            for j in range(part.start, part.stop, LANES):
                tile = pl.ds(j, LANES)
                value = pair_buf[slot, line, tile] + score[line, tile]
                out_buf[slot, line, tile] = value
                prob = jnp.exp(jnp.where(own == id_row[:, tile], value - log_sum, MASK_FILL))
                p_high[line, tile], p_low[line, tile] = halves(prob)
                grad = prob * d_prob[line, tile] + cot_buf[slot, line, tile]
                grad_buf[slot, line, tile] = grad
                g_high[line, tile], g_low[line, tile] = halves(grad)

    def both(left, high, low, dims):
        value = dot(left, high, dims) + dot(left, low, dims)
        return value[0:8] + value[8:16]

    def after(index, pair_of, part, there):
        q_pair, k_pair, m_pair = pair_of
        _, _, p_high, p_low, g_high, g_low = there
        head = rows_of(index)
        d_value = both(m_pair, p_high[:, part], p_low[:, part], NN)
        d_key = both(q_pair, g_high[:, part], g_low[:, part], NN)
        for n in range(part.start // rows, part.stop // rows):
            span = slice(n * rows - part.start, (n + 1) * rows - part.start)
            d_keys[n // 2, n % 2, head, :] = d_key[:, span]
            d_values[n // 2, n % 2, head, :] = d_value[:, span]
        return both(k_pair[:, part], g_high[:, part], g_low[:, part], NT)

    def stage(index, carry):
        slot = lax.rem(index, depth)
        for copy in inward(index):
            copy.wait()

        @pl.when(index >= depth)
        def _():
            for copy in outward(index - depth):
                copy.wait()

        @pl.when(index == 0)
        def _():
            for n in range(2, depth - 1):
                for copy in inward(n):
                    copy.start()

        @pl.when(index + depth - 1 < heads)
        def _():
            for copy in inward(index + depth - 1):
                copy.start()

        next_packs, own_pairs = packs(index), pairs(index)
        d_query = None
        before(next_packs, parts[0], here)
        for n, part in enumerate(parts):
            if n + 1 < len(parts):
                before(next_packs, parts[n + 1], here)
            middle(index, slot, part, here)
            if n >= 1:
                term = after(index, own_pairs, parts[n - 1], here)
                d_query = term if d_query is None else d_query + term
        term = after(index, own_pairs, parts[-1], here)
        d_query = term if d_query is None else d_query + term
        d_queries[rows_of(index), :] = d_query * (DH ** (-0.5))
        for copy in outward(index):
            copy.start()
        return carry

    lax.fori_loop(0, heads, stage, 0)
    for result in results:
        result.flush()
    for n in range(max(0, heads - depth), heads):
        for copy in outward(n):
            copy.wait()


def attend_back(pair, cot, queries, kept, mixed, d_mixed, log_sums, id_column, id_row):
    _, heads, rows, cols = pair.shape
    feats = heads * DH
    blocks = kept.shape[0]
    depth = 4
    split = (blocks // 2, 2, feats, rows)
    wide, thin = pltpu.VMEM((rows, cols), F32), pltpu.VMEM((rows, cols), BF16)
    return staged_call(
        attend_back_kernel,
        "attend_back",
        [queries, kept, d_mixed, mixed, id_column, id_row],
        [(feats, rows), split, split],
        [pltpu.VMEM((depth, rows, cols), F32)] * 2
        + [pltpu.VMEM((depth, rows, LANES), F32)]
        + [pltpu.VMEM((depth, rows, cols), F32)] * 2
        + [wide] * 2
        + [thin] * 4
        + [pltpu.SemaphoreType.DMA((3, depth)), pltpu.SemaphoreType.DMA((2, depth))],
        60,
        raw=(pair, cot, log_sums),
        raw_results=(pair.shape, pair.shape),
        cost=pl.CostEstimate(
            flops=2 * 400 * heads * rows * cols,
            bytes_accessed=16 * heads * rows * cols,
            transcendentals=heads * rows * cols,
        ),
    )


SMALL_LN1_GAIN, SMALL_LN1_BIAS, SMALL_LN2_GAIN, SMALL_LN2_BIAS = 0, 1, 2, 3
SMALL_B_OUT, SMALL_B_DOWN, SMALL_PENALTY = 4, 5, 6
SMALL_B_QUERY, SMALL_B_VALUE, SMALL_B_UP = 8, 9, 10
SMALL_ROWS = 16


def side_by_side(count, units, width):
    beside = width // units
    height = count // beside
    return [
        (slice(n * height, (n + 1) * height), slice(n * units, (n + 1) * units), slice(0, height))
        for n in range(beside)
    ]


def team_device(team, core, chips):
    return {"dp": lax.div(team, chips), "blk": lax.rem(team, chips) * 2 + core}


def front_kernel(operands, results, scratch, raw):
    (
        atoms, ids, gain_one, bias_one, w_key, w_value, b_value, w_query, b_query, w_out, cot, w_down, w_up, b_out,
        gain, bias, b_up, b_down,
    ) = operands
    (pair,) = raw
    (
        queries, kept, id_column, log_sums, mixed, id_row, d_mixed, out_mine, d_hidden, shares, small,
    ) = results[:11]
    parcels = results[11:]
    (
        pair_buf, score, high, low, q_part, q_land, q_all, k_all, w_all, squares, mixed_all, hidden_two, down, normal_two, rate_two,
        part, landed, back, back_landed, ups_part, ups_sib, ups_go, ups_got, downs_part, downs_sib, downs_go, downs_got,
        pair_sem, kept_send, kept_recv, kz_send, kf_send, ks_send, k_recv, q_send, q_recv, w_send, wx_send, wf_send, w_recv,
        mix_send, mix_recv, part_send, part_recv, back_send, back_recv, sib_send, sib_recv, g_send, g_recv,
    ) = scratch
    zs, feats, rows = mixed_all.shape
    blocks = kept.shape[0]
    chips = blocks // 2
    teams, width = ups_part.shape[0], atoms.shape[1]
    _, group, _, cols = pair_buf.shape
    heads = feats // DH
    groups = heads // group
    piece = rows // zs
    z, blk = lax.axis_index("head"), lax.axis_index("blk")
    core, chip = lax.rem(blk, 2), lax.div(blk, 2)
    dp, dps = lax.axis_index("dp"), lax.axis_size("dp")
    partners = others(dp, dps)
    team = dp * chips + chip
    other_core = 1 - core
    sib_blk = blk + 1 - 2 * core
    sibling = {"blk": sib_blk}
    peers, far_teams = others(z, zs), others(team, teams)
    far = [step * 2 + core for step in others(chip, chips)]
    far_siblings = [step * 2 + other_core for step in others(chip, chips)]
    mine = pl.ds(pl.multiple_of(z * piece, 8), piece)

    def pair_copy(index, slot):
        return pltpu.make_async_copy(
            pair.at[0, pl.ds(index * group, group)], pair_buf.at[slot], pair_sem.at[slot]
        )

    meeting = [{"head": peer} for peer in peers] + [sibling]
    meeting += [team_device(peer, core, chips) for peer in far_teams]
    greet(meeting)
    for n in range(2):
        pair_copy(n, n).start()

    normal, _ = normalize(atoms[...])
    normed = halves(normal * gain_one[...] + bias_one[...])
    meet(meeting)
    copies = []
    fewer = feats // (2 * dps)
    w_mine = w_out.source.at[pl.ds(pl.multiple_of((dp * 2 + core) * fewer, 8), fewer)]
    copies += [
        send(w_mine, w_all.at[z, dp, core], w_send.at[n], w_recv.at[z, dp, core], {"head": peer})
        for n, peer in enumerate(peers)
    ]
    kept[blk, 0:feats, :] = dot_halves(normed, halves(w_key[...])).T
    copies += [
        send(kept.at[blk, 0:feats], k_all.at[blk, z], kz_send.at[n], k_recv.at[blk, z], {"head": peer})
        for n, peer in enumerate(peers)
    ]
    kept[blk, feats : 2 * feats, :] = (dot_halves(normed, halves(w_value[...])) + b_value[...]).T
    id_line = ids[...].astype(F32)
    kept[blk, 2 * feats : 2 * feats + 8, :] = jnp.broadcast_to(id_line, (8, rows))
    copies += [
        send(kept.at[blk], kept.at[blk], kept_send.at[n], kept_recv.at[blk], {"blk": peer})
        for n, peer in enumerate([sib_blk] + far)
    ]
    q_rows = (dot_halves(normed, halves(w_query[...])) + b_query[...]) * (DH ** (-0.5))
    q_part[...] = q_rows.reshape(zs, piece, feats)
    queries[...] = q_rows.T
    queries.flush()
    q_land[z] = q_part[z]
    w_all[z] = w_out[...].reshape(dps, 2, fewer, width)
    id_column[...] = jnp.broadcast_to(id_line, (LANES, rows)).T
    id_column.flush()
    small[...] = jnp.zeros(small.shape, F32)
    for n, peer in enumerate(peers):
        ready = w_all.at[peer, dp, core]
        arrived(ready, w_recv.at[peer, dp, core])
        copies += [
            send(ready, ready, wx_send.at[n, m], w_recv.at[peer, dp, core], {"dp": partner})
            for m, partner in enumerate(partners)
        ]
    for n, source in enumerate(far):
        arrived(kept.at[source], kept_recv.at[source])
        copies.append(
            send(kept.at[source], kept.at[source], kept_send.at[chips + n], kept_recv.at[source], sibling)
        )
    for source in [sib_blk] + far_siblings:
        arrived(kept.at[source], kept_recv.at[source])
    kept.flush()
    one = joined(kept[n, 2 * feats : 2 * feats + 8, :] for n in range(blocks))
    id_row[...] = jnp.concatenate([one, one], axis=0)
    id_row.flush()

    def mix_copies(index):
        some = pl.ds(pl.multiple_of(index * (8 * group), 8 * group), 8 * group)
        return [
            pltpu.make_async_remote_copy(
                src_ref=mixed.at[some],
                dst_ref=mixed_all.at[z, some],
                send_sem=mix_send.at[n, index],
                recv_sem=mix_recv.at[z, index],
                device_id={"head": peer},
                device_id_type=MESH,
            )
            for n, peer in enumerate(peers)
        ]

    def step(index, carry):
        slot = lax.rem(index, 2)
        pair_copy(index, slot).wait()
        low_row = pl.multiple_of(index * (8 * group), 8 * group)
        some = pl.ds(low_row, 8 * group)
        values = pl.ds(pl.multiple_of(feats + low_row, 8), 8 * group)
        mixed[some, :] = attend_group(
            pair_buf.at[slot],
            queries[some, :],
            joined(kept[n, some, :] for n in range(blocks)),
            joined(kept[n, values, :] for n in range(blocks)),
            id_column, id_row, log_sums, index * group, score, high, low,
        )
        for copy in mix_copies(index):
            copy.start()

        @pl.when(index + 2 < groups)
        def _():
            pair_copy(index + 2, slot).start()

        return carry

    lax.fori_loop(0, groups, step, 0)
    mixed.flush()
    log_sums.flush()
    for n, peer in enumerate(peers):
        for kind in range(dps):
            ready = w_all.at[peer, kind, core]

            @pl.when(dp != kind)
            def _(ready=ready, sem=w_recv.at[peer, kind, core]):
                arrived(ready, sem)

            copies.append(send(ready, ready, wf_send.at[n, kind], w_recv.at[peer, kind, core], sibling))
    for n, peer in enumerate(peers):
        ready = k_all.at[blk, peer]
        arrived(ready, k_recv.at[blk, peer])
        copies += [
            send(ready, ready, kf_send.at[n, m], k_recv.at[blk, peer], {"blk": target})
            for m, target in enumerate([sib_blk] + far)
        ]

    small[SMALL_B_DOWN : SMALL_B_DOWN + 1, :] = column_sum(cot[mine, :])
    cots = halves(cot[...])
    downs = halves(w_down[...])
    d_act = dot_halves(cots, downs, NT)
    ups = halves(w_up[...])
    for peer in peers:
        for kind in range(dps):
            arrived(w_all.at[peer, kind, other_core], w_recv.at[peer, kind, other_core])
    outs = halves(w_all[...].reshape(zs * feats, width))
    mixed_all[z] = mixed[...]
    for peer in peers:
        for index in range(groups):
            some = pl.ds(index * (8 * group), 8 * group)
            arrived(mixed_all.at[peer, some], mix_recv.at[peer, index])
    copies += [
        send(q_part.at[peer], q_land.at[z], q_send.at[n], q_recv.at[z], {"head": peer})
        for n, peer in enumerate(peers)
    ]
    mixed_rows = mixed_all[...].reshape(zs * feats, rows).T
    hidden_rows = atoms[...] + dot_halves(halves(mixed_rows), outs) + b_out[...]
    hidden_two[...] = hidden_rows
    normal, rate = normalize(hidden_rows)
    normal_two[...] = normal
    rate_two[...] = jnp.broadcast_to(rate, rate_two.shape)
    normed = normal * gain[...] + bias[...]
    pre = dot_halves(halves(normed), ups) + b_up[...]
    phi = 0.5 * (1.0 + lax.erf(pre * math.sqrt(0.5)))
    act = pre * phi
    d_pre = d_act * (phi + pre * jnp.exp(-0.5 * pre * pre) * (1.0 / math.sqrt(2.0 * math.pi)))
    d_pres = halves(d_pre)
    part[...] = dot_halves(d_pres, ups, NT).reshape(zs, piece, width)
    copies += [
        send(part.at[peer], landed.at[z], part_send.at[n], part_recv.at[z], {"head": peer})
        for n, peer in enumerate(peers)
    ]
    landed[z] = part[z]
    ups_part[...] = dot_halves(halves(normed.T), d_pres).reshape(ups_part.shape)
    copies.append(send(ups_part.at[:, other_core], ups_sib, sib_send.at[0], sib_recv.at[0], sibling))
    downs_part[...] = dot_halves(halves(act.T), cots).reshape(downs_part.shape)
    copies.append(send(downs_part.at[:, other_core], downs_sib, sib_send.at[1], sib_recv.at[1], sibling))
    down[...] = dot_halves(halves(act), downs)
    out_mine[...] = hidden_two[mine, :] + down[mine, :] + b_down[...]
    out_mine.flush()
    small[SMALL_B_UP : SMALL_B_UP + 1, 0 : d_pre.shape[1]] = column_sum(d_pre)
    for kind, (parts, sib, go, got) in enumerate(
        [(ups_part, ups_sib, ups_go, ups_got), (downs_part, downs_sib, downs_go, downs_got)]
    ):
        arrived(sib, sib_recv.at[kind])
        go[...] = sib[...] + parts[:, core]
        copies += [
            send(
                go.at[peer], got.at[team], g_send.at[kind, n], g_recv.at[kind, team],
                team_device(peer, core, chips),
            )
            for n, peer in enumerate(far_teams)
        ]
        got[team] = go[team]
    for n, source in enumerate(far):
        for m, peer in enumerate(peers):
            ready = k_all.at[source, peer]
            arrived(ready, k_recv.at[source, peer])
            copies.append(send(ready, ready, ks_send.at[n, m], k_recv.at[source, peer], sibling))
    for peer in peers:
        arrived(q_land.at[peer], q_recv.at[peer])
    for n in range(zs):
        q_all[n] = q_land[n].T
    for n in range(blocks):
        k_all[n, z] = kept[n, 0:feats, :]
    for source in [sib_blk] + far_siblings:
        for peer in peers:
            arrived(k_all.at[source, peer], k_recv.at[source, peer])
    squares[...] = jnp.zeros(squares.shape, F32)
    at_once = 4
    rounds = heads // at_once

    def square_step(index, carry):
        there = lax.div(index, rounds)
        some = pl.ds(pl.multiple_of(lax.rem(index, rounds) * (8 * at_once), 8 * at_once), 8 * at_once)
        q_some = q_all[there, some, :]
        k_some = joined(k_all[n, there, some, :] for n in range(blocks))
        added = None
        for h in range(at_once):
            head = slice(8 * h, 8 * h + 8)
            q_high, q_low = wide_halves(q_some[head])
            k_high, k_low = wide_halves(k_some[head])
            value = dot(
                stacked([q_high, q_high, q_low, q_low]), stacked([k_high, k_low, k_high, k_low]), TN
            )
            added = value * value if added is None else added + value * value
        squares[...] += added
        return carry

    lax.fori_loop(0, zs * rounds, square_step, 0)
    same = id_column[mine, 0:1] == id_row[0:1, :]
    norms = jnp.sqrt(squares[...] + 1.0)
    terms = jnp.where(same, jnp.log1p(jnp.exp(norms - math.sqrt(zs * heads))), 0.0)
    number = jnp.where(same, 1.0, 0.0)

    def total(value):
        return jnp.sum(jnp.sum(value, axis=1, keepdims=True), axis=0, keepdims=True)

    lane = lax.broadcasted_iota(jnp.int32, (1, width), 1)
    small[SMALL_PENALTY : SMALL_PENALTY + 1, :] = jnp.where(
        lane == 0, total(terms), jnp.where(lane == 1, total(number), 0.0)
    )
    for peer in peers:
        arrived(landed.at[peer], part_recv.at[peer])
    d_normed = functools.reduce(jnp.add, [landed[n] for n in range(zs)])
    normal = normal_two[mine, :]
    d_rows = cot[mine, :] + normalize_back(d_normed, gain[...], normal, rate_two[mine, 0:1])
    d_halves = halves(d_rows)
    for n in range(zs):
        some = slice(n * feats, (n + 1) * feats)
        back[n] = dot_halves(d_halves, (outs[0][some], outs[1][some]), NT)
    copies += [
        send(back.at[peer], back_landed.at[z], back_send.at[n], back_recv.at[z], {"head": peer})
        for n, peer in enumerate(peers)
    ]
    back_landed[z] = back[z]
    d_hidden[...] = d_rows
    d_hidden.flush()
    for peer, parcel in zip(peers, parcels, strict=True):
        parcel[0:piece, :] = down[pl.ds(pl.multiple_of(peer * piece, 8), piece), :]
        parcel[piece : 2 * piece, :] = d_rows
        parcel.flush()
    small[SMALL_LN2_GAIN : SMALL_LN2_GAIN + 1, :] = column_sum(d_normed * normal)
    small[SMALL_LN2_BIAS : SMALL_LN2_BIAS + 1, :] = column_sum(d_normed)
    small[SMALL_B_OUT : SMALL_B_OUT + 1, :] = column_sum(d_rows)
    small.flush()
    for kind, got in enumerate([ups_got, downs_got]):
        for peer in far_teams:
            arrived(got.at[peer], g_recv.at[kind, peer])
    up_share, down_share = [
        functools.reduce(jnp.add, [got[n] for n in range(teams)]) for got in (ups_got, downs_got)
    ]
    for rows_of, columns_of, there in side_by_side(*up_share.shape, width):
        shares[there, columns_of] = up_share[rows_of]
    shares[there.stop :, :] = down_share
    shares.flush()
    for peer in peers:
        arrived(back_landed.at[peer], back_recv.at[peer])
    d_mixed[...] = back_landed[...].reshape(rows, feats).T
    d_mixed.flush()
    for copy in copies:
        copy.wait_send()

    def drain(index, carry):
        for copy in mix_copies(index):
            copy.wait_send()
        return carry

    lax.fori_loop(0, groups, drain, 0)


def front(zs, dps, teams, pair, *operands):
    _, heads, rows, cols = pair.shape
    feats, blocks = heads * DH, cols // rows
    width, units = operands[0].shape[1], operands[12].shape[1]
    piece, group = rows // zs, GROUP
    up_rows, down_rows = width // (2 * teams), units // (2 * teams)
    groups = heads // group
    slab = pltpu.VMEM((zs, piece, width), F32)
    narrow = pltpu.VMEM((zs, piece, feats), F32)
    one_up, one_down = pltpu.VMEM((teams, up_rows, units), F32), pltpu.VMEM((teams, down_rows, width), F32)
    dma = pltpu.SemaphoreType.DMA
    return staged_call(
        front_kernel,
        "front",
        operands,
        [
            (feats, rows), (blocks, 2 * feats + 8, rows), (rows, LANES), (heads, rows, LANES), (feats, rows),
            (STRIP, cols), (feats, rows), (piece, width), (piece, width),
            (up_rows * units // width + down_rows, width), (SMALL_ROWS, width),
        ]
        + [(2 * piece, width)] * (zs - 1),
        [
            pltpu.VMEM((2, group, rows, cols), F32),
            pltpu.VMEM((group, rows, cols), F32),
            pltpu.VMEM((group, rows, cols), BF16),
            pltpu.VMEM((group, rows, cols), BF16),
            narrow, narrow,
            pltpu.VMEM((zs, feats, piece), F32),
            pltpu.VMEM((blocks, zs, feats, rows), F32),
            pltpu.VMEM((zs, dps, 2, feats // (2 * dps), width), F32),
            pltpu.VMEM((piece, cols), F32),
            pltpu.VMEM((zs, feats, rows), F32),
            pltpu.VMEM((rows, width), F32),
            pltpu.VMEM((rows, width), F32),
            pltpu.VMEM((rows, width), F32),
            pltpu.VMEM((rows, LANES), F32),
            slab, slab, narrow, narrow,
            pltpu.VMEM((teams, 2, up_rows, units), F32),
            one_up, one_up, one_up,
            pltpu.VMEM((teams, 2, down_rows, width), F32),
            one_down, one_down, one_down,
            dma((2,)),
            dma((blocks,)), dma((blocks,)),
            dma((zs,)), dma((zs, blocks // 2)), dma((blocks // 2, zs)), dma((blocks, zs)),
            dma((zs,)), dma((zs,)),
            dma((zs,)), dma((zs, dps)), dma((zs, dps)), dma((zs, dps, 2)),
            dma((zs, groups)), dma((zs, groups)),
            dma((zs,)), dma((zs,)),
            dma((zs,)), dma((zs,)),
            dma((2,)), dma((2,)),
            dma((2, teams)), dma((2, teams)),
        ],
        58,
        remote=0,
        raw=(pair,),
    )


def finish_kernel(operands, results, scratch, raw):
    (
        d_keys, d_values, out_mine, d_hidden, d_queries, atoms, gain, bias, w_query, mixed, small_in, w_key, w_value,
    ) = operands[:13]
    parcels = operands[13 : 12 + lax.axis_size("head")]
    chip_shares = operands[12 + lax.axis_size("head") :]
    grad_atoms, out_atoms, total_grads, grad_up, grad_down, small, penalty = results
    (
        sib_keys, sib_values, go_keys, go_values, got_keys, got_values,
        part, landed, grads, sib_grads, go_grads, got_grads, hidden_all, small_z, small_all,
        sib_send, sib_recv, kv_send, kv_recv, part_send, part_recv, back_send, back_recv,
        g_send, g_recv, t_send, t_recv, f_send, b_send, b_recv, bf_send, out_send, out_recv,
        small_z_send, small_z_recv, small_send, small_recv,
    ) = scratch
    chips, _, feats, rows = d_keys.shape
    zs, piece, width = part.shape
    teams, _, share, _ = grads.shape
    blk, z, dp = lax.axis_index("blk"), lax.axis_index("head"), lax.axis_index("dp")
    core, chip = lax.rem(blk, 2), lax.div(blk, 2)
    other_core = 1 - core
    sibling = {"blk": blk + 1 - 2 * core}
    peers = others(z, zs)
    team = dp * chips + chip
    far_teams = others(team, teams)
    far_chips = others(chip, chips)
    place = team * 2 + core
    far_places = others(place, teams * 2)
    plane = [team_device(lax.div(value, 2), lax.rem(value, 2), chips) for value in far_places]
    meeting = [{"head": peer} for peer in peers] + plane
    greet(meeting)
    meet(meeting)
    copies = [
        send(d_keys.source.at[:, other_core], sib_keys, sib_send.at[0], sib_recv.at[0], sibling),
        send(d_values.source.at[:, other_core], sib_values, sib_send.at[1], sib_recv.at[1], sibling),
    ]
    mine = pl.ds(pl.multiple_of(z * piece, 8), piece)
    out_atoms[mine, :] = functools.reduce(jnp.add, [parcel[0:piece, :] for parcel in parcels], out_mine[...])
    copies += [
        send(out_atoms.at[mine], out_atoms.at[mine], out_send.at[n], out_recv.at[z], {"head": peer})
        for n, peer in enumerate(peers)
    ]

    def big_rows(result, source, kind):
        count = result.shape[0] // (2 * teams)
        return result.at[pl.ds(pl.multiple_of((source * 2 + kind) * count, 8), count)]

    partners = others(dp, lax.axis_size("dp"))
    for n in range(chips):
        source = dp * chips + lax.rem(chip + chips - n, chips)
        up_there, down_there = big_rows(grad_up, source, core), big_rows(grad_down, source, core)
        for rows_of, columns_of, there in side_by_side(*up_there.shape, width):
            up_there[rows_of, :] = chip_shares[n][there, columns_of]
        down_there[...] = chip_shares[n][there.stop :, :]
        for kind, ready in enumerate([up_there, down_there]):
            copies += [
                send(ready, ready, b_send.at[kind, n, m], b_recv.at[kind, source, core], {"dp": partner})
                for m, partner in enumerate(partners)
            ]
    own_keys, own_values = d_keys.ref, d_values.ref
    for kind, (sib, mine_too, go, got) in enumerate(
        [(sib_keys, own_keys, go_keys, got_keys), (sib_values, own_values, go_values, got_values)]
    ):
        arrived(sib, sib_recv.at[kind])
        go[...] = sib[...] + mine_too[:, core]
        copies += [
            send(
                go.at[peer], got.at[chip], kv_send.at[kind, n], kv_recv.at[kind, chip],
                {"blk": peer * 2 + core},
            )
            for n, peer in enumerate(far_chips)
        ]
    got_keys[chip] = go_keys[chip]
    got_values[chip] = go_values[chip]
    normal, rate = normalize(atoms[...])
    normed = halves(normal * gain[...] + bias[...])
    dq_rows = d_queries[...].T
    d_normed = dot_full(dq_rows, w_query[...], NT)
    grad_q = dot_halves(halves(d_queries[...]), normed)
    small_z[z] = small_in[0:8, :]
    hidden_all[z] = d_hidden[...]
    for n, parcel in enumerate(parcels):
        hidden_all[lax.rem(z + zs - 1 - n, zs)] = parcel[piece : 2 * piece, :]
    grad_o = dot_full(mixed[...], hidden_all[...].reshape(rows, width))
    for peer in far_chips:
        arrived(got_keys.at[peer], kv_recv.at[0, peer])
        arrived(got_values.at[peer], kv_recv.at[1, peer])
    dk = functools.reduce(jnp.add, [got_keys[n] for n in range(chips)])
    dv = functools.reduce(jnp.add, [got_values[n] for n in range(chips)])
    dv_rows = dv.T
    d_normed = (
        d_normed + dot_full(dk.T, w_key[...], NT) + dot_full(dv_rows, w_value[...], NT)
    )
    part[...] = d_normed.reshape(zs, piece, width)
    copies += [
        send(part.at[peer], landed.at[z], part_send.at[n], part_recv.at[z], {"head": peer})
        for n, peer in enumerate(peers)
    ]
    landed[z] = part[z]
    grad_k = dot_halves(halves(dk), normed)
    grad_v = dot_halves(halves(dv), normed)
    grads[...] = jnp.concatenate([grad_q, grad_k, grad_v, grad_o], axis=0).reshape(grads.shape)
    copies.append(send(grads.at[:, other_core], sib_grads, sib_send.at[2], sib_recv.at[2], sibling))
    arrived(sib_grads, sib_recv.at[2])
    go_grads[...] = sib_grads[...] + grads[:, core]
    copies += [
        send(
            go_grads.at[peer], got_grads.at[team], g_send.at[n], g_recv.at[team], team_device(peer, core, chips)
        )
        for n, peer in enumerate(far_teams)
    ]
    got_grads[team] = go_grads[team]
    for peer in peers:
        arrived(landed.at[peer], part_recv.at[peer])
    d_normed = functools.reduce(jnp.add, [landed[n] for n in range(zs)])
    normal, rate = normalize(atoms[mine, :])
    grad_atoms[mine, :] = d_hidden[...] + normalize_back(d_normed, gain[...], normal, rate)
    small_z[z, SMALL_LN1_GAIN : SMALL_LN1_GAIN + 1, :] = column_sum(d_normed * normal)
    small_z[z, SMALL_LN1_BIAS : SMALL_LN1_BIAS + 1, :] = column_sum(d_normed)
    copies += [
        send(small_z.at[z], small_z.at[z], small_z_send.at[n], small_z_recv.at[z], {"head": peer})
        for n, peer in enumerate(peers)
    ]
    copies += [
        send(grad_atoms.at[mine], grad_atoms.at[mine], back_send.at[n], back_recv.at[z], {"head": peer})
        for n, peer in enumerate(peers)
    ]
    for peer in far_teams:
        arrived(got_grads.at[peer], g_recv.at[peer])
    total_grads[team, core] = functools.reduce(jnp.add, [got_grads[n] for n in range(teams)])
    ready = total_grads.at[team, core]
    copies.append(send(ready, ready, t_send.at[0], t_recv.at[team, core], sibling))
    copies += [
        send(ready, ready, t_send.at[n + 1], t_recv.at[team, core], team_device(peer, core, chips))
        for n, peer in enumerate(far_teams)
    ]
    for peer in peers:
        arrived(small_z.at[peer], small_z_recv.at[peer])
    small_all[place, 0:8, :] = functools.reduce(jnp.add, [small_z[n] for n in range(zs)])
    small_all[place, 8:16, :] = small_in[8:16, :]
    small_all[place, SMALL_B_QUERY : SMALL_B_QUERY + 1, 0:feats] = column_sum(dq_rows)
    small_all[place, SMALL_B_VALUE : SMALL_B_VALUE + 1, 0:feats] = column_sum(dv_rows)
    copies += [
        send(small_all.at[place], small_all.at[place], small_send.at[n], small_recv.at[place], target)
        for n, target in enumerate(plane)
    ]
    for n, peer in enumerate(far_teams):
        ready = total_grads.at[peer, core]
        arrived(ready, t_recv.at[peer, core])
        copies.append(send(ready, ready, f_send.at[n], t_recv.at[peer, core], sibling))
    for kind, result in enumerate([grad_up, grad_down]):
        for n in range(teams):
            ready = big_rows(result, n, core)

            @pl.when(lax.div(n, chips) != dp)
            def _(ready=ready, sem=b_recv.at[kind, n, core]):
                arrived(ready, sem)

            copies.append(send(ready, ready, bf_send.at[kind, n], b_recv.at[kind, n, core], sibling))
    for source in far_places:
        arrived(small_all.at[source], small_recv.at[source])
    summed = functools.reduce(jnp.add, [small_all[n] for n in range(2 * teams)])
    small[...] = summed
    ends = summed[SMALL_PENALTY : SMALL_PENALTY + 1, :]
    penalty[...] = ends[:, 0:1] / ends[:, 1:2]
    for peer in [team] + far_teams:
        arrived(total_grads.at[peer, other_core], t_recv.at[peer, other_core])
    total_grads.flush()
    for kind, result in enumerate([grad_up, grad_down]):
        for n in range(teams):
            arrived(big_rows(result, n, other_core), b_recv.at[kind, n, other_core])
        result.flush()
    for peer in peers:
        there = pl.ds(pl.multiple_of(peer * piece, 8), piece)
        arrived(out_atoms.at[there], out_recv.at[peer])
    out_atoms.flush()
    for peer in peers:
        there = pl.ds(pl.multiple_of(peer * piece, 8), piece)
        arrived(grad_atoms.at[there], back_recv.at[peer])
    for copy in copies:
        copy.wait_send()


def finish(zs, dps, units, *operands):
    d_keys, atoms = operands[0], operands[5]
    chips, _, feats, rows = d_keys.shape
    width = atoms.shape[1]
    piece = rows // zs
    teams = dps * chips
    share = 4 * feats // (2 * teams)
    some = pltpu.VMEM((chips, feats, rows), F32)
    slab = pltpu.VMEM((zs, piece, width), F32)
    one = pltpu.VMEM((teams, share, width), F32)
    dma = pltpu.SemaphoreType.DMA
    return staged_call(
        finish_kernel,
        "finish",
        operands,
        [
            (rows, width),
            (rows, width),
            (teams, 2, share, width),
            (width, units),
            (units, width),
            (SMALL_ROWS, width),
            (1, 1),
        ],
        [some] * 6
        + [slab, slab, pltpu.VMEM((teams, 2, share, width), F32), one, one, one, slab]
        + [
            pltpu.VMEM((zs, 8, width), F32),
            pltpu.VMEM((2 * teams, SMALL_ROWS, width), F32),
            dma((3,)), dma((3,)),
            dma((2, chips)), dma((2, chips)),
            dma((zs,)), dma((zs,)),
            dma((zs,)), dma((zs,)),
            dma((teams,)), dma((teams,)),
            dma((teams,)), dma((teams, 2)), dma((teams,)),
            dma((2, chips, dps)), dma((2, teams, 2)), dma((2, teams)),
            dma((zs,)), dma((zs,)),
            dma((zs,)), dma((zs,)),
            dma((2 * teams,)), dma((2 * teams,)),
        ],
        58,
        remote=2,
    )


def place_kernel(operands, results, scratch, raw):
    total_grads, small = operands
    grad_query, grad_key, grad_value, grad_out = results[:4]
    feats, width = grad_out.shape
    done = total_grads[...].reshape(4 * feats, width)
    grad_query[...] = done[0:feats].T
    grad_query.flush()
    grad_key[...] = done[feats : 2 * feats].T
    grad_key.flush()
    grad_value[...] = done[2 * feats : 3 * feats].T
    grad_value.flush()
    grad_out[...] = done[3 * feats :]
    grad_out.flush()
    for result, row in zip(results[4:], SMALL_OUTPUTS, strict=True):
        result[...] = small[row : row + 1, 0 : result.shape[1]]


SMALL_OUTPUTS = (
    SMALL_LN1_GAIN, SMALL_LN1_BIAS, SMALL_B_QUERY, SMALL_B_VALUE, SMALL_B_OUT, SMALL_LN2_GAIN, SMALL_LN2_BIAS,
    SMALL_B_UP, SMALL_B_DOWN,
)


def place(feats, units, straight, *operands):
    width = operands[1].shape[1]
    lengths = {SMALL_B_QUERY: feats, SMALL_B_VALUE: feats, SMALL_B_UP: units}
    return staged_call(
        place_kernel,
        "place",
        operands,
        [(width, feats)] * 3
        + [(feats, width)]
        + [(1, lengths.get(row, width)) for row in SMALL_OUTPUTS],
        [],
        58,
        straight=straight,
    )


def local(
    zs, dps,
    atoms, pair, mol_ids, ln1_gain, ln1_bias, w_query, b_query, w_key, w_value, b_value, w_out, b_out,
    ln2_gain, ln2_bias, w_up, b_up, w_down, b_down, cot_atoms, cot_pair,
):
    blocks = pair.shape[3] // pair.shape[2]
    inputs, cot = atoms[0], cot_atoms[0]

    def line(value):
        return value.reshape(1, -1)

    (
        queries, kept, id_column, log_sums, mixed, id_row, d_mixed, out_mine, d_hidden, shares, small, *parcels,
    ) = front(
        zs, dps, dps * blocks // 2, pair,
        inputs, mol_ids, line(ln1_gain), line(ln1_bias), w_key, w_value, line(b_value), w_query, line(b_query),
        w_out, cot, w_down, w_up, line(b_out), line(ln2_gain), line(ln2_bias), line(b_up),
        line(b_down),
    )
    parcels = [
        lax.ppermute(parcel, "head", [(source, (source + n + 1) % zs) for source in range(zs)])
        for n, parcel in enumerate(parcels)
    ]
    chips = blocks // 2
    chip_shares = [shares] + [
        lax.ppermute(shares, "blk", [(2 * c + core, 2 * ((c + n) % chips) + core) for c in range(chips) for core in range(2)])
        for n in range(1, chips)
    ]
    out_pair, grad_pair, d_queries, d_keys, d_values = attend_back(
        pair, cot_pair, queries, kept, mixed, d_mixed, log_sums, id_column, id_row
    )
    grad_atoms, out_atoms, total_grads, grad_up, grad_down, small, penalty = finish(
        zs, dps, w_up.shape[1],
        d_keys, d_values, out_mine, d_hidden, d_queries, inputs, line(ln1_gain), line(ln1_bias), w_query, mixed,
        small, w_key, w_value, *parcels, *chip_shares,
    )
    placed = place(
        w_query.shape[1], w_up.shape[1],
        [grad_atoms, out_atoms, grad_up, grad_down],
        total_grads, small,
    )
    grad_atoms, out_atoms, grad_up, grad_down, grad_query, grad_key, grad_value, grad_out = placed[:8]
    (
        grad_ln1_gain, grad_ln1_bias, grad_b_query, grad_b_value, grad_b_out, grad_ln2_gain, grad_ln2_bias,
        grad_b_up, grad_b_down,
    ) = [value.reshape(-1) for value in placed[8:]]
    return (
        out_atoms[None],
        out_pair,
        penalty[0, 0],
        grad_atoms[None],
        grad_pair,
        grad_ln1_gain,
        grad_ln1_bias,
        grad_query,
        grad_b_query,
        grad_key,
        grad_value,
        grad_b_value,
        grad_out,
        grad_b_out,
        grad_ln2_gain,
        grad_ln2_bias,
        grad_up,
        grad_b_up,
        grad_down,
        grad_b_down,
    )


def solution(mesh):
    rows, pairs = P("dp", "blk", None), P("dp", "head", "blk", None)
    columns = P(None, "head")
    return jax.shard_map(
        functools.partial(local, mesh.shape["head"], mesh.shape["dp"]),
        mesh=mesh,
        in_specs=(
            rows, pairs, P("dp", "blk"), P(), P(), columns, P("head"), columns, columns, P("head"),
            P("head", None), P(), P(), P(), columns, P("head"), P("head", None), P(), rows, pairs,
        ),
        out_specs=(
            rows, pairs, P(), rows, pairs, P(), P(), columns, P("head"), columns, columns, P("head"),
            P("head", None), P(), P(), P(), columns, P("head"), P("head", None), P(),
        ),
        check_vma=False,
    )
```

```python
import functools
import math

import jax
import jax.numpy as jnp
from jax import lax
from jax.experimental import pallas as pl
from jax.experimental.pallas import tpu as pltpu
from jax.sharding import PartitionSpec as P

DH = 8
LANES = 128
STRIP = 16
CHUNK = 256
GROUP = 2
FRONT_MB, BACK_MB, FINISH_MB, PLACE_MB = 58, 60, 40, 32
NORM_EPS = 1e-05
MASK_FILL = -1e30
F32 = jnp.float32
BF16 = jnp.bfloat16
MESH = pl.DeviceIdType.MESH
NN = (((1,), (0,)), ((), ()))
NT = (((1,), (1,)), ((), ()))
TN = (((0,), (0,)), ((), ()))
VMEM = pl.BlockSpec(memory_space=pltpu.VMEM)


def dot(left, right, dims=NN):
    return lax.dot_general(left, right, dims, preferred_element_type=F32)


def halves(value):
    high = value.astype(BF16)
    return high, (value - high.astype(F32)).astype(BF16)


def dot_halves(left, right, dims=NN):
    return dot(left[0], right[0], dims) + (
        dot(left[0], right[1], dims) + dot(left[1], right[0], dims)
    )


def dot_full(left, right, dims=NN):
    return dot_halves(halves(left), halves(right), dims)


def normalize(inputs):
    centred = inputs - jnp.mean(inputs, -1, keepdims=True)
    rate = lax.rsqrt(jnp.mean(centred * centred, -1, keepdims=True) + NORM_EPS)
    return centred * rate, rate


def normalize_back(grad, gain, normal, rate):
    scaled = grad * gain
    return rate * (
        scaled
        - jnp.mean(scaled, -1, keepdims=True)
        - normal * jnp.mean(scaled * normal, -1, keepdims=True)
    )


def column_sum(value):
    return jnp.sum(value, 0, keepdims=True)


def send(src, dst, send_sem, recv_sem, target):
    copy = pltpu.make_async_remote_copy(
        src_ref=src,
        dst_ref=dst,
        send_sem=send_sem,
        recv_sem=recv_sem,
        device_id=target,
        device_id_type=MESH,
    )
    copy.start()
    return copy


def arrived(ref, sem):
    pltpu.make_async_remote_copy(
        src_ref=ref, dst_ref=ref, send_sem=sem, recv_sem=sem, device_id={}, device_id_type=MESH
    ).wait_recv()


def greet(targets):
    for target in targets:
        pl.semaphore_signal(pltpu.get_barrier_semaphore(), inc=1, device_id=target, device_id_type=MESH)


def meet(targets):
    pl.semaphore_wait(pltpu.get_barrier_semaphore(), len(targets))


def others(index, count):
    return [lax.rem(index + step, count) for step in range(1, count)]


class Operand:
    def __init__(self, source, slot, sem):
        self.source, self.slot, self.shape = source, slot, slot.shape
        self.copy = None if sem is None else pltpu.make_async_copy(source, slot, sem)
        if self.copy is not None:
            self.copy.start()

    @property
    def ref(self):
        if self.copy is not None:
            self.copy.wait()
            self.copy = None
        return self.slot

    def __getitem__(self, index):
        return self.ref[index]


class Result:
    def __init__(self, target, slot, sem):
        self.slot, self.shape, self.at = slot, slot.shape, slot.at
        self.copy = None if sem is None else pltpu.make_async_copy(slot, target, sem)
        self.begun = self.copy is None

    def __setitem__(self, index, value):
        self.slot[index] = value

    def __getitem__(self, index):
        return self.slot[index]

    def flush(self):
        if not self.begun:
            self.copy.start()
            self.begun = True


def staged_call(
    kernel, name, operands, results, scratch, megabytes,
    remote=None, raw=(), straight=(), raw_results=(), cost=None, near_in=(), near_out=(), near_straight=False,
):
    n_in, n_out, n_raw, n_straight = len(operands), len(results), len(raw), len(straight)
    n_left = len(raw_results)
    far_in = [n for n in range(n_in) if n not in near_in]
    far_out = [n for n in range(n_out) if n not in near_out]

    def body(*refs):
        sources, left, refs = refs[:n_in], refs[n_in : n_in + n_raw], refs[n_in + n_raw :]
        moved, refs = refs[:n_straight], refs[n_straight:]
        arrays, refs = refs[:n_straight], refs[n_straight:]
        left, refs = left + refs[:n_left], refs[n_left:]
        targets, refs = refs[:n_out], refs[n_out:]
        in_slots, refs = dict(zip(far_in, refs)), refs[len(far_in) :]
        out_slots, refs = dict(zip(far_out, refs)), refs[len(far_out) :]
        in_sem, out_sem, move_sem, refs = refs[0], refs[1], refs[2], refs[3:]
        through, loads = moved, []
        if not near_straight:
            through, refs = refs[:n_straight], refs[n_straight:]
            loads = [pltpu.make_async_copy(moved[n], through[n], move_sem.at[n]) for n in range(n_straight)]
        moves = [pltpu.make_async_copy(through[n], arrays[n], move_sem.at[n]) for n in range(n_straight)]
        for load in loads:
            load.start()
        ins = [
            Operand(sources[n], in_slots.get(n, sources[n]), in_sem.at[n] if n in in_slots else None)
            for n in range(n_in)
        ]
        outs = [
            Result(targets[n], out_slots.get(n, targets[n]), out_sem.at[n] if n in out_slots else None)
            for n in range(n_out)
        ]
        for load in loads:
            load.wait()
        for move in moves:
            move.start()
        kernel(ins, outs, refs, left)
        for operand in ins:
            operand.ref
        for result in outs:
            result.flush()
        for copy in moves + [result.copy for result in outs if result.copy is not None]:
            copy.wait()

    hbm, vmem = pl.BlockSpec(memory_space=pltpu.HBM), pl.BlockSpec(memory_space=pltpu.VMEM)
    extra = {} if remote is None else {"collective_id": remote, "has_side_effects": True}
    return pl.pallas_call(
        body,
        out_shape=[jax.ShapeDtypeStruct(value.shape, value.dtype) for value in straight]
        + [jax.ShapeDtypeStruct(shape, F32) for shape in raw_results]
        + [jax.ShapeDtypeStruct(shape, F32) for shape in results],
        in_specs=[vmem if n in near_in else hbm for n in range(n_in)]
        + [hbm] * n_raw
        + [vmem if near_straight else hbm] * n_straight,
        out_specs=[hbm] * (n_straight + n_left) + [vmem if n in near_out else hbm for n in range(n_out)],
        scratch_shapes=[pltpu.VMEM(operands[n].shape, operands[n].dtype) for n in far_in]
        + [pltpu.VMEM(results[n], F32) for n in far_out]
        + [pltpu.SemaphoreType.DMA((max(1, n),)) for n in (n_in, n_out, n_straight)]
        + ([] if near_straight else [pltpu.VMEM(value.shape, value.dtype) for value in straight])
        + list(scratch),
        compiler_params=pltpu.CompilerParams(vmem_limit_bytes=megabytes << 20, **extra),
        cost_estimate=cost,
        name=name,
    )(*operands, *raw, *straight)


def joined(pieces):
    return jnp.concatenate(list(pieces), axis=1)


def stacked(parts):
    return jnp.concatenate(parts, axis=0).astype(BF16)


def wide_halves(value):
    high = value.astype(BF16).astype(F32)
    return high, value - high


def attend_group(pair, queries, keys, values, id_column, id_row, log_sums, first, score, high, low):
    group, rows, cols = score.shape
    strips = rows // STRIP
    chunk = min(CHUNK, cols)
    mixed = []
    for g in range(group):
        head = slice(8 * g, 8 * g + 8)
        q_high, q_low = wide_halves(queries[head, :])
        k_high, k_low = wide_halves(keys[head, :])
        v_high, v_low = wide_halves(values[head, :])
        ones = jnp.ones_like(v_high)
        q_pack = stacked([q_high, q_high, q_low, q_low])
        k_pack = stacked([k_high, k_low, k_high, k_low])
        v_pack = stacked([v_high, v_low, ones, jnp.zeros_like(ones)])
        tops = [None] * strips
        for start in range(0, cols, chunk):
            part = slice(start, start + chunk)
            score[g, :, part] = dot(q_pack, k_pack[:, part], TN)
            for s in range(strips):
                line = pl.ds(s * STRIP, STRIP)
                own = id_column[line, :]
                for j in range(start, start + chunk, LANES):
                    tile = pl.ds(j, LANES)
                    value = pair[g, line, tile] + score[g, line, tile]
                    value = jnp.where(own == id_row[:, tile], value, MASK_FILL)
                    score[g, line, tile] = value
                    tops[s] = value if tops[s] is None else jnp.maximum(tops[s], value)
        tops = [
            jnp.broadcast_to(jnp.max(top, axis=1, keepdims=True), (STRIP, LANES)) for top in tops
        ]
        totals = [None] * strips
        gathered = None
        for start in range(0, cols, chunk):
            part = slice(start, start + chunk)
            for s in range(strips):
                line = pl.ds(s * STRIP, STRIP)
                for j in range(start, start + chunk, LANES):
                    tile = pl.ds(j, LANES)
                    weight = jnp.exp(score[g, line, tile] - tops[s])
                    high[g, line, tile], low[g, line, tile] = halves(weight)
                    totals[s] = weight if totals[s] is None else totals[s] + weight
            term = dot(v_pack[:, part], high[g, :, part], NT) + dot(
                v_pack[:, part], low[g, :, part], NT
            )
            gathered = term if gathered is None else gathered + term
        for s in range(strips):
            total = jnp.sum(totals[s], axis=1, keepdims=True)
            log_sums[first + g, pl.ds(s * STRIP, STRIP), :] = tops[s] + jnp.log(total)
        mixed.append((gathered[0:8] + gathered[8:16]) / gathered[16:17])
    return jnp.concatenate(mixed, axis=0)


def chunks_of(cols):
    chunk = min(CHUNK, cols)
    return [slice(start, start + chunk) for start in range(0, cols, chunk)]


def score_packs(queries, keys):
    q_high, q_low = wide_halves(queries)
    k_high, k_low = wide_halves(keys)
    return stacked([q_high, q_high, q_low, q_low]), stacked([k_high, k_low, k_high, k_low])


def attend_back_kernel(operands, results, scratch, raw):
    queries, kept, d_mixed, mixed, id_column, id_row = operands
    (d_heads,) = results
    pair, cot, log_sums, out_pair, grad_pair = raw
    pair_buf, cot_buf, log_buf, out_buf, grad_buf = scratch[:5]
    here = scratch[5:11]
    in_sem, out_sem = scratch[11:]
    heads = pair.shape[1]
    feats = heads * DH
    depth, rows, cols = pair_buf.shape
    blocks = kept.shape[0]
    parts = chunks_of(cols)
    place = lax.broadcasted_iota(jnp.int32, (8, rows), 0)

    def inward(index):
        slot = lax.rem(index, depth)
        sources = (pair.at[0, index], cot.at[0, index], log_sums.at[index])
        return [
            pltpu.make_async_copy(source, buf.at[slot], in_sem.at[n, slot])
            for n, (source, buf) in enumerate(zip(sources, (pair_buf, cot_buf, log_buf), strict=True))
        ]

    def outward(index):
        slot = lax.rem(index, depth)
        return [
            pltpu.make_async_copy(buf.at[slot], array.at[0, index], out_sem.at[n, slot])
            for n, (array, buf) in enumerate([(out_pair, out_buf), (grad_pair, grad_buf)])
        ]

    for n in range(2):
        for copy in inward(n):
            copy.start()
    for operand in operands:
        operand.ref

    def rows_of(index):
        return pl.ds(pl.multiple_of(index * 8, 8), 8)

    def key_rows(index):
        return joined(kept[n, rows_of(index), :] for n in range(blocks))

    def value_row(index):
        return pl.ds(pl.multiple_of(feats + index * 8, 8), 8)

    def value_rows(index):
        return joined(kept[n, value_row(index), :] for n in range(blocks))

    def packs(index):
        head = rows_of(index)
        q_pack, k_pack = score_packs(queries[head, :], key_rows(index))
        v_high, v_low = wide_halves(value_rows(index))
        m_high, m_low = wide_halves(d_mixed[head, :])
        delta_high, rest = wide_halves(-column_sum(mixed[head, :] * d_mixed[head, :]))
        delta_mid, delta_low = wide_halves(rest)
        deltas = jnp.where(
            place == 0, delta_high, jnp.where(place == 1, delta_mid, jnp.where(place == 2, delta_low, 0.0))
        )
        m_pack = stacked([m_high, m_high, m_low, deltas])
        v_pack = stacked([v_high, v_low, v_high, jnp.ones_like(v_high)])
        return q_pack, k_pack, m_pack, v_pack

    def pairs(index):
        head = rows_of(index)
        return [stacked(wide_halves(value)) for value in (queries[head, :], key_rows(index), d_mixed[head, :])]

    def before(pack, part, there):
        q_pack, k_pack, m_pack, v_pack = pack
        there[0][:, part] = dot(q_pack, k_pack[:, part], TN)
        there[1][:, part] = dot(m_pack, v_pack[:, part], TN)

    def middle(index, slot, part, here):
        score, d_prob, p_high, p_low, g_high, g_low = here
        for s in range(rows // STRIP):
            line = pl.ds(s * STRIP, STRIP)
            own = id_column[line, :]
            log_sum = log_buf[slot, line, :]
            for j in range(part.start, part.stop, LANES):
                tile = pl.ds(j, LANES)
                value = pair_buf[slot, line, tile] + score[line, tile]
                out_buf[slot, line, tile] = value
                prob = jnp.exp(jnp.where(own == id_row[:, tile], value - log_sum, MASK_FILL))
                p_high[line, tile], p_low[line, tile] = halves(prob)
                grad = prob * d_prob[line, tile] + cot_buf[slot, line, tile]
                grad_buf[slot, line, tile] = grad
                g_high[line, tile], g_low[line, tile] = halves(grad)

    def both(left, high, low, dims):
        value = dot(left, high, dims) + dot(left, low, dims)
        return value[0:8] + value[8:16]

    def after(index, pair_of, part, there):
        q_pair, k_pair, m_pair = pair_of
        _, _, p_high, p_low, g_high, g_low = there
        head = rows_of(index)
        d_value = both(m_pair, p_high[:, part], p_low[:, part], NN)
        d_key = both(q_pair, g_high[:, part], g_low[:, part], NN)
        for n in range(part.start // rows, part.stop // rows):
            span = slice(n * rows - part.start, (n + 1) * rows - part.start)
            d_heads[n // 2, n % 2, head, :] = d_key[:, span]
            d_heads[n // 2, n % 2, value_row(index), :] = d_value[:, span]
        return both(k_pair[:, part], g_high[:, part], g_low[:, part], NT)

    def stage(index, carry):
        slot = lax.rem(index, depth)
        for copy in inward(index):
            copy.wait()

        @pl.when(index >= depth)
        def _():
            for copy in outward(index - depth):
                copy.wait()

        @pl.when(index == 0)
        def _():
            for n in range(2, depth - 1):
                for copy in inward(n):
                    copy.start()

        @pl.when(index + depth - 1 < heads)
        def _():
            for copy in inward(index + depth - 1):
                copy.start()

        next_packs, own_pairs = packs(index), pairs(index)
        d_query = None
        before(next_packs, parts[0], here)
        for n, part in enumerate(parts):
            if n + 1 < len(parts):
                before(next_packs, parts[n + 1], here)
            middle(index, slot, part, here)
            if n >= 1:
                term = after(index, own_pairs, parts[n - 1], here)
                d_query = term if d_query is None else d_query + term
        term = after(index, own_pairs, parts[-1], here)
        d_query = term if d_query is None else d_query + term
        d_heads[blocks // 2, 0, rows_of(index), :] = d_query * (DH ** (-0.5))
        for copy in outward(index):
            copy.start()
        return carry

    lax.fori_loop(0, heads, stage, 0)
    for result in results:
        result.flush()
    for n in range(max(0, heads - depth), heads):
        for copy in outward(n):
            copy.wait()


def attend_back(pair, cot, queries, kept, mixed, d_mixed, log_sums, id_column, id_row):
    _, heads, rows, cols = pair.shape
    feats = heads * DH
    blocks = kept.shape[0]
    depth = 4
    wide, thin = pltpu.VMEM((rows, cols), F32), pltpu.VMEM((rows, cols), BF16)
    return staged_call(
        attend_back_kernel,
        "attend_back",
        [queries, kept, d_mixed, mixed, id_column, id_row],
        [(blocks // 2 + 1, 2, 2 * feats, rows)],
        [pltpu.VMEM((depth, rows, cols), F32)] * 2
        + [pltpu.VMEM((depth, rows, LANES), F32)]
        + [pltpu.VMEM((depth, rows, cols), F32)] * 2
        + [wide] * 2
        + [thin] * 4
        + [pltpu.SemaphoreType.DMA((3, depth)), pltpu.SemaphoreType.DMA((2, depth))],
        BACK_MB,
        raw=(pair, cot, log_sums),
        raw_results=(pair.shape, pair.shape),
        cost=pl.CostEstimate(
            flops=2 * 400 * heads * rows * cols,
            bytes_accessed=16 * heads * rows * cols,
            transcendentals=heads * rows * cols,
        ),
    )


SMALL_LN1_GAIN, SMALL_LN1_BIAS, SMALL_LN2_GAIN, SMALL_LN2_BIAS = 0, 1, 2, 3
SMALL_B_OUT, SMALL_B_DOWN, SMALL_PENALTY = 4, 5, 6
SMALL_B_QUERY, SMALL_B_VALUE, SMALL_B_UP = 8, 9, 10
SMALL_ROWS = 16


def side_by_side(count, units, width):
    beside = width // units
    height = count // beside
    return [
        (slice(n * height, (n + 1) * height), slice(n * units, (n + 1) * units), slice(0, height))
        for n in range(beside)
    ]


def team_device(team, core, chips):
    return {"dp": lax.div(team, chips), "blk": lax.rem(team, chips) * 2 + core}


def front_kernel(operands, results, scratch, raw):
    (
        atoms, ids, gain_one, bias_one, w_key, w_value, b_value, w_query, b_query, w_out, cot, w_down, w_up, b_out,
        gain, bias, b_up, b_down,
    ) = operands
    (pair,) = raw
    (
        queries, kept, id_column, log_sums, mixed, id_row, d_mixed, out_mine, d_hidden, shares, small,
    ) = results[:11]
    parcels = results[11:]
    (
        pair_buf, score, high, low, q_part, q_land, q_all, k_all, w_all, squares, mixed_all, hidden_two, down, normal_two, rate_two,
        part, landed, back, back_landed, ups_part, ups_sib, ups_go, ups_got, downs_part, downs_sib, downs_go, downs_got,
        pair_sem, kept_send, kept_recv, kz_send, kf_send, ks_send, k_recv, q_send, q_recv, w_send, wx_send, wf_send, w_recv,
        mix_send, mix_recv, part_send, part_recv, back_send, back_recv, sib_send, sib_recv, g_send, g_recv,
    ) = scratch
    zs, feats, rows = mixed_all.shape
    blocks = kept.shape[0]
    chips = blocks // 2
    teams, width = ups_part.shape[0], atoms.shape[1]
    _, group, _, cols = pair_buf.shape
    heads = feats // DH
    groups = heads // group
    piece = rows // zs
    z, blk = lax.axis_index("head"), lax.axis_index("blk")
    core, chip = lax.rem(blk, 2), lax.div(blk, 2)
    dp, dps = lax.axis_index("dp"), lax.axis_size("dp")
    partners = others(dp, dps)
    team = dp * chips + chip
    other_core = 1 - core
    sib_blk = blk + 1 - 2 * core
    sibling = {"blk": sib_blk}
    peers, far_teams = others(z, zs), others(team, teams)
    far = [step * 2 + core for step in others(chip, chips)]
    far_siblings = [step * 2 + other_core for step in others(chip, chips)]
    mine = pl.ds(pl.multiple_of(z * piece, 8), piece)

    def pair_copy(index, slot):
        return pltpu.make_async_copy(
            pair.at[0, pl.ds(index * group, group)], pair_buf.at[slot], pair_sem.at[slot]
        )

    meeting = [{"head": peer} for peer in peers] + [sibling]
    meeting += [team_device(peer, core, chips) for peer in far_teams]
    greet(meeting)
    for n in range(2):
        pair_copy(n, n).start()

    normal, _ = normalize(atoms[...])
    normed = halves(normal * gain_one[...] + bias_one[...])
    meet(meeting)
    copies = []
    fewer = feats // (2 * dps)
    w_mine = w_out.source.at[pl.ds(pl.multiple_of((dp * 2 + core) * fewer, 8), fewer)]
    copies += [
        send(w_mine, w_all.at[z, dp, core], w_send.at[n], w_recv.at[z, dp, core], {"head": peer})
        for n, peer in enumerate(peers)
    ]
    kept[blk, 0:feats, :] = dot_halves(normed, halves(w_key[...])).T
    copies += [
        send(kept.at[blk, 0:feats], k_all.at[blk, z], kz_send.at[n], k_recv.at[blk, z], {"head": peer})
        for n, peer in enumerate(peers)
    ]
    kept[blk, feats : 2 * feats, :] = (dot_halves(normed, halves(w_value[...])) + b_value[...]).T
    id_line = ids[...].astype(F32)
    kept[blk, 2 * feats : 2 * feats + 8, :] = jnp.broadcast_to(id_line, (8, rows))
    copies += [
        send(kept.at[blk], kept.at[blk], kept_send.at[n], kept_recv.at[blk], {"blk": peer})
        for n, peer in enumerate([sib_blk] + far)
    ]
    q_rows = (dot_halves(normed, halves(w_query[...])) + b_query[...]) * (DH ** (-0.5))
    q_part[...] = q_rows.reshape(zs, piece, feats)
    queries[...] = q_rows.T
    queries.flush()
    q_land[z] = q_part[z]
    w_all[z] = w_out[...].reshape(dps, 2, fewer, width)
    id_column[...] = jnp.broadcast_to(id_line, (LANES, rows)).T
    id_column.flush()
    small[...] = jnp.zeros(small.shape, F32)
    for n, peer in enumerate(peers):
        ready = w_all.at[peer, dp, core]
        arrived(ready, w_recv.at[peer, dp, core])
        copies += [
            send(ready, ready, wx_send.at[n, m], w_recv.at[peer, dp, core], {"dp": partner})
            for m, partner in enumerate(partners)
        ]
    for n, source in enumerate(far):
        arrived(kept.at[source], kept_recv.at[source])
        copies.append(
            send(kept.at[source], kept.at[source], kept_send.at[chips + n], kept_recv.at[source], sibling)
        )
    for source in [sib_blk] + far_siblings:
        arrived(kept.at[source], kept_recv.at[source])
    kept.flush()
    one = joined(kept[n, 2 * feats : 2 * feats + 8, :] for n in range(blocks))
    id_row[...] = jnp.concatenate([one, one], axis=0)
    id_row.flush()

    def mix_copies(index):
        some = pl.ds(pl.multiple_of(index * (8 * group), 8 * group), 8 * group)
        return [
            pltpu.make_async_remote_copy(
                src_ref=mixed.at[some],
                dst_ref=mixed_all.at[z, some],
                send_sem=mix_send.at[n, index],
                recv_sem=mix_recv.at[z, index],
                device_id={"head": peer},
                device_id_type=MESH,
            )
            for n, peer in enumerate(peers)
        ]

    def step(index, carry):
        slot = lax.rem(index, 2)
        pair_copy(index, slot).wait()
        low_row = pl.multiple_of(index * (8 * group), 8 * group)
        some = pl.ds(low_row, 8 * group)
        values = pl.ds(pl.multiple_of(feats + low_row, 8), 8 * group)
        mixed[some, :] = attend_group(
            pair_buf.at[slot],
            queries[some, :],
            joined(kept[n, some, :] for n in range(blocks)),
            joined(kept[n, values, :] for n in range(blocks)),
            id_column, id_row, log_sums, index * group, score, high, low,
        )
        for copy in mix_copies(index):
            copy.start()

        @pl.when(index + 2 < groups)
        def _():
            pair_copy(index + 2, slot).start()

        return carry

    lax.fori_loop(0, groups, step, 0)
    mixed.flush()
    log_sums.flush()
    for n, peer in enumerate(peers):
        for kind in range(dps):
            ready = w_all.at[peer, kind, core]

            @pl.when(dp != kind)
            def _(ready=ready, sem=w_recv.at[peer, kind, core]):
                arrived(ready, sem)

            copies.append(send(ready, ready, wf_send.at[n, kind], w_recv.at[peer, kind, core], sibling))
    for n, peer in enumerate(peers):
        ready = k_all.at[blk, peer]
        arrived(ready, k_recv.at[blk, peer])
        copies += [
            send(ready, ready, kf_send.at[n, m], k_recv.at[blk, peer], {"blk": target})
            for m, target in enumerate([sib_blk] + far)
        ]

    small[SMALL_B_DOWN : SMALL_B_DOWN + 1, :] = column_sum(cot[mine, :])
    cots = halves(cot[...])
    downs = halves(w_down[...])
    d_act = dot_halves(cots, downs, NT)
    ups = halves(w_up[...])
    for peer in peers:
        for kind in range(dps):
            arrived(w_all.at[peer, kind, other_core], w_recv.at[peer, kind, other_core])
    outs = halves(w_all[...].reshape(zs * feats, width))
    mixed_all[z] = mixed[...]
    for peer in peers:
        for index in range(groups):
            some = pl.ds(index * (8 * group), 8 * group)
            arrived(mixed_all.at[peer, some], mix_recv.at[peer, index])
    copies += [
        send(q_part.at[peer], q_land.at[z], q_send.at[n], q_recv.at[z], {"head": peer})
        for n, peer in enumerate(peers)
    ]
    mixed_rows = mixed_all[...].reshape(zs * feats, rows).T
    hidden_rows = atoms[...] + dot_halves(halves(mixed_rows), outs) + b_out[...]
    hidden_two[...] = hidden_rows
    normal, rate = normalize(hidden_rows)
    normal_two[...] = normal
    rate_two[...] = jnp.broadcast_to(rate, rate_two.shape)
    normed = normal * gain[...] + bias[...]
    pre = dot_halves(halves(normed), ups) + b_up[...]
    phi = 0.5 * (1.0 + lax.erf(pre * math.sqrt(0.5)))
    act = pre * phi
    d_pre = d_act * (phi + pre * jnp.exp(-0.5 * pre * pre) * (1.0 / math.sqrt(2.0 * math.pi)))
    d_pres = halves(d_pre)
    part[...] = dot_halves(d_pres, ups, NT).reshape(zs, piece, width)
    copies += [
        send(part.at[peer], landed.at[z], part_send.at[n], part_recv.at[z], {"head": peer})
        for n, peer in enumerate(peers)
    ]
    landed[z] = part[z]
    ups_part[...] = dot_halves(halves(normed.T), d_pres).reshape(ups_part.shape)
    copies.append(send(ups_part.at[:, other_core], ups_sib, sib_send.at[0], sib_recv.at[0], sibling))
    downs_part[...] = dot_halves(halves(act.T), cots).reshape(downs_part.shape)
    copies.append(send(downs_part.at[:, other_core], downs_sib, sib_send.at[1], sib_recv.at[1], sibling))
    down[...] = dot_halves(halves(act), downs)
    out_mine[...] = hidden_two[mine, :] + down[mine, :] + b_down[...]
    out_mine.flush()
    small[SMALL_B_UP : SMALL_B_UP + 1, 0 : d_pre.shape[1]] = column_sum(d_pre)
    for kind, (parts, sib, go, got) in enumerate(
        [(ups_part, ups_sib, ups_go, ups_got), (downs_part, downs_sib, downs_go, downs_got)]
    ):
        arrived(sib, sib_recv.at[kind])
        go[...] = sib[...] + parts[:, core]
        copies += [
            send(
                go.at[peer], got.at[team], g_send.at[kind, n], g_recv.at[kind, team],
                team_device(peer, core, chips),
            )
            for n, peer in enumerate(far_teams)
        ]
        got[team] = go[team]
    for n, source in enumerate(far):
        for m, peer in enumerate(peers):
            ready = k_all.at[source, peer]
            arrived(ready, k_recv.at[source, peer])
            copies.append(send(ready, ready, ks_send.at[n, m], k_recv.at[source, peer], sibling))
    for peer in peers:
        arrived(q_land.at[peer], q_recv.at[peer])
    for n in range(zs):
        q_all[n] = q_land[n].T
    for n in range(blocks):
        k_all[n, z] = kept[n, 0:feats, :]
    for source in [sib_blk] + far_siblings:
        for peer in peers:
            arrived(k_all.at[source, peer], k_recv.at[source, peer])
    squares[...] = jnp.zeros(squares.shape, F32)
    at_once = 4
    rounds = heads // at_once

    def square_step(index, carry):
        there = lax.div(index, rounds)
        some = pl.ds(pl.multiple_of(lax.rem(index, rounds) * (8 * at_once), 8 * at_once), 8 * at_once)
        q_some = q_all[there, some, :]
        k_some = joined(k_all[n, there, some, :] for n in range(blocks))
        added = None
        for h in range(at_once):
            head = slice(8 * h, 8 * h + 8)
            q_high, q_low = wide_halves(q_some[head])
            k_high, k_low = wide_halves(k_some[head])
            value = dot(
                stacked([q_high, q_high, q_low, q_low]), stacked([k_high, k_low, k_high, k_low]), TN
            )
            added = value * value if added is None else added + value * value
        squares[...] += added
        return carry

    lax.fori_loop(0, zs * rounds, square_step, 0)
    same = id_column[mine, 0:1] == id_row[0:1, :]
    norms = jnp.sqrt(squares[...] + 1.0)
    terms = jnp.where(same, jnp.log1p(jnp.exp(norms - math.sqrt(zs * heads))), 0.0)
    number = jnp.where(same, 1.0, 0.0)

    def total(value):
        return jnp.sum(jnp.sum(value, axis=1, keepdims=True), axis=0, keepdims=True)

    lane = lax.broadcasted_iota(jnp.int32, (1, width), 1)
    small[SMALL_PENALTY : SMALL_PENALTY + 1, :] = jnp.where(
        lane == 0, total(terms), jnp.where(lane == 1, total(number), 0.0)
    )
    for peer in peers:
        arrived(landed.at[peer], part_recv.at[peer])
    d_normed = functools.reduce(jnp.add, [landed[n] for n in range(zs)])
    normal = normal_two[mine, :]
    d_rows = cot[mine, :] + normalize_back(d_normed, gain[...], normal, rate_two[mine, 0:1])
    d_halves = halves(d_rows)
    for n in range(zs):
        some = slice(n * feats, (n + 1) * feats)
        back[n] = dot_halves(d_halves, (outs[0][some], outs[1][some]), NT)
    copies += [
        send(back.at[peer], back_landed.at[z], back_send.at[n], back_recv.at[z], {"head": peer})
        for n, peer in enumerate(peers)
    ]
    back_landed[z] = back[z]
    d_hidden[...] = d_rows
    d_hidden.flush()
    for peer, parcel in zip(peers, parcels, strict=True):
        parcel[0:piece, :] = down[pl.ds(pl.multiple_of(peer * piece, 8), piece), :]
        parcel[piece : 2 * piece, :] = d_rows
        parcel.flush()
    small[SMALL_LN2_GAIN : SMALL_LN2_GAIN + 1, :] = column_sum(d_normed * normal)
    small[SMALL_LN2_BIAS : SMALL_LN2_BIAS + 1, :] = column_sum(d_normed)
    small[SMALL_B_OUT : SMALL_B_OUT + 1, :] = column_sum(d_rows)
    small.flush()
    for kind, got in enumerate([ups_got, downs_got]):
        for peer in far_teams:
            arrived(got.at[peer], g_recv.at[kind, peer])
    up_share, down_share = [
        functools.reduce(jnp.add, [got[n] for n in range(teams)]) for got in (ups_got, downs_got)
    ]
    for rows_of, columns_of, there in side_by_side(*up_share.shape, width):
        shares[there, columns_of] = up_share[rows_of]
    shares[there.stop :, :] = down_share
    shares.flush()
    for peer in peers:
        arrived(back_landed.at[peer], back_recv.at[peer])
    d_mixed[...] = back_landed[...].reshape(rows, feats).T
    d_mixed.flush()
    for copy in copies:
        copy.wait_send()

    def drain(index, carry):
        for copy in mix_copies(index):
            copy.wait_send()
        return carry

    lax.fori_loop(0, groups, drain, 0)


def front(zs, dps, teams, pair, *operands):
    _, heads, rows, cols = pair.shape
    feats, blocks = heads * DH, cols // rows
    width, units = operands[0].shape[1], operands[12].shape[1]
    piece, group = rows // zs, GROUP
    up_rows, down_rows = width // (2 * teams), units // (2 * teams)
    groups = heads // group
    slab = pltpu.VMEM((zs, piece, width), F32)
    narrow = pltpu.VMEM((zs, piece, feats), F32)
    one_up, one_down = pltpu.VMEM((teams, up_rows, units), F32), pltpu.VMEM((teams, down_rows, width), F32)
    dma = pltpu.SemaphoreType.DMA
    return staged_call(
        front_kernel,
        "front",
        operands,
        [
            (feats, rows), (blocks, 2 * feats + 8, rows), (rows, LANES), (heads, rows, LANES), (feats, rows),
            (STRIP, cols), (feats, rows), (piece, width), (piece, width),
            (up_rows * units // width + down_rows, width), (SMALL_ROWS, width),
        ]
        + [(2 * piece, width)] * (zs - 1),
        [
            pltpu.VMEM((2, group, rows, cols), F32),
            pltpu.VMEM((group, rows, cols), F32),
            pltpu.VMEM((group, rows, cols), BF16),
            pltpu.VMEM((group, rows, cols), BF16),
            narrow, narrow,
            pltpu.VMEM((zs, feats, piece), F32),
            pltpu.VMEM((blocks, zs, feats, rows), F32),
            pltpu.VMEM((zs, dps, 2, feats // (2 * dps), width), F32),
            pltpu.VMEM((piece, cols), F32),
            pltpu.VMEM((zs, feats, rows), F32),
            pltpu.VMEM((rows, width), F32),
            pltpu.VMEM((rows, width), F32),
            pltpu.VMEM((rows, width), F32),
            pltpu.VMEM((rows, LANES), F32),
            slab, slab, narrow, narrow,
            pltpu.VMEM((teams, 2, up_rows, units), F32),
            one_up, one_up, one_up,
            pltpu.VMEM((teams, 2, down_rows, width), F32),
            one_down, one_down, one_down,
            dma((2,)),
            dma((blocks,)), dma((blocks,)),
            dma((zs,)), dma((zs, blocks // 2)), dma((blocks // 2, zs)), dma((blocks, zs)),
            dma((zs,)), dma((zs,)),
            dma((zs,)), dma((zs, dps)), dma((zs, dps)), dma((zs, dps, 2)),
            dma((zs, groups)), dma((zs, groups)),
            dma((zs,)), dma((zs,)),
            dma((zs,)), dma((zs,)),
            dma((2,)), dma((2,)),
            dma((2, teams)), dma((2, teams)),
        ],
        FRONT_MB,
        remote=0,
        raw=(pair,),
    )


def finish_kernel(operands, results, scratch, raw):
    (
        d_heads, out_mine, d_hidden, atoms, gain, bias, w_query, mixed, small_in, w_key, w_value,
    ) = operands[:11]
    parcels = operands[11 : 10 + lax.axis_size("head")]
    chip_shares = operands[10 + lax.axis_size("head") :]
    grad_atoms, out_atoms, total_grads, grad_up, grad_down, small, penalty = results
    (
        sib_keys, sib_values, go_keys, go_values, got_keys, got_values,
        part, landed, grads, sib_grads, go_grads, got_grads, hidden_all, small_z, small_all,
        sib_send, sib_recv, kv_send, kv_recv, part_send, part_recv, back_send, back_recv,
        g_send, g_recv, t_send, t_recv, f_send, b_send, b_recv, bf_send, out_send, out_recv,
        small_z_send, small_z_recv, small_send, small_recv,
    ) = scratch
    chips, feats, rows = d_heads.shape[0] - 1, d_heads.shape[2] // 2, d_heads.shape[3]
    zs, piece, width = part.shape
    teams, _, share, _ = grads.shape
    blk, z, dp = lax.axis_index("blk"), lax.axis_index("head"), lax.axis_index("dp")
    core, chip = lax.rem(blk, 2), lax.div(blk, 2)
    other_core = 1 - core
    sibling = {"blk": blk + 1 - 2 * core}
    peers = others(z, zs)
    team = dp * chips + chip
    far_teams = others(team, teams)
    far_chips = others(chip, chips)
    place = team * 2 + core
    far_places = others(place, teams * 2)
    plane = [team_device(lax.div(value, 2), lax.rem(value, 2), chips) for value in far_places]
    meeting = [{"head": peer} for peer in peers] + plane
    greet(meeting)
    meet(meeting)
    copies = [
        send(
            d_heads.source.at[pl.ds(0, chips), other_core, pl.ds(kind * feats, feats)],
            sib, sib_send.at[kind], sib_recv.at[kind], sibling,
        )
        for kind, sib in enumerate([sib_keys, sib_values])
    ]
    mine = pl.ds(pl.multiple_of(z * piece, 8), piece)
    out_atoms[mine, :] = functools.reduce(jnp.add, [parcel[0:piece, :] for parcel in parcels], out_mine[...])
    copies += [
        send(out_atoms.at[mine], out_atoms.at[mine], out_send.at[n], out_recv.at[z], {"head": peer})
        for n, peer in enumerate(peers)
    ]

    def big_rows(result, source, kind):
        count = result.shape[0] // (2 * teams)
        return result.at[pl.ds(pl.multiple_of((source * 2 + kind) * count, 8), count)]

    partners = others(dp, lax.axis_size("dp"))
    for n in range(chips):
        source = dp * chips + lax.rem(chip + chips - n, chips)
        up_there, down_there = big_rows(grad_up, source, core), big_rows(grad_down, source, core)
        for rows_of, columns_of, there in side_by_side(*up_there.shape, width):
            up_there[rows_of, :] = chip_shares[n][there, columns_of]
        down_there[...] = chip_shares[n][there.stop :, :]
        for kind, ready in enumerate([up_there, down_there]):
            copies += [
                send(ready, ready, b_send.at[kind, n, m], b_recv.at[kind, source, core], {"dp": partner})
                for m, partner in enumerate(partners)
            ]
    own_heads = d_heads.ref
    d_queries = own_heads[chips, 0, 0:feats, :]
    for kind, (sib, go, got) in enumerate([(sib_keys, go_keys, got_keys), (sib_values, go_values, got_values)]):
        arrived(sib, sib_recv.at[kind])
        go[...] = sib[...] + own_heads[0:chips, core, kind * feats : (kind + 1) * feats, :]
        copies += [
            send(
                go.at[peer], got.at[chip], kv_send.at[kind, n], kv_recv.at[kind, chip],
                {"blk": peer * 2 + core},
            )
            for n, peer in enumerate(far_chips)
        ]
    got_keys[chip] = go_keys[chip]
    got_values[chip] = go_values[chip]
    normal, rate = normalize(atoms[...])
    normed = halves(normal * gain[...] + bias[...])
    dq_rows = d_queries.T
    d_normed = dot_full(dq_rows, w_query[...], NT)
    grad_q = dot_halves(halves(d_queries), normed)
    small_z[z] = small_in[0:8, :]
    hidden_all[z] = d_hidden[...]
    for n, parcel in enumerate(parcels):
        hidden_all[lax.rem(z + zs - 1 - n, zs)] = parcel[piece : 2 * piece, :]
    grad_o = dot_full(mixed[...], hidden_all[...].reshape(rows, width))
    for peer in far_chips:
        arrived(got_keys.at[peer], kv_recv.at[0, peer])
        arrived(got_values.at[peer], kv_recv.at[1, peer])
    dk = functools.reduce(jnp.add, [got_keys[n] for n in range(chips)])
    dv = functools.reduce(jnp.add, [got_values[n] for n in range(chips)])
    dv_rows = dv.T
    d_normed = (
        d_normed + dot_full(dk.T, w_key[...], NT) + dot_full(dv_rows, w_value[...], NT)
    )
    part[...] = d_normed.reshape(zs, piece, width)
    copies += [
        send(part.at[peer], landed.at[z], part_send.at[n], part_recv.at[z], {"head": peer})
        for n, peer in enumerate(peers)
    ]
    landed[z] = part[z]
    grad_k = dot_halves(halves(dk), normed)
    grad_v = dot_halves(halves(dv), normed)
    grads[...] = jnp.concatenate([grad_q, grad_k, grad_v, grad_o], axis=0).reshape(grads.shape)
    copies.append(send(grads.at[:, other_core], sib_grads, sib_send.at[2], sib_recv.at[2], sibling))
    arrived(sib_grads, sib_recv.at[2])
    go_grads[...] = sib_grads[...] + grads[:, core]
    copies += [
        send(
            go_grads.at[peer], got_grads.at[team], g_send.at[n], g_recv.at[team], team_device(peer, core, chips)
        )
        for n, peer in enumerate(far_teams)
    ]
    got_grads[team] = go_grads[team]
    for peer in peers:
        arrived(landed.at[peer], part_recv.at[peer])
    d_normed = functools.reduce(jnp.add, [landed[n] for n in range(zs)])
    normal, rate = normalize(atoms[mine, :])
    grad_atoms[mine, :] = d_hidden[...] + normalize_back(d_normed, gain[...], normal, rate)
    small_z[z, SMALL_LN1_GAIN : SMALL_LN1_GAIN + 1, :] = column_sum(d_normed * normal)
    small_z[z, SMALL_LN1_BIAS : SMALL_LN1_BIAS + 1, :] = column_sum(d_normed)
    copies += [
        send(small_z.at[z], small_z.at[z], small_z_send.at[n], small_z_recv.at[z], {"head": peer})
        for n, peer in enumerate(peers)
    ]
    copies += [
        send(grad_atoms.at[mine], grad_atoms.at[mine], back_send.at[n], back_recv.at[z], {"head": peer})
        for n, peer in enumerate(peers)
    ]
    for peer in far_teams:
        arrived(got_grads.at[peer], g_recv.at[peer])
    total_grads[team, core] = functools.reduce(jnp.add, [got_grads[n] for n in range(teams)])
    ready = total_grads.at[team, core]
    copies.append(send(ready, ready, t_send.at[0], t_recv.at[team, core], sibling))
    copies += [
        send(ready, ready, t_send.at[n + 1], t_recv.at[team, core], team_device(peer, core, chips))
        for n, peer in enumerate(far_teams)
    ]
    for peer in peers:
        arrived(small_z.at[peer], small_z_recv.at[peer])
    small_all[place, 0:8, :] = functools.reduce(jnp.add, [small_z[n] for n in range(zs)])
    small_all[place, 8:16, :] = small_in[8:16, :]
    small_all[place, SMALL_B_QUERY : SMALL_B_QUERY + 1, 0:feats] = column_sum(dq_rows)
    small_all[place, SMALL_B_VALUE : SMALL_B_VALUE + 1, 0:feats] = column_sum(dv_rows)
    copies += [
        send(small_all.at[place], small_all.at[place], small_send.at[n], small_recv.at[place], target)
        for n, target in enumerate(plane)
    ]
    for n, peer in enumerate(far_teams):
        ready = total_grads.at[peer, core]
        arrived(ready, t_recv.at[peer, core])
        copies.append(send(ready, ready, f_send.at[n], t_recv.at[peer, core], sibling))
    for kind, result in enumerate([grad_up, grad_down]):
        for n in range(teams):
            ready = big_rows(result, n, core)

            @pl.when(lax.div(n, chips) != dp)
            def _(ready=ready, sem=b_recv.at[kind, n, core]):
                arrived(ready, sem)

            copies.append(send(ready, ready, bf_send.at[kind, n], b_recv.at[kind, n, core], sibling))
    for source in far_places:
        arrived(small_all.at[source], small_recv.at[source])
    summed = functools.reduce(jnp.add, [small_all[n] for n in range(2 * teams)])
    small[...] = summed
    ends = summed[SMALL_PENALTY : SMALL_PENALTY + 1, :]
    penalty[...] = ends[:, 0:1] / ends[:, 1:2]
    for peer in [team] + far_teams:
        arrived(total_grads.at[peer, other_core], t_recv.at[peer, other_core])
    total_grads.flush()
    for kind, result in enumerate([grad_up, grad_down]):
        for n in range(teams):
            arrived(big_rows(result, n, other_core), b_recv.at[kind, n, other_core])
        result.flush()
    for peer in peers:
        there = pl.ds(pl.multiple_of(peer * piece, 8), piece)
        arrived(out_atoms.at[there], out_recv.at[peer])
    out_atoms.flush()
    for peer in peers:
        there = pl.ds(pl.multiple_of(peer * piece, 8), piece)
        arrived(grad_atoms.at[there], back_recv.at[peer])
    for copy in copies:
        copy.wait_send()


def finish(zs, dps, units, *operands):
    d_heads, atoms = operands[0], operands[3]
    chips, feats, rows = d_heads.shape[0] - 1, d_heads.shape[2] // 2, d_heads.shape[3]
    width = atoms.shape[1]
    piece = rows // zs
    teams = dps * chips
    share = 4 * feats // (2 * teams)
    some = pltpu.VMEM((chips, feats, rows), F32)
    slab = pltpu.VMEM((zs, piece, width), F32)
    one = pltpu.VMEM((teams, share, width), F32)
    dma = pltpu.SemaphoreType.DMA
    return staged_call(
        finish_kernel,
        "finish",
        operands,
        [
            (rows, width),
            (rows, width),
            (teams, 2, share, width),
            (width, units),
            (units, width),
            (SMALL_ROWS, width),
            (1, 1),
        ],
        [some] * 6
        + [slab, slab, pltpu.VMEM((teams, 2, share, width), F32), one, one, one, slab]
        + [
            pltpu.VMEM((zs, 8, width), F32),
            pltpu.VMEM((2 * teams, SMALL_ROWS, width), F32),
            dma((3,)), dma((3,)),
            dma((2, chips)), dma((2, chips)),
            dma((zs,)), dma((zs,)),
            dma((zs,)), dma((zs,)),
            dma((teams,)), dma((teams,)),
            dma((teams,)), dma((teams, 2)), dma((teams,)),
            dma((2, chips, dps)), dma((2, teams, 2)), dma((2, teams)),
            dma((zs,)), dma((zs,)),
            dma((zs,)), dma((zs,)),
            dma((2 * teams,)), dma((2 * teams,)),
        ],
        FINISH_MB,
        remote=2,
        near_in=[0] + list(range(11, len(operands))),
        near_out=range(7),
    )


def place_kernel(operands, results, scratch, raw):
    total_grads, small, penalty_in = operands
    penalty, grad_query, grad_key, grad_value, grad_out = results[:5]
    penalty[...] = penalty_in[...]
    feats, width = grad_out.shape
    done = total_grads[...].reshape(4 * feats, width)
    grad_query[...] = done[0:feats].T
    grad_query.flush()
    grad_key[...] = done[feats : 2 * feats].T
    grad_key.flush()
    grad_value[...] = done[2 * feats : 3 * feats].T
    grad_value.flush()
    grad_out[...] = done[3 * feats :]
    grad_out.flush()
    for result, row in zip(results[5:], SMALL_OUTPUTS, strict=True):
        result[...] = small[row : row + 1, 0 : result.shape[1]]


SMALL_OUTPUTS = (
    SMALL_LN1_GAIN, SMALL_LN1_BIAS, SMALL_B_QUERY, SMALL_B_VALUE, SMALL_B_OUT, SMALL_LN2_GAIN, SMALL_LN2_BIAS,
    SMALL_B_UP, SMALL_B_DOWN,
)


def place(feats, units, straight, *operands):
    width = operands[1].shape[1]
    lengths = {SMALL_B_QUERY: feats, SMALL_B_VALUE: feats, SMALL_B_UP: units}
    return staged_call(
        place_kernel,
        "place",
        operands,
        [(1, 1)]
        + [(width, feats)] * 3
        + [(feats, width)]
        + [(1, lengths.get(row, width)) for row in SMALL_OUTPUTS],
        [],
        PLACE_MB,
        straight=straight,
        near_in=(0, 1, 2),
        near_straight=True,
    )


def local(
    zs, dps,
    atoms, pair, mol_ids, ln1_gain, ln1_bias, w_query, b_query, w_key, w_value, b_value, w_out, b_out,
    ln2_gain, ln2_bias, w_up, b_up, w_down, b_down, cot_atoms, cot_pair,
):
    blocks = pair.shape[3] // pair.shape[2]
    inputs, cot = atoms[0], cot_atoms[0]

    def line(value):
        return value.reshape(1, -1)

    (
        queries, kept, id_column, log_sums, mixed, id_row, d_mixed, out_mine, d_hidden, shares, small, *parcels,
    ) = front(
        zs, dps, dps * blocks // 2, pair,
        inputs, mol_ids, line(ln1_gain), line(ln1_bias), w_key, w_value, line(b_value), w_query, line(b_query),
        w_out, cot, w_down, w_up, line(b_out), line(ln2_gain), line(ln2_bias), line(b_up),
        line(b_down),
    )
    parcels = [
        lax.ppermute(parcel, "head", [(source, (source + n + 1) % zs) for source in range(zs)])
        for n, parcel in enumerate(parcels)
    ]
    chips = blocks // 2
    chip_shares = [shares] + [
        lax.ppermute(shares, "blk", [(2 * c + core, 2 * ((c + n) % chips) + core) for c in range(chips) for core in range(2)])
        for n in range(1, chips)
    ]
    out_pair, grad_pair, d_heads = attend_back(
        pair, cot_pair, queries, kept, mixed, d_mixed, log_sums, id_column, id_row
    )
    grad_atoms, out_atoms, total_grads, grad_up, grad_down, small, penalty = finish(
        zs, dps, w_up.shape[1],
        d_heads, out_mine, d_hidden, inputs, line(ln1_gain), line(ln1_bias), w_query, mixed,
        small, w_key, w_value, *parcels, *chip_shares,
    )
    placed = place(
        w_query.shape[1], w_up.shape[1],
        [grad_atoms, out_atoms, grad_up, grad_down],
        total_grads, small, penalty,
    )
    grad_atoms, out_atoms, grad_up, grad_down, penalty, grad_query, grad_key, grad_value, grad_out = placed[:9]
    (
        grad_ln1_gain, grad_ln1_bias, grad_b_query, grad_b_value, grad_b_out, grad_ln2_gain, grad_ln2_bias,
        grad_b_up, grad_b_down,
    ) = [value.reshape(-1) for value in placed[9:]]
    return (
        out_atoms[None],
        out_pair,
        penalty[0, 0],
        grad_atoms[None],
        grad_pair,
        grad_ln1_gain,
        grad_ln1_bias,
        grad_query,
        grad_b_query,
        grad_key,
        grad_value,
        grad_b_value,
        grad_out,
        grad_b_out,
        grad_ln2_gain,
        grad_ln2_bias,
        grad_up,
        grad_b_up,
        grad_down,
        grad_b_down,
    )


def solution(mesh):
    rows, pairs = P("dp", "blk", None), P("dp", "head", "blk", None)
    columns = P(None, "head")
    return jax.shard_map(
        functools.partial(local, mesh.shape["head"], mesh.shape["dp"]),
        mesh=mesh,
        in_specs=(
            rows, pairs, P("dp", "blk"), P(), P(), columns, P("head"), columns, columns, P("head"),
            P("head", None), P(), P(), P(), columns, P("head"), P("head", None), P(), rows, pairs,
        ),
        out_specs=(
            rows, pairs, P(), rows, pairs, P(), P(), columns, P("head"), columns, columns, P("head"),
            P("head", None), P(), P(), P(), columns, P("head"), P("head", None), P(),
        ),
        check_vma=False,
    )
```

```python
import functools
import math

import jax
import jax.numpy as jnp
from jax import lax
from jax.experimental import pallas as pl
from jax.experimental.pallas import tpu as pltpu
from jax.sharding import PartitionSpec as P

DH = 8
LANES = 128
STRIP = 16
CHUNK = 256
GROUP = 2
FRONT_MB, BACK_MB, FINISH_MB, PLACE_MB = 58, 60, 40, 32
NORM_EPS = 1e-05
MASK_FILL = -1e30
F32 = jnp.float32
BF16 = jnp.bfloat16
MESH = pl.DeviceIdType.MESH
NN = (((1,), (0,)), ((), ()))
NT = (((1,), (1,)), ((), ()))
TN = (((0,), (0,)), ((), ()))
VMEM = pl.BlockSpec(memory_space=pltpu.VMEM)


def dot(left, right, dims=NN):
    return lax.dot_general(left, right, dims, preferred_element_type=F32)


def halves(value):
    high = value.astype(BF16)
    return high, (value - high.astype(F32)).astype(BF16)


def dot_halves(left, right, dims=NN):
    return dot(left[0], right[0], dims) + (
        dot(left[0], right[1], dims) + dot(left[1], right[0], dims)
    )


def dot_full(left, right, dims=NN):
    return dot_halves(halves(left), halves(right), dims)


def normalize(inputs):
    centred = inputs - jnp.mean(inputs, -1, keepdims=True)
    rate = lax.rsqrt(jnp.mean(centred * centred, -1, keepdims=True) + NORM_EPS)
    return centred * rate, rate


def normalize_back(grad, gain, normal, rate):
    scaled = grad * gain
    return rate * (
        scaled
        - jnp.mean(scaled, -1, keepdims=True)
        - normal * jnp.mean(scaled * normal, -1, keepdims=True)
    )


def column_sum(value):
    return jnp.sum(value, 0, keepdims=True)


def send(src, dst, send_sem, recv_sem, target):
    copy = pltpu.make_async_remote_copy(
        src_ref=src,
        dst_ref=dst,
        send_sem=send_sem,
        recv_sem=recv_sem,
        device_id=target,
        device_id_type=MESH,
    )
    copy.start()
    return copy


def arrived(ref, sem):
    pltpu.make_async_remote_copy(
        src_ref=ref, dst_ref=ref, send_sem=sem, recv_sem=sem, device_id={}, device_id_type=MESH
    ).wait_recv()


def greet(targets):
    for target in targets:
        pl.semaphore_signal(pltpu.get_barrier_semaphore(), inc=1, device_id=target, device_id_type=MESH)


def meet(targets):
    pl.semaphore_wait(pltpu.get_barrier_semaphore(), len(targets))


def others(index, count):
    return [lax.rem(index + step, count) for step in range(1, count)]


class Operand:
    def __init__(self, source, slot, sem):
        self.source, self.slot, self.shape = source, slot, slot.shape
        self.copy = None if sem is None else pltpu.make_async_copy(source, slot, sem)
        if self.copy is not None:
            self.copy.start()

    @property
    def ref(self):
        if self.copy is not None:
            self.copy.wait()
            self.copy = None
        return self.slot

    def __getitem__(self, index):
        return self.ref[index]


class Result:
    def __init__(self, target, slot, sem):
        self.slot, self.shape, self.at = slot, slot.shape, slot.at
        self.copy = None if sem is None else pltpu.make_async_copy(slot, target, sem)
        self.begun = self.copy is None

    def __setitem__(self, index, value):
        self.slot[index] = value

    def __getitem__(self, index):
        return self.slot[index]

    def flush(self):
        if not self.begun:
            self.copy.start()
            self.begun = True


def staged_call(
    kernel, name, operands, results, scratch, megabytes,
    remote=None, raw=(), straight=(), raw_results=(), cost=None, near_in=(), near_out=(), near_straight=False,
):
    n_in, n_out, n_raw, n_straight = len(operands), len(results), len(raw), len(straight)
    n_left = len(raw_results)
    far_in = [n for n in range(n_in) if n not in near_in]
    far_out = [n for n in range(n_out) if n not in near_out]

    def body(*refs):
        sources, left, refs = refs[:n_in], refs[n_in : n_in + n_raw], refs[n_in + n_raw :]
        moved, refs = refs[:n_straight], refs[n_straight:]
        arrays, refs = refs[:n_straight], refs[n_straight:]
        left, refs = left + refs[:n_left], refs[n_left:]
        targets, refs = refs[:n_out], refs[n_out:]
        in_slots, refs = dict(zip(far_in, refs)), refs[len(far_in) :]
        out_slots, refs = dict(zip(far_out, refs)), refs[len(far_out) :]
        in_sem, out_sem, move_sem, refs = refs[0], refs[1], refs[2], refs[3:]
        through, loads = moved, []
        if not near_straight:
            through, refs = refs[:n_straight], refs[n_straight:]
            loads = [pltpu.make_async_copy(moved[n], through[n], move_sem.at[n]) for n in range(n_straight)]
        moves = [pltpu.make_async_copy(through[n], arrays[n], move_sem.at[n]) for n in range(n_straight)]
        for load in loads:
            load.start()
        ins = [
            Operand(sources[n], in_slots.get(n, sources[n]), in_sem.at[far_in.index(n)] if n in in_slots else None)
            for n in range(n_in)
        ]
        outs = [
            Result(targets[n], out_slots.get(n, targets[n]), out_sem.at[far_out.index(n)] if n in out_slots else None)
            for n in range(n_out)
        ]
        for load in loads:
            load.wait()
        for move in moves:
            move.start()
        kernel(ins, outs, refs, left)
        for operand in ins:
            operand.ref
        for result in outs:
            result.flush()
        for copy in moves + [result.copy for result in outs if result.copy is not None]:
            copy.wait()

    hbm, vmem = pl.BlockSpec(memory_space=pltpu.HBM), pl.BlockSpec(memory_space=pltpu.VMEM)
    extra = {} if remote is None else {"collective_id": remote, "has_side_effects": True}
    return pl.pallas_call(
        body,
        out_shape=[jax.ShapeDtypeStruct(value.shape, value.dtype) for value in straight]
        + [jax.ShapeDtypeStruct(shape, F32) for shape in raw_results]
        + [jax.ShapeDtypeStruct(shape, F32) for shape in results],
        in_specs=[vmem if n in near_in else hbm for n in range(n_in)]
        + [hbm] * n_raw
        + [vmem if near_straight else hbm] * n_straight,
        out_specs=[hbm] * (n_straight + n_left) + [vmem if n in near_out else hbm for n in range(n_out)],
        scratch_shapes=[pltpu.VMEM(operands[n].shape, operands[n].dtype) for n in far_in]
        + [pltpu.VMEM(results[n], F32) for n in far_out]
        + [pltpu.SemaphoreType.DMA((max(1, n),)) for n in (len(far_in), len(far_out), n_straight)]
        + ([] if near_straight else [pltpu.VMEM(value.shape, value.dtype) for value in straight])
        + list(scratch),
        compiler_params=pltpu.CompilerParams(vmem_limit_bytes=megabytes << 20, **extra),
        cost_estimate=cost,
        name=name,
    )(*operands, *raw, *straight)


def joined(pieces):
    return jnp.concatenate(list(pieces), axis=1)


def stacked(parts):
    return jnp.concatenate(parts, axis=0).astype(BF16)


def wide_halves(value):
    high = value.astype(BF16).astype(F32)
    return high, value - high


def attend_group(pair, queries, keys, values, id_column, id_row, log_sums, first, score, high, low):
    group, rows, cols = score.shape
    strips = rows // STRIP
    chunk = min(CHUNK, cols)
    mixed = []
    for g in range(group):
        head = slice(8 * g, 8 * g + 8)
        q_high, q_low = wide_halves(queries[head, :])
        k_high, k_low = wide_halves(keys[head, :])
        v_high, v_low = wide_halves(values[head, :])
        ones = jnp.ones_like(v_high)
        q_pack = stacked([q_high, q_high, q_low, q_low])
        k_pack = stacked([k_high, k_low, k_high, k_low])
        v_pack = stacked([v_high, v_low, ones, jnp.zeros_like(ones)])
        tops = [None] * strips
        for start in range(0, cols, chunk):
            part = slice(start, start + chunk)
            score[g, :, part] = dot(q_pack, k_pack[:, part], TN)
            for s in range(strips):
                line = pl.ds(s * STRIP, STRIP)
                own = id_column[line, :]
                for j in range(start, start + chunk, LANES):
                    tile = pl.ds(j, LANES)
                    value = pair[g, line, tile] + score[g, line, tile]
                    value = jnp.where(own == id_row[:, tile], value, MASK_FILL)
                    score[g, line, tile] = value
                    tops[s] = value if tops[s] is None else jnp.maximum(tops[s], value)
        tops = [
            jnp.broadcast_to(jnp.max(top, axis=1, keepdims=True), (STRIP, LANES)) for top in tops
        ]
        totals = [None] * strips
        gathered = None
        for start in range(0, cols, chunk):
            part = slice(start, start + chunk)
            for s in range(strips):
                line = pl.ds(s * STRIP, STRIP)
                for j in range(start, start + chunk, LANES):
                    tile = pl.ds(j, LANES)
                    weight = jnp.exp(score[g, line, tile] - tops[s])
                    high[g, line, tile], low[g, line, tile] = halves(weight)
                    totals[s] = weight if totals[s] is None else totals[s] + weight
            term = dot(v_pack[:, part], high[g, :, part], NT) + dot(
                v_pack[:, part], low[g, :, part], NT
            )
            gathered = term if gathered is None else gathered + term
        for s in range(strips):
            total = jnp.sum(totals[s], axis=1, keepdims=True)
            log_sums[first + g, pl.ds(s * STRIP, STRIP), :] = tops[s] + jnp.log(total)
        mixed.append((gathered[0:8] + gathered[8:16]) / gathered[16:17])
    return jnp.concatenate(mixed, axis=0)


def chunks_of(cols):
    chunk = min(CHUNK, cols)
    return [slice(start, start + chunk) for start in range(0, cols, chunk)]


def score_packs(queries, keys):
    q_high, q_low = wide_halves(queries)
    k_high, k_low = wide_halves(keys)
    return stacked([q_high, q_high, q_low, q_low]), stacked([k_high, k_low, k_high, k_low])


def attend_back_kernel(operands, results, scratch, raw):
    queries, kept, d_mixed, mixed, id_column, id_row = operands
    (d_heads,) = results
    pair, cot, log_sums, out_pair, grad_pair = raw
    pair_buf, cot_buf, log_buf, out_buf, grad_buf = scratch[:5]
    here = scratch[5:11]
    in_sem, out_sem = scratch[11:]
    heads = pair.shape[1]
    feats = heads * DH
    depth, rows, cols = pair_buf.shape
    blocks = kept.shape[0]
    parts = chunks_of(cols)
    place = lax.broadcasted_iota(jnp.int32, (8, rows), 0)

    def inward(index):
        slot = lax.rem(index, depth)
        sources = (pair.at[0, index], cot.at[0, index], log_sums.at[index])
        return [
            pltpu.make_async_copy(source, buf.at[slot], in_sem.at[n, slot])
            for n, (source, buf) in enumerate(zip(sources, (pair_buf, cot_buf, log_buf), strict=True))
        ]

    def outward(index):
        slot = lax.rem(index, depth)
        return [
            pltpu.make_async_copy(buf.at[slot], array.at[0, index], out_sem.at[n, slot])
            for n, (array, buf) in enumerate([(out_pair, out_buf), (grad_pair, grad_buf)])
        ]

    for n in range(2):
        for copy in inward(n):
            copy.start()
    for operand in operands:
        operand.ref

    def rows_of(index):
        return pl.ds(pl.multiple_of(index * 8, 8), 8)

    def key_rows(index):
        return joined(kept[n, rows_of(index), :] for n in range(blocks))

    def value_row(index):
        return pl.ds(pl.multiple_of(feats + index * 8, 8), 8)

    def value_rows(index):
        return joined(kept[n, value_row(index), :] for n in range(blocks))

    def packs(index):
        head = rows_of(index)
        q_pack, k_pack = score_packs(queries[head, :], key_rows(index))
        v_high, v_low = wide_halves(value_rows(index))
        m_high, m_low = wide_halves(d_mixed[head, :])
        delta_high, rest = wide_halves(-column_sum(mixed[head, :] * d_mixed[head, :]))
        delta_mid, delta_low = wide_halves(rest)
        deltas = jnp.where(
            place == 0, delta_high, jnp.where(place == 1, delta_mid, jnp.where(place == 2, delta_low, 0.0))
        )
        m_pack = stacked([m_high, m_high, m_low, deltas])
        v_pack = stacked([v_high, v_low, v_high, jnp.ones_like(v_high)])
        return q_pack, k_pack, m_pack, v_pack

    def pairs(index):
        head = rows_of(index)
        return [stacked(wide_halves(value)) for value in (queries[head, :], key_rows(index), d_mixed[head, :])]

    def before(pack, part, there):
        q_pack, k_pack, m_pack, v_pack = pack
        there[0][:, part] = dot(q_pack, k_pack[:, part], TN)
        there[1][:, part] = dot(m_pack, v_pack[:, part], TN)

    def middle(index, slot, part, here):
        score, d_prob, p_high, p_low, g_high, g_low = here
        for s in range(rows // STRIP):
            line = pl.ds(s * STRIP, STRIP)
            own = id_column[line, :]
            log_sum = log_buf[slot, line, :]
            for j in range(part.start, part.stop, LANES):
                tile = pl.ds(j, LANES)
                value = pair_buf[slot, line, tile] + score[line, tile]
                out_buf[slot, line, tile] = value
                prob = jnp.exp(jnp.where(own == id_row[:, tile], value - log_sum, MASK_FILL))
                p_high[line, tile], p_low[line, tile] = halves(prob)
                grad = prob * d_prob[line, tile] + cot_buf[slot, line, tile]
                grad_buf[slot, line, tile] = grad
                g_high[line, tile], g_low[line, tile] = halves(grad)

    def both(left, high, low, dims):
        value = dot(left, high, dims) + dot(left, low, dims)
        return value[0:8] + value[8:16]

    def after(index, pair_of, part, there):
        q_pair, k_pair, m_pair = pair_of
        _, _, p_high, p_low, g_high, g_low = there
        head = rows_of(index)
        d_value = both(m_pair, p_high[:, part], p_low[:, part], NN)
        d_key = both(q_pair, g_high[:, part], g_low[:, part], NN)
        for n in range(part.start // rows, part.stop // rows):
            span = slice(n * rows - part.start, (n + 1) * rows - part.start)
            d_heads[n // 2, n % 2, head, :] = d_key[:, span]
            d_heads[n // 2, n % 2, value_row(index), :] = d_value[:, span]
        return both(k_pair[:, part], g_high[:, part], g_low[:, part], NT)

    def stage(index, carry):
        slot = lax.rem(index, depth)
        for copy in inward(index):
            copy.wait()

        @pl.when(index >= depth)
        def _():
            for copy in outward(index - depth):
                copy.wait()

        @pl.when(index == 0)
        def _():
            for n in range(2, depth - 1):
                for copy in inward(n):
                    copy.start()

        @pl.when(index + depth - 1 < heads)
        def _():
            for copy in inward(index + depth - 1):
                copy.start()

        next_packs, own_pairs = packs(index), pairs(index)
        d_query = None
        before(next_packs, parts[0], here)
        for n, part in enumerate(parts):
            if n + 1 < len(parts):
                before(next_packs, parts[n + 1], here)
            middle(index, slot, part, here)
            if n >= 1:
                term = after(index, own_pairs, parts[n - 1], here)
                d_query = term if d_query is None else d_query + term
        term = after(index, own_pairs, parts[-1], here)
        d_query = term if d_query is None else d_query + term
        d_heads[blocks // 2, 0, rows_of(index), :] = d_query * (DH ** (-0.5))
        for copy in outward(index):
            copy.start()
        return carry

    lax.fori_loop(0, heads, stage, 0)
    for result in results:
        result.flush()
    for n in range(max(0, heads - depth), heads):
        for copy in outward(n):
            copy.wait()


def attend_back(pair, cot, queries, kept, mixed, d_mixed, log_sums, id_column, id_row):
    _, heads, rows, cols = pair.shape
    feats = heads * DH
    blocks = kept.shape[0]
    depth = 4
    wide, thin = pltpu.VMEM((rows, cols), F32), pltpu.VMEM((rows, cols), BF16)
    return staged_call(
        attend_back_kernel,
        "attend_back",
        [queries, kept, d_mixed, mixed, id_column, id_row],
        [(blocks // 2 + 1, 2, 2 * feats, rows)],
        [pltpu.VMEM((depth, rows, cols), F32)] * 2
        + [pltpu.VMEM((depth, rows, LANES), F32)]
        + [pltpu.VMEM((depth, rows, cols), F32)] * 2
        + [wide] * 2
        + [thin] * 4
        + [pltpu.SemaphoreType.DMA((3, depth)), pltpu.SemaphoreType.DMA((2, depth))],
        BACK_MB,
        raw=(pair, cot, log_sums),
        raw_results=(pair.shape, pair.shape),
        cost=pl.CostEstimate(
            flops=2 * 400 * heads * rows * cols,
            bytes_accessed=16 * heads * rows * cols,
            transcendentals=heads * rows * cols,
        ),
    )


SMALL_LN1_GAIN, SMALL_LN1_BIAS, SMALL_LN2_GAIN, SMALL_LN2_BIAS = 0, 1, 2, 3
SMALL_B_OUT, SMALL_B_DOWN, SMALL_PENALTY = 4, 5, 6
SMALL_B_QUERY, SMALL_B_VALUE, SMALL_B_UP = 8, 9, 10
SMALL_ROWS = 16


def side_by_side(count, units, width):
    beside = width // units
    height = count // beside
    return [
        (slice(n * height, (n + 1) * height), slice(n * units, (n + 1) * units), slice(0, height))
        for n in range(beside)
    ]


def team_device(team, core, chips):
    return {"dp": lax.div(team, chips), "blk": lax.rem(team, chips) * 2 + core}


def front_kernel(operands, results, scratch, raw):
    (
        atoms, ids, gain_one, bias_one, w_key, w_value, b_value, w_query, b_query, w_out, cot, w_down, w_up, b_out,
        gain, bias, b_up, b_down,
    ) = operands
    (pair,) = raw
    (
        queries, kept, id_column, log_sums, mixed, id_row, d_mixed, out_mine, d_hidden, shares, small,
    ) = results[:11]
    parcels = results[11:]
    (
        pair_buf, score, high, low, q_part, q_land, q_all, k_all, w_all, squares, mixed_all, hidden_two, down, normal_two, rate_two,
        part, landed, back, back_landed, ups_part, ups_sib, ups_go, ups_got, downs_part, downs_sib, downs_go, downs_got,
        pair_sem, kept_send, kept_recv, kz_send, kf_send, ks_send, k_recv, q_send, q_recv, w_send, w_recv, wx_send, wx_recv, wf_send, wf_recv,
        mix_send, mix_recv, part_send, part_recv, back_send, back_recv, sib_send, sib_recv, g_send, g_recv,
    ) = scratch
    zs, feats, rows = mixed_all.shape
    blocks = kept.shape[0]
    chips = blocks // 2
    teams, width = ups_part.shape[0], atoms.shape[1]
    _, group, _, cols = pair_buf.shape
    heads = feats // DH
    groups = heads // group
    piece = rows // zs
    z, blk = lax.axis_index("head"), lax.axis_index("blk")
    core, chip = lax.rem(blk, 2), lax.div(blk, 2)
    dp, dps = lax.axis_index("dp"), lax.axis_size("dp")
    team = dp * chips + chip
    other_core = 1 - core
    sib_blk = blk + 1 - 2 * core
    sibling = {"blk": sib_blk}
    peers, far_teams = others(z, zs), others(team, teams)
    sources = [lax.rem(z + zs - n, zs) for n in range(1, zs)]
    far = [step * 2 + core for step in others(chip, chips)]
    far_siblings = [step * 2 + other_core for step in others(chip, chips)]
    mine = pl.ds(pl.multiple_of(z * piece, 8), piece)

    def pair_copy(index, slot):
        return pltpu.make_async_copy(
            pair.at[0, pl.ds(index * group, group)], pair_buf.at[slot], pair_sem.at[slot]
        )

    meeting = [{"head": peer} for peer in peers] + [sibling]
    meeting += [team_device(peer, core, chips) for peer in far_teams]
    greet(meeting)
    for n in range(2):
        pair_copy(n, n).start()

    normal, _ = normalize(atoms[...])
    normed = halves(normal * gain_one[...] + bias_one[...])
    meet(meeting)
    copies = []
    squads, _, _, fewer, _ = w_all.shape
    close = squads // dps
    base = chip - lax.rem(chip, close)
    squad = dp * close + chip - base
    w_mine = w_out.source.at[pl.ds(pl.multiple_of((squad * 2 + core) * fewer, 8), fewer)]
    copies += [
        send(w_mine, w_all.at[squad, core, z], w_send.at[n], w_recv.at[n], {"head": peer})
        for n, peer in enumerate(peers)
    ]
    kept[blk, 0:feats, :] = dot_halves(normed, halves(w_key[...])).T
    copies += [
        send(kept.at[blk, 0:feats], k_all.at[blk, z], kz_send.at[n], k_recv.at[blk, z], {"head": peer})
        for n, peer in enumerate(peers)
    ]
    kept[blk, feats : 2 * feats, :] = (dot_halves(normed, halves(w_value[...])) + b_value[...]).T
    id_line = ids[...].astype(F32)
    kept[blk, 2 * feats : 2 * feats + 8, :] = jnp.broadcast_to(id_line, (8, rows))
    copies += [
        send(kept.at[blk], kept.at[blk], kept_send.at[n], kept_recv.at[blk], {"blk": peer})
        for n, peer in enumerate([sib_blk] + far)
    ]
    q_rows = (dot_halves(normed, halves(w_query[...])) + b_query[...]) * (DH ** (-0.5))
    q_part[...] = q_rows.reshape(zs, piece, feats)
    queries[...] = q_rows.T
    queries.flush()
    q_land[z] = q_part[z]
    w_all[squad, core, z] = w_out[pl.ds(pl.multiple_of((squad * 2 + core) * fewer, 8), fewer), :]
    id_column[...] = jnp.broadcast_to(id_line, (LANES, rows)).T
    id_column.flush()
    small[...] = jnp.zeros(small.shape, F32)
    for n, source in enumerate(far):
        arrived(kept.at[source], kept_recv.at[source])
        copies.append(
            send(kept.at[source], kept.at[source], kept_send.at[chips + n], kept_recv.at[source], sibling)
        )
    for source in [sib_blk] + far_siblings:
        arrived(kept.at[source], kept_recv.at[source])
    kept.flush()
    one = joined(kept[n, 2 * feats : 2 * feats + 8, :] for n in range(blocks))
    id_row[...] = jnp.concatenate([one, one], axis=0)
    id_row.flush()

    def mix_copies(index):
        some = pl.ds(pl.multiple_of(index * (8 * group), 8 * group), 8 * group)
        return [
            pltpu.make_async_remote_copy(
                src_ref=mixed.at[some],
                dst_ref=mixed_all.at[z, some],
                send_sem=mix_send.at[n, index],
                recv_sem=mix_recv.at[n, index],
                device_id={"head": peer},
                device_id_type=MESH,
            )
            for n, peer in enumerate(peers)
        ]

    squad_copies = [
        pltpu.make_async_remote_copy(
            src_ref=w_all.at[squad, core],
            dst_ref=w_all.at[squad, core],
            send_sem=wx_send.at[n - 1],
            recv_sem=wx_recv.at[n - 1],
            device_id={
                "dp": lax.div(lax.rem(squad + n, squads), close),
                "blk": (base + lax.rem(lax.rem(squad + n, squads), close)) * 2 + core,
            },
            device_id_type=MESH,
        )
        for n in range(1, squads)
    ]

    key_copies = [
        pltpu.make_async_remote_copy(
            src_ref=k_all.at[blk, peer],
            dst_ref=k_all.at[blk, peer],
            send_sem=kf_send.at[n, m],
            recv_sem=k_recv.at[blk, peer],
            device_id={"blk": target},
            device_id_type=MESH,
        )
        for n, peer in enumerate(peers)
        for m, target in enumerate([sib_blk] + far)
    ]

    def step(index, carry):
        slot = lax.rem(index, 2)
        pair_copy(index, slot).wait()
        low_row = pl.multiple_of(index * (8 * group), 8 * group)
        some = pl.ds(low_row, 8 * group)
        values = pl.ds(pl.multiple_of(feats + low_row, 8), 8 * group)
        mixed[some, :] = attend_group(
            pair_buf.at[slot],
            queries[some, :],
            joined(kept[n, some, :] for n in range(blocks)),
            joined(kept[n, values, :] for n in range(blocks)),
            id_column, id_row, log_sums, index * group, score, high, low,
        )
        for copy in mix_copies(index):
            copy.start()

        @pl.when(index == groups // 2)
        def _():
            for n, source in enumerate(sources):
                arrived(w_all.at[squad, core, source], w_recv.at[n])
            for copy in squad_copies:
                copy.start()

        @pl.when(index == max(0, groups - 2))
        def _():
            for peer in peers:
                arrived(k_all.at[blk, peer], k_recv.at[blk, peer])
            for copy in key_copies:
                copy.start()

        @pl.when(index + 2 < groups)
        def _():
            pair_copy(index + 2, slot).start()

        return carry

    lax.fori_loop(0, groups, step, 0)
    mixed.flush()
    log_sums.flush()
    squad_sources = [lax.rem(squad + squads - n, squads) for n in range(squads)]
    for n, source in enumerate(squad_sources):
        ready = w_all.at[source, core]
        if n >= 1:
            arrived(ready, wx_recv.at[n - 1])
        copies.append(send(ready, ready, wf_send.at[n], wf_recv.at[n], sibling))
    small[SMALL_B_DOWN : SMALL_B_DOWN + 1, :] = column_sum(cot[mine, :])
    cots = halves(cot[...])
    downs = halves(w_down[...])
    d_act = dot_halves(cots, downs, NT)
    ups = halves(w_up[...])
    for n, source in enumerate(squad_sources):
        arrived(w_all.at[source, other_core], wf_recv.at[n])
    outs = halves(
        jnp.concatenate([w_all[s, kind, n] for n in range(zs) for s in range(squads) for kind in range(2)], axis=0)
    )
    mixed_all[z] = mixed[...]
    for n, source in enumerate(sources):
        for index in range(groups):
            some = pl.ds(index * (8 * group), 8 * group)
            arrived(mixed_all.at[source, some], mix_recv.at[n, index])
    copies += [
        send(q_part.at[peer], q_land.at[z], q_send.at[n], q_recv.at[n], {"head": peer})
        for n, peer in enumerate(peers)
    ]
    mixed_rows = mixed_all[...].reshape(zs * feats, rows).T
    hidden_rows = atoms[...] + dot_halves(halves(mixed_rows), outs) + b_out[...]
    hidden_two[...] = hidden_rows
    normal, rate = normalize(hidden_rows)
    normal_two[...] = normal
    rate_two[...] = jnp.broadcast_to(rate, rate_two.shape)
    normed = normal * gain[...] + bias[...]
    pre = dot_halves(halves(normed), ups) + b_up[...]
    phi = 0.5 * (1.0 + lax.erf(pre * math.sqrt(0.5)))
    act = pre * phi
    d_pre = d_act * (phi + pre * jnp.exp(-0.5 * pre * pre) * (1.0 / math.sqrt(2.0 * math.pi)))
    d_pres = halves(d_pre)
    part[...] = dot_halves(d_pres, ups, NT).reshape(zs, piece, width)
    copies += [
        send(part.at[peer], landed.at[z], part_send.at[n], part_recv.at[n], {"head": peer})
        for n, peer in enumerate(peers)
    ]
    landed[z] = part[z]
    ups_part[...] = dot_halves(halves(normed.T), d_pres).reshape(ups_part.shape)
    copies.append(send(ups_part.at[:, other_core], ups_sib, sib_send.at[0], sib_recv.at[0], sibling))
    downs_part[...] = dot_halves(halves(act.T), cots).reshape(downs_part.shape)
    copies.append(send(downs_part.at[:, other_core], downs_sib, sib_send.at[1], sib_recv.at[1], sibling))
    down[...] = dot_halves(halves(act), downs)
    out_mine[...] = hidden_two[mine, :] + down[mine, :] + b_down[...]
    out_mine.flush()
    small[SMALL_B_UP : SMALL_B_UP + 1, 0 : d_pre.shape[1]] = column_sum(d_pre)
    for kind, (parts, sib, go, got) in enumerate(
        [(ups_part, ups_sib, ups_go, ups_got), (downs_part, downs_sib, downs_go, downs_got)]
    ):
        arrived(sib, sib_recv.at[kind])
        go[...] = sib[...] + parts[:, core]
        copies += [
            send(
                go.at[peer], got.at[team], g_send.at[kind, n], g_recv.at[kind, team],
                team_device(peer, core, chips),
            )
            for n, peer in enumerate(far_teams)
        ]
        got[team] = go[team]
    for n, source in enumerate(far):
        for m, peer in enumerate(peers):
            ready = k_all.at[source, peer]
            arrived(ready, k_recv.at[source, peer])
            copies.append(send(ready, ready, ks_send.at[n, m], k_recv.at[source, peer], sibling))
    for n, source in enumerate(sources):
        arrived(q_land.at[source], q_recv.at[n])
    for n in range(zs):
        q_all[n] = q_land[n].T
    for n in range(blocks):
        k_all[n, z] = kept[n, 0:feats, :]
    for source in [sib_blk] + far_siblings:
        for peer in peers:
            arrived(k_all.at[source, peer], k_recv.at[source, peer])
    squares[...] = jnp.zeros(squares.shape, F32)
    at_once = 4
    rounds = heads // at_once

    def square_step(index, carry):
        there = lax.div(index, rounds)
        some = pl.ds(pl.multiple_of(lax.rem(index, rounds) * (8 * at_once), 8 * at_once), 8 * at_once)
        q_some = q_all[there, some, :]
        k_some = joined(k_all[n, there, some, :] for n in range(blocks))
        added = None
        for h in range(at_once):
            head = slice(8 * h, 8 * h + 8)
            q_high, q_low = wide_halves(q_some[head])
            k_high, k_low = wide_halves(k_some[head])
            value = dot(
                stacked([q_high, q_high, q_low, q_low]), stacked([k_high, k_low, k_high, k_low]), TN
            )
            added = value * value if added is None else added + value * value
        squares[...] += added
        return carry

    lax.fori_loop(0, zs * rounds, square_step, 0)
    same = id_column[mine, 0:1] == id_row[0:1, :]
    norms = jnp.sqrt(squares[...] + 1.0)
    terms = jnp.where(same, jnp.log1p(jnp.exp(norms - math.sqrt(zs * heads))), 0.0)
    number = jnp.where(same, 1.0, 0.0)

    def total(value):
        return jnp.sum(jnp.sum(value, axis=1, keepdims=True), axis=0, keepdims=True)

    lane = lax.broadcasted_iota(jnp.int32, (1, width), 1)
    small[SMALL_PENALTY : SMALL_PENALTY + 1, :] = jnp.where(
        lane == 0, total(terms), jnp.where(lane == 1, total(number), 0.0)
    )
    for n, source in enumerate(sources):
        arrived(landed.at[source], part_recv.at[n])
    d_normed = functools.reduce(jnp.add, [landed[n] for n in range(zs)])
    normal = normal_two[mine, :]
    d_rows = cot[mine, :] + normalize_back(d_normed, gain[...], normal, rate_two[mine, 0:1])
    d_halves = halves(d_rows)
    for n in range(zs):
        some = slice(n * feats, (n + 1) * feats)
        back[n] = dot_halves(d_halves, (outs[0][some], outs[1][some]), NT)
    copies += [
        send(back.at[peer], back_landed.at[z], back_send.at[n], back_recv.at[n], {"head": peer})
        for n, peer in enumerate(peers)
    ]
    back_landed[z] = back[z]
    d_hidden[...] = d_rows
    d_hidden.flush()
    for peer, parcel in zip(peers, parcels, strict=True):
        parcel[0:piece, :] = down[pl.ds(pl.multiple_of(peer * piece, 8), piece), :]
        parcel[piece : 2 * piece, :] = d_rows
        parcel.flush()
    small[SMALL_LN2_GAIN : SMALL_LN2_GAIN + 1, :] = column_sum(d_normed * normal)
    small[SMALL_LN2_BIAS : SMALL_LN2_BIAS + 1, :] = column_sum(d_normed)
    small[SMALL_B_OUT : SMALL_B_OUT + 1, :] = column_sum(d_rows)
    small.flush()
    for kind, got in enumerate([ups_got, downs_got]):
        for peer in far_teams:
            arrived(got.at[peer], g_recv.at[kind, peer])
    up_share, down_share = [
        functools.reduce(jnp.add, [got[n] for n in range(teams)]) for got in (ups_got, downs_got)
    ]
    for rows_of, columns_of, there in side_by_side(*up_share.shape, width):
        shares[there, columns_of] = up_share[rows_of]
    shares[there.stop :, :] = down_share
    shares.flush()
    for n, source in enumerate(sources):
        arrived(back_landed.at[source], back_recv.at[n])
    d_mixed[...] = back_landed[...].reshape(rows, feats).T
    d_mixed.flush()
    for copy in copies + squad_copies + key_copies:
        copy.wait_send()

    def drain(index, carry):
        for copy in mix_copies(index):
            copy.wait_send()
        return carry

    lax.fori_loop(0, groups, drain, 0)


def front(zs, dps, teams, pair, *operands):
    _, heads, rows, cols = pair.shape
    feats, blocks = heads * DH, cols // rows
    width, units = operands[0].shape[1], operands[12].shape[1]
    piece, group, hops = rows // zs, GROUP, zs - 1
    squads = dps * min(blocks // 2, max(1, feats // (2 * dps * 8)))
    up_rows, down_rows = width // (2 * teams), units // (2 * teams)
    groups = heads // group
    slab = pltpu.VMEM((zs, piece, width), F32)
    narrow = pltpu.VMEM((zs, piece, feats), F32)
    one_up, one_down = pltpu.VMEM((teams, up_rows, units), F32), pltpu.VMEM((teams, down_rows, width), F32)
    dma = pltpu.SemaphoreType.DMA
    return staged_call(
        front_kernel,
        "front",
        operands,
        [
            (feats, rows), (blocks, 2 * feats + 8, rows), (rows, LANES), (heads, rows, LANES), (feats, rows),
            (STRIP, cols), (feats, rows), (piece, width), (piece, width),
            (up_rows * units // width + down_rows, width), (SMALL_ROWS, width),
        ]
        + [(2 * piece, width)] * (zs - 1),
        [
            pltpu.VMEM((2, group, rows, cols), F32),
            pltpu.VMEM((group, rows, cols), F32),
            pltpu.VMEM((group, rows, cols), BF16),
            pltpu.VMEM((group, rows, cols), BF16),
            narrow, narrow,
            pltpu.VMEM((zs, feats, piece), F32),
            pltpu.VMEM((blocks, zs, feats, rows), F32),
            pltpu.VMEM((squads, 2, zs, feats // (2 * squads), width), F32),
            pltpu.VMEM((piece, cols), F32),
            pltpu.VMEM((zs, feats, rows), F32),
            pltpu.VMEM((rows, width), F32),
            pltpu.VMEM((rows, width), F32),
            pltpu.VMEM((rows, width), F32),
            pltpu.VMEM((rows, LANES), F32),
            slab, slab, narrow, narrow,
            pltpu.VMEM((teams, 2, up_rows, units), F32),
            one_up, one_up, one_up,
            pltpu.VMEM((teams, 2, down_rows, width), F32),
            one_down, one_down, one_down,
            dma((2,)),
            dma((blocks,)), dma((blocks,)),
            dma((hops,)), dma((hops, blocks // 2)), dma((max(1, blocks // 2 - 1), hops)), dma((blocks, zs)),
            dma((hops,)), dma((hops,)),
            dma((hops,)), dma((hops,)), dma((max(1, squads - 1),)), dma((max(1, squads - 1),)),
            dma((squads,)), dma((squads,)),
            dma((hops, groups)), dma((hops, groups)),
            dma((hops,)), dma((hops,)),
            dma((hops,)), dma((hops,)),
            dma((2,)), dma((2,)),
            dma((2, teams)), dma((2, teams)),
        ],
        FRONT_MB,
        remote=0,
        raw=(pair,),
    )


def finish_kernel(operands, results, scratch, raw):
    (
        d_heads, out_mine, d_hidden, atoms, gain, bias, w_query, mixed, small_in, w_key, w_value,
    ) = operands[:11]
    parcels = operands[11 : 10 + lax.axis_size("head")]
    chip_shares = operands[10 + lax.axis_size("head") :]
    grad_atoms, out_atoms, total_grads, grad_up, grad_down, small, penalty = results
    (
        sib_keys, sib_values, go_keys, go_values, got_keys, got_values,
        part, landed, grads, sib_grads, go_grads, got_grads, hidden_all, small_z, small_all,
        sib_send, sib_recv, kv_send, kv_recv, part_send, part_recv, back_send, back_recv,
        g_send, g_recv, t_send, t_recv, f_send, b_send, b_recv, bf_send, out_send, out_recv,
        small_z_send, small_z_recv, small_send, small_recv,
    ) = scratch
    chips, feats, rows = d_heads.shape[0] - 1, d_heads.shape[2] // 2, d_heads.shape[3]
    zs, piece, width = part.shape
    teams, _, share, _ = grads.shape
    blk, z, dp = lax.axis_index("blk"), lax.axis_index("head"), lax.axis_index("dp")
    core, chip = lax.rem(blk, 2), lax.div(blk, 2)
    other_core = 1 - core
    sibling = {"blk": blk + 1 - 2 * core}
    peers = others(z, zs)
    team = dp * chips + chip
    far_teams = others(team, teams)
    far_chips = others(chip, chips)
    place = team * 2 + core
    far_places = others(place, teams * 2)
    plane = [team_device(lax.div(value, 2), lax.rem(value, 2), chips) for value in far_places]
    meeting = [{"head": peer} for peer in peers] + plane
    greet(meeting)
    meet(meeting)
    copies = [
        send(
            d_heads.source.at[pl.ds(0, chips), other_core, pl.ds(kind * feats, feats)],
            sib, sib_send.at[kind], sib_recv.at[kind], sibling,
        )
        for kind, sib in enumerate([sib_keys, sib_values])
    ]
    mine = pl.ds(pl.multiple_of(z * piece, 8), piece)
    out_atoms[mine, :] = functools.reduce(jnp.add, [parcel[0:piece, :] for parcel in parcels], out_mine[...])
    copies += [
        send(out_atoms.at[mine], out_atoms.at[mine], out_send.at[n], out_recv.at[z], {"head": peer})
        for n, peer in enumerate(peers)
    ]

    def big_rows(result, source, kind):
        count = result.shape[0] // (2 * teams)
        return result.at[pl.ds(pl.multiple_of((source * 2 + kind) * count, 8), count)]

    partners = others(dp, lax.axis_size("dp"))
    for n in range(chips):
        source = dp * chips + lax.rem(chip + chips - n, chips)
        up_there, down_there = big_rows(grad_up, source, core), big_rows(grad_down, source, core)
        for rows_of, columns_of, there in side_by_side(*up_there.shape, width):
            up_there[rows_of, :] = chip_shares[n][there, columns_of]
        down_there[...] = chip_shares[n][there.stop :, :]
        for kind, ready in enumerate([up_there, down_there]):
            copies += [
                send(ready, ready, b_send.at[kind, n, m], b_recv.at[kind, source, core], {"dp": partner})
                for m, partner in enumerate(partners)
            ]
    own_heads = d_heads.ref
    d_queries = own_heads[chips, 0, 0:feats, :]
    for kind, (sib, go, got) in enumerate([(sib_keys, go_keys, got_keys), (sib_values, go_values, got_values)]):
        arrived(sib, sib_recv.at[kind])
        go[...] = sib[...] + own_heads[0:chips, core, kind * feats : (kind + 1) * feats, :]
        copies += [
            send(
                go.at[peer], got.at[chip], kv_send.at[kind, n], kv_recv.at[kind, chip],
                {"blk": peer * 2 + core},
            )
            for n, peer in enumerate(far_chips)
        ]
    got_keys[chip] = go_keys[chip]
    got_values[chip] = go_values[chip]
    normal, rate = normalize(atoms[...])
    normed = halves(normal * gain[...] + bias[...])
    dq_rows = d_queries.T
    d_normed = dot_full(dq_rows, w_query[...], NT)
    grad_q = dot_halves(halves(d_queries), normed)
    small_z[z] = small_in[0:8, :]
    hidden_all[z] = d_hidden[...]
    for n, parcel in enumerate(parcels):
        hidden_all[lax.rem(z + zs - 1 - n, zs)] = parcel[piece : 2 * piece, :]
    grad_o = dot_full(mixed[...], hidden_all[...].reshape(rows, width))
    for peer in far_chips:
        arrived(got_keys.at[peer], kv_recv.at[0, peer])
        arrived(got_values.at[peer], kv_recv.at[1, peer])
    dk = functools.reduce(jnp.add, [got_keys[n] for n in range(chips)])
    dv = functools.reduce(jnp.add, [got_values[n] for n in range(chips)])
    dv_rows = dv.T
    d_normed = (
        d_normed + dot_full(dk.T, w_key[...], NT) + dot_full(dv_rows, w_value[...], NT)
    )
    part[...] = d_normed.reshape(zs, piece, width)
    copies += [
        send(part.at[peer], landed.at[z], part_send.at[n], part_recv.at[z], {"head": peer})
        for n, peer in enumerate(peers)
    ]
    landed[z] = part[z]
    grad_k = dot_halves(halves(dk), normed)
    grad_v = dot_halves(halves(dv), normed)
    grads[...] = jnp.concatenate([grad_q, grad_k, grad_v, grad_o], axis=0).reshape(grads.shape)
    copies.append(send(grads.at[:, other_core], sib_grads, sib_send.at[2], sib_recv.at[2], sibling))
    arrived(sib_grads, sib_recv.at[2])
    go_grads[...] = sib_grads[...] + grads[:, core]
    copies += [
        send(
            go_grads.at[peer], got_grads.at[team], g_send.at[n], g_recv.at[team], team_device(peer, core, chips)
        )
        for n, peer in enumerate(far_teams)
    ]
    got_grads[team] = go_grads[team]
    for peer in peers:
        arrived(landed.at[peer], part_recv.at[peer])
    d_normed = functools.reduce(jnp.add, [landed[n] for n in range(zs)])
    normal, rate = normalize(atoms[mine, :])
    grad_atoms[mine, :] = d_hidden[...] + normalize_back(d_normed, gain[...], normal, rate)
    small_z[z, SMALL_LN1_GAIN : SMALL_LN1_GAIN + 1, :] = column_sum(d_normed * normal)
    small_z[z, SMALL_LN1_BIAS : SMALL_LN1_BIAS + 1, :] = column_sum(d_normed)
    copies += [
        send(small_z.at[z], small_z.at[z], small_z_send.at[n], small_z_recv.at[z], {"head": peer})
        for n, peer in enumerate(peers)
    ]
    copies += [
        send(grad_atoms.at[mine], grad_atoms.at[mine], back_send.at[n], back_recv.at[z], {"head": peer})
        for n, peer in enumerate(peers)
    ]
    for peer in far_teams:
        arrived(got_grads.at[peer], g_recv.at[peer])
    total_grads[team, core] = functools.reduce(jnp.add, [got_grads[n] for n in range(teams)])
    ready = total_grads.at[team, core]
    copies.append(send(ready, ready, t_send.at[0], t_recv.at[team, core], sibling))
    copies += [
        send(ready, ready, t_send.at[n + 1], t_recv.at[team, core], team_device(peer, core, chips))
        for n, peer in enumerate(far_teams)
    ]
    for peer in peers:
        arrived(small_z.at[peer], small_z_recv.at[peer])
    small_all[place, 0:8, :] = functools.reduce(jnp.add, [small_z[n] for n in range(zs)])
    small_all[place, 8:16, :] = small_in[8:16, :]
    small_all[place, SMALL_B_QUERY : SMALL_B_QUERY + 1, 0:feats] = column_sum(dq_rows)
    small_all[place, SMALL_B_VALUE : SMALL_B_VALUE + 1, 0:feats] = column_sum(dv_rows)
    copies += [
        send(small_all.at[place], small_all.at[place], small_send.at[n], small_recv.at[place], target)
        for n, target in enumerate(plane)
    ]
    for n, peer in enumerate(far_teams):
        ready = total_grads.at[peer, core]
        arrived(ready, t_recv.at[peer, core])
        copies.append(send(ready, ready, f_send.at[n], t_recv.at[peer, core], sibling))
    for kind, result in enumerate([grad_up, grad_down]):
        for n in range(teams):
            ready = big_rows(result, n, core)

            @pl.when(lax.div(n, chips) != dp)
            def _(ready=ready, sem=b_recv.at[kind, n, core]):
                arrived(ready, sem)

            copies.append(send(ready, ready, bf_send.at[kind, n], b_recv.at[kind, n, core], sibling))
    for source in far_places:
        arrived(small_all.at[source], small_recv.at[source])
    summed = functools.reduce(jnp.add, [small_all[n] for n in range(2 * teams)])
    small[...] = summed
    ends = summed[SMALL_PENALTY : SMALL_PENALTY + 1, :]
    penalty[...] = ends[:, 0:1] / ends[:, 1:2]
    for peer in [team] + far_teams:
        arrived(total_grads.at[peer, other_core], t_recv.at[peer, other_core])
    total_grads.flush()
    for kind, result in enumerate([grad_up, grad_down]):
        for n in range(teams):
            arrived(big_rows(result, n, other_core), b_recv.at[kind, n, other_core])
        result.flush()
    for peer in peers:
        there = pl.ds(pl.multiple_of(peer * piece, 8), piece)
        arrived(out_atoms.at[there], out_recv.at[peer])
    out_atoms.flush()
    for peer in peers:
        there = pl.ds(pl.multiple_of(peer * piece, 8), piece)
        arrived(grad_atoms.at[there], back_recv.at[peer])
    for copy in copies:
        copy.wait_send()


def finish(zs, dps, units, *operands):
    d_heads, atoms = operands[0], operands[3]
    chips, feats, rows = d_heads.shape[0] - 1, d_heads.shape[2] // 2, d_heads.shape[3]
    width = atoms.shape[1]
    piece = rows // zs
    teams = dps * chips
    share = 4 * feats // (2 * teams)
    some = pltpu.VMEM((chips, feats, rows), F32)
    slab = pltpu.VMEM((zs, piece, width), F32)
    one = pltpu.VMEM((teams, share, width), F32)
    dma = pltpu.SemaphoreType.DMA
    return staged_call(
        finish_kernel,
        "finish",
        operands,
        [
            (rows, width),
            (rows, width),
            (teams, 2, share, width),
            (width, units),
            (units, width),
            (SMALL_ROWS, width),
            (1, 1),
        ],
        [some] * 6
        + [slab, slab, pltpu.VMEM((teams, 2, share, width), F32), one, one, one, slab]
        + [
            pltpu.VMEM((zs, 8, width), F32),
            pltpu.VMEM((2 * teams, SMALL_ROWS, width), F32),
            dma((3,)), dma((3,)),
            dma((2, chips)), dma((2, chips)),
            dma((zs,)), dma((zs,)),
            dma((zs,)), dma((zs,)),
            dma((teams,)), dma((teams,)),
            dma((teams,)), dma((teams, 2)), dma((teams,)),
            dma((2, chips, dps)), dma((2, teams, 2)), dma((2, teams)),
            dma((zs,)), dma((zs,)),
            dma((zs,)), dma((zs,)),
            dma((2 * teams,)), dma((2 * teams,)),
        ],
        FINISH_MB,
        remote=2,
        near_in=[0] + list(range(11, len(operands))),
        near_out=range(7),
    )


def place_kernel(operands, results, scratch, raw):
    total_grads, small, penalty_in = operands
    penalty, grad_query, grad_key, grad_value, grad_out = results[:5]
    penalty[...] = penalty_in[...]
    feats, width = grad_out.shape
    done = total_grads[...].reshape(4 * feats, width)
    grad_query[...] = done[0:feats].T
    grad_query.flush()
    grad_key[...] = done[feats : 2 * feats].T
    grad_key.flush()
    grad_value[...] = done[2 * feats : 3 * feats].T
    grad_value.flush()
    grad_out[...] = done[3 * feats :]
    grad_out.flush()
    for result, row in zip(results[5:], SMALL_OUTPUTS, strict=True):
        result[...] = small[row : row + 1, 0 : result.shape[1]]


SMALL_OUTPUTS = (
    SMALL_LN1_GAIN, SMALL_LN1_BIAS, SMALL_B_QUERY, SMALL_B_VALUE, SMALL_B_OUT, SMALL_LN2_GAIN, SMALL_LN2_BIAS,
    SMALL_B_UP, SMALL_B_DOWN,
)


def place(feats, units, straight, *operands):
    width = operands[1].shape[1]
    lengths = {SMALL_B_QUERY: feats, SMALL_B_VALUE: feats, SMALL_B_UP: units}
    return staged_call(
        place_kernel,
        "place",
        operands,
        [(1, 1)]
        + [(width, feats)] * 3
        + [(feats, width)]
        + [(1, lengths.get(row, width)) for row in SMALL_OUTPUTS],
        [],
        PLACE_MB,
        straight=straight,
        near_in=(0, 1, 2),
        near_straight=True,
    )


def local(
    zs, dps,
    atoms, pair, mol_ids, ln1_gain, ln1_bias, w_query, b_query, w_key, w_value, b_value, w_out, b_out,
    ln2_gain, ln2_bias, w_up, b_up, w_down, b_down, cot_atoms, cot_pair,
):
    blocks = pair.shape[3] // pair.shape[2]
    inputs, cot = atoms[0], cot_atoms[0]

    def line(value):
        return value.reshape(1, -1)

    (
        queries, kept, id_column, log_sums, mixed, id_row, d_mixed, out_mine, d_hidden, shares, small, *parcels,
    ) = front(
        zs, dps, dps * blocks // 2, pair,
        inputs, mol_ids, line(ln1_gain), line(ln1_bias), w_key, w_value, line(b_value), w_query, line(b_query),
        w_out, cot, w_down, w_up, line(b_out), line(ln2_gain), line(ln2_bias), line(b_up),
        line(b_down),
    )
    parcels = [
        lax.ppermute(parcel, "head", [(source, (source + n + 1) % zs) for source in range(zs)])
        for n, parcel in enumerate(parcels)
    ]
    chips = blocks // 2
    chip_shares = [shares] + [
        lax.ppermute(shares, "blk", [(2 * c + core, 2 * ((c + n) % chips) + core) for c in range(chips) for core in range(2)])
        for n in range(1, chips)
    ]
    out_pair, grad_pair, d_heads = attend_back(
        pair, cot_pair, queries, kept, mixed, d_mixed, log_sums, id_column, id_row
    )
    grad_atoms, out_atoms, total_grads, grad_up, grad_down, small, penalty = finish(
        zs, dps, w_up.shape[1],
        d_heads, out_mine, d_hidden, inputs, line(ln1_gain), line(ln1_bias), w_query, mixed,
        small, w_key, w_value, *parcels, *chip_shares,
    )
    placed = place(
        w_query.shape[1], w_up.shape[1],
        [grad_atoms, out_atoms, grad_up, grad_down],
        total_grads, small, penalty,
    )
    grad_atoms, out_atoms, grad_up, grad_down, penalty, grad_query, grad_key, grad_value, grad_out = placed[:9]
    (
        grad_ln1_gain, grad_ln1_bias, grad_b_query, grad_b_value, grad_b_out, grad_ln2_gain, grad_ln2_bias,
        grad_b_up, grad_b_down,
    ) = [value.reshape(-1) for value in placed[9:]]
    return (
        out_atoms[None],
        out_pair,
        penalty[0, 0],
        grad_atoms[None],
        grad_pair,
        grad_ln1_gain,
        grad_ln1_bias,
        grad_query,
        grad_b_query,
        grad_key,
        grad_value,
        grad_b_value,
        grad_out,
        grad_b_out,
        grad_ln2_gain,
        grad_ln2_bias,
        grad_up,
        grad_b_up,
        grad_down,
        grad_b_down,
    )


def solution(mesh):
    rows, pairs = P("dp", "blk", None), P("dp", "head", "blk", None)
    columns = P(None, "head")
    return jax.shard_map(
        functools.partial(local, mesh.shape["head"], mesh.shape["dp"]),
        mesh=mesh,
        in_specs=(
            rows, pairs, P("dp", "blk"), P(), P(), columns, P("head"), columns, columns, P("head"),
            P("head", None), P(), P(), P(), columns, P("head"), P("head", None), P(), rows, pairs,
        ),
        out_specs=(
            rows, pairs, P(), rows, pairs, P(), P(), columns, P("head"), columns, columns, P("head"),
            P("head", None), P(), P(), P(), columns, P("head"), P("head", None), P(),
        ),
        check_vma=False,
    )
```

```python
import functools
import math

import jax
import jax.numpy as jnp
from jax import lax
from jax.experimental import pallas as pl
from jax.experimental.pallas import tpu as pltpu
from jax.sharding import PartitionSpec as P

DH = 8
LANES = 128
STRIP = 16
CHUNK = 256
GROUP = 2
FRONT_MB, BACK_MB, FINISH_MB, PLACE_MB = 58, 60, 40, 32
NORM_EPS = 1e-05
MASK_FILL = -1e30
F32 = jnp.float32
BF16 = jnp.bfloat16
MESH = pl.DeviceIdType.MESH
NN = (((1,), (0,)), ((), ()))
NT = (((1,), (1,)), ((), ()))
TN = (((0,), (0,)), ((), ()))
VMEM = pl.BlockSpec(memory_space=pltpu.VMEM)


def dot(left, right, dims=NN):
    return lax.dot_general(left, right, dims, preferred_element_type=F32)


def halves(value):
    high = value.astype(BF16)
    return high, (value - high.astype(F32)).astype(BF16)


def dot_halves(left, right, dims=NN):
    return dot(left[0], right[0], dims) + (
        dot(left[0], right[1], dims) + dot(left[1], right[0], dims)
    )


def dot_full(left, right, dims=NN):
    return dot_halves(halves(left), halves(right), dims)


def normalize(inputs):
    centred = inputs - jnp.mean(inputs, -1, keepdims=True)
    rate = lax.rsqrt(jnp.mean(centred * centred, -1, keepdims=True) + NORM_EPS)
    return centred * rate, rate


def normalize_back(grad, gain, normal, rate):
    scaled = grad * gain
    return rate * (
        scaled
        - jnp.mean(scaled, -1, keepdims=True)
        - normal * jnp.mean(scaled * normal, -1, keepdims=True)
    )


def column_sum(value):
    return jnp.sum(value, 0, keepdims=True)


def send(src, dst, send_sem, recv_sem, target):
    copy = pltpu.make_async_remote_copy(
        src_ref=src,
        dst_ref=dst,
        send_sem=send_sem,
        recv_sem=recv_sem,
        device_id=target,
        device_id_type=MESH,
    )
    copy.start()
    return copy


def arrived(ref, sem):
    pltpu.make_async_remote_copy(
        src_ref=ref, dst_ref=ref, send_sem=sem, recv_sem=sem, device_id={}, device_id_type=MESH
    ).wait_recv()


def greet(targets):
    for target in targets:
        pl.semaphore_signal(pltpu.get_barrier_semaphore(), inc=1, device_id=target, device_id_type=MESH)


def meet(targets):
    pl.semaphore_wait(pltpu.get_barrier_semaphore(), len(targets))


def others(index, count):
    return [lax.rem(index + step, count) for step in range(1, count)]


class Operand:
    def __init__(self, source, slot, sem):
        self.source, self.slot, self.shape = source, slot, slot.shape
        self.copy = None if sem is None else pltpu.make_async_copy(source, slot, sem)
        if self.copy is not None:
            self.copy.start()

    @property
    def ref(self):
        if self.copy is not None:
            self.copy.wait()
            self.copy = None
        return self.slot

    def __getitem__(self, index):
        return self.ref[index]


class Result:
    def __init__(self, target, slot, sem):
        self.slot, self.shape, self.at = slot, slot.shape, slot.at
        self.copy = None if sem is None else pltpu.make_async_copy(slot, target, sem)
        self.begun = self.copy is None

    def __setitem__(self, index, value):
        self.slot[index] = value

    def __getitem__(self, index):
        return self.slot[index]

    def flush(self):
        if not self.begun:
            self.copy.start()
            self.begun = True


def staged_call(
    kernel, name, operands, results, scratch, megabytes,
    remote=None, raw=(), straight=(), raw_results=(), cost=None, near_in=(), near_out=(), near_straight=False,
):
    n_in, n_out, n_raw, n_straight = len(operands), len(results), len(raw), len(straight)
    n_left = len(raw_results)
    far_in = [n for n in range(n_in) if n not in near_in]
    far_out = [n for n in range(n_out) if n not in near_out]

    def body(*refs):
        sources, left, refs = refs[:n_in], refs[n_in : n_in + n_raw], refs[n_in + n_raw :]
        moved, refs = refs[:n_straight], refs[n_straight:]
        arrays, refs = refs[:n_straight], refs[n_straight:]
        left, refs = left + refs[:n_left], refs[n_left:]
        targets, refs = refs[:n_out], refs[n_out:]
        in_slots, refs = dict(zip(far_in, refs)), refs[len(far_in) :]
        out_slots, refs = dict(zip(far_out, refs)), refs[len(far_out) :]
        in_sem, out_sem, move_sem, refs = refs[0], refs[1], refs[2], refs[3:]
        through, loads = moved, []
        if not near_straight:
            through, refs = refs[:n_straight], refs[n_straight:]
            loads = [pltpu.make_async_copy(moved[n], through[n], move_sem.at[n]) for n in range(n_straight)]
        moves = [pltpu.make_async_copy(through[n], arrays[n], move_sem.at[n]) for n in range(n_straight)]
        for load in loads:
            load.start()
        ins = [
            Operand(sources[n], in_slots.get(n, sources[n]), in_sem.at[far_in.index(n)] if n in in_slots else None)
            for n in range(n_in)
        ]
        outs = [
            Result(targets[n], out_slots.get(n, targets[n]), out_sem.at[far_out.index(n)] if n in out_slots else None)
            for n in range(n_out)
        ]
        for load in loads:
            load.wait()
        for move in moves:
            move.start()
        kernel(ins, outs, refs, left)
        for operand in ins:
            operand.ref
        for result in outs:
            result.flush()
        for copy in moves + [result.copy for result in outs if result.copy is not None]:
            copy.wait()

    hbm, vmem = pl.BlockSpec(memory_space=pltpu.HBM), pl.BlockSpec(memory_space=pltpu.VMEM)
    extra = {} if remote is None else {"collective_id": remote, "has_side_effects": True}
    return pl.pallas_call(
        body,
        out_shape=[jax.ShapeDtypeStruct(value.shape, value.dtype) for value in straight]
        + [jax.ShapeDtypeStruct(shape, F32) for shape in raw_results]
        + [jax.ShapeDtypeStruct(shape, F32) for shape in results],
        in_specs=[vmem if n in near_in else hbm for n in range(n_in)]
        + [hbm] * n_raw
        + [vmem if near_straight else hbm] * n_straight,
        out_specs=[hbm] * (n_straight + n_left) + [vmem if n in near_out else hbm for n in range(n_out)],
        scratch_shapes=[pltpu.VMEM(operands[n].shape, operands[n].dtype) for n in far_in]
        + [pltpu.VMEM(results[n], F32) for n in far_out]
        + [pltpu.SemaphoreType.DMA((max(1, n),)) for n in (len(far_in), len(far_out), n_straight)]
        + ([] if near_straight else [pltpu.VMEM(value.shape, value.dtype) for value in straight])
        + list(scratch),
        compiler_params=pltpu.CompilerParams(vmem_limit_bytes=megabytes << 20, **extra),
        cost_estimate=cost,
        name=name,
    )(*operands, *raw, *straight)


def joined(pieces):
    return jnp.concatenate(list(pieces), axis=1)


def stacked(parts):
    return jnp.concatenate(parts, axis=0).astype(BF16)


def wide_halves(value):
    high = value.astype(BF16).astype(F32)
    return high, value - high


def attend_group(pair, queries, keys, values, id_column, id_row, log_sums, first, score, high, low):
    group, rows, cols = score.shape
    strips = rows // STRIP
    chunk = min(CHUNK, cols)
    mixed = []
    for g in range(group):
        head = slice(8 * g, 8 * g + 8)
        q_high, q_low = wide_halves(queries[head, :])
        k_high, k_low = wide_halves(keys[head, :])
        v_high, v_low = wide_halves(values[head, :])
        ones = jnp.ones_like(v_high)
        q_pack = stacked([q_high, q_high, q_low, q_low])
        k_pack = stacked([k_high, k_low, k_high, k_low])
        v_pack = stacked([v_high, v_low, ones, jnp.zeros_like(ones)])
        tops = [None] * strips
        for start in range(0, cols, chunk):
            part = slice(start, start + chunk)
            score[g, :, part] = dot(q_pack, k_pack[:, part], TN)
            for s in range(strips):
                line = pl.ds(s * STRIP, STRIP)
                own = id_column[line, :]
                for j in range(start, start + chunk, LANES):
                    tile = pl.ds(j, LANES)
                    value = pair[g, line, tile] + score[g, line, tile]
                    value = jnp.where(own == id_row[:, tile], value, MASK_FILL)
                    score[g, line, tile] = value
                    tops[s] = value if tops[s] is None else jnp.maximum(tops[s], value)
        tops = [
            jnp.broadcast_to(jnp.max(top, axis=1, keepdims=True), (STRIP, LANES)) for top in tops
        ]
        totals = [None] * strips
        gathered = None
        for start in range(0, cols, chunk):
            part = slice(start, start + chunk)
            for s in range(strips):
                line = pl.ds(s * STRIP, STRIP)
                for j in range(start, start + chunk, LANES):
                    tile = pl.ds(j, LANES)
                    weight = jnp.exp(score[g, line, tile] - tops[s])
                    high[g, line, tile], low[g, line, tile] = halves(weight)
                    totals[s] = weight if totals[s] is None else totals[s] + weight
            term = dot(v_pack[:, part], high[g, :, part], NT) + dot(
                v_pack[:, part], low[g, :, part], NT
            )
            gathered = term if gathered is None else gathered + term
        for s in range(strips):
            total = jnp.sum(totals[s], axis=1, keepdims=True)
            log_sums[first + g, pl.ds(s * STRIP, STRIP), :] = tops[s] + jnp.log(total)
        mixed.append((gathered[0:8] + gathered[8:16]) / gathered[16:17])
    return jnp.concatenate(mixed, axis=0)


def chunks_of(cols):
    chunk = min(CHUNK, cols)
    return [slice(start, start + chunk) for start in range(0, cols, chunk)]


def score_packs(queries, keys):
    q_high, q_low = wide_halves(queries)
    k_high, k_low = wide_halves(keys)
    return stacked([q_high, q_high, q_low, q_low]), stacked([k_high, k_low, k_high, k_low])


def attend_back_kernel(operands, results, scratch, raw):
    queries, kept, d_mixed, mixed, id_column, id_row = operands
    pair, cot, log_sums, out_pair, grad_pair, heads_out = raw
    pair_buf, cot_buf, log_buf, out_buf, grad_buf = scratch[:5]
    here = scratch[5:11]
    d_heads, in_sem, out_sem, heads_sem = scratch[11:]
    heads = pair.shape[1]
    feats = heads * DH
    depth, rows, cols = pair_buf.shape
    blocks = kept.shape[0]
    parts = chunks_of(cols)
    place = lax.broadcasted_iota(jnp.int32, (8, rows), 0)

    def inward(index):
        slot = lax.rem(index, depth)
        sources = (pair.at[0, index], cot.at[0, index], log_sums.at[index])
        return [
            pltpu.make_async_copy(source, buf.at[slot], in_sem.at[n, slot])
            for n, (source, buf) in enumerate(zip(sources, (pair_buf, cot_buf, log_buf), strict=True))
        ]

    def outward(index):
        slot = lax.rem(index, depth)
        return [
            pltpu.make_async_copy(buf.at[slot], array.at[0, index], out_sem.at[n, slot])
            for n, (array, buf) in enumerate([(out_pair, out_buf), (grad_pair, grad_buf)])
        ]

    for n in range(2):
        for copy in inward(n):
            copy.start()
    for operand in operands:
        operand.ref

    def rows_of(index):
        return pl.ds(pl.multiple_of(index * 8, 8), 8)

    def key_rows(index):
        return joined(kept[n, rows_of(index), :] for n in range(blocks))

    def value_row(index):
        return pl.ds(pl.multiple_of(feats + index * 8, 8), 8)

    def value_rows(index):
        return joined(kept[n, value_row(index), :] for n in range(blocks))

    def packs(index):
        head = rows_of(index)
        q_pack, k_pack = score_packs(queries[head, :], key_rows(index))
        v_high, v_low = wide_halves(value_rows(index))
        m_high, m_low = wide_halves(d_mixed[head, :])
        delta_high, rest = wide_halves(-column_sum(mixed[head, :] * d_mixed[head, :]))
        delta_mid, delta_low = wide_halves(rest)
        deltas = jnp.where(
            place == 0, delta_high, jnp.where(place == 1, delta_mid, jnp.where(place == 2, delta_low, 0.0))
        )
        m_pack = stacked([m_high, m_high, m_low, deltas])
        v_pack = stacked([v_high, v_low, v_high, jnp.ones_like(v_high)])
        return q_pack, k_pack, m_pack, v_pack

    def pairs(index):
        head = rows_of(index)
        return [stacked(wide_halves(value)) for value in (queries[head, :], key_rows(index), d_mixed[head, :])]

    def before(pack, part, there):
        q_pack, k_pack, m_pack, v_pack = pack
        there[0][:, part] = dot(q_pack, k_pack[:, part], TN)
        there[1][:, part] = dot(m_pack, v_pack[:, part], TN)

    def middle(index, slot, part, here):
        score, d_prob, p_high, p_low, g_high, g_low = here
        for s in range(rows // STRIP):
            line = pl.ds(s * STRIP, STRIP)
            own = id_column[line, :]
            log_sum = log_buf[slot, line, :]
            for j in range(part.start, part.stop, LANES):
                tile = pl.ds(j, LANES)
                value = pair_buf[slot, line, tile] + score[line, tile]
                out_buf[slot, line, tile] = value
                prob = jnp.exp(jnp.where(own == id_row[:, tile], value - log_sum, MASK_FILL))
                p_high[line, tile], p_low[line, tile] = halves(prob)
                grad = prob * d_prob[line, tile] + cot_buf[slot, line, tile]
                grad_buf[slot, line, tile] = grad
                g_high[line, tile], g_low[line, tile] = halves(grad)

    def both(left, high, low, dims):
        value = dot(left, high, dims) + dot(left, low, dims)
        return value[0:8] + value[8:16]

    def after(index, pair_of, part, there):
        q_pair, k_pair, m_pair = pair_of
        _, _, p_high, p_low, g_high, g_low = there
        head = rows_of(index)
        d_value = both(m_pair, p_high[:, part], p_low[:, part], NN)
        d_key = both(q_pair, g_high[:, part], g_low[:, part], NN)
        for n in range(part.start // rows, part.stop // rows):
            span = slice(n * rows - part.start, (n + 1) * rows - part.start)
            d_heads[n // 2, n % 2, head, :] = d_key[:, span]
            d_heads[n // 2, n % 2, value_row(index), :] = d_value[:, span]
        return both(k_pair[:, part], g_high[:, part], g_low[:, part], NT)

    def stage(index, carry):
        slot = lax.rem(index, depth)
        for copy in inward(index):
            copy.wait()

        @pl.when(index >= depth)
        def _():
            for copy in outward(index - depth):
                copy.wait()

        @pl.when(index == 0)
        def _():
            for n in range(2, depth - 1):
                for copy in inward(n):
                    copy.start()

        @pl.when(index + depth - 1 < heads)
        def _():
            for copy in inward(index + depth - 1):
                copy.start()

        next_packs, own_pairs = packs(index), pairs(index)
        d_query = None
        before(next_packs, parts[0], here)
        for n, part in enumerate(parts):
            if n + 1 < len(parts):
                before(next_packs, parts[n + 1], here)
            middle(index, slot, part, here)
            if n >= 1:
                term = after(index, own_pairs, parts[n - 1], here)
                d_query = term if d_query is None else d_query + term
        term = after(index, own_pairs, parts[-1], here)
        d_query = term if d_query is None else d_query + term
        d_heads[blocks // 2, 0, rows_of(index), :] = d_query * (DH ** (-0.5))
        for copy in outward(index):
            copy.start()
        return carry

    lax.fori_loop(0, heads, stage, 0)
    last = pltpu.make_async_copy(d_heads, heads_out.at[pl.ds(0, d_heads.shape[0])], heads_sem.at[0])
    last.start()
    for n in range(max(0, heads - depth), heads):
        for copy in outward(n):
            copy.wait()
    last.wait()


def attend_back(pair, cot, queries, kept, mixed, d_mixed, log_sums, id_column, id_row):
    _, heads, rows, cols = pair.shape
    feats = heads * DH
    blocks = kept.shape[0]
    depth = 6
    entries = max(blocks // 2 + 1, (26 << 20) // (16 * feats * rows))
    wide, thin = pltpu.VMEM((rows, cols), F32), pltpu.VMEM((rows, cols), BF16)
    return staged_call(
        attend_back_kernel,
        "attend_back",
        [queries, kept, d_mixed, mixed, id_column, id_row],
        [],
        [pltpu.VMEM((depth, rows, cols), F32)] * 2
        + [pltpu.VMEM((depth, rows, LANES), F32)]
        + [pltpu.VMEM((depth, rows, cols), F32)] * 2
        + [wide] * 2
        + [thin] * 4
        + [pltpu.VMEM((blocks // 2 + 1, 2, 2 * feats, rows), F32)]
        + [pltpu.SemaphoreType.DMA((n, depth)) for n in (3, 2)]
        + [pltpu.SemaphoreType.DMA((1,))],
        BACK_MB,
        raw=(pair, cot, log_sums),
        raw_results=(pair.shape, pair.shape, (entries, 2, 2 * feats, rows)),
        cost=pl.CostEstimate(
            flops=2 * 400 * heads * rows * cols,
            bytes_accessed=16 * heads * rows * cols,
            transcendentals=heads * rows * cols,
        ),
    )


SMALL_LN1_GAIN, SMALL_LN1_BIAS, SMALL_LN2_GAIN, SMALL_LN2_BIAS = 0, 1, 2, 3
SMALL_B_OUT, SMALL_B_DOWN, SMALL_PENALTY = 4, 5, 6
SMALL_B_QUERY, SMALL_B_VALUE, SMALL_B_UP = 8, 9, 10
SMALL_ROWS = 16


def side_by_side(count, units, width):
    beside = width // units
    height = count // beside
    return [
        (slice(n * height, (n + 1) * height), slice(n * units, (n + 1) * units), slice(0, height))
        for n in range(beside)
    ]


def team_device(team, core, chips):
    return {"dp": lax.div(team, chips), "blk": lax.rem(team, chips) * 2 + core}


def front_kernel(operands, results, scratch, raw):
    (
        atoms, ids, gain_one, bias_one, w_key, w_value, b_value, w_query, b_query, w_out, cot, w_down, w_up, b_out,
        gain, bias, b_up, b_down,
    ) = operands
    (pair,) = raw
    (
        queries, kept, id_column, log_sums, mixed, id_row, d_mixed, out_mine, d_hidden, shares, small,
    ) = results[:11]
    parcels = results[11:]
    (
        pair_buf, score, high, low, q_part, q_land, q_all, k_all, w_all, squares, mixed_all, hidden_two, down, d_act, up_high, up_low, normal_two, rate_two,
        part, landed, back, back_landed, ups_part, ups_sib, ups_go, ups_got, downs_part, downs_sib, downs_go, downs_got,
        pair_sem, kept_send, kept_recv, kz_send, kf_send, ks_send, k_recv, q_send, q_recv, w_send, w_recv, wx_send, wx_recv, wf_send, wf_recv,
        mix_send, mix_recv, part_send, part_recv, back_send, back_recv, sib_send, sib_recv, g_send, g_recv,
    ) = scratch
    zs, feats, rows = mixed_all.shape
    blocks = kept.shape[0]
    chips = blocks // 2
    teams, width = ups_part.shape[0], atoms.shape[1]
    _, group, _, cols = pair_buf.shape
    heads = feats // DH
    groups = heads // group
    piece = rows // zs
    z, blk = lax.axis_index("head"), lax.axis_index("blk")
    core, chip = lax.rem(blk, 2), lax.div(blk, 2)
    dp, dps = lax.axis_index("dp"), lax.axis_size("dp")
    team = dp * chips + chip
    other_core = 1 - core
    sib_blk = blk + 1 - 2 * core
    sibling = {"blk": sib_blk}
    peers, far_teams = others(z, zs), others(team, teams)
    sources = [lax.rem(z + zs - n, zs) for n in range(1, zs)]
    far = [step * 2 + core for step in others(chip, chips)]
    far_siblings = [step * 2 + other_core for step in others(chip, chips)]
    mine = pl.ds(pl.multiple_of(z * piece, 8), piece)

    def pair_copy(index, slot):
        return pltpu.make_async_copy(
            pair.at[0, pl.ds(index * group, group)], pair_buf.at[slot], pair_sem.at[slot]
        )

    meeting = [{"head": peer} for peer in peers] + [sibling]
    meeting += [team_device(peer, core, chips) for peer in far_teams]
    greet(meeting)
    for n in range(2):
        pair_copy(n, n).start()

    normal, _ = normalize(atoms[...])
    normed = halves(normal * gain_one[...] + bias_one[...])
    meet(meeting)
    copies = []
    squads, _, _, fewer, _ = w_all.shape
    close = squads // dps
    base = chip - lax.rem(chip, close)
    squad = dp * close + chip - base
    w_mine = w_out.source.at[pl.ds(pl.multiple_of((squad * 2 + core) * fewer, 8), fewer)]
    copies += [
        send(w_mine, w_all.at[squad, core, z], w_send.at[n], w_recv.at[n], {"head": peer})
        for n, peer in enumerate(peers)
    ]
    kept[blk, 0:feats, :] = dot_halves(normed, halves(w_key[...])).T
    copies += [
        send(kept.at[blk, 0:feats], k_all.at[blk, z], kz_send.at[n], k_recv.at[blk, z], {"head": peer})
        for n, peer in enumerate(peers)
    ]
    kept[blk, feats : 2 * feats, :] = (dot_halves(normed, halves(w_value[...])) + b_value[...]).T
    id_line = ids[...].astype(F32)
    kept[blk, 2 * feats : 2 * feats + 8, :] = jnp.broadcast_to(id_line, (8, rows))
    copies += [
        send(kept.at[blk], kept.at[blk], kept_send.at[n], kept_recv.at[blk], {"blk": peer})
        for n, peer in enumerate([sib_blk] + far)
    ]
    q_rows = (dot_halves(normed, halves(w_query[...])) + b_query[...]) * (DH ** (-0.5))
    q_part[...] = q_rows.reshape(zs, piece, feats)
    queries[...] = q_rows.T
    queries.flush()
    q_land[z] = q_part[z]
    w_all[squad, core, z] = w_out[pl.ds(pl.multiple_of((squad * 2 + core) * fewer, 8), fewer), :]
    id_column[...] = jnp.broadcast_to(id_line, (LANES, rows)).T
    id_column.flush()
    small[...] = jnp.zeros(small.shape, F32)
    small[SMALL_B_DOWN : SMALL_B_DOWN + 1, :] = column_sum(cot[mine, :])
    d_act[...] = dot_full(cot[...], w_down[...], NT)
    up_high[...], up_low[...] = halves(w_up[...])
    for n, source in enumerate(far):
        arrived(kept.at[source], kept_recv.at[source])
        copies.append(
            send(kept.at[source], kept.at[source], kept_send.at[chips + n], kept_recv.at[source], sibling)
        )
    for source in [sib_blk] + far_siblings:
        arrived(kept.at[source], kept_recv.at[source])
    kept.flush()
    one = joined(kept[n, 2 * feats : 2 * feats + 8, :] for n in range(blocks))
    id_row[...] = jnp.concatenate([one, one], axis=0)
    id_row.flush()

    def mix_copies(index):
        some = pl.ds(pl.multiple_of(index * (8 * group), 8 * group), 8 * group)
        return [
            pltpu.make_async_remote_copy(
                src_ref=mixed.at[some],
                dst_ref=mixed_all.at[z, some],
                send_sem=mix_send.at[n, index],
                recv_sem=mix_recv.at[n, index],
                device_id={"head": peer},
                device_id_type=MESH,
            )
            for n, peer in enumerate(peers)
        ]

    squad_copies = [
        pltpu.make_async_remote_copy(
            src_ref=w_all.at[squad, core],
            dst_ref=w_all.at[squad, core],
            send_sem=wx_send.at[n - 1],
            recv_sem=wx_recv.at[n - 1],
            device_id={
                "dp": lax.div(lax.rem(squad + n, squads), close),
                "blk": (base + lax.rem(lax.rem(squad + n, squads), close)) * 2 + core,
            },
            device_id_type=MESH,
        )
        for n in range(1, squads)
    ]

    key_copies = [
        pltpu.make_async_remote_copy(
            src_ref=k_all.at[blk, peer],
            dst_ref=k_all.at[blk, peer],
            send_sem=kf_send.at[n, m],
            recv_sem=k_recv.at[blk, peer],
            device_id={"blk": target},
            device_id_type=MESH,
        )
        for n, peer in enumerate(peers)
        for m, target in enumerate([sib_blk] + far)
    ]

    def step(index, carry):
        slot = lax.rem(index, 2)
        pair_copy(index, slot).wait()
        low_row = pl.multiple_of(index * (8 * group), 8 * group)
        some = pl.ds(low_row, 8 * group)
        values = pl.ds(pl.multiple_of(feats + low_row, 8), 8 * group)
        mixed[some, :] = attend_group(
            pair_buf.at[slot],
            queries[some, :],
            joined(kept[n, some, :] for n in range(blocks)),
            joined(kept[n, values, :] for n in range(blocks)),
            id_column, id_row, log_sums, index * group, score, high, low,
        )
        for copy in mix_copies(index):
            copy.start()

        @pl.when(index == groups // 2)
        def _():
            for n, source in enumerate(sources):
                arrived(w_all.at[squad, core, source], w_recv.at[n])
            for copy in squad_copies:
                copy.start()

        @pl.when(index == max(0, groups - 2))
        def _():
            for peer in peers:
                arrived(k_all.at[blk, peer], k_recv.at[blk, peer])
            for copy in key_copies:
                copy.start()

        @pl.when(index + 2 < groups)
        def _():
            pair_copy(index + 2, slot).start()

        return carry

    lax.fori_loop(0, groups, step, 0)
    mixed.flush()
    log_sums.flush()
    squad_sources = [lax.rem(squad + squads - n, squads) for n in range(squads)]
    for n, source in enumerate(squad_sources):
        ready = w_all.at[source, core]
        if n >= 1:
            arrived(ready, wx_recv.at[n - 1])
        copies.append(send(ready, ready, wf_send.at[n], wf_recv.at[n], sibling))
    for n, source in enumerate(squad_sources):
        arrived(w_all.at[source, other_core], wf_recv.at[n])
    outs = halves(
        jnp.concatenate([w_all[s, kind, n] for n in range(zs) for s in range(squads) for kind in range(2)], axis=0)
    )
    mixed_all[z] = mixed[...]
    for n, source in enumerate(sources):
        for index in range(groups):
            some = pl.ds(index * (8 * group), 8 * group)
            arrived(mixed_all.at[source, some], mix_recv.at[n, index])
    copies += [
        send(q_part.at[peer], q_land.at[z], q_send.at[n], q_recv.at[n], {"head": peer})
        for n, peer in enumerate(peers)
    ]
    ups = up_high[...], up_low[...]
    mixed_rows = mixed_all[...].reshape(zs * feats, rows).T
    hidden_rows = atoms[...] + dot_halves(halves(mixed_rows), outs) + b_out[...]
    hidden_two[...] = hidden_rows
    normal, rate = normalize(hidden_rows)
    normal_two[...] = normal
    rate_two[...] = jnp.broadcast_to(rate, rate_two.shape)
    normed = normal * gain[...] + bias[...]
    pre = dot_halves(halves(normed), ups) + b_up[...]
    phi = 0.5 * (1.0 + lax.erf(pre * math.sqrt(0.5)))
    act = pre * phi
    d_pre = d_act[...] * (phi + pre * jnp.exp(-0.5 * pre * pre) * (1.0 / math.sqrt(2.0 * math.pi)))
    d_pres = halves(d_pre)
    cots, downs = halves(cot[...]), halves(w_down[...])
    part[...] = dot_halves(d_pres, ups, NT).reshape(zs, piece, width)
    copies += [
        send(part.at[peer], landed.at[z], part_send.at[n], part_recv.at[n], {"head": peer})
        for n, peer in enumerate(peers)
    ]
    landed[z] = part[z]
    ups_part[...] = dot_halves(halves(normed.T), d_pres).reshape(ups_part.shape)
    copies.append(send(ups_part.at[:, other_core], ups_sib, sib_send.at[0], sib_recv.at[0], sibling))
    downs_part[...] = dot_halves(halves(act.T), cots).reshape(downs_part.shape)
    copies.append(send(downs_part.at[:, other_core], downs_sib, sib_send.at[1], sib_recv.at[1], sibling))
    down[...] = dot_halves(halves(act), downs)
    out_mine[...] = hidden_two[mine, :] + down[mine, :] + b_down[...]
    out_mine.flush()
    small[SMALL_B_UP : SMALL_B_UP + 1, 0 : d_pre.shape[1]] = column_sum(d_pre)
    for kind, (parts, sib, go, got) in enumerate(
        [(ups_part, ups_sib, ups_go, ups_got), (downs_part, downs_sib, downs_go, downs_got)]
    ):
        arrived(sib, sib_recv.at[kind])
        go[...] = sib[...] + parts[:, core]
        copies += [
            send(
                go.at[peer], got.at[team], g_send.at[kind, n], g_recv.at[kind, team],
                team_device(peer, core, chips),
            )
            for n, peer in enumerate(far_teams)
        ]
        got[team] = go[team]
    for n, source in enumerate(far):
        for m, peer in enumerate(peers):
            ready = k_all.at[source, peer]
            arrived(ready, k_recv.at[source, peer])
            copies.append(send(ready, ready, ks_send.at[n, m], k_recv.at[source, peer], sibling))
    for n, source in enumerate(sources):
        arrived(q_land.at[source], q_recv.at[n])
    for n in range(zs):
        q_all[n] = q_land[n].T
    for n in range(blocks):
        k_all[n, z] = kept[n, 0:feats, :]
    for source in [sib_blk] + far_siblings:
        for peer in peers:
            arrived(k_all.at[source, peer], k_recv.at[source, peer])
    squares[...] = jnp.zeros(squares.shape, F32)
    at_once = 4
    rounds = heads // at_once

    def square_step(index, carry):
        there = lax.div(index, rounds)
        some = pl.ds(pl.multiple_of(lax.rem(index, rounds) * (8 * at_once), 8 * at_once), 8 * at_once)
        q_some = q_all[there, some, :]
        k_some = joined(k_all[n, there, some, :] for n in range(blocks))
        added = None
        for h in range(at_once):
            head = slice(8 * h, 8 * h + 8)
            q_high, q_low = wide_halves(q_some[head])
            k_high, k_low = wide_halves(k_some[head])
            value = dot(
                stacked([q_high, q_high, q_low, q_low]), stacked([k_high, k_low, k_high, k_low]), TN
            )
            added = value * value if added is None else added + value * value
        squares[...] += added
        return carry

    lax.fori_loop(0, zs * rounds, square_step, 0)
    same = id_column[mine, 0:1] == id_row[0:1, :]
    norms = jnp.sqrt(squares[...] + 1.0)
    terms = jnp.where(same, jnp.log1p(jnp.exp(norms - math.sqrt(zs * heads))), 0.0)
    number = jnp.where(same, 1.0, 0.0)

    def total(value):
        return jnp.sum(jnp.sum(value, axis=1, keepdims=True), axis=0, keepdims=True)

    lane = lax.broadcasted_iota(jnp.int32, (1, width), 1)
    small[SMALL_PENALTY : SMALL_PENALTY + 1, :] = jnp.where(
        lane == 0, total(terms), jnp.where(lane == 1, total(number), 0.0)
    )
    for n, source in enumerate(sources):
        arrived(landed.at[source], part_recv.at[n])
    d_normed = functools.reduce(jnp.add, [landed[n] for n in range(zs)])
    normal = normal_two[mine, :]
    d_rows = cot[mine, :] + normalize_back(d_normed, gain[...], normal, rate_two[mine, 0:1])
    d_halves = halves(d_rows)
    for n in range(zs):
        some = slice(n * feats, (n + 1) * feats)
        back[n] = dot_halves(d_halves, (outs[0][some], outs[1][some]), NT)
    copies += [
        send(back.at[peer], back_landed.at[z], back_send.at[n], back_recv.at[n], {"head": peer})
        for n, peer in enumerate(peers)
    ]
    back_landed[z] = back[z]
    d_hidden[...] = d_rows
    d_hidden.flush()
    for peer, parcel in zip(peers, parcels, strict=True):
        parcel[0:piece, :] = down[pl.ds(pl.multiple_of(peer * piece, 8), piece), :]
        parcel[piece : 2 * piece, :] = d_rows
        parcel.flush()
    small[SMALL_LN2_GAIN : SMALL_LN2_GAIN + 1, :] = column_sum(d_normed * normal)
    small[SMALL_LN2_BIAS : SMALL_LN2_BIAS + 1, :] = column_sum(d_normed)
    small[SMALL_B_OUT : SMALL_B_OUT + 1, :] = column_sum(d_rows)
    small.flush()
    for kind, got in enumerate([ups_got, downs_got]):
        for peer in far_teams:
            arrived(got.at[peer], g_recv.at[kind, peer])
    up_share, down_share = [
        functools.reduce(jnp.add, [got[n] for n in range(teams)]) for got in (ups_got, downs_got)
    ]
    for rows_of, columns_of, there in side_by_side(*up_share.shape, width):
        shares[there, columns_of] = up_share[rows_of]
    shares[there.stop :, :] = down_share
    shares.flush()
    for n, source in enumerate(sources):
        arrived(back_landed.at[source], back_recv.at[n])
    d_mixed[...] = back_landed[...].reshape(rows, feats).T
    d_mixed.flush()
    for copy in copies + squad_copies + key_copies:
        copy.wait_send()

    def drain(index, carry):
        for copy in mix_copies(index):
            copy.wait_send()
        return carry

    lax.fori_loop(0, groups, drain, 0)


def front(zs, dps, teams, pair, *operands):
    _, heads, rows, cols = pair.shape
    feats, blocks = heads * DH, cols // rows
    width, units = operands[0].shape[1], operands[12].shape[1]
    piece, group, hops = rows // zs, GROUP, zs - 1
    squads = dps * min(blocks // 2, max(1, feats // (2 * dps * 8)))
    up_rows, down_rows = width // (2 * teams), units // (2 * teams)
    groups = heads // group
    slab = pltpu.VMEM((zs, piece, width), F32)
    narrow = pltpu.VMEM((zs, piece, feats), F32)
    one_up, one_down = pltpu.VMEM((teams, up_rows, units), F32), pltpu.VMEM((teams, down_rows, width), F32)
    dma = pltpu.SemaphoreType.DMA
    return staged_call(
        front_kernel,
        "front",
        operands,
        [
            (feats, rows), (blocks, 2 * feats + 8, rows), (rows, LANES), (heads, rows, LANES), (feats, rows),
            (STRIP, cols), (feats, rows), (piece, width), (piece, width),
            (up_rows * units // width + down_rows, width), (SMALL_ROWS, width),
        ]
        + [(2 * piece, width)] * (zs - 1),
        [
            pltpu.VMEM((2, group, rows, cols), F32),
            pltpu.VMEM((group, rows, cols), F32),
            pltpu.VMEM((group, rows, cols), BF16),
            pltpu.VMEM((group, rows, cols), BF16),
            narrow, narrow,
            pltpu.VMEM((zs, feats, piece), F32),
            pltpu.VMEM((blocks, zs, feats, rows), F32),
            pltpu.VMEM((squads, 2, zs, feats // (2 * squads), width), F32),
            pltpu.VMEM((piece, cols), F32),
            pltpu.VMEM((zs, feats, rows), F32),
            pltpu.VMEM((rows, width), F32),
            pltpu.VMEM((rows, width), F32),
            pltpu.VMEM((rows, units), F32),
            pltpu.VMEM((width, units), BF16),
            pltpu.VMEM((width, units), BF16),
            pltpu.VMEM((rows, width), F32),
            pltpu.VMEM((rows, LANES), F32),
            slab, slab, narrow, narrow,
            pltpu.VMEM((teams, 2, up_rows, units), F32),
            one_up, one_up, one_up,
            pltpu.VMEM((teams, 2, down_rows, width), F32),
            one_down, one_down, one_down,
            dma((2,)),
            dma((blocks,)), dma((blocks,)),
            dma((hops,)), dma((hops, blocks // 2)), dma((max(1, blocks // 2 - 1), hops)), dma((blocks, zs)),
            dma((hops,)), dma((hops,)),
            dma((hops,)), dma((hops,)), dma((max(1, squads - 1),)), dma((max(1, squads - 1),)),
            dma((squads,)), dma((squads,)),
            dma((hops, groups)), dma((hops, groups)),
            dma((hops,)), dma((hops,)),
            dma((hops,)), dma((hops,)),
            dma((2,)), dma((2,)),
            dma((2, teams)), dma((2, teams)),
        ],
        FRONT_MB,
        remote=0,
        raw=(pair,),
    )


def finish_kernel(operands, results, scratch, raw):
    (
        out_mine, d_hidden, atoms, gain, bias, w_query, mixed, small_in, w_key, w_value,
    ) = operands[:10]
    parcels = operands[10 : 9 + lax.axis_size("head")]
    chip_shares = operands[9 + lax.axis_size("head") :]
    grad_atoms, out_atoms, total_grads, grad_up, grad_down, small, penalty = results
    (
        sib_keys, sib_values, go_keys, go_values, got_keys, got_values,
        part, landed, grads, sib_grads, go_grads, got_grads, hidden_all, small_z, small_all,
        sib_send, sib_recv, kv_send, kv_recv, part_send, part_recv, back_send, back_recv,
        g_send, g_recv, t_send, t_recv, f_send, b_send, b_recv, bf_send, out_send, out_recv,
        small_z_send, small_z_recv, small_send, small_recv, own_heads, heads_sem,
    ) = scratch
    (d_heads,) = raw
    chips, feats, rows = own_heads.shape[0] - 1, d_heads.shape[2] // 2, d_heads.shape[3]
    heads_copy = pltpu.make_async_copy(d_heads.at[pl.ds(0, chips + 1)], own_heads, heads_sem.at[0])
    heads_copy.start()
    zs, piece, width = part.shape
    teams, _, share, _ = grads.shape
    blk, z, dp = lax.axis_index("blk"), lax.axis_index("head"), lax.axis_index("dp")
    core, chip = lax.rem(blk, 2), lax.div(blk, 2)
    other_core = 1 - core
    sibling = {"blk": blk + 1 - 2 * core}
    peers = others(z, zs)
    team = dp * chips + chip
    far_teams = others(team, teams)
    far_chips = others(chip, chips)
    place = team * 2 + core
    far_places = others(place, teams * 2)
    plane = [team_device(lax.div(value, 2), lax.rem(value, 2), chips) for value in far_places]
    meeting = [{"head": peer} for peer in peers] + plane
    greet(meeting)
    meet(meeting)
    copies = [
        send(
            d_heads.at[pl.ds(0, chips), other_core, pl.ds(kind * feats, feats)],
            sib, sib_send.at[kind], sib_recv.at[kind], sibling,
        )
        for kind, sib in enumerate([sib_keys, sib_values])
    ]
    mine = pl.ds(pl.multiple_of(z * piece, 8), piece)
    out_atoms[mine, :] = functools.reduce(jnp.add, [parcel[0:piece, :] for parcel in parcels], out_mine[...])
    copies += [
        send(out_atoms.at[mine], out_atoms.at[mine], out_send.at[n], out_recv.at[z], {"head": peer})
        for n, peer in enumerate(peers)
    ]

    def big_rows(result, source, kind):
        count = result.shape[0] // (2 * teams)
        return result.at[pl.ds(pl.multiple_of((source * 2 + kind) * count, 8), count)]

    partners = others(dp, lax.axis_size("dp"))
    for n in range(chips):
        source = dp * chips + lax.rem(chip + chips - n, chips)
        up_there, down_there = big_rows(grad_up, source, core), big_rows(grad_down, source, core)
        for rows_of, columns_of, there in side_by_side(*up_there.shape, width):
            up_there[rows_of, :] = chip_shares[n][there, columns_of]
        down_there[...] = chip_shares[n][there.stop :, :]
        for kind, ready in enumerate([up_there, down_there]):
            copies += [
                send(ready, ready, b_send.at[kind, n, m], b_recv.at[kind, source, core], {"dp": partner})
                for m, partner in enumerate(partners)
            ]
    heads_copy.wait()
    d_queries = own_heads[chips, 0, 0:feats, :]
    for kind, (sib, go, got) in enumerate([(sib_keys, go_keys, got_keys), (sib_values, go_values, got_values)]):
        arrived(sib, sib_recv.at[kind])
        go[...] = sib[...] + own_heads[0:chips, core, kind * feats : (kind + 1) * feats, :]
        copies += [
            send(
                go.at[peer], got.at[chip], kv_send.at[kind, n], kv_recv.at[kind, chip],
                {"blk": peer * 2 + core},
            )
            for n, peer in enumerate(far_chips)
        ]
    got_keys[chip] = go_keys[chip]
    got_values[chip] = go_values[chip]
    normal, rate = normalize(atoms[...])
    normed = halves(normal * gain[...] + bias[...])
    dq_rows = d_queries.T
    d_normed = dot_full(dq_rows, w_query[...], NT)
    grad_q = dot_halves(halves(d_queries), normed)
    small_z[z] = small_in[0:8, :]
    hidden_all[z] = d_hidden[...]
    for n, parcel in enumerate(parcels):
        hidden_all[lax.rem(z + zs - 1 - n, zs)] = parcel[piece : 2 * piece, :]
    grad_o = dot_full(mixed[...], hidden_all[...].reshape(rows, width))
    for peer in far_chips:
        arrived(got_keys.at[peer], kv_recv.at[0, peer])
        arrived(got_values.at[peer], kv_recv.at[1, peer])
    dk = functools.reduce(jnp.add, [got_keys[n] for n in range(chips)])
    dv = functools.reduce(jnp.add, [got_values[n] for n in range(chips)])
    dv_rows = dv.T
    d_normed = (
        d_normed + dot_full(dk.T, w_key[...], NT) + dot_full(dv_rows, w_value[...], NT)
    )
    part[...] = d_normed.reshape(zs, piece, width)
    copies += [
        send(part.at[peer], landed.at[z], part_send.at[n], part_recv.at[z], {"head": peer})
        for n, peer in enumerate(peers)
    ]
    landed[z] = part[z]
    grad_k = dot_halves(halves(dk), normed)
    grad_v = dot_halves(halves(dv), normed)
    grads[...] = jnp.concatenate([grad_q, grad_k, grad_v, grad_o], axis=0).reshape(grads.shape)
    copies.append(send(grads.at[:, other_core], sib_grads, sib_send.at[2], sib_recv.at[2], sibling))
    arrived(sib_grads, sib_recv.at[2])
    go_grads[...] = sib_grads[...] + grads[:, core]
    copies += [
        send(
            go_grads.at[peer], got_grads.at[team], g_send.at[n], g_recv.at[team], team_device(peer, core, chips)
        )
        for n, peer in enumerate(far_teams)
    ]
    got_grads[team] = go_grads[team]
    for peer in peers:
        arrived(landed.at[peer], part_recv.at[peer])
    d_normed = functools.reduce(jnp.add, [landed[n] for n in range(zs)])
    normal, rate = normalize(atoms[mine, :])
    grad_atoms[mine, :] = d_hidden[...] + normalize_back(d_normed, gain[...], normal, rate)
    small_z[z, SMALL_LN1_GAIN : SMALL_LN1_GAIN + 1, :] = column_sum(d_normed * normal)
    small_z[z, SMALL_LN1_BIAS : SMALL_LN1_BIAS + 1, :] = column_sum(d_normed)
    copies += [
        send(small_z.at[z], small_z.at[z], small_z_send.at[n], small_z_recv.at[z], {"head": peer})
        for n, peer in enumerate(peers)
    ]
    copies += [
        send(grad_atoms.at[mine], grad_atoms.at[mine], back_send.at[n], back_recv.at[z], {"head": peer})
        for n, peer in enumerate(peers)
    ]
    for peer in far_teams:
        arrived(got_grads.at[peer], g_recv.at[peer])
    total_grads[team, core] = functools.reduce(jnp.add, [got_grads[n] for n in range(teams)])
    ready = total_grads.at[team, core]
    copies.append(send(ready, ready, t_send.at[0], t_recv.at[team, core], sibling))
    copies += [
        send(ready, ready, t_send.at[n + 1], t_recv.at[team, core], team_device(peer, core, chips))
        for n, peer in enumerate(far_teams)
    ]
    for peer in peers:
        arrived(small_z.at[peer], small_z_recv.at[peer])
    small_all[place, 0:8, :] = functools.reduce(jnp.add, [small_z[n] for n in range(zs)])
    small_all[place, 8:16, :] = small_in[8:16, :]
    small_all[place, SMALL_B_QUERY : SMALL_B_QUERY + 1, 0:feats] = column_sum(dq_rows)
    small_all[place, SMALL_B_VALUE : SMALL_B_VALUE + 1, 0:feats] = column_sum(dv_rows)
    copies += [
        send(small_all.at[place], small_all.at[place], small_send.at[n], small_recv.at[place], target)
        for n, target in enumerate(plane)
    ]
    for n, peer in enumerate(far_teams):
        ready = total_grads.at[peer, core]
        arrived(ready, t_recv.at[peer, core])
        copies.append(send(ready, ready, f_send.at[n], t_recv.at[peer, core], sibling))
    for kind, result in enumerate([grad_up, grad_down]):
        for n in range(teams):
            ready = big_rows(result, n, core)

            @pl.when(lax.div(n, chips) != dp)
            def _(ready=ready, sem=b_recv.at[kind, n, core]):
                arrived(ready, sem)

            copies.append(send(ready, ready, bf_send.at[kind, n], b_recv.at[kind, n, core], sibling))
    for source in far_places:
        arrived(small_all.at[source], small_recv.at[source])
    summed = functools.reduce(jnp.add, [small_all[n] for n in range(2 * teams)])
    small[...] = summed
    ends = summed[SMALL_PENALTY : SMALL_PENALTY + 1, :]
    penalty[...] = ends[:, 0:1] / ends[:, 1:2]
    for peer in [team] + far_teams:
        arrived(total_grads.at[peer, other_core], t_recv.at[peer, other_core])
    total_grads.flush()
    for kind, result in enumerate([grad_up, grad_down]):
        for n in range(teams):
            arrived(big_rows(result, n, other_core), b_recv.at[kind, n, other_core])
        result.flush()
    for peer in peers:
        there = pl.ds(pl.multiple_of(peer * piece, 8), piece)
        arrived(out_atoms.at[there], out_recv.at[peer])
    out_atoms.flush()
    for peer in peers:
        there = pl.ds(pl.multiple_of(peer * piece, 8), piece)
        arrived(grad_atoms.at[there], back_recv.at[peer])
    for copy in copies:
        copy.wait_send()


def finish(zs, dps, units, d_heads, *operands):
    atoms = operands[2]
    chips, feats, rows = lax.axis_size("blk") // 2, d_heads.shape[2] // 2, d_heads.shape[3]
    width = atoms.shape[1]
    piece = rows // zs
    teams = dps * chips
    share = 4 * feats // (2 * teams)
    some = pltpu.VMEM((chips, feats, rows), F32)
    slab = pltpu.VMEM((zs, piece, width), F32)
    one = pltpu.VMEM((teams, share, width), F32)
    dma = pltpu.SemaphoreType.DMA
    return staged_call(
        finish_kernel,
        "finish",
        operands,
        [
            (rows, width),
            (rows, width),
            (teams, 2, share, width),
            (width, units),
            (units, width),
            (SMALL_ROWS, width),
            (1, 1),
        ],
        [some] * 6
        + [slab, slab, pltpu.VMEM((teams, 2, share, width), F32), one, one, one, slab]
        + [
            pltpu.VMEM((zs, 8, width), F32),
            pltpu.VMEM((2 * teams, SMALL_ROWS, width), F32),
            dma((3,)), dma((3,)),
            dma((2, chips)), dma((2, chips)),
            dma((zs,)), dma((zs,)),
            dma((zs,)), dma((zs,)),
            dma((teams,)), dma((teams,)),
            dma((teams,)), dma((teams, 2)), dma((teams,)),
            dma((2, chips, dps)), dma((2, teams, 2)), dma((2, teams)),
            dma((zs,)), dma((zs,)),
            dma((zs,)), dma((zs,)),
            dma((2 * teams,)), dma((2 * teams,)),
            pltpu.VMEM((chips + 1, 2, 2 * feats, rows), F32), dma((1,)),
        ],
        FINISH_MB,
        remote=2,
        near_in=range(10, len(operands)),
        raw=(d_heads,),
        near_out=range(7),
    )


def place_kernel(operands, results, scratch, raw):
    total_grads, small, penalty_in = operands
    penalty, grad_query, grad_key, grad_value, grad_out = results[:5]
    penalty[...] = penalty_in[...]
    feats, width = grad_out.shape
    done = total_grads[...].reshape(4 * feats, width)
    grad_query[...] = done[0:feats].T
    grad_query.flush()
    grad_key[...] = done[feats : 2 * feats].T
    grad_key.flush()
    grad_value[...] = done[2 * feats : 3 * feats].T
    grad_value.flush()
    grad_out[...] = done[3 * feats :]
    grad_out.flush()
    for result, row in zip(results[5:], SMALL_OUTPUTS, strict=True):
        result[...] = small[row : row + 1, 0 : result.shape[1]]


SMALL_OUTPUTS = (
    SMALL_LN1_GAIN, SMALL_LN1_BIAS, SMALL_B_QUERY, SMALL_B_VALUE, SMALL_B_OUT, SMALL_LN2_GAIN, SMALL_LN2_BIAS,
    SMALL_B_UP, SMALL_B_DOWN,
)


def place(feats, units, straight, *operands):
    width = operands[1].shape[1]
    lengths = {SMALL_B_QUERY: feats, SMALL_B_VALUE: feats, SMALL_B_UP: units}
    return staged_call(
        place_kernel,
        "place",
        operands,
        [(1, 1)]
        + [(width, feats)] * 3
        + [(feats, width)]
        + [(1, lengths.get(row, width)) for row in SMALL_OUTPUTS],
        [],
        PLACE_MB,
        straight=straight,
        near_in=(0, 1, 2),
        near_straight=True,
    )


def local(
    zs, dps,
    atoms, pair, mol_ids, ln1_gain, ln1_bias, w_query, b_query, w_key, w_value, b_value, w_out, b_out,
    ln2_gain, ln2_bias, w_up, b_up, w_down, b_down, cot_atoms, cot_pair,
):
    blocks = pair.shape[3] // pair.shape[2]
    inputs, cot = atoms[0], cot_atoms[0]

    def line(value):
        return value.reshape(1, -1)

    (
        queries, kept, id_column, log_sums, mixed, id_row, d_mixed, out_mine, d_hidden, shares, small, *parcels,
    ) = front(
        zs, dps, dps * blocks // 2, pair,
        inputs, mol_ids, line(ln1_gain), line(ln1_bias), w_key, w_value, line(b_value), w_query, line(b_query),
        w_out, cot, w_down, w_up, line(b_out), line(ln2_gain), line(ln2_bias), line(b_up),
        line(b_down),
    )
    parcels = [
        lax.ppermute(parcel, "head", [(source, (source + n + 1) % zs) for source in range(zs)])
        for n, parcel in enumerate(parcels)
    ]
    chips = blocks // 2
    chip_shares = [shares] + [
        lax.ppermute(shares, "blk", [(2 * c + core, 2 * ((c + n) % chips) + core) for c in range(chips) for core in range(2)])
        for n in range(1, chips)
    ]
    out_pair, grad_pair, d_heads = attend_back(
        pair, cot_pair, queries, kept, mixed, d_mixed, log_sums, id_column, id_row
    )
    grad_atoms, out_atoms, total_grads, grad_up, grad_down, small, penalty = finish(
        zs, dps, w_up.shape[1],
        d_heads, out_mine, d_hidden, inputs, line(ln1_gain), line(ln1_bias), w_query, mixed,
        small, w_key, w_value, *parcels, *chip_shares,
    )
    placed = place(
        w_query.shape[1], w_up.shape[1],
        [grad_atoms, out_atoms, grad_up, grad_down],
        total_grads, small, penalty,
    )
    grad_atoms, out_atoms, grad_up, grad_down, penalty, grad_query, grad_key, grad_value, grad_out = placed[:9]
    (
        grad_ln1_gain, grad_ln1_bias, grad_b_query, grad_b_value, grad_b_out, grad_ln2_gain, grad_ln2_bias,
        grad_b_up, grad_b_down,
    ) = [value.reshape(-1) for value in placed[9:]]
    return (
        out_atoms[None],
        out_pair,
        penalty[0, 0],
        grad_atoms[None],
        grad_pair,
        grad_ln1_gain,
        grad_ln1_bias,
        grad_query,
        grad_b_query,
        grad_key,
        grad_value,
        grad_b_value,
        grad_out,
        grad_b_out,
        grad_ln2_gain,
        grad_ln2_bias,
        grad_up,
        grad_b_up,
        grad_down,
        grad_b_down,
    )


def solution(mesh):
    rows, pairs = P("dp", "blk", None), P("dp", "head", "blk", None)
    columns = P(None, "head")
    return jax.shard_map(
        functools.partial(local, mesh.shape["head"], mesh.shape["dp"]),
        mesh=mesh,
        in_specs=(
            rows, pairs, P("dp", "blk"), P(), P(), columns, P("head"), columns, columns, P("head"),
            P("head", None), P(), P(), P(), columns, P("head"), P("head", None), P(), rows, pairs,
        ),
        out_specs=(
            rows, pairs, P(), rows, pairs, P(), P(), columns, P("head"), columns, columns, P("head"),
            P("head", None), P(), P(), P(), columns, P("head"), P("head", None), P(),
        ),
        check_vma=False,
    )
```

```python
import functools
import math

import jax
import jax.numpy as jnp
from jax import lax
from jax.experimental import pallas as pl
from jax.experimental.pallas import tpu as pltpu
from jax.sharding import PartitionSpec as P

DH = 8
LANES = 128
STRIP = 16
CHUNK = 256
GROUP = 2
FRONT_MB, BACK_MB, FINISH_MB, PLACE_MB = 58, 60, 40, 32
NORM_EPS = 1e-05
MASK_FILL = -1e30
F32 = jnp.float32
BF16 = jnp.bfloat16
MESH = pl.DeviceIdType.MESH
NN = (((1,), (0,)), ((), ()))
NT = (((1,), (1,)), ((), ()))
TN = (((0,), (0,)), ((), ()))
VMEM = pl.BlockSpec(memory_space=pltpu.VMEM)


def dot(left, right, dims=NN):
    return lax.dot_general(left, right, dims, preferred_element_type=F32)


def halves(value):
    high = value.astype(BF16)
    return high, (value - high.astype(F32)).astype(BF16)


def dot_halves(left, right, dims=NN):
    return dot(left[0], right[0], dims) + (
        dot(left[0], right[1], dims) + dot(left[1], right[0], dims)
    )


def dot_full(left, right, dims=NN):
    return dot_halves(halves(left), halves(right), dims)


def normalize(inputs):
    centred = inputs - jnp.mean(inputs, -1, keepdims=True)
    rate = lax.rsqrt(jnp.mean(centred * centred, -1, keepdims=True) + NORM_EPS)
    return centred * rate, rate


def normalize_back(grad, gain, normal, rate):
    scaled = grad * gain
    return rate * (
        scaled
        - jnp.mean(scaled, -1, keepdims=True)
        - normal * jnp.mean(scaled * normal, -1, keepdims=True)
    )


def column_sum(value):
    return jnp.sum(value, 0, keepdims=True)


def send(src, dst, send_sem, recv_sem, target):
    copy = pltpu.make_async_remote_copy(
        src_ref=src,
        dst_ref=dst,
        send_sem=send_sem,
        recv_sem=recv_sem,
        device_id=target,
        device_id_type=MESH,
    )
    copy.start()
    return copy


def arrived(ref, sem):
    pltpu.make_async_remote_copy(
        src_ref=ref, dst_ref=ref, send_sem=sem, recv_sem=sem, device_id={}, device_id_type=MESH
    ).wait_recv()


def greet(targets):
    for target in targets:
        pl.semaphore_signal(pltpu.get_barrier_semaphore(), inc=1, device_id=target, device_id_type=MESH)


def meet(targets):
    pl.semaphore_wait(pltpu.get_barrier_semaphore(), len(targets))


def others(index, count):
    return [lax.rem(index + step, count) for step in range(1, count)]


class Operand:
    def __init__(self, source, slot, sem):
        self.source, self.slot, self.shape = source, slot, slot.shape
        self.copy = None if sem is None else pltpu.make_async_copy(source, slot, sem)
        if self.copy is not None:
            self.copy.start()

    @property
    def ref(self):
        if self.copy is not None:
            self.copy.wait()
            self.copy = None
        return self.slot

    def __getitem__(self, index):
        return self.ref[index]


class Result:
    def __init__(self, target, slot, sem):
        self.slot, self.shape, self.at = slot, slot.shape, slot.at
        self.copy = None if sem is None else pltpu.make_async_copy(slot, target, sem)
        self.begun = self.copy is None

    def __setitem__(self, index, value):
        self.slot[index] = value

    def __getitem__(self, index):
        return self.slot[index]

    def flush(self):
        if not self.begun:
            self.copy.start()
            self.begun = True


def staged_call(
    kernel, name, operands, results, scratch, megabytes,
    remote=None, raw=(), straight=(), raw_results=(), cost=None, near_in=(), near_out=(), near_straight=False,
):
    n_in, n_out, n_raw, n_straight = len(operands), len(results), len(raw), len(straight)
    n_left = len(raw_results)
    far_in = [n for n in range(n_in) if n not in near_in]
    far_out = [n for n in range(n_out) if n not in near_out]

    def body(*refs):
        sources, left, refs = refs[:n_in], refs[n_in : n_in + n_raw], refs[n_in + n_raw :]
        moved, refs = refs[:n_straight], refs[n_straight:]
        arrays, refs = refs[:n_straight], refs[n_straight:]
        left, refs = left + refs[:n_left], refs[n_left:]
        targets, refs = refs[:n_out], refs[n_out:]
        in_slots, refs = dict(zip(far_in, refs)), refs[len(far_in) :]
        out_slots, refs = dict(zip(far_out, refs)), refs[len(far_out) :]
        in_sem, out_sem, move_sem, refs = refs[0], refs[1], refs[2], refs[3:]
        through, loads = moved, []
        if not near_straight:
            through, refs = refs[:n_straight], refs[n_straight:]
            loads = [pltpu.make_async_copy(moved[n], through[n], move_sem.at[n]) for n in range(n_straight)]
        moves = [pltpu.make_async_copy(through[n], arrays[n], move_sem.at[n]) for n in range(n_straight)]
        for load in loads:
            load.start()
        ins = [
            Operand(sources[n], in_slots.get(n, sources[n]), in_sem.at[far_in.index(n)] if n in in_slots else None)
            for n in range(n_in)
        ]
        outs = [
            Result(targets[n], out_slots.get(n, targets[n]), out_sem.at[far_out.index(n)] if n in out_slots else None)
            for n in range(n_out)
        ]
        for load in loads:
            load.wait()
        for move in moves:
            move.start()
        kernel(ins, outs, refs, left)
        for operand in ins:
            operand.ref
        for result in outs:
            result.flush()
        for copy in moves + [result.copy for result in outs if result.copy is not None]:
            copy.wait()

    hbm, vmem = pl.BlockSpec(memory_space=pltpu.HBM), pl.BlockSpec(memory_space=pltpu.VMEM)
    extra = {} if remote is None else {"collective_id": remote, "has_side_effects": True}
    return pl.pallas_call(
        body,
        out_shape=[jax.ShapeDtypeStruct(value.shape, value.dtype) for value in straight]
        + [jax.ShapeDtypeStruct(shape, F32) for shape in raw_results]
        + [jax.ShapeDtypeStruct(shape, F32) for shape in results],
        in_specs=[vmem if n in near_in else hbm for n in range(n_in)]
        + [hbm] * n_raw
        + [vmem if near_straight else hbm] * n_straight,
        out_specs=[hbm] * (n_straight + n_left) + [vmem if n in near_out else hbm for n in range(n_out)],
        scratch_shapes=[pltpu.VMEM(operands[n].shape, operands[n].dtype) for n in far_in]
        + [pltpu.VMEM(results[n], F32) for n in far_out]
        + [pltpu.SemaphoreType.DMA((max(1, n),)) for n in (len(far_in), len(far_out), n_straight)]
        + ([] if near_straight else [pltpu.VMEM(value.shape, value.dtype) for value in straight])
        + list(scratch),
        compiler_params=pltpu.CompilerParams(vmem_limit_bytes=megabytes << 20, **extra),
        cost_estimate=cost,
        name=name,
    )(*operands, *raw, *straight)


def joined(pieces):
    return jnp.concatenate(list(pieces), axis=1)


def stacked(parts):
    return jnp.concatenate(parts, axis=0).astype(BF16)


def wide_halves(value):
    high = value.astype(BF16).astype(F32)
    return high, value - high


def attend_group(pair, queries, keys, values, id_column, id_row, log_sums, first, score, high, low):
    group, rows, cols = score.shape
    strips = rows // STRIP
    chunk = min(CHUNK, cols)
    mixed = []
    for g in range(group):
        head = slice(8 * g, 8 * g + 8)
        q_high, q_low = wide_halves(queries[head, :])
        k_high, k_low = wide_halves(keys[head, :])
        v_high, v_low = wide_halves(values[head, :])
        ones = jnp.ones_like(v_high)
        q_pack = stacked([q_high, q_high, q_low, q_low])
        k_pack = stacked([k_high, k_low, k_high, k_low])
        v_pack = stacked([v_high, v_low, ones, jnp.zeros_like(ones)])
        tops = [None] * strips
        for start in range(0, cols, chunk):
            part = slice(start, start + chunk)
            score[g, :, part] = dot(q_pack, k_pack[:, part], TN)
            for s in range(strips):
                line = pl.ds(s * STRIP, STRIP)
                own = id_column[line, :]
                for j in range(start, start + chunk, LANES):
                    tile = pl.ds(j, LANES)
                    value = pair[g, line, tile] + score[g, line, tile]
                    value = jnp.where(own == id_row[:, tile], value, MASK_FILL)
                    score[g, line, tile] = value
                    tops[s] = value if tops[s] is None else jnp.maximum(tops[s], value)
        tops = [
            jnp.broadcast_to(jnp.max(top, axis=1, keepdims=True), (STRIP, LANES)) for top in tops
        ]
        totals = [None] * strips
        gathered = None
        for start in range(0, cols, chunk):
            part = slice(start, start + chunk)
            for s in range(strips):
                line = pl.ds(s * STRIP, STRIP)
                for j in range(start, start + chunk, LANES):
                    tile = pl.ds(j, LANES)
                    weight = jnp.exp(score[g, line, tile] - tops[s])
                    high[g, line, tile], low[g, line, tile] = halves(weight)
                    totals[s] = weight if totals[s] is None else totals[s] + weight
            term = dot(v_pack[:, part], high[g, :, part], NT) + dot(
                v_pack[:, part], low[g, :, part], NT
            )
            gathered = term if gathered is None else gathered + term
        for s in range(strips):
            total = jnp.sum(totals[s], axis=1, keepdims=True)
            log_sums[first + g, pl.ds(s * STRIP, STRIP), :] = tops[s] + jnp.log(total)
        mixed.append((gathered[0:8] + gathered[8:16]) / gathered[16:17])
    return jnp.concatenate(mixed, axis=0)


def chunks_of(cols):
    chunk = min(CHUNK, cols)
    return [slice(start, start + chunk) for start in range(0, cols, chunk)]


def score_packs(queries, keys):
    q_high, q_low = wide_halves(queries)
    k_high, k_low = wide_halves(keys)
    return stacked([q_high, q_high, q_low, q_low]), stacked([k_high, k_low, k_high, k_low])


def attend_back_kernel(operands, results, scratch, raw):
    queries, kept, d_mixed, mixed, id_column, id_row = operands
    pair, cot, log_sums, out_pair, grad_pair, heads_out = raw
    pair_buf, cot_buf, log_buf, out_buf, grad_buf = scratch[:5]
    here = scratch[5:11]
    d_heads, in_sem, out_sem, heads_sem = scratch[11:]
    heads = pair.shape[1]
    feats = heads * DH
    depth, rows, cols = pair_buf.shape
    blocks = kept.shape[0]
    parts = chunks_of(cols)
    place = lax.broadcasted_iota(jnp.int32, (8, rows), 0)

    def inward(index):
        slot = lax.rem(index, depth)
        sources = (pair.at[0, index], cot.at[0, index], log_sums.at[index])
        return [
            pltpu.make_async_copy(source, buf.at[slot], in_sem.at[n, slot])
            for n, (source, buf) in enumerate(zip(sources, (pair_buf, cot_buf, log_buf), strict=True))
        ]

    def outward(index):
        slot = lax.rem(index, depth)
        return [
            pltpu.make_async_copy(buf.at[slot], array.at[0, index], out_sem.at[n, slot])
            for n, (array, buf) in enumerate([(out_pair, out_buf), (grad_pair, grad_buf)])
        ]

    for n in range(2):
        for copy in inward(n):
            copy.start()
    for operand in operands:
        operand.ref

    def rows_of(index):
        return pl.ds(pl.multiple_of(index * 8, 8), 8)

    def key_rows(index):
        return joined(kept[n, rows_of(index), :] for n in range(blocks))

    def value_row(index):
        return pl.ds(pl.multiple_of(feats + index * 8, 8), 8)

    def value_rows(index):
        return joined(kept[n, value_row(index), :] for n in range(blocks))

    def packs(index):
        head = rows_of(index)
        q_pack, k_pack = score_packs(queries[head, :], key_rows(index))
        v_high, v_low = wide_halves(value_rows(index))
        m_high, m_low = wide_halves(d_mixed[head, :])
        delta_high, rest = wide_halves(-column_sum(mixed[head, :] * d_mixed[head, :]))
        delta_mid, delta_low = wide_halves(rest)
        deltas = jnp.where(
            place == 0, delta_high, jnp.where(place == 1, delta_mid, jnp.where(place == 2, delta_low, 0.0))
        )
        m_pack = stacked([m_high, m_high, m_low, deltas])
        v_pack = stacked([v_high, v_low, v_high, jnp.ones_like(v_high)])
        return q_pack, k_pack, m_pack, v_pack

    def pairs(index):
        head = rows_of(index)
        return [stacked(wide_halves(value)) for value in (queries[head, :], key_rows(index), d_mixed[head, :])]

    def before(pack, part, there):
        q_pack, k_pack, m_pack, v_pack = pack
        there[0][:, part] = dot(q_pack, k_pack[:, part], TN)
        there[1][:, part] = dot(m_pack, v_pack[:, part], TN)

    def middle(index, slot, part, here):
        score, d_prob, p_high, p_low, g_high, g_low = here
        for s in range(rows // STRIP):
            line = pl.ds(s * STRIP, STRIP)
            own = id_column[line, :]
            log_sum = log_buf[slot, line, :]
            for j in range(part.start, part.stop, LANES):
                tile = pl.ds(j, LANES)
                value = pair_buf[slot, line, tile] + score[line, tile]
                out_buf[slot, line, tile] = value
                prob = jnp.exp(jnp.where(own == id_row[:, tile], value - log_sum, MASK_FILL))
                p_high[line, tile], p_low[line, tile] = halves(prob)
                grad = prob * d_prob[line, tile] + cot_buf[slot, line, tile]
                grad_buf[slot, line, tile] = grad
                g_high[line, tile], g_low[line, tile] = halves(grad)

    def both(left, high, low, dims):
        value = dot(left, high, dims) + dot(left, low, dims)
        return value[0:8] + value[8:16]

    def after(index, pair_of, part, there):
        q_pair, k_pair, m_pair = pair_of
        _, _, p_high, p_low, g_high, g_low = there
        head = rows_of(index)
        d_value = both(m_pair, p_high[:, part], p_low[:, part], NN)
        d_key = both(q_pair, g_high[:, part], g_low[:, part], NN)
        for n in range(part.start // rows, part.stop // rows):
            span = slice(n * rows - part.start, (n + 1) * rows - part.start)
            d_heads[n // 2, n % 2, head, :] = d_key[:, span]
            d_heads[n // 2, n % 2, value_row(index), :] = d_value[:, span]
        return both(k_pair[:, part], g_high[:, part], g_low[:, part], NT)

    def stage(index, carry):
        slot = lax.rem(index, depth)
        for copy in inward(index):
            copy.wait()

        @pl.when(index >= depth)
        def _():
            for copy in outward(index - depth):
                copy.wait()

        @pl.when(index == 0)
        def _():
            for n in range(2, depth - 1):
                for copy in inward(n):
                    copy.start()

        @pl.when(index + depth - 1 < heads)
        def _():
            for copy in inward(index + depth - 1):
                copy.start()

        next_packs, own_pairs = packs(index), pairs(index)
        d_query = None
        before(next_packs, parts[0], here)
        if len(parts) > 1:
            before(next_packs, parts[1], here)
        for n, part in enumerate(parts):
            if n + 2 < len(parts):
                before(next_packs, parts[n + 2], here)
            middle(index, slot, part, here)
            if n >= 1:
                term = after(index, own_pairs, parts[n - 1], here)
                d_query = term if d_query is None else d_query + term
        term = after(index, own_pairs, parts[-1], here)
        d_query = term if d_query is None else d_query + term
        d_heads[blocks // 2, 0, rows_of(index), :] = d_query * (DH ** (-0.5))
        for copy in outward(index):
            copy.start()
        return carry

    lax.fori_loop(0, heads, stage, 0)
    last = pltpu.make_async_copy(d_heads, heads_out.at[pl.ds(0, d_heads.shape[0])], heads_sem.at[0])
    last.start()
    for n in range(max(0, heads - depth), heads):
        for copy in outward(n):
            copy.wait()
    last.wait()


def attend_back(pair, cot, queries, kept, mixed, d_mixed, log_sums, id_column, id_row):
    _, heads, rows, cols = pair.shape
    feats = heads * DH
    blocks = kept.shape[0]
    depth = 6
    entries = max(blocks // 2 + 1, (26 << 20) // (16 * feats * rows))
    wide, thin = pltpu.VMEM((rows, cols), F32), pltpu.VMEM((rows, cols), BF16)
    return staged_call(
        attend_back_kernel,
        "attend_back",
        [queries, kept, d_mixed, mixed, id_column, id_row],
        [],
        [pltpu.VMEM((depth, rows, cols), F32)] * 2
        + [pltpu.VMEM((depth, rows, LANES), F32)]
        + [pltpu.VMEM((depth, rows, cols), F32)] * 2
        + [wide] * 2
        + [thin] * 4
        + [pltpu.VMEM((blocks // 2 + 1, 2, 2 * feats, rows), F32)]
        + [pltpu.SemaphoreType.DMA((n, depth)) for n in (3, 2)]
        + [pltpu.SemaphoreType.DMA((1,))],
        BACK_MB,
        raw=(pair, cot, log_sums),
        raw_results=(pair.shape, pair.shape, (entries, 2, 2 * feats, rows)),
        cost=pl.CostEstimate(
            flops=2 * 400 * heads * rows * cols,
            bytes_accessed=16 * heads * rows * cols,
            transcendentals=heads * rows * cols,
        ),
    )


SMALL_LN1_GAIN, SMALL_LN1_BIAS, SMALL_LN2_GAIN, SMALL_LN2_BIAS = 0, 1, 2, 3
SMALL_B_OUT, SMALL_B_DOWN, SMALL_PENALTY = 4, 5, 6
SMALL_B_QUERY, SMALL_B_VALUE, SMALL_B_UP = 8, 9, 10
SMALL_ROWS = 16


def side_by_side(count, units, width):
    beside = width // units
    height = count // beside
    return [
        (slice(n * height, (n + 1) * height), slice(n * units, (n + 1) * units), slice(0, height))
        for n in range(beside)
    ]


def team_device(team, core, chips):
    return {"dp": lax.div(team, chips), "blk": lax.rem(team, chips) * 2 + core}


def front_kernel(operands, results, scratch, raw):
    (
        atoms, ids, gain_one, bias_one, w_key, w_value, b_value, w_query, b_query, w_out, cot, w_down, w_up, b_out,
        gain, bias, b_up, b_down,
    ) = operands
    (pair,) = raw
    (
        queries, kept, id_column, log_sums, mixed, id_row, d_mixed, out_mine, d_hidden, shares, small,
    ) = results[:11]
    parcels = results[11:]
    (
        pair_buf, score, high, low, q_part, q_land, q_all, k_all, w_all, squares, mixed_all, hidden_two, down, d_act, up_high, up_low, normal_two, rate_two,
        part, landed, back, back_landed, ups_part, ups_sib, ups_go, ups_got, downs_part, downs_sib, downs_go, downs_got,
        pair_sem, kept_send, kept_recv, kz_send, kf_send, ks_send, k_recv, q_send, q_recv, w_send, w_recv, wx_send, wx_recv, wf_send, wf_recv,
        mix_send, mix_recv, part_send, part_recv, back_send, back_recv, sib_send, sib_recv, g_send, g_recv,
    ) = scratch
    zs, feats, rows = mixed_all.shape
    blocks = kept.shape[0]
    chips = blocks // 2
    teams, width = ups_part.shape[0], atoms.shape[1]
    _, group, _, cols = pair_buf.shape
    heads = feats // DH
    groups = heads // group
    piece = rows // zs
    z, blk = lax.axis_index("head"), lax.axis_index("blk")
    core, chip = lax.rem(blk, 2), lax.div(blk, 2)
    dp, dps = lax.axis_index("dp"), lax.axis_size("dp")
    team = dp * chips + chip
    other_core = 1 - core
    sib_blk = blk + 1 - 2 * core
    sibling = {"blk": sib_blk}
    peers, far_teams = others(z, zs), others(team, teams)
    sources = [lax.rem(z + zs - n, zs) for n in range(1, zs)]
    far = [step * 2 + core for step in others(chip, chips)]
    far_siblings = [step * 2 + other_core for step in others(chip, chips)]
    mine = pl.ds(pl.multiple_of(z * piece, 8), piece)

    def pair_copies(index, slot):
        return [
            pltpu.make_async_copy(pair.at[0, index * group + n], pair_buf.at[slot, n], pair_sem.at[slot, n])
            for n in range(group)
        ]

    meeting = [{"head": peer} for peer in peers] + [sibling]
    meeting += [team_device(peer, core, chips) for peer in far_teams]
    greet(meeting)

    normal, _ = normalize(atoms[...])
    normed = halves(normal * gain_one[...] + bias_one[...])
    meet(meeting)
    for n in range(2):
        for copy in pair_copies(n, n):
            copy.start()
    copies = []
    squads, _, _, fewer, _ = w_all.shape
    close = squads // dps
    base = chip - lax.rem(chip, close)
    squad = dp * close + chip - base
    w_mine = w_out.source.at[pl.ds(pl.multiple_of((squad * 2 + core) * fewer, 8), fewer)]
    copies += [
        send(w_mine, w_all.at[squad, core, z], w_send.at[n], w_recv.at[n], {"head": peer})
        for n, peer in enumerate(peers)
    ]
    kept[blk, 0:feats, :] = dot_halves(normed, halves(w_key[...])).T
    copies += [
        send(kept.at[blk, 0:feats], k_all.at[blk, z], kz_send.at[n], k_recv.at[blk, z], {"head": peer})
        for n, peer in enumerate(peers)
    ]
    kept[blk, feats : 2 * feats, :] = (dot_halves(normed, halves(w_value[...])) + b_value[...]).T
    id_line = ids[...].astype(F32)
    kept[blk, 2 * feats : 2 * feats + 8, :] = jnp.broadcast_to(id_line, (8, rows))
    copies += [
        send(kept.at[blk], kept.at[blk], kept_send.at[n], kept_recv.at[blk], {"blk": peer})
        for n, peer in enumerate([sib_blk] + far)
    ]
    q_rows = (dot_halves(normed, halves(w_query[...])) + b_query[...]) * (DH ** (-0.5))
    q_part[...] = q_rows.reshape(zs, piece, feats)
    queries[...] = q_rows.T
    queries.flush()
    q_land[z] = q_part[z]
    w_all[squad, core, z] = w_out[pl.ds(pl.multiple_of((squad * 2 + core) * fewer, 8), fewer), :]
    id_column[...] = jnp.broadcast_to(id_line, (LANES, rows)).T
    id_column.flush()
    small[...] = jnp.zeros(small.shape, F32)
    small[SMALL_B_DOWN : SMALL_B_DOWN + 1, :] = column_sum(cot[mine, :])
    d_act[...] = dot_full(cot[...], w_down[...], NT)
    up_high[...], up_low[...] = halves(w_up[...])
    for n, source in enumerate(far):
        arrived(kept.at[source], kept_recv.at[source])
        copies.append(
            send(kept.at[source], kept.at[source], kept_send.at[chips + n], kept_recv.at[source], sibling)
        )
    for source in [sib_blk] + far_siblings:
        arrived(kept.at[source], kept_recv.at[source])
    kept.flush()
    one = joined(kept[n, 2 * feats : 2 * feats + 8, :] for n in range(blocks))
    id_row[...] = jnp.concatenate([one, one], axis=0)
    id_row.flush()

    def mix_copies(index):
        some = pl.ds(pl.multiple_of(index * (8 * group), 8 * group), 8 * group)
        return [
            pltpu.make_async_remote_copy(
                src_ref=mixed.at[some],
                dst_ref=mixed_all.at[z, some],
                send_sem=mix_send.at[n, index],
                recv_sem=mix_recv.at[n, index],
                device_id={"head": peer},
                device_id_type=MESH,
            )
            for n, peer in enumerate(peers)
        ]

    squad_copies = [
        pltpu.make_async_remote_copy(
            src_ref=w_all.at[squad, core],
            dst_ref=w_all.at[squad, core],
            send_sem=wx_send.at[n - 1],
            recv_sem=wx_recv.at[n - 1],
            device_id={
                "dp": lax.div(lax.rem(squad + n, squads), close),
                "blk": (base + lax.rem(lax.rem(squad + n, squads), close)) * 2 + core,
            },
            device_id_type=MESH,
        )
        for n in range(1, squads)
    ]

    key_copies = [
        pltpu.make_async_remote_copy(
            src_ref=k_all.at[blk, peer],
            dst_ref=k_all.at[blk, peer],
            send_sem=kf_send.at[n, m],
            recv_sem=k_recv.at[blk, peer],
            device_id={"blk": target},
            device_id_type=MESH,
        )
        for n, peer in enumerate(peers)
        for m, target in enumerate([sib_blk] + far)
    ]

    def step(index, carry):
        slot = lax.rem(index, 2)
        for copy in pair_copies(index, slot):
            copy.wait()
        low_row = pl.multiple_of(index * (8 * group), 8 * group)
        some = pl.ds(low_row, 8 * group)
        values = pl.ds(pl.multiple_of(feats + low_row, 8), 8 * group)
        mixed[some, :] = attend_group(
            pair_buf.at[slot],
            queries[some, :],
            joined(kept[n, some, :] for n in range(blocks)),
            joined(kept[n, values, :] for n in range(blocks)),
            id_column, id_row, log_sums, index * group, score, high, low,
        )
        for copy in mix_copies(index):
            copy.start()

        @pl.when(index == groups // 2)
        def _():
            for n, source in enumerate(sources):
                arrived(w_all.at[squad, core, source], w_recv.at[n])
            for copy in squad_copies:
                copy.start()

        @pl.when(index == max(0, groups - 2))
        def _():
            for peer in peers:
                arrived(k_all.at[blk, peer], k_recv.at[blk, peer])
            for copy in key_copies:
                copy.start()

        @pl.when(index + 2 < groups)
        def _():
            for copy in pair_copies(index + 2, slot):
                copy.start()

        return carry

    lax.fori_loop(0, groups, step, 0)
    mixed.flush()
    log_sums.flush()
    squad_sources = [lax.rem(squad + squads - n, squads) for n in range(squads)]
    for n, source in enumerate(squad_sources):
        ready = w_all.at[source, core]
        if n >= 1:
            arrived(ready, wx_recv.at[n - 1])
        copies.append(send(ready, ready, wf_send.at[n], wf_recv.at[n], sibling))
    for n, source in enumerate(squad_sources):
        arrived(w_all.at[source, other_core], wf_recv.at[n])
    outs = halves(
        jnp.concatenate([w_all[s, kind, n] for n in range(zs) for s in range(squads) for kind in range(2)], axis=0)
    )
    mixed_all[z] = mixed[...]
    for n, source in enumerate(sources):
        for index in range(groups):
            some = pl.ds(index * (8 * group), 8 * group)
            arrived(mixed_all.at[source, some], mix_recv.at[n, index])
    copies += [
        send(q_part.at[peer], q_land.at[z], q_send.at[n], q_recv.at[n], {"head": peer})
        for n, peer in enumerate(peers)
    ]
    ups = up_high[...], up_low[...]
    mixed_rows = mixed_all[...].reshape(zs * feats, rows).T
    hidden_rows = atoms[...] + dot_halves(halves(mixed_rows), outs) + b_out[...]
    hidden_two[...] = hidden_rows
    normal, rate = normalize(hidden_rows)
    normal_two[...] = normal
    rate_two[...] = jnp.broadcast_to(rate, rate_two.shape)
    normed = normal * gain[...] + bias[...]
    pre = dot_halves(halves(normed), ups) + b_up[...]
    phi = 0.5 * (1.0 + lax.erf(pre * math.sqrt(0.5)))
    act = pre * phi
    d_pre = d_act[...] * (phi + pre * jnp.exp(-0.5 * pre * pre) * (1.0 / math.sqrt(2.0 * math.pi)))
    d_pres = halves(d_pre)
    cots, downs = halves(cot[...]), halves(w_down[...])
    part[...] = dot_halves(d_pres, ups, NT).reshape(zs, piece, width)
    copies += [
        send(part.at[peer], landed.at[z], part_send.at[n], part_recv.at[n], {"head": peer})
        for n, peer in enumerate(peers)
    ]
    landed[z] = part[z]
    ups_part[...] = dot_halves(halves(normed.T), d_pres).reshape(ups_part.shape)
    copies.append(send(ups_part.at[:, other_core], ups_sib, sib_send.at[0], sib_recv.at[0], sibling))
    downs_part[...] = dot_halves(halves(act.T), cots).reshape(downs_part.shape)
    copies.append(send(downs_part.at[:, other_core], downs_sib, sib_send.at[1], sib_recv.at[1], sibling))
    down[...] = dot_halves(halves(act), downs)
    out_mine[...] = hidden_two[mine, :] + down[mine, :] + b_down[...]
    out_mine.flush()
    small[SMALL_B_UP : SMALL_B_UP + 1, 0 : d_pre.shape[1]] = column_sum(d_pre)
    for kind, (parts, sib, go, got) in enumerate(
        [(ups_part, ups_sib, ups_go, ups_got), (downs_part, downs_sib, downs_go, downs_got)]
    ):
        arrived(sib, sib_recv.at[kind])
        go[...] = sib[...] + parts[:, core]
        copies += [
            send(
                go.at[peer], got.at[team], g_send.at[kind, n], g_recv.at[kind, team],
                team_device(peer, core, chips),
            )
            for n, peer in enumerate(far_teams)
        ]
        got[team] = go[team]
    for n, source in enumerate(far):
        for m, peer in enumerate(peers):
            ready = k_all.at[source, peer]
            arrived(ready, k_recv.at[source, peer])
            copies.append(send(ready, ready, ks_send.at[n, m], k_recv.at[source, peer], sibling))
    for n, source in enumerate(sources):
        arrived(q_land.at[source], q_recv.at[n])
    for n in range(zs):
        q_all[n] = q_land[n].T
    for n in range(blocks):
        k_all[n, z] = kept[n, 0:feats, :]
    for source in [sib_blk] + far_siblings:
        for peer in peers:
            arrived(k_all.at[source, peer], k_recv.at[source, peer])
    squares[...] = jnp.zeros(squares.shape, F32)
    at_once = 4
    rounds = heads // at_once

    def square_step(index, carry):
        there = lax.div(index, rounds)
        some = pl.ds(pl.multiple_of(lax.rem(index, rounds) * (8 * at_once), 8 * at_once), 8 * at_once)
        q_some = q_all[there, some, :]
        k_some = joined(k_all[n, there, some, :] for n in range(blocks))
        added = None
        for h in range(at_once):
            head = slice(8 * h, 8 * h + 8)
            q_high, q_low = wide_halves(q_some[head])
            k_high, k_low = wide_halves(k_some[head])
            value = dot(
                stacked([q_high, q_high, q_low, q_low]), stacked([k_high, k_low, k_high, k_low]), TN
            )
            added = value * value if added is None else added + value * value
        squares[...] += added
        return carry

    lax.fori_loop(0, zs * rounds, square_step, 0)
    same = id_column[mine, 0:1] == id_row[0:1, :]
    norms = jnp.sqrt(squares[...] + 1.0)
    terms = jnp.where(same, jnp.log1p(jnp.exp(norms - math.sqrt(zs * heads))), 0.0)
    number = jnp.where(same, 1.0, 0.0)

    def total(value):
        return jnp.sum(jnp.sum(value, axis=1, keepdims=True), axis=0, keepdims=True)

    lane = lax.broadcasted_iota(jnp.int32, (1, width), 1)
    small[SMALL_PENALTY : SMALL_PENALTY + 1, :] = jnp.where(
        lane == 0, total(terms), jnp.where(lane == 1, total(number), 0.0)
    )
    for n, source in enumerate(sources):
        arrived(landed.at[source], part_recv.at[n])
    d_normed = functools.reduce(jnp.add, [landed[n] for n in range(zs)])
    normal = normal_two[mine, :]
    d_rows = cot[mine, :] + normalize_back(d_normed, gain[...], normal, rate_two[mine, 0:1])
    d_halves = halves(d_rows)
    for n in range(zs):
        some = slice(n * feats, (n + 1) * feats)
        back[n] = dot_halves(d_halves, (outs[0][some], outs[1][some]), NT)
    copies += [
        send(back.at[peer], back_landed.at[z], back_send.at[n], back_recv.at[n], {"head": peer})
        for n, peer in enumerate(peers)
    ]
    back_landed[z] = back[z]
    d_hidden[...] = d_rows
    d_hidden.flush()
    for peer, parcel in zip(peers, parcels, strict=True):
        parcel[0:piece, :] = down[pl.ds(pl.multiple_of(peer * piece, 8), piece), :]
        parcel[piece : 2 * piece, :] = d_rows
        parcel.flush()
    small[SMALL_LN2_GAIN : SMALL_LN2_GAIN + 1, :] = column_sum(d_normed * normal)
    small[SMALL_LN2_BIAS : SMALL_LN2_BIAS + 1, :] = column_sum(d_normed)
    small[SMALL_B_OUT : SMALL_B_OUT + 1, :] = column_sum(d_rows)
    small.flush()
    for kind, got in enumerate([ups_got, downs_got]):
        for peer in far_teams:
            arrived(got.at[peer], g_recv.at[kind, peer])
    up_share, down_share = [
        functools.reduce(jnp.add, [got[n] for n in range(teams)]) for got in (ups_got, downs_got)
    ]
    for rows_of, columns_of, there in side_by_side(*up_share.shape, width):
        shares[there, columns_of] = up_share[rows_of]
    shares[there.stop :, :] = down_share
    shares.flush()
    for n, source in enumerate(sources):
        arrived(back_landed.at[source], back_recv.at[n])
    d_mixed[...] = back_landed[...].reshape(rows, feats).T
    d_mixed.flush()
    for copy in copies + squad_copies + key_copies:
        copy.wait_send()

    def drain(index, carry):
        for copy in mix_copies(index):
            copy.wait_send()
        return carry

    lax.fori_loop(0, groups, drain, 0)


def front(zs, dps, teams, pair, *operands):
    _, heads, rows, cols = pair.shape
    feats, blocks = heads * DH, cols // rows
    width, units = operands[0].shape[1], operands[12].shape[1]
    piece, group, hops = rows // zs, GROUP, zs - 1
    squads = dps * min(blocks // 2, max(1, feats // (2 * dps * 8)))
    up_rows, down_rows = width // (2 * teams), units // (2 * teams)
    groups = heads // group
    slab = pltpu.VMEM((zs, piece, width), F32)
    narrow = pltpu.VMEM((zs, piece, feats), F32)
    one_up, one_down = pltpu.VMEM((teams, up_rows, units), F32), pltpu.VMEM((teams, down_rows, width), F32)
    dma = pltpu.SemaphoreType.DMA
    return staged_call(
        front_kernel,
        "front",
        operands,
        [
            (feats, rows), (blocks, 2 * feats + 8, rows), (rows, LANES), (heads, rows, LANES), (feats, rows),
            (STRIP, cols), (feats, rows), (piece, width), (piece, width),
            (up_rows * units // width + down_rows, width), (SMALL_ROWS, width),
        ]
        + [(2 * piece, width)] * (zs - 1),
        [
            pltpu.VMEM((2, group, rows, cols), F32),
            pltpu.VMEM((group, rows, cols), F32),
            pltpu.VMEM((group, rows, cols), BF16),
            pltpu.VMEM((group, rows, cols), BF16),
            narrow, narrow,
            pltpu.VMEM((zs, feats, piece), F32),
            pltpu.VMEM((blocks, zs, feats, rows), F32),
            pltpu.VMEM((squads, 2, zs, feats // (2 * squads), width), F32),
            pltpu.VMEM((piece, cols), F32),
            pltpu.VMEM((zs, feats, rows), F32),
            pltpu.VMEM((rows, width), F32),
            pltpu.VMEM((rows, width), F32),
            pltpu.VMEM((rows, units), F32),
            pltpu.VMEM((width, units), BF16),
            pltpu.VMEM((width, units), BF16),
            pltpu.VMEM((rows, width), F32),
            pltpu.VMEM((rows, LANES), F32),
            slab, slab, narrow, narrow,
            pltpu.VMEM((teams, 2, up_rows, units), F32),
            one_up, one_up, one_up,
            pltpu.VMEM((teams, 2, down_rows, width), F32),
            one_down, one_down, one_down,
            dma((2, group)),
            dma((blocks,)), dma((blocks,)),
            dma((hops,)), dma((hops, blocks // 2)), dma((max(1, blocks // 2 - 1), hops)), dma((blocks, zs)),
            dma((hops,)), dma((hops,)),
            dma((hops,)), dma((hops,)), dma((max(1, squads - 1),)), dma((max(1, squads - 1),)),
            dma((squads,)), dma((squads,)),
            dma((hops, groups)), dma((hops, groups)),
            dma((hops,)), dma((hops,)),
            dma((hops,)), dma((hops,)),
            dma((2,)), dma((2,)),
            dma((2, teams)), dma((2, teams)),
        ],
        FRONT_MB,
        remote=0,
        raw=(pair,),
    )


def finish_kernel(operands, results, scratch, raw):
    (
        out_mine, d_hidden, atoms, gain, bias, w_query, mixed, small_in, w_key, w_value,
    ) = operands[:10]
    parcels = operands[10 : 9 + lax.axis_size("head")]
    chip_shares = operands[9 + lax.axis_size("head") :]
    grad_atoms, out_atoms, total_grads, grad_up, grad_down, small, penalty = results
    (
        sib_keys, sib_values, go_keys, go_values, got_keys, got_values,
        part, landed, grads, sib_grads, go_grads, got_grads, hidden_all, small_z, small_all,
        sib_send, sib_recv, kv_send, kv_recv, part_send, part_recv, back_send, back_recv,
        g_send, g_recv, t_send, t_recv, f_send, b_send, b_recv, bf_send, out_send, out_recv,
        small_z_send, small_z_recv, small_send, small_recv, own_heads, heads_sem,
    ) = scratch
    (d_heads,) = raw
    chips, feats, rows = own_heads.shape[0] - 1, d_heads.shape[2] // 2, d_heads.shape[3]
    heads_copy = pltpu.make_async_copy(d_heads.at[pl.ds(0, chips + 1)], own_heads, heads_sem.at[0])
    heads_copy.start()
    zs, piece, width = part.shape
    teams, _, share, _ = grads.shape
    blk, z, dp = lax.axis_index("blk"), lax.axis_index("head"), lax.axis_index("dp")
    core, chip = lax.rem(blk, 2), lax.div(blk, 2)
    other_core = 1 - core
    sibling = {"blk": blk + 1 - 2 * core}
    peers = others(z, zs)
    team = dp * chips + chip
    far_teams = others(team, teams)
    far_chips = others(chip, chips)
    place = team * 2 + core
    far_places = others(place, teams * 2)
    plane = [team_device(lax.div(value, 2), lax.rem(value, 2), chips) for value in far_places]
    meeting = [{"head": peer} for peer in peers] + plane
    greet(meeting)
    meet(meeting)
    copies = [
        send(
            d_heads.at[pl.ds(0, chips), other_core, pl.ds(kind * feats, feats)],
            sib, sib_send.at[kind], sib_recv.at[kind], sibling,
        )
        for kind, sib in enumerate([sib_keys, sib_values])
    ]
    mine = pl.ds(pl.multiple_of(z * piece, 8), piece)
    out_atoms[mine, :] = functools.reduce(jnp.add, [parcel[0:piece, :] for parcel in parcels], out_mine[...])
    copies += [
        send(out_atoms.at[mine], out_atoms.at[mine], out_send.at[n], out_recv.at[z], {"head": peer})
        for n, peer in enumerate(peers)
    ]

    def big_rows(result, source, kind):
        count = result.shape[0] // (2 * teams)
        return result.at[pl.ds(pl.multiple_of((source * 2 + kind) * count, 8), count)]

    partners = others(dp, lax.axis_size("dp"))
    for n in range(chips):
        source = dp * chips + lax.rem(chip + chips - n, chips)
        up_there, down_there = big_rows(grad_up, source, core), big_rows(grad_down, source, core)
        for rows_of, columns_of, there in side_by_side(*up_there.shape, width):
            up_there[rows_of, :] = chip_shares[n][there, columns_of]
        down_there[...] = chip_shares[n][there.stop :, :]
        for kind, ready in enumerate([up_there, down_there]):
            copies += [
                send(ready, ready, b_send.at[kind, n, m], b_recv.at[kind, source, core], {"dp": partner})
                for m, partner in enumerate(partners)
            ]
    heads_copy.wait()
    d_queries = own_heads[chips, 0, 0:feats, :]
    for kind, (sib, go, got) in enumerate([(sib_keys, go_keys, got_keys), (sib_values, go_values, got_values)]):
        arrived(sib, sib_recv.at[kind])
        go[...] = sib[...] + own_heads[0:chips, core, kind * feats : (kind + 1) * feats, :]
        copies += [
            send(
                go.at[peer], got.at[chip], kv_send.at[kind, n], kv_recv.at[kind, chip],
                {"blk": peer * 2 + core},
            )
            for n, peer in enumerate(far_chips)
        ]
    got_keys[chip] = go_keys[chip]
    got_values[chip] = go_values[chip]
    normal, rate = normalize(atoms[...])
    normed = halves(normal * gain[...] + bias[...])
    dq_rows = d_queries.T
    d_normed = dot_full(dq_rows, w_query[...], NT)
    grad_q = dot_halves(halves(d_queries), normed)
    small_z[z] = small_in[0:8, :]
    hidden_all[z] = d_hidden[...]
    for n, parcel in enumerate(parcels):
        hidden_all[lax.rem(z + zs - 1 - n, zs)] = parcel[piece : 2 * piece, :]
    grad_o = dot_full(mixed[...], hidden_all[...].reshape(rows, width))
    for peer in far_chips:
        arrived(got_keys.at[peer], kv_recv.at[0, peer])
        arrived(got_values.at[peer], kv_recv.at[1, peer])
    dk = functools.reduce(jnp.add, [got_keys[n] for n in range(chips)])
    dv = functools.reduce(jnp.add, [got_values[n] for n in range(chips)])
    dv_rows = dv.T
    d_normed = (
        d_normed + dot_full(dk.T, w_key[...], NT) + dot_full(dv_rows, w_value[...], NT)
    )
    part[...] = d_normed.reshape(zs, piece, width)
    copies += [
        send(part.at[peer], landed.at[z], part_send.at[n], part_recv.at[z], {"head": peer})
        for n, peer in enumerate(peers)
    ]
    landed[z] = part[z]
    grad_k = dot_halves(halves(dk), normed)
    grad_v = dot_halves(halves(dv), normed)
    grads[...] = jnp.concatenate([grad_q, grad_k, grad_v, grad_o], axis=0).reshape(grads.shape)
    copies.append(send(grads.at[:, other_core], sib_grads, sib_send.at[2], sib_recv.at[2], sibling))
    arrived(sib_grads, sib_recv.at[2])
    go_grads[...] = sib_grads[...] + grads[:, core]
    copies += [
        send(
            go_grads.at[peer], got_grads.at[team], g_send.at[n], g_recv.at[team], team_device(peer, core, chips)
        )
        for n, peer in enumerate(far_teams)
    ]
    got_grads[team] = go_grads[team]
    for peer in peers:
        arrived(landed.at[peer], part_recv.at[peer])
    d_normed = functools.reduce(jnp.add, [landed[n] for n in range(zs)])
    normal, rate = normalize(atoms[mine, :])
    grad_atoms[mine, :] = d_hidden[...] + normalize_back(d_normed, gain[...], normal, rate)
    small_z[z, SMALL_LN1_GAIN : SMALL_LN1_GAIN + 1, :] = column_sum(d_normed * normal)
    small_z[z, SMALL_LN1_BIAS : SMALL_LN1_BIAS + 1, :] = column_sum(d_normed)
    copies += [
        send(small_z.at[z], small_z.at[z], small_z_send.at[n], small_z_recv.at[z], {"head": peer})
        for n, peer in enumerate(peers)
    ]
    copies += [
        send(grad_atoms.at[mine], grad_atoms.at[mine], back_send.at[n], back_recv.at[z], {"head": peer})
        for n, peer in enumerate(peers)
    ]
    for peer in far_teams:
        arrived(got_grads.at[peer], g_recv.at[peer])
    total_grads[team, core] = functools.reduce(jnp.add, [got_grads[n] for n in range(teams)])
    ready = total_grads.at[team, core]
    copies.append(send(ready, ready, t_send.at[0], t_recv.at[team, core], sibling))
    copies += [
        send(ready, ready, t_send.at[n + 1], t_recv.at[team, core], team_device(peer, core, chips))
        for n, peer in enumerate(far_teams)
    ]
    for peer in peers:
        arrived(small_z.at[peer], small_z_recv.at[peer])
    small_all[place, 0:8, :] = functools.reduce(jnp.add, [small_z[n] for n in range(zs)])
    small_all[place, 8:16, :] = small_in[8:16, :]
    small_all[place, SMALL_B_QUERY : SMALL_B_QUERY + 1, 0:feats] = column_sum(dq_rows)
    small_all[place, SMALL_B_VALUE : SMALL_B_VALUE + 1, 0:feats] = column_sum(dv_rows)
    copies += [
        send(small_all.at[place], small_all.at[place], small_send.at[n], small_recv.at[place], target)
        for n, target in enumerate(plane)
    ]
    for n, peer in enumerate(far_teams):
        ready = total_grads.at[peer, core]
        arrived(ready, t_recv.at[peer, core])
        copies.append(send(ready, ready, f_send.at[n], t_recv.at[peer, core], sibling))
    for kind, result in enumerate([grad_up, grad_down]):
        for n in range(teams):
            ready = big_rows(result, n, core)

            @pl.when(lax.div(n, chips) != dp)
            def _(ready=ready, sem=b_recv.at[kind, n, core]):
                arrived(ready, sem)

            copies.append(send(ready, ready, bf_send.at[kind, n], b_recv.at[kind, n, core], sibling))
    for source in far_places:
        arrived(small_all.at[source], small_recv.at[source])
    summed = functools.reduce(jnp.add, [small_all[n] for n in range(2 * teams)])
    small[...] = summed
    ends = summed[SMALL_PENALTY : SMALL_PENALTY + 1, :]
    penalty[...] = ends[:, 0:1] / ends[:, 1:2]
    for peer in [team] + far_teams:
        arrived(total_grads.at[peer, other_core], t_recv.at[peer, other_core])
    total_grads.flush()
    for kind, result in enumerate([grad_up, grad_down]):
        for n in range(teams):
            arrived(big_rows(result, n, other_core), b_recv.at[kind, n, other_core])
        result.flush()
    for peer in peers:
        there = pl.ds(pl.multiple_of(peer * piece, 8), piece)
        arrived(out_atoms.at[there], out_recv.at[peer])
    out_atoms.flush()
    for peer in peers:
        there = pl.ds(pl.multiple_of(peer * piece, 8), piece)
        arrived(grad_atoms.at[there], back_recv.at[peer])
    for copy in copies:
        copy.wait_send()


def finish(zs, dps, units, d_heads, *operands):
    atoms = operands[2]
    chips, feats, rows = lax.axis_size("blk") // 2, d_heads.shape[2] // 2, d_heads.shape[3]
    width = atoms.shape[1]
    piece = rows // zs
    teams = dps * chips
    share = 4 * feats // (2 * teams)
    some = pltpu.VMEM((chips, feats, rows), F32)
    slab = pltpu.VMEM((zs, piece, width), F32)
    one = pltpu.VMEM((teams, share, width), F32)
    dma = pltpu.SemaphoreType.DMA
    return staged_call(
        finish_kernel,
        "finish",
        operands,
        [
            (rows, width),
            (rows, width),
            (teams, 2, share, width),
            (width, units),
            (units, width),
            (SMALL_ROWS, width),
            (1, 1),
        ],
        [some] * 6
        + [slab, slab, pltpu.VMEM((teams, 2, share, width), F32), one, one, one, slab]
        + [
            pltpu.VMEM((zs, 8, width), F32),
            pltpu.VMEM((2 * teams, SMALL_ROWS, width), F32),
            dma((3,)), dma((3,)),
            dma((2, chips)), dma((2, chips)),
            dma((zs,)), dma((zs,)),
            dma((zs,)), dma((zs,)),
            dma((teams,)), dma((teams,)),
            dma((teams,)), dma((teams, 2)), dma((teams,)),
            dma((2, chips, dps)), dma((2, teams, 2)), dma((2, teams)),
            dma((zs,)), dma((zs,)),
            dma((zs,)), dma((zs,)),
            dma((2 * teams,)), dma((2 * teams,)),
            pltpu.VMEM((chips + 1, 2, 2 * feats, rows), F32), dma((1,)),
        ],
        FINISH_MB,
        remote=2,
        near_in=range(10, len(operands)),
        raw=(d_heads,),
        near_out=range(7),
    )


def place_kernel(operands, results, scratch, raw):
    total_grads, small, penalty_in = operands
    penalty, grad_query, grad_key, grad_value, grad_out = results[:5]
    penalty[...] = penalty_in[...]
    feats, width = grad_out.shape
    done = total_grads[...].reshape(4 * feats, width)
    grad_query[...] = done[0:feats].T
    grad_query.flush()
    grad_key[...] = done[feats : 2 * feats].T
    grad_key.flush()
    grad_value[...] = done[2 * feats : 3 * feats].T
    grad_value.flush()
    grad_out[...] = done[3 * feats :]
    grad_out.flush()
    for result, row in zip(results[5:], SMALL_OUTPUTS, strict=True):
        result[...] = small[row : row + 1, 0 : result.shape[1]]


SMALL_OUTPUTS = (
    SMALL_LN1_GAIN, SMALL_LN1_BIAS, SMALL_B_QUERY, SMALL_B_VALUE, SMALL_B_OUT, SMALL_LN2_GAIN, SMALL_LN2_BIAS,
    SMALL_B_UP, SMALL_B_DOWN,
)


def place(feats, units, straight, *operands):
    width = operands[1].shape[1]
    lengths = {SMALL_B_QUERY: feats, SMALL_B_VALUE: feats, SMALL_B_UP: units}
    return staged_call(
        place_kernel,
        "place",
        operands,
        [(1, 1)]
        + [(width, feats)] * 3
        + [(feats, width)]
        + [(1, lengths.get(row, width)) for row in SMALL_OUTPUTS],
        [],
        PLACE_MB,
        straight=straight,
        near_in=(0, 1, 2),
        near_straight=True,
    )


def local(
    zs, dps,
    atoms, pair, mol_ids, ln1_gain, ln1_bias, w_query, b_query, w_key, w_value, b_value, w_out, b_out,
    ln2_gain, ln2_bias, w_up, b_up, w_down, b_down, cot_atoms, cot_pair,
):
    blocks = pair.shape[3] // pair.shape[2]
    inputs, cot = atoms[0], cot_atoms[0]

    def line(value):
        return value.reshape(1, -1)

    (
        queries, kept, id_column, log_sums, mixed, id_row, d_mixed, out_mine, d_hidden, shares, small, *parcels,
    ) = front(
        zs, dps, dps * blocks // 2, pair,
        inputs, mol_ids, line(ln1_gain), line(ln1_bias), w_key, w_value, line(b_value), w_query, line(b_query),
        w_out, cot, w_down, w_up, line(b_out), line(ln2_gain), line(ln2_bias), line(b_up),
        line(b_down),
    )
    parcels = [
        lax.ppermute(parcel, "head", [(source, (source + n + 1) % zs) for source in range(zs)])
        for n, parcel in enumerate(parcels)
    ]
    chips = blocks // 2
    chip_shares = [shares] + [
        lax.ppermute(shares, "blk", [(2 * c + core, 2 * ((c + n) % chips) + core) for c in range(chips) for core in range(2)])
        for n in range(1, chips)
    ]
    out_pair, grad_pair, d_heads = attend_back(
        pair, cot_pair, queries, kept, mixed, d_mixed, log_sums, id_column, id_row
    )
    grad_atoms, out_atoms, total_grads, grad_up, grad_down, small, penalty = finish(
        zs, dps, w_up.shape[1],
        d_heads, out_mine, d_hidden, inputs, line(ln1_gain), line(ln1_bias), w_query, mixed,
        small, w_key, w_value, *parcels, *chip_shares,
    )
    placed = place(
        w_query.shape[1], w_up.shape[1],
        [grad_atoms, out_atoms, grad_up, grad_down],
        total_grads, small, penalty,
    )
    grad_atoms, out_atoms, grad_up, grad_down, penalty, grad_query, grad_key, grad_value, grad_out = placed[:9]
    (
        grad_ln1_gain, grad_ln1_bias, grad_b_query, grad_b_value, grad_b_out, grad_ln2_gain, grad_ln2_bias,
        grad_b_up, grad_b_down,
    ) = [value.reshape(-1) for value in placed[9:]]
    return (
        out_atoms[None],
        out_pair,
        penalty[0, 0],
        grad_atoms[None],
        grad_pair,
        grad_ln1_gain,
        grad_ln1_bias,
        grad_query,
        grad_b_query,
        grad_key,
        grad_value,
        grad_b_value,
        grad_out,
        grad_b_out,
        grad_ln2_gain,
        grad_ln2_bias,
        grad_up,
        grad_b_up,
        grad_down,
        grad_b_down,
    )


def solution(mesh):
    rows, pairs = P("dp", "blk", None), P("dp", "head", "blk", None)
    columns = P(None, "head")
    return jax.shard_map(
        functools.partial(local, mesh.shape["head"], mesh.shape["dp"]),
        mesh=mesh,
        in_specs=(
            rows, pairs, P("dp", "blk"), P(), P(), columns, P("head"), columns, columns, P("head"),
            P("head", None), P(), P(), P(), columns, P("head"), P("head", None), P(), rows, pairs,
        ),
        out_specs=(
            rows, pairs, P(), rows, pairs, P(), P(), columns, P("head"), columns, columns, P("head"),
            P("head", None), P(), P(), P(), columns, P("head"), P("head", None), P(),
        ),
        check_vma=False,
    )
```

```python
import functools
import math

import jax
import jax.numpy as jnp
from jax import lax
from jax.experimental import pallas as pl
from jax.experimental.pallas import tpu as pltpu
from jax.sharding import PartitionSpec as P

DH = 8
LANES = 128
STRIP = 16
CHUNK = 256
GROUP = 2
FRONT_MB, BACK_MB, FINISH_MB, PLACE_MB = 58, 60, 40, 32
NORM_EPS = 1e-05
MASK_FILL = -1e30
F32 = jnp.float32
BF16 = jnp.bfloat16
MESH = pl.DeviceIdType.MESH
NN = (((1,), (0,)), ((), ()))
NT = (((1,), (1,)), ((), ()))
TN = (((0,), (0,)), ((), ()))
VMEM = pl.BlockSpec(memory_space=pltpu.VMEM)


def dot(left, right, dims=NN):
    return lax.dot_general(left, right, dims, preferred_element_type=F32)


def halves(value):
    high = value.astype(BF16)
    return high, (value - high.astype(F32)).astype(BF16)


def dot_halves(left, right, dims=NN):
    return dot(left[0], right[0], dims) + (
        dot(left[0], right[1], dims) + dot(left[1], right[0], dims)
    )


def dot_full(left, right, dims=NN):
    return dot_halves(halves(left), halves(right), dims)


def normalize(inputs):
    centred = inputs - jnp.mean(inputs, -1, keepdims=True)
    rate = lax.rsqrt(jnp.mean(centred * centred, -1, keepdims=True) + NORM_EPS)
    return centred * rate, rate


def normalize_back(grad, gain, normal, rate):
    scaled = grad * gain
    return rate * (
        scaled
        - jnp.mean(scaled, -1, keepdims=True)
        - normal * jnp.mean(scaled * normal, -1, keepdims=True)
    )


def column_sum(value):
    return jnp.sum(value, 0, keepdims=True)


def send(src, dst, send_sem, recv_sem, target):
    copy = pltpu.make_async_remote_copy(
        src_ref=src,
        dst_ref=dst,
        send_sem=send_sem,
        recv_sem=recv_sem,
        device_id=target,
        device_id_type=MESH,
    )
    copy.start()
    return copy


def arrived(ref, sem):
    pltpu.make_async_remote_copy(
        src_ref=ref, dst_ref=ref, send_sem=sem, recv_sem=sem, device_id={}, device_id_type=MESH
    ).wait_recv()


def greet(targets):
    for target in targets:
        pl.semaphore_signal(pltpu.get_barrier_semaphore(), inc=1, device_id=target, device_id_type=MESH)


def meet(targets):
    pl.semaphore_wait(pltpu.get_barrier_semaphore(), len(targets))


def others(index, count):
    return [lax.rem(index + step, count) for step in range(1, count)]


class Operand:
    def __init__(self, source, slot, sem):
        self.source, self.slot, self.shape = source, slot, slot.shape
        self.copy = None if sem is None else pltpu.make_async_copy(source, slot, sem)
        if self.copy is not None:
            self.copy.start()

    @property
    def ref(self):
        if self.copy is not None:
            self.copy.wait()
            self.copy = None
        return self.slot

    def __getitem__(self, index):
        return self.ref[index]


class Result:
    def __init__(self, target, slot, sem):
        self.slot, self.shape, self.at = slot, slot.shape, slot.at
        self.copy = None if sem is None else pltpu.make_async_copy(slot, target, sem)
        self.begun = self.copy is None

    def __setitem__(self, index, value):
        self.slot[index] = value

    def __getitem__(self, index):
        return self.slot[index]

    def flush(self):
        if not self.begun:
            self.copy.start()
            self.begun = True


def staged_call(
    kernel, name, operands, results, scratch, megabytes,
    remote=None, raw=(), straight=(), raw_results=(), cost=None, near_in=(), near_out=(), near_straight=False,
):
    n_in, n_out, n_raw, n_straight = len(operands), len(results), len(raw), len(straight)
    n_left = len(raw_results)
    far_in = [n for n in range(n_in) if n not in near_in]
    far_out = [n for n in range(n_out) if n not in near_out]

    def body(*refs):
        sources, left, refs = refs[:n_in], refs[n_in : n_in + n_raw], refs[n_in + n_raw :]
        moved, refs = refs[:n_straight], refs[n_straight:]
        arrays, refs = refs[:n_straight], refs[n_straight:]
        left, refs = left + refs[:n_left], refs[n_left:]
        targets, refs = refs[:n_out], refs[n_out:]
        in_slots, refs = dict(zip(far_in, refs)), refs[len(far_in) :]
        out_slots, refs = dict(zip(far_out, refs)), refs[len(far_out) :]
        in_sem, out_sem, move_sem, refs = refs[0], refs[1], refs[2], refs[3:]
        through, loads = moved, []
        if not near_straight:
            through, refs = refs[:n_straight], refs[n_straight:]
            loads = [pltpu.make_async_copy(moved[n], through[n], move_sem.at[n]) for n in range(n_straight)]
        moves = [pltpu.make_async_copy(through[n], arrays[n], move_sem.at[n]) for n in range(n_straight)]
        for load in loads:
            load.start()
        ins = [
            Operand(sources[n], in_slots.get(n, sources[n]), in_sem.at[far_in.index(n)] if n in in_slots else None)
            for n in range(n_in)
        ]
        outs = [
            Result(targets[n], out_slots.get(n, targets[n]), out_sem.at[far_out.index(n)] if n in out_slots else None)
            for n in range(n_out)
        ]
        for load in loads:
            load.wait()
        for move in moves:
            move.start()
        kernel(ins, outs, refs, left)
        for operand in ins:
            operand.ref
        for result in outs:
            result.flush()
        for copy in moves + [result.copy for result in outs if result.copy is not None]:
            copy.wait()

    hbm, vmem = pl.BlockSpec(memory_space=pltpu.HBM), pl.BlockSpec(memory_space=pltpu.VMEM)
    extra = {} if remote is None else {"collective_id": remote, "has_side_effects": True}
    return pl.pallas_call(
        body,
        out_shape=[jax.ShapeDtypeStruct(value.shape, value.dtype) for value in straight]
        + [jax.ShapeDtypeStruct(shape, F32) for shape in raw_results]
        + [jax.ShapeDtypeStruct(shape, F32) for shape in results],
        in_specs=[vmem if n in near_in else hbm for n in range(n_in)]
        + [hbm] * n_raw
        + [vmem if near_straight else hbm] * n_straight,
        out_specs=[hbm] * (n_straight + n_left) + [vmem if n in near_out else hbm for n in range(n_out)],
        scratch_shapes=[pltpu.VMEM(operands[n].shape, operands[n].dtype) for n in far_in]
        + [pltpu.VMEM(results[n], F32) for n in far_out]
        + [pltpu.SemaphoreType.DMA((max(1, n),)) for n in (len(far_in), len(far_out), n_straight)]
        + ([] if near_straight else [pltpu.VMEM(value.shape, value.dtype) for value in straight])
        + list(scratch),
        compiler_params=pltpu.CompilerParams(vmem_limit_bytes=megabytes << 20, **extra),
        cost_estimate=cost,
        name=name,
    )(*operands, *raw, *straight)


def joined(pieces):
    return jnp.concatenate(list(pieces), axis=1)


def stacked(parts):
    return jnp.concatenate(parts, axis=0).astype(BF16)


def wide_halves(value):
    high = value.astype(BF16).astype(F32)
    return high, value - high


def attend_group(pair, queries, keys, values, id_column, id_row, log_sums, first, score, high, low):
    group, rows, cols = score.shape
    strips = rows // STRIP
    chunk = min(CHUNK, cols)
    mixed = []
    for g in range(group):
        head = slice(8 * g, 8 * g + 8)
        q_high, q_low = wide_halves(queries[head, :])
        k_high, k_low = wide_halves(keys[head, :])
        v_high, v_low = wide_halves(values[head, :])
        ones = jnp.ones_like(v_high)
        q_pack = stacked([q_high, q_high, q_low, q_low])
        k_pack = stacked([k_high, k_low, k_high, k_low])
        v_pack = stacked([v_high, v_low, ones, jnp.zeros_like(ones)])
        tops = [None] * strips
        for start in range(0, cols, chunk):
            part = slice(start, start + chunk)
            score[g, :, part] = dot(q_pack, k_pack[:, part], TN)
            for s in range(strips):
                line = pl.ds(s * STRIP, STRIP)
                own = id_column[line, :]
                for j in range(start, start + chunk, LANES):
                    tile = pl.ds(j, LANES)
                    value = pair[g, line, tile] + score[g, line, tile]
                    value = jnp.where(own == id_row[:, tile], value, MASK_FILL)
                    score[g, line, tile] = value
                    tops[s] = value if tops[s] is None else jnp.maximum(tops[s], value)
        tops = [
            jnp.broadcast_to(jnp.max(top, axis=1, keepdims=True), (STRIP, LANES)) for top in tops
        ]
        totals = [None] * strips
        gathered = None
        for start in range(0, cols, chunk):
            part = slice(start, start + chunk)
            for s in range(strips):
                line = pl.ds(s * STRIP, STRIP)
                for j in range(start, start + chunk, LANES):
                    tile = pl.ds(j, LANES)
                    weight = jnp.exp(score[g, line, tile] - tops[s])
                    high[g, line, tile], low[g, line, tile] = halves(weight)
                    totals[s] = weight if totals[s] is None else totals[s] + weight
            term = dot(v_pack[:, part], high[g, :, part], NT) + dot(
                v_pack[:, part], low[g, :, part], NT
            )
            gathered = term if gathered is None else gathered + term
        for s in range(strips):
            total = jnp.sum(totals[s], axis=1, keepdims=True)
            log_sums[first + g, pl.ds(s * STRIP, STRIP), :] = tops[s] + jnp.log(total)
        mixed.append((gathered[0:8] + gathered[8:16]) / gathered[16:17])
    return jnp.concatenate(mixed, axis=0)


def chunks_of(cols):
    chunk = min(CHUNK, cols)
    return [slice(start, start + chunk) for start in range(0, cols, chunk)]


def score_packs(queries, keys):
    q_high, q_low = wide_halves(queries)
    k_high, k_low = wide_halves(keys)
    return stacked([q_high, q_high, q_low, q_low]), stacked([k_high, k_low, k_high, k_low])


def attend_back_kernel(operands, results, scratch, raw):
    queries, kept, d_mixed, mixed, id_column, id_row = operands
    pair, cot, log_sums, out_pair, grad_pair, heads_out = raw
    pair_buf, cot_buf, log_buf, out_buf, grad_buf = scratch[:5]
    here = scratch[5:11]
    d_heads, in_sem, out_sem, heads_sem = scratch[11:]
    heads = pair.shape[1]
    feats = heads * DH
    depth, rows, cols = pair_buf.shape
    blocks = kept.shape[0]
    parts = chunks_of(cols)
    place = lax.broadcasted_iota(jnp.int32, (8, rows), 0)

    def inward(index):
        slot = lax.rem(index, depth)
        sources = (pair.at[0, index], cot.at[0, index], log_sums.at[index])
        return [
            pltpu.make_async_copy(source, buf.at[slot], in_sem.at[n, slot])
            for n, (source, buf) in enumerate(zip(sources, (pair_buf, cot_buf, log_buf), strict=True))
        ]

    def outward(index):
        slot = lax.rem(index, depth)
        return [
            pltpu.make_async_copy(buf.at[slot], array.at[0, index], out_sem.at[n, slot])
            for n, (array, buf) in enumerate([(out_pair, out_buf), (grad_pair, grad_buf)])
        ]

    for n in range(2):
        for copy in inward(n):
            copy.start()
    for operand in operands:
        operand.ref

    def rows_of(index):
        return pl.ds(pl.multiple_of(index * 8, 8), 8)

    def key_rows(index):
        return joined(kept[n, rows_of(index), :] for n in range(blocks))

    def value_row(index):
        return pl.ds(pl.multiple_of(feats + index * 8, 8), 8)

    def value_rows(index):
        return joined(kept[n, value_row(index), :] for n in range(blocks))

    def packs(index):
        head = rows_of(index)
        q_pack, k_pack = score_packs(queries[head, :], key_rows(index))
        v_high, v_low = wide_halves(value_rows(index))
        m_high, m_low = wide_halves(d_mixed[head, :])
        delta_high, rest = wide_halves(-column_sum(mixed[head, :] * d_mixed[head, :]))
        delta_mid, delta_low = wide_halves(rest)
        deltas = jnp.where(
            place == 0, delta_high, jnp.where(place == 1, delta_mid, jnp.where(place == 2, delta_low, 0.0))
        )
        m_pack = stacked([m_high, m_high, m_low, deltas])
        v_pack = stacked([v_high, v_low, v_high, jnp.ones_like(v_high)])
        return q_pack, k_pack, m_pack, v_pack

    def pairs(index):
        head = rows_of(index)
        return [stacked(wide_halves(value)) for value in (queries[head, :], key_rows(index), d_mixed[head, :])]

    def before(pack, part, there):
        q_pack, k_pack, m_pack, v_pack = pack
        there[0][:, part] = dot(q_pack, k_pack[:, part], TN)
        there[1][:, part] = dot(m_pack, v_pack[:, part], TN)

    def middle(index, slot, part, here):
        score, d_prob, p_high, p_low, g_high, g_low = here
        for s in range(rows // STRIP):
            line = pl.ds(s * STRIP, STRIP)
            own = id_column[line, :]
            log_sum = log_buf[slot, line, :]
            for j in range(part.start, part.stop, LANES):
                tile = pl.ds(j, LANES)
                value = pair_buf[slot, line, tile] + score[line, tile]
                out_buf[slot, line, tile] = value
                prob = jnp.exp(jnp.where(own == id_row[:, tile], value - log_sum, MASK_FILL))
                p_high[line, tile], p_low[line, tile] = halves(prob)
                grad = prob * d_prob[line, tile] + cot_buf[slot, line, tile]
                grad_buf[slot, line, tile] = grad
                g_high[line, tile], g_low[line, tile] = halves(grad)

    def both(left, high, low, dims):
        value = dot(left, high, dims) + dot(left, low, dims)
        return value[0:8] + value[8:16]

    def after(index, pair_of, part, there):
        q_pair, k_pair, m_pair = pair_of
        _, _, p_high, p_low, g_high, g_low = there
        head = rows_of(index)
        d_value = both(m_pair, p_high[:, part], p_low[:, part], NN)
        d_key = both(q_pair, g_high[:, part], g_low[:, part], NN)
        for n in range(part.start // rows, part.stop // rows):
            span = slice(n * rows - part.start, (n + 1) * rows - part.start)
            d_heads[n // 2, n % 2, head, :] = d_key[:, span]
            d_heads[n // 2, n % 2, value_row(index), :] = d_value[:, span]
        return both(k_pair[:, part], g_high[:, part], g_low[:, part], NT)

    def stage(index, carry):
        slot = lax.rem(index, depth)
        for copy in inward(index):
            copy.wait()

        @pl.when(index >= depth)
        def _():
            for copy in outward(index - depth):
                copy.wait()

        @pl.when(index == 0)
        def _():
            for n in range(2, depth - 1):
                for copy in inward(n):
                    copy.start()

        @pl.when(index + depth - 1 < heads)
        def _():
            for copy in inward(index + depth - 1):
                copy.start()

        next_packs, own_pairs = packs(index), pairs(index)
        d_query = None
        before(next_packs, parts[0], here)
        if len(parts) > 1:
            before(next_packs, parts[1], here)
        for n, part in enumerate(parts):
            if n + 2 < len(parts):
                before(next_packs, parts[n + 2], here)
            middle(index, slot, part, here)
            if n >= 1:
                term = after(index, own_pairs, parts[n - 1], here)
                d_query = term if d_query is None else d_query + term
        term = after(index, own_pairs, parts[-1], here)
        d_query = term if d_query is None else d_query + term
        d_heads[blocks // 2, 0, rows_of(index), :] = d_query * (DH ** (-0.5))
        for copy in outward(index):
            copy.start()
        return carry

    lax.fori_loop(0, heads, stage, 0)
    last = pltpu.make_async_copy(d_heads, heads_out.at[pl.ds(0, d_heads.shape[0])], heads_sem.at[0])
    last.start()
    for n in range(max(0, heads - depth), heads):
        for copy in outward(n):
            copy.wait()
    last.wait()


def attend_back(pair, cot, queries, kept, mixed, d_mixed, log_sums, id_column, id_row):
    _, heads, rows, cols = pair.shape
    feats = heads * DH
    blocks = kept.shape[0]
    depth = 6
    entries = max(blocks // 2 + 1, (26 << 20) // (16 * feats * rows))
    wide, thin = pltpu.VMEM((rows, cols), F32), pltpu.VMEM((rows, cols), BF16)
    return staged_call(
        attend_back_kernel,
        "attend_back",
        [queries, kept, d_mixed, mixed, id_column, id_row],
        [],
        [pltpu.VMEM((depth, rows, cols), F32)] * 2
        + [pltpu.VMEM((depth, rows, LANES), F32)]
        + [pltpu.VMEM((depth, rows, cols), F32)] * 2
        + [wide] * 2
        + [thin] * 4
        + [pltpu.VMEM((blocks // 2 + 1, 2, 2 * feats, rows), F32)]
        + [pltpu.SemaphoreType.DMA((n, depth)) for n in (3, 2)]
        + [pltpu.SemaphoreType.DMA((1,))],
        BACK_MB,
        raw=(pair, cot, log_sums),
        raw_results=(pair.shape, pair.shape, (entries, 2, 2 * feats, rows)),
        cost=pl.CostEstimate(
            flops=2 * 400 * heads * rows * cols,
            bytes_accessed=16 * heads * rows * cols,
            transcendentals=heads * rows * cols,
        ),
    )


SMALL_LN1_GAIN, SMALL_LN1_BIAS, SMALL_LN2_GAIN, SMALL_LN2_BIAS = 0, 1, 2, 3
SMALL_B_OUT, SMALL_B_DOWN, SMALL_PENALTY = 4, 5, 6
SMALL_B_QUERY, SMALL_B_VALUE, SMALL_B_UP = 8, 9, 10
SMALL_ROWS = 16


def side_by_side(count, units, width):
    beside = width // units
    height = count // beside
    return [
        (slice(n * height, (n + 1) * height), slice(n * units, (n + 1) * units), slice(0, height))
        for n in range(beside)
    ]


def team_device(team, core, chips):
    return {"dp": lax.div(team, chips), "blk": lax.rem(team, chips) * 2 + core}


def front_kernel(operands, results, scratch, raw):
    (
        atoms, ids, gain_one, bias_one, w_key, w_value, b_value, w_query, b_query, w_out, cot, w_down, w_up, b_out,
        gain, bias, b_up, b_down,
    ) = operands
    (pair,) = raw
    (
        queries, kept, id_column, log_sums, mixed, id_row, d_mixed, out_mine, d_hidden, shares, small,
    ) = results[:11]
    parcels = results[11:]
    (
        pair_buf, score, high, low, q_part, q_land, q_all, k_all, w_all, squares, mixed_all, hidden_two, down, d_act, up_high, up_low, normal_two, rate_two,
        part, landed, back, back_landed, ups_part, ups_sib, ups_go, ups_got, downs_part, downs_sib, downs_go, downs_got,
        pair_sem, kept_send, kept_recv, kz_send, kf_send, ks_send, k_recv, q_send, q_recv, w_send, w_recv, wx_send, wx_recv, wf_send, wf_recv,
        mix_send, mix_recv, part_send, part_recv, back_send, back_recv, sib_send, sib_recv, g_send, g_recv,
    ) = scratch
    zs, feats, rows = mixed_all.shape
    blocks = kept.shape[0]
    chips = blocks // 2
    teams, width = ups_part.shape[0], atoms.shape[1]
    _, group, _, cols = pair_buf.shape
    heads = feats // DH
    groups = heads // group
    piece = rows // zs
    z, blk = lax.axis_index("head"), lax.axis_index("blk")
    core, chip = lax.rem(blk, 2), lax.div(blk, 2)
    dp, dps = lax.axis_index("dp"), lax.axis_size("dp")
    team = dp * chips + chip
    other_core = 1 - core
    sib_blk = blk + 1 - 2 * core
    sibling = {"blk": sib_blk}
    peers, far_teams = others(z, zs), others(team, teams)
    sources = [lax.rem(z + zs - n, zs) for n in range(1, zs)]
    far = [step * 2 + core for step in others(chip, chips)]
    far_siblings = [step * 2 + other_core for step in others(chip, chips)]
    mine = pl.ds(pl.multiple_of(z * piece, 8), piece)

    def pair_copies(index, slot):
        return [
            pltpu.make_async_copy(pair.at[0, index * group + n], pair_buf.at[slot, n], pair_sem.at[slot, n])
            for n in range(group)
        ]

    meeting = [{"head": peer} for peer in peers] + [sibling]
    meeting += [team_device(peer, core, chips) for peer in far_teams]
    greet(meeting)

    normal, _ = normalize(atoms[...])
    normed = halves(normal * gain_one[...] + bias_one[...])
    meet(meeting)
    for n in range(2):
        for copy in pair_copies(n, n):
            copy.start()
    copies = []
    squads, _, _, fewer, _ = w_all.shape
    close = squads // dps
    base = chip - lax.rem(chip, close)
    squad = dp * close + chip - base
    w_mine = w_out.source.at[pl.ds(pl.multiple_of((squad * 2 + core) * fewer, 8), fewer)]
    copies += [
        send(w_mine, w_all.at[squad, core, z], w_send.at[n], w_recv.at[n], {"head": peer})
        for n, peer in enumerate(peers)
    ]
    kept[blk, 0:feats, :] = dot_halves(normed, halves(w_key[...])).T
    copies += [
        send(kept.at[blk, 0:feats], k_all.at[blk, z], kz_send.at[n], k_recv.at[blk, z], {"head": peer})
        for n, peer in enumerate(peers)
    ]
    kept[blk, feats : 2 * feats, :] = (dot_halves(normed, halves(w_value[...])) + b_value[...]).T
    id_line = ids[...].astype(F32)
    kept[blk, 2 * feats : 2 * feats + 8, :] = jnp.broadcast_to(id_line, (8, rows))
    copies += [
        send(kept.at[blk], kept.at[blk], kept_send.at[n], kept_recv.at[blk], {"blk": peer})
        for n, peer in enumerate([sib_blk] + far)
    ]
    q_rows = (dot_halves(normed, halves(w_query[...])) + b_query[...]) * (DH ** (-0.5))
    q_part[...] = q_rows.reshape(zs, piece, feats)
    queries[...] = q_rows.T
    queries.flush()
    q_land[z] = q_part[z]
    w_all[squad, core, z] = w_out[pl.ds(pl.multiple_of((squad * 2 + core) * fewer, 8), fewer), :]
    id_column[...] = jnp.broadcast_to(id_line, (LANES, rows)).T
    id_column.flush()
    small[...] = jnp.zeros(small.shape, F32)
    small[SMALL_B_DOWN : SMALL_B_DOWN + 1, :] = column_sum(cot[mine, :])
    d_act[...] = dot_full(cot[...], w_down[...], NT)
    up_high[...], up_low[...] = halves(w_up[...])
    for n, source in enumerate(far):
        arrived(kept.at[source], kept_recv.at[source])
        copies.append(
            send(kept.at[source], kept.at[source], kept_send.at[chips + n], kept_recv.at[source], sibling)
        )
    for source in [sib_blk] + far_siblings:
        arrived(kept.at[source], kept_recv.at[source])
    kept.flush()
    one = joined(kept[n, 2 * feats : 2 * feats + 8, :] for n in range(blocks))
    id_row[...] = jnp.concatenate([one, one], axis=0)
    id_row.flush()

    def mix_copies(index):
        some = pl.ds(pl.multiple_of(index * (8 * group), 8 * group), 8 * group)
        return [
            pltpu.make_async_remote_copy(
                src_ref=mixed.at[some],
                dst_ref=mixed_all.at[z, some],
                send_sem=mix_send.at[n, index],
                recv_sem=mix_recv.at[n, index],
                device_id={"head": peer},
                device_id_type=MESH,
            )
            for n, peer in enumerate(peers)
        ]

    squad_copies = [
        pltpu.make_async_remote_copy(
            src_ref=w_all.at[squad, core],
            dst_ref=w_all.at[squad, core],
            send_sem=wx_send.at[n - 1],
            recv_sem=wx_recv.at[n - 1],
            device_id={
                "dp": lax.div(lax.rem(squad + n, squads), close),
                "blk": (base + lax.rem(lax.rem(squad + n, squads), close)) * 2 + core,
            },
            device_id_type=MESH,
        )
        for n in range(1, squads)
    ]

    key_copies = [
        pltpu.make_async_remote_copy(
            src_ref=k_all.at[blk, peer],
            dst_ref=k_all.at[blk, peer],
            send_sem=kf_send.at[n, m],
            recv_sem=k_recv.at[blk, peer],
            device_id={"blk": target},
            device_id_type=MESH,
        )
        for n, peer in enumerate(peers)
        for m, target in enumerate([sib_blk] + far)
    ]

    def step(index, carry):
        slot = lax.rem(index, 2)
        for copy in pair_copies(index, slot):
            copy.wait()
        low_row = pl.multiple_of(index * (8 * group), 8 * group)
        some = pl.ds(low_row, 8 * group)
        values = pl.ds(pl.multiple_of(feats + low_row, 8), 8 * group)
        mixed[some, :] = attend_group(
            pair_buf.at[slot],
            queries[some, :],
            joined(kept[n, some, :] for n in range(blocks)),
            joined(kept[n, values, :] for n in range(blocks)),
            id_column, id_row, log_sums, index * group, score, high, low,
        )
        for copy in mix_copies(index):
            copy.start()

        @pl.when(index == groups // 2)
        def _():
            for n, source in enumerate(sources):
                arrived(w_all.at[squad, core, source], w_recv.at[n])
            for copy in squad_copies:
                copy.start()

        @pl.when(index == max(0, groups - 2))
        def _():
            for peer in peers:
                arrived(k_all.at[blk, peer], k_recv.at[blk, peer])
            for copy in key_copies:
                copy.start()

        @pl.when(index + 2 < groups)
        def _():
            for copy in pair_copies(index + 2, slot):
                copy.start()

        return carry

    lax.fori_loop(0, groups, step, 0)
    mixed.flush()
    log_sums.flush()
    squad_sources = [lax.rem(squad + squads - n, squads) for n in range(squads)]
    for n, source in enumerate(squad_sources):
        ready = w_all.at[source, core]
        if n >= 1:
            arrived(ready, wx_recv.at[n - 1])
        copies.append(send(ready, ready, wf_send.at[n], wf_recv.at[n], sibling))
    for n, source in enumerate(squad_sources):
        arrived(w_all.at[source, other_core], wf_recv.at[n])
    outs = halves(
        jnp.concatenate([w_all[s, kind, n] for n in range(zs) for s in range(squads) for kind in range(2)], axis=0)
    )
    mixed_all[z] = mixed[...]
    for n, source in enumerate(sources):
        for index in range(groups):
            some = pl.ds(index * (8 * group), 8 * group)
            arrived(mixed_all.at[source, some], mix_recv.at[n, index])
    copies += [
        send(q_part.at[peer], q_land.at[z], q_send.at[n], q_recv.at[n], {"head": peer})
        for n, peer in enumerate(peers)
    ]
    ups = up_high[...], up_low[...]
    mixed_rows = mixed_all[...].reshape(zs * feats, rows).T
    hidden_rows = atoms[...] + dot_halves(halves(mixed_rows), outs) + b_out[...]
    hidden_two[...] = hidden_rows
    normal, rate = normalize(hidden_rows)
    normal_two[...] = normal
    rate_two[...] = jnp.broadcast_to(rate, rate_two.shape)
    normed = normal * gain[...] + bias[...]
    pre = dot_halves(halves(normed), ups) + b_up[...]
    phi = 0.5 * (1.0 + lax.erf(pre * math.sqrt(0.5)))
    act = pre * phi
    d_pre = d_act[...] * (phi + pre * jnp.exp(-0.5 * pre * pre) * (1.0 / math.sqrt(2.0 * math.pi)))
    d_pres = halves(d_pre)
    cots, downs = halves(cot[...]), halves(w_down[...])
    part[...] = dot_halves(d_pres, ups, NT).reshape(zs, piece, width)
    copies += [
        send(part.at[peer], landed.at[z], part_send.at[n], part_recv.at[n], {"head": peer})
        for n, peer in enumerate(peers)
    ]
    landed[z] = part[z]
    ups_part[...] = dot_halves(halves(normed.T), d_pres).reshape(ups_part.shape)
    copies.append(send(ups_part.at[:, other_core], ups_sib, sib_send.at[0], sib_recv.at[0], sibling))
    downs_part[...] = dot_halves(halves(act.T), cots).reshape(downs_part.shape)
    copies.append(send(downs_part.at[:, other_core], downs_sib, sib_send.at[1], sib_recv.at[1], sibling))
    down[...] = dot_halves(halves(act), downs)
    out_mine[...] = hidden_two[mine, :] + down[mine, :] + b_down[...]
    out_mine.flush()
    small[SMALL_B_UP : SMALL_B_UP + 1, 0 : d_pre.shape[1]] = column_sum(d_pre)
    for kind, (parts, sib, go, got) in enumerate(
        [(ups_part, ups_sib, ups_go, ups_got), (downs_part, downs_sib, downs_go, downs_got)]
    ):
        arrived(sib, sib_recv.at[kind])
        go[...] = sib[...] + parts[:, core]
        copies += [
            send(
                go.at[peer], got.at[team], g_send.at[kind, n], g_recv.at[kind, team],
                team_device(peer, core, chips),
            )
            for n, peer in enumerate(far_teams)
        ]
        got[team] = go[team]
    for n, source in enumerate(far):
        for m, peer in enumerate(peers):
            ready = k_all.at[source, peer]
            arrived(ready, k_recv.at[source, peer])
            copies.append(send(ready, ready, ks_send.at[n, m], k_recv.at[source, peer], sibling))
    for n, source in enumerate(sources):
        arrived(q_land.at[source], q_recv.at[n])
    for n in range(zs):
        q_all[n] = q_land[n].T
    for n in range(blocks):
        k_all[n, z] = kept[n, 0:feats, :]
    for source in [sib_blk] + far_siblings:
        for peer in peers:
            arrived(k_all.at[source, peer], k_recv.at[source, peer])
    squares[...] = jnp.zeros(squares.shape, F32)
    at_once = 4
    rounds = heads // at_once

    def square_step(index, carry):
        there = lax.div(index, rounds)
        some = pl.ds(pl.multiple_of(lax.rem(index, rounds) * (8 * at_once), 8 * at_once), 8 * at_once)
        q_some = q_all[there, some, :]
        k_some = joined(k_all[n, there, some, :] for n in range(blocks))
        added = None
        for h in range(at_once):
            head = slice(8 * h, 8 * h + 8)
            q_high, q_low = wide_halves(q_some[head])
            k_high, k_low = wide_halves(k_some[head])
            value = dot(
                stacked([q_high, q_high, q_low, q_low]), stacked([k_high, k_low, k_high, k_low]), TN
            )
            added = value * value if added is None else added + value * value
        squares[...] += added
        return carry

    lax.fori_loop(0, zs * rounds, square_step, 0)
    same = id_column[mine, 0:1] == id_row[0:1, :]
    norms = jnp.sqrt(squares[...] + 1.0)
    terms = jnp.where(same, jnp.log1p(jnp.exp(norms - math.sqrt(zs * heads))), 0.0)
    number = jnp.where(same, 1.0, 0.0)

    def total(value):
        return jnp.sum(jnp.sum(value, axis=1, keepdims=True), axis=0, keepdims=True)

    lane = lax.broadcasted_iota(jnp.int32, (1, width), 1)
    small[SMALL_PENALTY : SMALL_PENALTY + 1, :] = jnp.where(
        lane == 0, total(terms), jnp.where(lane == 1, total(number), 0.0)
    )
    for n, source in enumerate(sources):
        arrived(landed.at[source], part_recv.at[n])
    d_normed = functools.reduce(jnp.add, [landed[n] for n in range(zs)])
    normal = normal_two[mine, :]
    d_rows = cot[mine, :] + normalize_back(d_normed, gain[...], normal, rate_two[mine, 0:1])
    d_halves = halves(d_rows)
    for n in range(zs):
        some = slice(n * feats, (n + 1) * feats)
        back[n] = dot_halves(d_halves, (outs[0][some], outs[1][some]), NT)
    settled = len(copies)
    copies += [
        send(back.at[peer], back_landed.at[z], back_send.at[n], back_recv.at[n], {"head": peer})
        for n, peer in enumerate(peers)
    ]
    back_landed[z] = back[z]
    d_hidden[...] = d_rows
    d_hidden.flush()
    for peer, parcel in zip(peers, parcels, strict=True):
        parcel[0:piece, :] = down[pl.ds(pl.multiple_of(peer * piece, 8), piece), :]
        parcel[piece : 2 * piece, :] = d_rows
        parcel.flush()
    small[SMALL_LN2_GAIN : SMALL_LN2_GAIN + 1, :] = column_sum(d_normed * normal)
    small[SMALL_LN2_BIAS : SMALL_LN2_BIAS + 1, :] = column_sum(d_normed)
    small[SMALL_B_OUT : SMALL_B_OUT + 1, :] = column_sum(d_rows)
    small.flush()
    for kind, got in enumerate([ups_got, downs_got]):
        for peer in far_teams:
            arrived(got.at[peer], g_recv.at[kind, peer])
    up_share, down_share = [
        functools.reduce(jnp.add, [got[n] for n in range(teams)]) for got in (ups_got, downs_got)
    ]
    for rows_of, columns_of, there in side_by_side(*up_share.shape, width):
        shares[there, columns_of] = up_share[rows_of]
    shares[there.stop :, :] = down_share
    shares.flush()
    for copy in copies[:settled] + squad_copies + key_copies:
        copy.wait_send()

    def drain(index, carry):
        for copy in mix_copies(index):
            copy.wait_send()
        return carry

    lax.fori_loop(0, groups, drain, 0)
    for n, source in enumerate(sources):
        arrived(back_landed.at[source], back_recv.at[n])
    d_mixed[...] = back_landed[...].reshape(rows, feats).T
    d_mixed.flush()
    for copy in copies[settled:]:
        copy.wait_send()


def front(zs, dps, teams, pair, *operands):
    _, heads, rows, cols = pair.shape
    feats, blocks = heads * DH, cols // rows
    width, units = operands[0].shape[1], operands[12].shape[1]
    piece, group, hops = rows // zs, GROUP, zs - 1
    squads = dps * min(blocks // 2, max(1, feats // (2 * dps * 8)))
    up_rows, down_rows = width // (2 * teams), units // (2 * teams)
    groups = heads // group
    slab = pltpu.VMEM((zs, piece, width), F32)
    narrow = pltpu.VMEM((zs, piece, feats), F32)
    one_up, one_down = pltpu.VMEM((teams, up_rows, units), F32), pltpu.VMEM((teams, down_rows, width), F32)
    dma = pltpu.SemaphoreType.DMA
    return staged_call(
        front_kernel,
        "front",
        operands,
        [
            (feats, rows), (blocks, 2 * feats + 8, rows), (rows, LANES), (heads, rows, LANES), (feats, rows),
            (STRIP, cols), (feats, rows), (piece, width), (piece, width),
            (up_rows * units // width + down_rows, width), (SMALL_ROWS, width),
        ]
        + [(2 * piece, width)] * (zs - 1),
        [
            pltpu.VMEM((2, group, rows, cols), F32),
            pltpu.VMEM((group, rows, cols), F32),
            pltpu.VMEM((group, rows, cols), BF16),
            pltpu.VMEM((group, rows, cols), BF16),
            narrow, narrow,
            pltpu.VMEM((zs, feats, piece), F32),
            pltpu.VMEM((blocks, zs, feats, rows), F32),
            pltpu.VMEM((squads, 2, zs, feats // (2 * squads), width), F32),
            pltpu.VMEM((piece, cols), F32),
            pltpu.VMEM((zs, feats, rows), F32),
            pltpu.VMEM((rows, width), F32),
            pltpu.VMEM((rows, width), F32),
            pltpu.VMEM((rows, units), F32),
            pltpu.VMEM((width, units), BF16),
            pltpu.VMEM((width, units), BF16),
            pltpu.VMEM((rows, width), F32),
            pltpu.VMEM((rows, LANES), F32),
            slab, slab, narrow, narrow,
            pltpu.VMEM((teams, 2, up_rows, units), F32),
            one_up, one_up, one_up,
            pltpu.VMEM((teams, 2, down_rows, width), F32),
            one_down, one_down, one_down,
            dma((2, group)),
            dma((blocks,)), dma((blocks,)),
            dma((hops,)), dma((hops, blocks // 2)), dma((max(1, blocks // 2 - 1), hops)), dma((blocks, zs)),
            dma((hops,)), dma((hops,)),
            dma((hops,)), dma((hops,)), dma((max(1, squads - 1),)), dma((max(1, squads - 1),)),
            dma((squads,)), dma((squads,)),
            dma((hops, groups)), dma((hops, groups)),
            dma((hops,)), dma((hops,)),
            dma((hops,)), dma((hops,)),
            dma((2,)), dma((2,)),
            dma((2, teams)), dma((2, teams)),
        ],
        FRONT_MB,
        remote=0,
        raw=(pair,),
    )


def finish_kernel(operands, results, scratch, raw):
    (
        out_mine, d_hidden, atoms, gain, bias, w_query, mixed, small_in, w_key, w_value,
    ) = operands[:10]
    parcels = operands[10 : 9 + lax.axis_size("head")]
    chip_shares = operands[9 + lax.axis_size("head") :]
    grad_atoms, out_atoms, total_grads, grad_up, grad_down, small, penalty = results
    (
        sib_keys, sib_values, go_keys, go_values, got_keys, got_values,
        part, landed, grads, sib_grads, go_grads, got_grads, hidden_all, small_z, small_all,
        sib_send, sib_recv, kv_send, kv_recv, part_send, part_recv, back_send, back_recv,
        g_send, g_recv, t_send, t_recv, f_send, b_send, b_recv, bf_send, out_send, out_recv,
        small_z_send, small_z_recv, small_send, small_recv, own_heads, heads_sem,
    ) = scratch
    (d_heads,) = raw
    chips, feats, rows = own_heads.shape[0] - 1, d_heads.shape[2] // 2, d_heads.shape[3]
    heads_copy = pltpu.make_async_copy(d_heads.at[pl.ds(0, chips + 1)], own_heads, heads_sem.at[0])
    heads_copy.start()
    zs, piece, width = part.shape
    teams, _, share, _ = grads.shape
    blk, z, dp = lax.axis_index("blk"), lax.axis_index("head"), lax.axis_index("dp")
    core, chip = lax.rem(blk, 2), lax.div(blk, 2)
    other_core = 1 - core
    sibling = {"blk": blk + 1 - 2 * core}
    peers = others(z, zs)
    team = dp * chips + chip
    far_teams = others(team, teams)
    far_chips = others(chip, chips)
    place = team * 2 + core
    far_places = others(place, teams * 2)
    plane = [team_device(lax.div(value, 2), lax.rem(value, 2), chips) for value in far_places]
    meeting = [{"head": peer} for peer in peers] + plane
    greet(meeting)
    meet(meeting)
    copies = [
        send(
            d_heads.at[pl.ds(0, chips), other_core, pl.ds(kind * feats, feats)],
            sib, sib_send.at[kind], sib_recv.at[kind], sibling,
        )
        for kind, sib in enumerate([sib_keys, sib_values])
    ]
    mine = pl.ds(pl.multiple_of(z * piece, 8), piece)
    out_atoms[mine, :] = functools.reduce(jnp.add, [parcel[0:piece, :] for parcel in parcels], out_mine[...])
    copies += [
        send(out_atoms.at[mine], out_atoms.at[mine], out_send.at[n], out_recv.at[z], {"head": peer})
        for n, peer in enumerate(peers)
    ]

    def big_rows(result, source, kind):
        count = result.shape[0] // (2 * teams)
        return result.at[pl.ds(pl.multiple_of((source * 2 + kind) * count, 8), count)]

    partners = others(dp, lax.axis_size("dp"))
    for n in range(chips):
        source = dp * chips + lax.rem(chip + chips - n, chips)
        up_there, down_there = big_rows(grad_up, source, core), big_rows(grad_down, source, core)
        for rows_of, columns_of, there in side_by_side(*up_there.shape, width):
            up_there[rows_of, :] = chip_shares[n][there, columns_of]
        down_there[...] = chip_shares[n][there.stop :, :]
        for kind, ready in enumerate([up_there, down_there]):
            copies += [
                send(ready, ready, b_send.at[kind, n, m], b_recv.at[kind, source, core], {"dp": partner})
                for m, partner in enumerate(partners)
            ]
    heads_copy.wait()
    d_queries = own_heads[chips, 0, 0:feats, :]
    for kind, (sib, go, got) in enumerate([(sib_keys, go_keys, got_keys), (sib_values, go_values, got_values)]):
        arrived(sib, sib_recv.at[kind])
        go[...] = sib[...] + own_heads[0:chips, core, kind * feats : (kind + 1) * feats, :]
        copies += [
            send(
                go.at[peer], got.at[chip], kv_send.at[kind, n], kv_recv.at[kind, chip],
                {"blk": peer * 2 + core},
            )
            for n, peer in enumerate(far_chips)
        ]
    got_keys[chip] = go_keys[chip]
    got_values[chip] = go_values[chip]
    normal, rate = normalize(atoms[...])
    normed = halves(normal * gain[...] + bias[...])
    dq_rows = d_queries.T
    d_normed = dot_full(dq_rows, w_query[...], NT)
    grad_q = dot_halves(halves(d_queries), normed)
    small_z[z] = small_in[0:8, :]
    hidden_all[z] = d_hidden[...]
    for n, parcel in enumerate(parcels):
        hidden_all[lax.rem(z + zs - 1 - n, zs)] = parcel[piece : 2 * piece, :]
    grad_o = dot_full(mixed[...], hidden_all[...].reshape(rows, width))
    for peer in far_chips:
        arrived(got_keys.at[peer], kv_recv.at[0, peer])
        arrived(got_values.at[peer], kv_recv.at[1, peer])
    dk = functools.reduce(jnp.add, [got_keys[n] for n in range(chips)])
    dv = functools.reduce(jnp.add, [got_values[n] for n in range(chips)])
    dv_rows = dv.T
    d_normed = (
        d_normed + dot_full(dk.T, w_key[...], NT) + dot_full(dv_rows, w_value[...], NT)
    )
    part[...] = d_normed.reshape(zs, piece, width)
    copies += [
        send(part.at[peer], landed.at[z], part_send.at[n], part_recv.at[z], {"head": peer})
        for n, peer in enumerate(peers)
    ]
    landed[z] = part[z]
    grad_k = dot_halves(halves(dk), normed)
    grad_v = dot_halves(halves(dv), normed)
    grads[...] = jnp.concatenate([grad_q, grad_k, grad_v, grad_o], axis=0).reshape(grads.shape)
    copies.append(send(grads.at[:, other_core], sib_grads, sib_send.at[2], sib_recv.at[2], sibling))
    arrived(sib_grads, sib_recv.at[2])
    go_grads[...] = sib_grads[...] + grads[:, core]
    copies += [
        send(
            go_grads.at[peer], got_grads.at[team], g_send.at[n], g_recv.at[team], team_device(peer, core, chips)
        )
        for n, peer in enumerate(far_teams)
    ]
    got_grads[team] = go_grads[team]
    for peer in peers:
        arrived(landed.at[peer], part_recv.at[peer])
    d_normed = functools.reduce(jnp.add, [landed[n] for n in range(zs)])
    normal, rate = normalize(atoms[mine, :])
    grad_atoms[mine, :] = d_hidden[...] + normalize_back(d_normed, gain[...], normal, rate)
    small_z[z, SMALL_LN1_GAIN : SMALL_LN1_GAIN + 1, :] = column_sum(d_normed * normal)
    small_z[z, SMALL_LN1_BIAS : SMALL_LN1_BIAS + 1, :] = column_sum(d_normed)
    settled = len(copies)
    copies += [
        send(small_z.at[z], small_z.at[z], small_z_send.at[n], small_z_recv.at[z], {"head": peer})
        for n, peer in enumerate(peers)
    ]
    copies += [
        send(grad_atoms.at[mine], grad_atoms.at[mine], back_send.at[n], back_recv.at[z], {"head": peer})
        for n, peer in enumerate(peers)
    ]
    for peer in far_teams:
        arrived(got_grads.at[peer], g_recv.at[peer])
    total_grads[team, core] = functools.reduce(jnp.add, [got_grads[n] for n in range(teams)])
    ready = total_grads.at[team, core]
    copies.append(send(ready, ready, t_send.at[0], t_recv.at[team, core], sibling))
    copies += [
        send(ready, ready, t_send.at[n + 1], t_recv.at[team, core], team_device(peer, core, chips))
        for n, peer in enumerate(far_teams)
    ]
    for peer in peers:
        arrived(small_z.at[peer], small_z_recv.at[peer])
    small_all[place, 0:8, :] = functools.reduce(jnp.add, [small_z[n] for n in range(zs)])
    small_all[place, 8:16, :] = small_in[8:16, :]
    small_all[place, SMALL_B_QUERY : SMALL_B_QUERY + 1, 0:feats] = column_sum(dq_rows)
    small_all[place, SMALL_B_VALUE : SMALL_B_VALUE + 1, 0:feats] = column_sum(dv_rows)
    copies += [
        send(small_all.at[place], small_all.at[place], small_send.at[n], small_recv.at[place], target)
        for n, target in enumerate(plane)
    ]
    for n, peer in enumerate(far_teams):
        ready = total_grads.at[peer, core]
        arrived(ready, t_recv.at[peer, core])
        copies.append(send(ready, ready, f_send.at[n], t_recv.at[peer, core], sibling))
    for kind, result in enumerate([grad_up, grad_down]):
        for n in range(teams):
            ready = big_rows(result, n, core)

            @pl.when(lax.div(n, chips) != dp)
            def _(ready=ready, sem=b_recv.at[kind, n, core]):
                arrived(ready, sem)

            copies.append(send(ready, ready, bf_send.at[kind, n], b_recv.at[kind, n, core], sibling))
    for copy in copies[:settled]:
        copy.wait_send()
    for source in far_places:
        arrived(small_all.at[source], small_recv.at[source])
    summed = functools.reduce(jnp.add, [small_all[n] for n in range(2 * teams)])
    small[...] = summed
    ends = summed[SMALL_PENALTY : SMALL_PENALTY + 1, :]
    penalty[...] = ends[:, 0:1] / ends[:, 1:2]
    for peer in [team] + far_teams:
        arrived(total_grads.at[peer, other_core], t_recv.at[peer, other_core])
    total_grads.flush()
    for kind, result in enumerate([grad_up, grad_down]):
        for n in range(teams):
            arrived(big_rows(result, n, other_core), b_recv.at[kind, n, other_core])
        result.flush()
    for peer in peers:
        there = pl.ds(pl.multiple_of(peer * piece, 8), piece)
        arrived(out_atoms.at[there], out_recv.at[peer])
    out_atoms.flush()
    for peer in peers:
        there = pl.ds(pl.multiple_of(peer * piece, 8), piece)
        arrived(grad_atoms.at[there], back_recv.at[peer])
    for copy in copies[settled:]:
        copy.wait_send()


def finish(zs, dps, units, d_heads, *operands):
    atoms = operands[2]
    chips, feats, rows = lax.axis_size("blk") // 2, d_heads.shape[2] // 2, d_heads.shape[3]
    width = atoms.shape[1]
    piece = rows // zs
    teams = dps * chips
    share = 4 * feats // (2 * teams)
    some = pltpu.VMEM((chips, feats, rows), F32)
    slab = pltpu.VMEM((zs, piece, width), F32)
    one = pltpu.VMEM((teams, share, width), F32)
    dma = pltpu.SemaphoreType.DMA
    return staged_call(
        finish_kernel,
        "finish",
        operands,
        [
            (rows, width),
            (rows, width),
            (teams, 2, share, width),
            (width, units),
            (units, width),
            (SMALL_ROWS, width),
            (1, 1),
        ],
        [some] * 6
        + [slab, slab, pltpu.VMEM((teams, 2, share, width), F32), one, one, one, slab]
        + [
            pltpu.VMEM((zs, 8, width), F32),
            pltpu.VMEM((2 * teams, SMALL_ROWS, width), F32),
            dma((3,)), dma((3,)),
            dma((2, chips)), dma((2, chips)),
            dma((zs,)), dma((zs,)),
            dma((zs,)), dma((zs,)),
            dma((teams,)), dma((teams,)),
            dma((teams,)), dma((teams, 2)), dma((teams,)),
            dma((2, chips, dps)), dma((2, teams, 2)), dma((2, teams)),
            dma((zs,)), dma((zs,)),
            dma((zs,)), dma((zs,)),
            dma((2 * teams,)), dma((2 * teams,)),
            pltpu.VMEM((chips + 1, 2, 2 * feats, rows), F32), dma((1,)),
        ],
        FINISH_MB,
        remote=2,
        near_in=range(10, len(operands)),
        raw=(d_heads,),
        near_out=range(7),
    )


def place_kernel(operands, results, scratch, raw):
    total_grads, small, penalty_in = operands
    penalty, grad_query, grad_key, grad_value, grad_out = results[:5]
    penalty[...] = penalty_in[...]
    feats, width = grad_out.shape
    done = total_grads[...].reshape(4 * feats, width)
    grad_query[...] = done[0:feats].T
    grad_query.flush()
    grad_key[...] = done[feats : 2 * feats].T
    grad_key.flush()
    grad_value[...] = done[2 * feats : 3 * feats].T
    grad_value.flush()
    grad_out[...] = done[3 * feats :]
    grad_out.flush()
    for result, row in zip(results[5:], SMALL_OUTPUTS, strict=True):
        result[...] = small[row : row + 1, 0 : result.shape[1]]


SMALL_OUTPUTS = (
    SMALL_LN1_GAIN, SMALL_LN1_BIAS, SMALL_B_QUERY, SMALL_B_VALUE, SMALL_B_OUT, SMALL_LN2_GAIN, SMALL_LN2_BIAS,
    SMALL_B_UP, SMALL_B_DOWN,
)


def place(feats, units, straight, *operands):
    width = operands[1].shape[1]
    lengths = {SMALL_B_QUERY: feats, SMALL_B_VALUE: feats, SMALL_B_UP: units}
    return staged_call(
        place_kernel,
        "place",
        operands,
        [(1, 1)]
        + [(width, feats)] * 3
        + [(feats, width)]
        + [(1, lengths.get(row, width)) for row in SMALL_OUTPUTS],
        [],
        PLACE_MB,
        straight=straight,
        near_in=(0, 1, 2),
        near_straight=True,
    )


def local(
    zs, dps,
    atoms, pair, mol_ids, ln1_gain, ln1_bias, w_query, b_query, w_key, w_value, b_value, w_out, b_out,
    ln2_gain, ln2_bias, w_up, b_up, w_down, b_down, cot_atoms, cot_pair,
):
    blocks = pair.shape[3] // pair.shape[2]
    inputs, cot = atoms[0], cot_atoms[0]

    def line(value):
        return value.reshape(1, -1)

    (
        queries, kept, id_column, log_sums, mixed, id_row, d_mixed, out_mine, d_hidden, shares, small, *parcels,
    ) = front(
        zs, dps, dps * blocks // 2, pair,
        inputs, mol_ids, line(ln1_gain), line(ln1_bias), w_key, w_value, line(b_value), w_query, line(b_query),
        w_out, cot, w_down, w_up, line(b_out), line(ln2_gain), line(ln2_bias), line(b_up),
        line(b_down),
    )
    parcels = [
        lax.ppermute(parcel, "head", [(source, (source + n + 1) % zs) for source in range(zs)])
        for n, parcel in enumerate(parcels)
    ]
    chips = blocks // 2
    chip_shares = [shares] + [
        lax.ppermute(shares, "blk", [(2 * c + core, 2 * ((c + n) % chips) + core) for c in range(chips) for core in range(2)])
        for n in range(1, chips)
    ]
    out_pair, grad_pair, d_heads = attend_back(
        pair, cot_pair, queries, kept, mixed, d_mixed, log_sums, id_column, id_row
    )
    grad_atoms, out_atoms, total_grads, grad_up, grad_down, small, penalty = finish(
        zs, dps, w_up.shape[1],
        d_heads, out_mine, d_hidden, inputs, line(ln1_gain), line(ln1_bias), w_query, mixed,
        small, w_key, w_value, *parcels, *chip_shares,
    )
    placed = place(
        w_query.shape[1], w_up.shape[1],
        [grad_atoms, out_atoms, grad_up, grad_down],
        total_grads, small, penalty,
    )
    grad_atoms, out_atoms, grad_up, grad_down, penalty, grad_query, grad_key, grad_value, grad_out = placed[:9]
    (
        grad_ln1_gain, grad_ln1_bias, grad_b_query, grad_b_value, grad_b_out, grad_ln2_gain, grad_ln2_bias,
        grad_b_up, grad_b_down,
    ) = [value.reshape(-1) for value in placed[9:]]
    return (
        out_atoms[None],
        out_pair,
        penalty[0, 0],
        grad_atoms[None],
        grad_pair,
        grad_ln1_gain,
        grad_ln1_bias,
        grad_query,
        grad_b_query,
        grad_key,
        grad_value,
        grad_b_value,
        grad_out,
        grad_b_out,
        grad_ln2_gain,
        grad_ln2_bias,
        grad_up,
        grad_b_up,
        grad_down,
        grad_b_down,
    )


def solution(mesh):
    rows, pairs = P("dp", "blk", None), P("dp", "head", "blk", None)
    columns = P(None, "head")
    return jax.shard_map(
        functools.partial(local, mesh.shape["head"], mesh.shape["dp"]),
        mesh=mesh,
        in_specs=(
            rows, pairs, P("dp", "blk"), P(), P(), columns, P("head"), columns, columns, P("head"),
            P("head", None), P(), P(), P(), columns, P("head"), P("head", None), P(), rows, pairs,
        ),
        out_specs=(
            rows, pairs, P(), rows, pairs, P(), P(), columns, P("head"), columns, columns, P("head"),
            P("head", None), P(), P(), P(), columns, P("head"), P("head", None), P(),
        ),
        check_vma=False,
    )
```

```python
import functools
import math

import jax
import jax.numpy as jnp
from jax import lax
from jax.experimental import pallas as pl
from jax.experimental.pallas import tpu as pltpu
from jax.sharding import PartitionSpec as P

DH = 8
LANES = 128
STRIP = 16
CHUNK = 256
GROUP = 2
FRONT_MB, BACK_MB, FINISH_MB, PLACE_MB = 58, 60, 40, 32
NORM_EPS = 1e-05
MASK_FILL = -1e30
F32 = jnp.float32
BF16 = jnp.bfloat16
MESH = pl.DeviceIdType.MESH
NN = (((1,), (0,)), ((), ()))
NT = (((1,), (1,)), ((), ()))
TN = (((0,), (0,)), ((), ()))
VMEM = pl.BlockSpec(memory_space=pltpu.VMEM)


def dot(left, right, dims=NN):
    return lax.dot_general(left, right, dims, preferred_element_type=F32)


def halves(value):
    high = value.astype(BF16)
    return high, (value - high.astype(F32)).astype(BF16)


def dot_halves(left, right, dims=NN):
    return dot(left[0], right[0], dims) + (
        dot(left[0], right[1], dims) + dot(left[1], right[0], dims)
    )


def dot_full(left, right, dims=NN):
    return dot_halves(halves(left), halves(right), dims)


def normalize(inputs):
    centred = inputs - jnp.mean(inputs, -1, keepdims=True)
    rate = lax.rsqrt(jnp.mean(centred * centred, -1, keepdims=True) + NORM_EPS)
    return centred * rate, rate


def normalize_back(grad, gain, normal, rate):
    scaled = grad * gain
    return rate * (
        scaled
        - jnp.mean(scaled, -1, keepdims=True)
        - normal * jnp.mean(scaled * normal, -1, keepdims=True)
    )


def column_sum(value):
    return jnp.sum(value, 0, keepdims=True)


def send(src, dst, send_sem, recv_sem, target):
    copy = pltpu.make_async_remote_copy(
        src_ref=src,
        dst_ref=dst,
        send_sem=send_sem,
        recv_sem=recv_sem,
        device_id=target,
        device_id_type=MESH,
    )
    copy.start()
    return copy


def arrived(ref, sem):
    pltpu.make_async_remote_copy(
        src_ref=ref, dst_ref=ref, send_sem=sem, recv_sem=sem, device_id={}, device_id_type=MESH
    ).wait_recv()


def greet(targets):
    for target in targets:
        pl.semaphore_signal(pltpu.get_barrier_semaphore(), inc=1, device_id=target, device_id_type=MESH)


def meet(targets):
    pl.semaphore_wait(pltpu.get_barrier_semaphore(), len(targets))


def others(index, count):
    return [lax.rem(index + step, count) for step in range(1, count)]


class Operand:
    def __init__(self, source, slot, sem):
        self.source, self.slot, self.shape = source, slot, slot.shape
        self.copy = None if sem is None else pltpu.make_async_copy(source, slot, sem)
        if self.copy is not None:
            self.copy.start()

    @property
    def ref(self):
        if self.copy is not None:
            self.copy.wait()
            self.copy = None
        return self.slot

    def __getitem__(self, index):
        return self.ref[index]


class Result:
    def __init__(self, target, slot, sem):
        self.slot, self.shape, self.at = slot, slot.shape, slot.at
        self.copy = None if sem is None else pltpu.make_async_copy(slot, target, sem)
        self.begun = self.copy is None

    def __setitem__(self, index, value):
        self.slot[index] = value

    def __getitem__(self, index):
        return self.slot[index]

    def flush(self):
        if not self.begun:
            self.copy.start()
            self.begun = True


def staged_call(
    kernel, name, operands, results, scratch, megabytes,
    remote=None, raw=(), straight=(), raw_results=(), cost=None, near_in=(), near_out=(), near_straight=False,
):
    n_in, n_out, n_raw, n_straight = len(operands), len(results), len(raw), len(straight)
    n_left = len(raw_results)
    far_in = [n for n in range(n_in) if n not in near_in]
    far_out = [n for n in range(n_out) if n not in near_out]

    def body(*refs):
        sources, left, refs = refs[:n_in], refs[n_in : n_in + n_raw], refs[n_in + n_raw :]
        moved, refs = refs[:n_straight], refs[n_straight:]
        arrays, refs = refs[:n_straight], refs[n_straight:]
        left, refs = left + refs[:n_left], refs[n_left:]
        targets, refs = refs[:n_out], refs[n_out:]
        in_slots, refs = dict(zip(far_in, refs)), refs[len(far_in) :]
        out_slots, refs = dict(zip(far_out, refs)), refs[len(far_out) :]
        in_sem, out_sem, move_sem, refs = refs[0], refs[1], refs[2], refs[3:]
        through, loads = moved, []
        if not near_straight:
            through, refs = refs[:n_straight], refs[n_straight:]
            loads = [pltpu.make_async_copy(moved[n], through[n], move_sem.at[n]) for n in range(n_straight)]
        moves = [pltpu.make_async_copy(through[n], arrays[n], move_sem.at[n]) for n in range(n_straight)]
        for load in loads:
            load.start()
        ins = [
            Operand(sources[n], in_slots.get(n, sources[n]), in_sem.at[far_in.index(n)] if n in in_slots else None)
            for n in range(n_in)
        ]
        outs = [
            Result(targets[n], out_slots.get(n, targets[n]), out_sem.at[far_out.index(n)] if n in out_slots else None)
            for n in range(n_out)
        ]
        for load in loads:
            load.wait()
        for move in moves:
            move.start()
        kernel(ins, outs, refs, left)
        for operand in ins:
            operand.ref
        for result in outs:
            result.flush()
        for copy in moves + [result.copy for result in outs if result.copy is not None]:
            copy.wait()

    hbm, vmem = pl.BlockSpec(memory_space=pltpu.HBM), pl.BlockSpec(memory_space=pltpu.VMEM)
    extra = {} if remote is None else {"collective_id": remote, "has_side_effects": True}
    return pl.pallas_call(
        body,
        out_shape=[jax.ShapeDtypeStruct(value.shape, value.dtype) for value in straight]
        + [jax.ShapeDtypeStruct(shape, F32) for shape in raw_results]
        + [jax.ShapeDtypeStruct(shape, F32) for shape in results],
        in_specs=[vmem if n in near_in else hbm for n in range(n_in)]
        + [hbm] * n_raw
        + [vmem if near_straight else hbm] * n_straight,
        out_specs=[hbm] * (n_straight + n_left) + [vmem if n in near_out else hbm for n in range(n_out)],
        scratch_shapes=[pltpu.VMEM(operands[n].shape, operands[n].dtype) for n in far_in]
        + [pltpu.VMEM(results[n], F32) for n in far_out]
        + [pltpu.SemaphoreType.DMA((max(1, n),)) for n in (len(far_in), len(far_out), n_straight)]
        + ([] if near_straight else [pltpu.VMEM(value.shape, value.dtype) for value in straight])
        + list(scratch),
        compiler_params=pltpu.CompilerParams(vmem_limit_bytes=megabytes << 20, **extra),
        cost_estimate=cost,
        name=name,
    )(*operands, *raw, *straight)


def joined(pieces):
    return jnp.concatenate(list(pieces), axis=1)


def stacked(parts):
    return jnp.concatenate(parts, axis=0).astype(BF16)


def wide_halves(value):
    high = value.astype(BF16).astype(F32)
    return high, value - high


def attend_group(pair, queries, keys, values, id_column, id_row, log_sums, first, score, high, low):
    group, rows, cols = score.shape
    strips = rows // STRIP
    chunk = min(CHUNK, cols)
    mixed = []
    for g in range(group):
        head = slice(8 * g, 8 * g + 8)
        q_high, q_low = wide_halves(queries[head, :])
        k_high, k_low = wide_halves(keys[head, :])
        v_high, v_low = wide_halves(values[head, :])
        ones = jnp.ones_like(v_high)
        q_pack = stacked([q_high, q_high, q_low, q_low])
        k_pack = stacked([k_high, k_low, k_high, k_low])
        v_pack = stacked([v_high, v_low, ones, jnp.zeros_like(ones)])
        tops = [None] * strips
        for start in range(0, cols, chunk):
            part = slice(start, start + chunk)
            score[g, :, part] = dot(q_pack, k_pack[:, part], TN)
            for s in range(strips):
                line = pl.ds(s * STRIP, STRIP)
                own = id_column[line, :]
                for j in range(start, start + chunk, LANES):
                    tile = pl.ds(j, LANES)
                    value = pair[g, line, tile] + score[g, line, tile]
                    value = jnp.where(own == id_row[:, tile], value, MASK_FILL)
                    score[g, line, tile] = value
                    tops[s] = value if tops[s] is None else jnp.maximum(tops[s], value)
        tops = [
            jnp.broadcast_to(jnp.max(top, axis=1, keepdims=True), (STRIP, LANES)) for top in tops
        ]
        totals = [None] * strips
        gathered = None
        for start in range(0, cols, chunk):
            part = slice(start, start + chunk)
            for s in range(strips):
                line = pl.ds(s * STRIP, STRIP)
                for j in range(start, start + chunk, LANES):
                    tile = pl.ds(j, LANES)
                    weight = jnp.exp(score[g, line, tile] - tops[s])
                    high[g, line, tile], low[g, line, tile] = halves(weight)
                    totals[s] = weight if totals[s] is None else totals[s] + weight
            term = dot(v_pack[:, part], high[g, :, part], NT) + dot(
                v_pack[:, part], low[g, :, part], NT
            )
            gathered = term if gathered is None else gathered + term
        for s in range(strips):
            total = jnp.sum(totals[s], axis=1, keepdims=True)
            log_sums[first + g, pl.ds(s * STRIP, STRIP), :] = tops[s] + jnp.log(total)
        mixed.append((gathered[0:8] + gathered[8:16]) / gathered[16:17])
    return jnp.concatenate(mixed, axis=0)


def chunks_of(cols):
    chunk = min(CHUNK, cols)
    return [slice(start, start + chunk) for start in range(0, cols, chunk)]


def score_packs(queries, keys):
    q_high, q_low = wide_halves(queries)
    k_high, k_low = wide_halves(keys)
    return stacked([q_high, q_high, q_low, q_low]), stacked([k_high, k_low, k_high, k_low])


def attend_back_kernel(operands, results, scratch, raw):
    queries, kept, d_mixed, mixed, id_column, id_row = operands
    pair, cot, log_sums, out_pair, grad_pair, heads_out = raw
    pair_buf, cot_buf, log_buf, out_buf, grad_buf = scratch[:5]
    here = scratch[5:11]
    d_heads, in_sem, out_sem, heads_sem = scratch[11:]
    heads = pair.shape[1]
    feats = heads * DH
    depth, rows, cols = pair_buf.shape
    blocks = kept.shape[0]
    parts = chunks_of(cols)
    place = lax.broadcasted_iota(jnp.int32, (8, rows), 0)

    def inward(index):
        slot = lax.rem(index, depth)
        sources = (pair.at[0, index], cot.at[0, index], log_sums.at[index])
        return [
            pltpu.make_async_copy(source, buf.at[slot], in_sem.at[n, slot])
            for n, (source, buf) in enumerate(zip(sources, (pair_buf, cot_buf, log_buf), strict=True))
        ]

    def outward(index):
        slot = lax.rem(index, depth)
        return [
            pltpu.make_async_copy(buf.at[slot], array.at[0, index], out_sem.at[n, slot])
            for n, (array, buf) in enumerate([(out_pair, out_buf), (grad_pair, grad_buf)])
        ]

    for n in range(2):
        for copy in inward(n):
            copy.start()
    for operand in operands:
        operand.ref

    def rows_of(index):
        return pl.ds(pl.multiple_of(index * 8, 8), 8)

    def key_rows(index):
        return joined(kept[n, rows_of(index), :] for n in range(blocks))

    def value_row(index):
        return pl.ds(pl.multiple_of(feats + index * 8, 8), 8)

    def value_rows(index):
        return joined(kept[n, value_row(index), :] for n in range(blocks))

    def packs(index):
        head = rows_of(index)
        q_pack, k_pack = score_packs(queries[head, :], key_rows(index))
        v_high, v_low = wide_halves(value_rows(index))
        m_high, m_low = wide_halves(d_mixed[head, :])
        delta_high, rest = wide_halves(-column_sum(mixed[head, :] * d_mixed[head, :]))
        delta_mid, delta_low = wide_halves(rest)
        deltas = jnp.where(
            place == 0, delta_high, jnp.where(place == 1, delta_mid, jnp.where(place == 2, delta_low, 0.0))
        )
        m_pack = stacked([m_high, m_high, m_low, deltas])
        v_pack = stacked([v_high, v_low, v_high, jnp.ones_like(v_high)])
        return q_pack, k_pack, m_pack, v_pack

    def pairs(index):
        head = rows_of(index)
        return [stacked(wide_halves(value)) for value in (queries[head, :], key_rows(index), d_mixed[head, :])]

    def before(pack, part, there):
        q_pack, k_pack, m_pack, v_pack = pack
        there[0][:, part] = dot(q_pack, k_pack[:, part], TN)
        there[1][:, part] = dot(m_pack, v_pack[:, part], TN)

    def middle(index, slot, part, here):
        score, d_prob, p_high, p_low, g_high, g_low = here
        for s in range(rows // STRIP):
            line = pl.ds(s * STRIP, STRIP)
            own = id_column[line, :]
            log_sum = log_buf[slot, line, :]
            for j in range(part.start, part.stop, LANES):
                tile = pl.ds(j, LANES)
                value = pair_buf[slot, line, tile] + score[line, tile]
                out_buf[slot, line, tile] = value
                prob = jnp.exp(jnp.where(own == id_row[:, tile], value - log_sum, MASK_FILL))
                p_high[line, tile], p_low[line, tile] = halves(prob)
                grad = prob * d_prob[line, tile] + cot_buf[slot, line, tile]
                grad_buf[slot, line, tile] = grad
                g_high[line, tile], g_low[line, tile] = halves(grad)

    def both(left, high, low, dims):
        value = dot(left, high, dims) + dot(left, low, dims)
        return value[0:8] + value[8:16]

    def after(index, pair_of, part, there):
        q_pair, k_pair, m_pair = pair_of
        _, _, p_high, p_low, g_high, g_low = there
        head = rows_of(index)
        d_value = both(m_pair, p_high[:, part], p_low[:, part], NN)
        d_key = both(q_pair, g_high[:, part], g_low[:, part], NN)
        for n in range(part.start // rows, part.stop // rows):
            span = slice(n * rows - part.start, (n + 1) * rows - part.start)
            d_heads[n // 2, n % 2, head, :] = d_key[:, span]
            d_heads[n // 2, n % 2, value_row(index), :] = d_value[:, span]
        return both(k_pair[:, part], g_high[:, part], g_low[:, part], NT)

    def stage(index, carry):
        slot = lax.rem(index, depth)
        for copy in inward(index):
            copy.wait()

        @pl.when(index >= depth)
        def _():
            for copy in outward(index - depth):
                copy.wait()

        @pl.when(index == 0)
        def _():
            for n in range(2, depth - 1):
                for copy in inward(n):
                    copy.start()

        @pl.when(index + depth - 1 < heads)
        def _():
            for copy in inward(index + depth - 1):
                copy.start()

        next_packs, own_pairs = packs(index), pairs(index)
        d_query = None
        ahead, behind = 3, 1
        for n in range(-ahead, len(parts) + behind):
            if 0 <= n + ahead < len(parts):
                before(next_packs, parts[n + ahead], here)
            if 0 <= n < len(parts):
                middle(index, slot, parts[n], here)
            if 0 <= n - behind < len(parts):
                term = after(index, own_pairs, parts[n - behind], here)
                d_query = term if d_query is None else d_query + term
        d_heads[blocks // 2, 0, rows_of(index), :] = d_query * (DH ** (-0.5))
        for copy in outward(index):
            copy.start()
        return carry

    lax.fori_loop(0, heads, stage, 0)
    last = pltpu.make_async_copy(d_heads, heads_out.at[pl.ds(0, d_heads.shape[0])], heads_sem.at[0])
    last.start()
    for n in range(max(0, heads - depth), heads):
        for copy in outward(n):
            copy.wait()
    last.wait()


def attend_back(pair, cot, queries, kept, mixed, d_mixed, log_sums, id_column, id_row):
    _, heads, rows, cols = pair.shape
    feats = heads * DH
    blocks = kept.shape[0]
    depth = 6
    entries = max(blocks // 2 + 1, (26 << 20) // (16 * feats * rows))
    wide, thin = pltpu.VMEM((rows, cols), F32), pltpu.VMEM((rows, cols), BF16)
    return staged_call(
        attend_back_kernel,
        "attend_back",
        [queries, kept, d_mixed, mixed, id_column, id_row],
        [],
        [pltpu.VMEM((depth, rows, cols), F32)] * 2
        + [pltpu.VMEM((depth, rows, LANES), F32)]
        + [pltpu.VMEM((depth, rows, cols), F32)] * 2
        + [wide] * 2
        + [thin] * 4
        + [pltpu.VMEM((blocks // 2 + 1, 2, 2 * feats, rows), F32)]
        + [pltpu.SemaphoreType.DMA((n, depth)) for n in (3, 2)]
        + [pltpu.SemaphoreType.DMA((1,))],
        BACK_MB,
        raw=(pair, cot, log_sums),
        raw_results=(pair.shape, pair.shape, (entries, 2, 2 * feats, rows)),
        cost=pl.CostEstimate(
            flops=2 * 400 * heads * rows * cols,
            bytes_accessed=16 * heads * rows * cols,
            transcendentals=heads * rows * cols,
        ),
    )


SMALL_LN1_GAIN, SMALL_LN1_BIAS, SMALL_LN2_GAIN, SMALL_LN2_BIAS = 0, 1, 2, 3
SMALL_B_OUT, SMALL_B_DOWN, SMALL_PENALTY = 4, 5, 6
SMALL_B_QUERY, SMALL_B_VALUE, SMALL_B_UP = 8, 9, 10
SMALL_ROWS = 16


def side_by_side(count, units, width):
    beside = width // units
    height = count // beside
    return [
        (slice(n * height, (n + 1) * height), slice(n * units, (n + 1) * units), slice(0, height))
        for n in range(beside)
    ]


def team_device(team, core, chips):
    return {"dp": lax.div(team, chips), "blk": lax.rem(team, chips) * 2 + core}


def front_kernel(operands, results, scratch, raw):
    (
        atoms, ids, gain_one, bias_one, w_key, w_value, b_value, w_query, b_query, w_out, cot, w_down, w_up, b_out,
        gain, bias, b_up, b_down,
    ) = operands
    (pair,) = raw
    (
        queries, kept, id_column, log_sums, mixed, id_row, d_mixed, out_mine, d_hidden, shares, small,
    ) = results[:11]
    parcels = results[11:]
    (
        pair_buf, score, high, low, q_part, q_land, q_all, k_all, w_all, squares, mixed_all, hidden_two, down, d_act, up_high, up_low, normal_two, rate_two,
        part, landed, back, back_landed, ups_part, ups_sib, ups_go, ups_got, downs_part, downs_sib, downs_go, downs_got,
        pair_sem, kept_send, kept_recv, kz_send, kf_send, ks_send, k_recv, q_send, q_recv, w_send, w_recv, wx_send, wx_recv, wf_send, wf_recv,
        mix_send, mix_recv, part_send, part_recv, back_send, back_recv, sib_send, sib_recv, g_send, g_recv,
    ) = scratch
    zs, feats, rows = mixed_all.shape
    blocks = kept.shape[0]
    chips = blocks // 2
    teams, width = ups_part.shape[0], atoms.shape[1]
    _, group, _, cols = pair_buf.shape
    heads = feats // DH
    groups = heads // group
    piece = rows // zs
    z, blk = lax.axis_index("head"), lax.axis_index("blk")
    core, chip = lax.rem(blk, 2), lax.div(blk, 2)
    dp, dps = lax.axis_index("dp"), lax.axis_size("dp")
    team = dp * chips + chip
    other_core = 1 - core
    sib_blk = blk + 1 - 2 * core
    sibling = {"blk": sib_blk}
    peers, far_teams = others(z, zs), others(team, teams)
    sources = [lax.rem(z + zs - n, zs) for n in range(1, zs)]
    far = [step * 2 + core for step in others(chip, chips)]
    far_siblings = [step * 2 + other_core for step in others(chip, chips)]
    mine = pl.ds(pl.multiple_of(z * piece, 8), piece)

    def pair_copies(index, slot):
        return [
            pltpu.make_async_copy(pair.at[0, index * group + n], pair_buf.at[slot, n], pair_sem.at[slot, n])
            for n in range(group)
        ]

    meeting = [{"head": peer} for peer in peers] + [sibling]
    meeting += [team_device(peer, core, chips) for peer in far_teams]
    greet(meeting)

    normal, _ = normalize(atoms[...])
    normed = halves(normal * gain_one[...] + bias_one[...])
    meet(meeting)
    for n in range(2):
        for copy in pair_copies(n, n):
            copy.start()
    copies = []
    squads, _, _, fewer, _ = w_all.shape
    close = squads // dps
    base = chip - lax.rem(chip, close)
    squad = dp * close + chip - base
    w_mine = w_out.source.at[pl.ds(pl.multiple_of((squad * 2 + core) * fewer, 8), fewer)]
    copies += [
        send(w_mine, w_all.at[squad, core, z], w_send.at[n], w_recv.at[n], {"head": peer})
        for n, peer in enumerate(peers)
    ]
    kept[blk, 0:feats, :] = dot_halves(normed, halves(w_key[...])).T
    copies += [
        send(kept.at[blk, 0:feats], k_all.at[blk, z], kz_send.at[n], k_recv.at[blk, z], {"head": peer})
        for n, peer in enumerate(peers)
    ]
    kept[blk, feats : 2 * feats, :] = (dot_halves(normed, halves(w_value[...])) + b_value[...]).T
    id_line = ids[...].astype(F32)
    kept[blk, 2 * feats : 2 * feats + 8, :] = jnp.broadcast_to(id_line, (8, rows))
    copies += [
        send(kept.at[blk], kept.at[blk], kept_send.at[n], kept_recv.at[blk], {"blk": peer})
        for n, peer in enumerate([sib_blk] + far)
    ]
    q_rows = (dot_halves(normed, halves(w_query[...])) + b_query[...]) * (DH ** (-0.5))
    q_part[...] = q_rows.reshape(zs, piece, feats)
    queries[...] = q_rows.T
    queries.flush()
    q_land[z] = q_part[z]
    w_all[squad, core, z] = w_out[pl.ds(pl.multiple_of((squad * 2 + core) * fewer, 8), fewer), :]
    id_column[...] = jnp.broadcast_to(id_line, (LANES, rows)).T
    id_column.flush()
    small[...] = jnp.zeros(small.shape, F32)
    small[SMALL_B_DOWN : SMALL_B_DOWN + 1, :] = column_sum(cot[mine, :])
    d_act[...] = dot_full(cot[...], w_down[...], NT)
    up_high[...], up_low[...] = halves(w_up[...])
    for n, source in enumerate(far):
        arrived(kept.at[source], kept_recv.at[source])
        copies.append(
            send(kept.at[source], kept.at[source], kept_send.at[chips + n], kept_recv.at[source], sibling)
        )
    for source in [sib_blk] + far_siblings:
        arrived(kept.at[source], kept_recv.at[source])
    kept.flush()
    one = joined(kept[n, 2 * feats : 2 * feats + 8, :] for n in range(blocks))
    id_row[...] = jnp.concatenate([one, one], axis=0)
    id_row.flush()

    def mix_copies(index):
        some = pl.ds(pl.multiple_of(index * (8 * group), 8 * group), 8 * group)
        return [
            pltpu.make_async_remote_copy(
                src_ref=mixed.at[some],
                dst_ref=mixed_all.at[z, some],
                send_sem=mix_send.at[n, index],
                recv_sem=mix_recv.at[n, index],
                device_id={"head": peer},
                device_id_type=MESH,
            )
            for n, peer in enumerate(peers)
        ]

    squad_copies = [
        pltpu.make_async_remote_copy(
            src_ref=w_all.at[squad, core],
            dst_ref=w_all.at[squad, core],
            send_sem=wx_send.at[n - 1],
            recv_sem=wx_recv.at[n - 1],
            device_id={
                "dp": lax.div(lax.rem(squad + n, squads), close),
                "blk": (base + lax.rem(lax.rem(squad + n, squads), close)) * 2 + core,
            },
            device_id_type=MESH,
        )
        for n in range(1, squads)
    ]

    key_copies = [
        pltpu.make_async_remote_copy(
            src_ref=k_all.at[blk, peer],
            dst_ref=k_all.at[blk, peer],
            send_sem=kf_send.at[n, m],
            recv_sem=k_recv.at[blk, peer],
            device_id={"blk": target},
            device_id_type=MESH,
        )
        for n, peer in enumerate(peers)
        for m, target in enumerate([sib_blk] + far)
    ]

    def step(index, carry):
        slot = lax.rem(index, 2)
        for copy in pair_copies(index, slot):
            copy.wait()
        low_row = pl.multiple_of(index * (8 * group), 8 * group)
        some = pl.ds(low_row, 8 * group)
        values = pl.ds(pl.multiple_of(feats + low_row, 8), 8 * group)
        mixed[some, :] = attend_group(
            pair_buf.at[slot],
            queries[some, :],
            joined(kept[n, some, :] for n in range(blocks)),
            joined(kept[n, values, :] for n in range(blocks)),
            id_column, id_row, log_sums, index * group, score, high, low,
        )
        for copy in mix_copies(index):
            copy.start()

        @pl.when(index == groups // 2)
        def _():
            for n, source in enumerate(sources):
                arrived(w_all.at[squad, core, source], w_recv.at[n])
            for copy in squad_copies:
                copy.start()

        @pl.when(index == max(0, groups - 2))
        def _():
            for peer in peers:
                arrived(k_all.at[blk, peer], k_recv.at[blk, peer])
            for copy in key_copies:
                copy.start()

        @pl.when(index + 2 < groups)
        def _():
            for copy in pair_copies(index + 2, slot):
                copy.start()

        return carry

    lax.fori_loop(0, groups, step, 0)
    mixed.flush()
    log_sums.flush()
    squad_sources = [lax.rem(squad + squads - n, squads) for n in range(squads)]
    for n, source in enumerate(squad_sources):
        ready = w_all.at[source, core]
        if n >= 1:
            arrived(ready, wx_recv.at[n - 1])
        copies.append(send(ready, ready, wf_send.at[n], wf_recv.at[n], sibling))
    for n, source in enumerate(squad_sources):
        arrived(w_all.at[source, other_core], wf_recv.at[n])
    outs = halves(
        jnp.concatenate([w_all[s, kind, n] for n in range(zs) for s in range(squads) for kind in range(2)], axis=0)
    )
    mixed_all[z] = mixed[...]
    for n, source in enumerate(sources):
        for index in range(groups):
            some = pl.ds(index * (8 * group), 8 * group)
            arrived(mixed_all.at[source, some], mix_recv.at[n, index])
    copies += [
        send(q_part.at[peer], q_land.at[z], q_send.at[n], q_recv.at[n], {"head": peer})
        for n, peer in enumerate(peers)
    ]
    ups = up_high[...], up_low[...]
    mixed_rows = mixed_all[...].reshape(zs * feats, rows).T
    hidden_rows = atoms[...] + dot_halves(halves(mixed_rows), outs) + b_out[...]
    hidden_two[...] = hidden_rows
    normal, rate = normalize(hidden_rows)
    normal_two[...] = normal
    rate_two[...] = jnp.broadcast_to(rate, rate_two.shape)
    normed = normal * gain[...] + bias[...]
    pre = dot_halves(halves(normed), ups) + b_up[...]
    phi = 0.5 * (1.0 + lax.erf(pre * math.sqrt(0.5)))
    act = pre * phi
    d_pre = d_act[...] * (phi + pre * jnp.exp(-0.5 * pre * pre) * (1.0 / math.sqrt(2.0 * math.pi)))
    d_pres = halves(d_pre)
    cots, downs = halves(cot[...]), halves(w_down[...])
    part[...] = dot_halves(d_pres, ups, NT).reshape(zs, piece, width)
    copies += [
        send(part.at[peer], landed.at[z], part_send.at[n], part_recv.at[n], {"head": peer})
        for n, peer in enumerate(peers)
    ]
    landed[z] = part[z]
    ups_part[...] = dot_halves(halves(normed.T), d_pres).reshape(ups_part.shape)
    copies.append(send(ups_part.at[:, other_core], ups_sib, sib_send.at[0], sib_recv.at[0], sibling))
    downs_part[...] = dot_halves(halves(act.T), cots).reshape(downs_part.shape)
    copies.append(send(downs_part.at[:, other_core], downs_sib, sib_send.at[1], sib_recv.at[1], sibling))
    down[...] = dot_halves(halves(act), downs)
    out_mine[...] = hidden_two[mine, :] + down[mine, :] + b_down[...]
    out_mine.flush()
    small[SMALL_B_UP : SMALL_B_UP + 1, 0 : d_pre.shape[1]] = column_sum(d_pre)
    for kind, (parts, sib, go, got) in enumerate(
        [(ups_part, ups_sib, ups_go, ups_got), (downs_part, downs_sib, downs_go, downs_got)]
    ):
        arrived(sib, sib_recv.at[kind])
        go[...] = sib[...] + parts[:, core]
        copies += [
            send(
                go.at[peer], got.at[team], g_send.at[kind, n], g_recv.at[kind, team],
                team_device(peer, core, chips),
            )
            for n, peer in enumerate(far_teams)
        ]
        got[team] = go[team]
    for n, source in enumerate(far):
        for m, peer in enumerate(peers):
            ready = k_all.at[source, peer]
            arrived(ready, k_recv.at[source, peer])
            copies.append(send(ready, ready, ks_send.at[n, m], k_recv.at[source, peer], sibling))
    for n, source in enumerate(sources):
        arrived(q_land.at[source], q_recv.at[n])
    for n in range(zs):
        q_all[n] = q_land[n].T
    for n in range(blocks):
        k_all[n, z] = kept[n, 0:feats, :]
    for source in [sib_blk] + far_siblings:
        for peer in peers:
            arrived(k_all.at[source, peer], k_recv.at[source, peer])
    squares[...] = jnp.zeros(squares.shape, F32)
    at_once = 4
    rounds = heads // at_once

    def square_step(index, carry):
        there = lax.div(index, rounds)
        some = pl.ds(pl.multiple_of(lax.rem(index, rounds) * (8 * at_once), 8 * at_once), 8 * at_once)
        q_some = q_all[there, some, :]
        k_some = joined(k_all[n, there, some, :] for n in range(blocks))
        added = None
        for h in range(at_once):
            head = slice(8 * h, 8 * h + 8)
            q_high, q_low = wide_halves(q_some[head])
            k_high, k_low = wide_halves(k_some[head])
            value = dot(
                stacked([q_high, q_high, q_low, q_low]), stacked([k_high, k_low, k_high, k_low]), TN
            )
            added = value * value if added is None else added + value * value
        squares[...] += added
        return carry

    lax.fori_loop(0, zs * rounds, square_step, 0)
    same = id_column[mine, 0:1] == id_row[0:1, :]
    norms = jnp.sqrt(squares[...] + 1.0)
    terms = jnp.where(same, jnp.log1p(jnp.exp(norms - math.sqrt(zs * heads))), 0.0)
    number = jnp.where(same, 1.0, 0.0)

    def total(value):
        return jnp.sum(jnp.sum(value, axis=1, keepdims=True), axis=0, keepdims=True)

    lane = lax.broadcasted_iota(jnp.int32, (1, width), 1)
    small[SMALL_PENALTY : SMALL_PENALTY + 1, :] = jnp.where(
        lane == 0, total(terms), jnp.where(lane == 1, total(number), 0.0)
    )
    for n, source in enumerate(sources):
        arrived(landed.at[source], part_recv.at[n])
    d_normed = functools.reduce(jnp.add, [landed[n] for n in range(zs)])
    normal = normal_two[mine, :]
    d_rows = cot[mine, :] + normalize_back(d_normed, gain[...], normal, rate_two[mine, 0:1])
    d_halves = halves(d_rows)
    for n in range(zs):
        some = slice(n * feats, (n + 1) * feats)
        back[n] = dot_halves(d_halves, (outs[0][some], outs[1][some]), NT)
    copies += [
        send(back.at[peer], back_landed.at[z], back_send.at[n], back_recv.at[n], {"head": peer})
        for n, peer in enumerate(peers)
    ]
    back_landed[z] = back[z]
    d_hidden[...] = d_rows
    d_hidden.flush()
    for peer, parcel in zip(peers, parcels, strict=True):
        parcel[0:piece, :] = down[pl.ds(pl.multiple_of(peer * piece, 8), piece), :]
        parcel[piece : 2 * piece, :] = d_rows
        parcel.flush()
    small[SMALL_LN2_GAIN : SMALL_LN2_GAIN + 1, :] = column_sum(d_normed * normal)
    small[SMALL_LN2_BIAS : SMALL_LN2_BIAS + 1, :] = column_sum(d_normed)
    small[SMALL_B_OUT : SMALL_B_OUT + 1, :] = column_sum(d_rows)
    small.flush()
    for kind, got in enumerate([ups_got, downs_got]):
        for peer in far_teams:
            arrived(got.at[peer], g_recv.at[kind, peer])
    up_share, down_share = [
        functools.reduce(jnp.add, [got[n] for n in range(teams)]) for got in (ups_got, downs_got)
    ]
    for rows_of, columns_of, there in side_by_side(*up_share.shape, width):
        shares[there, columns_of] = up_share[rows_of]
    shares[there.stop :, :] = down_share
    shares.flush()
    for n, source in enumerate(sources):
        arrived(back_landed.at[source], back_recv.at[n])
    d_mixed[...] = back_landed[...].reshape(rows, feats).T
    d_mixed.flush()
    for copy in copies + squad_copies + key_copies:
        copy.wait_send()

    def drain(index, carry):
        for copy in mix_copies(index):
            copy.wait_send()
        return carry

    lax.fori_loop(0, groups, drain, 0)


def front(zs, dps, teams, pair, *operands):
    _, heads, rows, cols = pair.shape
    feats, blocks = heads * DH, cols // rows
    width, units = operands[0].shape[1], operands[12].shape[1]
    piece, group, hops = rows // zs, GROUP, zs - 1
    squads = dps * min(blocks // 2, max(1, feats // (2 * dps * 8)))
    up_rows, down_rows = width // (2 * teams), units // (2 * teams)
    groups = heads // group
    slab = pltpu.VMEM((zs, piece, width), F32)
    narrow = pltpu.VMEM((zs, piece, feats), F32)
    one_up, one_down = pltpu.VMEM((teams, up_rows, units), F32), pltpu.VMEM((teams, down_rows, width), F32)
    dma = pltpu.SemaphoreType.DMA
    return staged_call(
        front_kernel,
        "front",
        operands,
        [
            (feats, rows), (blocks, 2 * feats + 8, rows), (rows, LANES), (heads, rows, LANES), (feats, rows),
            (STRIP, cols), (feats, rows), (piece, width), (piece, width),
            (up_rows * units // width + down_rows, width), (SMALL_ROWS, width),
        ]
        + [(2 * piece, width)] * (zs - 1),
        [
            pltpu.VMEM((2, group, rows, cols), F32),
            pltpu.VMEM((group, rows, cols), F32),
            pltpu.VMEM((group, rows, cols), BF16),
            pltpu.VMEM((group, rows, cols), BF16),
            narrow, narrow,
            pltpu.VMEM((zs, feats, piece), F32),
            pltpu.VMEM((blocks, zs, feats, rows), F32),
            pltpu.VMEM((squads, 2, zs, feats // (2 * squads), width), F32),
            pltpu.VMEM((piece, cols), F32),
            pltpu.VMEM((zs, feats, rows), F32),
            pltpu.VMEM((rows, width), F32),
            pltpu.VMEM((rows, width), F32),
            pltpu.VMEM((rows, units), F32),
            pltpu.VMEM((width, units), BF16),
            pltpu.VMEM((width, units), BF16),
            pltpu.VMEM((rows, width), F32),
            pltpu.VMEM((rows, LANES), F32),
            slab, slab, narrow, narrow,
            pltpu.VMEM((teams, 2, up_rows, units), F32),
            one_up, one_up, one_up,
            pltpu.VMEM((teams, 2, down_rows, width), F32),
            one_down, one_down, one_down,
            dma((2, group)),
            dma((blocks,)), dma((blocks,)),
            dma((hops,)), dma((hops, blocks // 2)), dma((max(1, blocks // 2 - 1), hops)), dma((blocks, zs)),
            dma((hops,)), dma((hops,)),
            dma((hops,)), dma((hops,)), dma((max(1, squads - 1),)), dma((max(1, squads - 1),)),
            dma((squads,)), dma((squads,)),
            dma((hops, groups)), dma((hops, groups)),
            dma((hops,)), dma((hops,)),
            dma((hops,)), dma((hops,)),
            dma((2,)), dma((2,)),
            dma((2, teams)), dma((2, teams)),
        ],
        FRONT_MB,
        remote=0,
        raw=(pair,),
    )


def finish_kernel(operands, results, scratch, raw):
    (
        out_mine, d_hidden, atoms, gain, bias, w_query, mixed, small_in, w_key, w_value,
    ) = operands[:10]
    parcels = operands[10 : 9 + lax.axis_size("head")]
    chip_shares = operands[9 + lax.axis_size("head") :]
    grad_atoms, out_atoms, total_grads, grad_up, grad_down, small, penalty = results
    (
        sib_keys, sib_values, go_keys, go_values, got_keys, got_values,
        part, landed, grads, sib_grads, go_grads, got_grads, hidden_all, small_z, small_all,
        sib_send, sib_recv, kv_send, kv_recv, part_send, part_recv, back_send, back_recv,
        g_send, g_recv, t_send, t_recv, f_send, b_send, b_recv, bf_send, out_send, out_recv,
        small_z_send, small_z_recv, small_send, small_recv, own_heads, heads_sem,
    ) = scratch
    (d_heads,) = raw
    chips, feats, rows = own_heads.shape[0] - 1, d_heads.shape[2] // 2, d_heads.shape[3]
    heads_copy = pltpu.make_async_copy(d_heads.at[pl.ds(0, chips + 1)], own_heads, heads_sem.at[0])
    heads_copy.start()
    zs, piece, width = part.shape
    teams, _, share, _ = grads.shape
    blk, z, dp = lax.axis_index("blk"), lax.axis_index("head"), lax.axis_index("dp")
    core, chip = lax.rem(blk, 2), lax.div(blk, 2)
    other_core = 1 - core
    sibling = {"blk": blk + 1 - 2 * core}
    peers = others(z, zs)
    team = dp * chips + chip
    far_teams = others(team, teams)
    far_chips = others(chip, chips)
    place = team * 2 + core
    far_places = others(place, teams * 2)
    plane = [team_device(lax.div(value, 2), lax.rem(value, 2), chips) for value in far_places]
    meeting = [{"head": peer} for peer in peers] + plane
    greet(meeting)
    meet(meeting)
    copies = [
        send(
            d_heads.at[pl.ds(0, chips), other_core, pl.ds(kind * feats, feats)],
            sib, sib_send.at[kind], sib_recv.at[kind], sibling,
        )
        for kind, sib in enumerate([sib_keys, sib_values])
    ]
    mine = pl.ds(pl.multiple_of(z * piece, 8), piece)
    out_atoms[mine, :] = functools.reduce(jnp.add, [parcel[0:piece, :] for parcel in parcels], out_mine[...])
    copies += [
        send(out_atoms.at[mine], out_atoms.at[mine], out_send.at[n], out_recv.at[z], {"head": peer})
        for n, peer in enumerate(peers)
    ]

    def big_rows(result, source, kind):
        count = result.shape[0] // (2 * teams)
        return result.at[pl.ds(pl.multiple_of((source * 2 + kind) * count, 8), count)]

    partners = others(dp, lax.axis_size("dp"))
    for n in range(chips):
        source = dp * chips + lax.rem(chip + chips - n, chips)
        up_there, down_there = big_rows(grad_up, source, core), big_rows(grad_down, source, core)
        for rows_of, columns_of, there in side_by_side(*up_there.shape, width):
            up_there[rows_of, :] = chip_shares[n][there, columns_of]
        down_there[...] = chip_shares[n][there.stop :, :]
        for kind, ready in enumerate([up_there, down_there]):
            copies += [
                send(ready, ready, b_send.at[kind, n, m], b_recv.at[kind, source, core], {"dp": partner})
                for m, partner in enumerate(partners)
            ]
    heads_copy.wait()
    d_queries = own_heads[chips, 0, 0:feats, :]
    for kind, (sib, go, got) in enumerate([(sib_keys, go_keys, got_keys), (sib_values, go_values, got_values)]):
        arrived(sib, sib_recv.at[kind])
        go[...] = sib[...] + own_heads[0:chips, core, kind * feats : (kind + 1) * feats, :]
        copies += [
            send(
                go.at[peer], got.at[chip], kv_send.at[kind, n], kv_recv.at[kind, chip],
                {"blk": peer * 2 + core},
            )
            for n, peer in enumerate(far_chips)
        ]
    got_keys[chip] = go_keys[chip]
    got_values[chip] = go_values[chip]
    normal, rate = normalize(atoms[...])
    normed = halves(normal * gain[...] + bias[...])
    dq_rows = d_queries.T
    d_normed = dot_full(dq_rows, w_query[...], NT)
    grad_q = dot_halves(halves(d_queries), normed)
    small_z[z] = small_in[0:8, :]
    hidden_all[z] = d_hidden[...]
    for n, parcel in enumerate(parcels):
        hidden_all[lax.rem(z + zs - 1 - n, zs)] = parcel[piece : 2 * piece, :]
    grad_o = dot_full(mixed[...], hidden_all[...].reshape(rows, width))
    for peer in far_chips:
        arrived(got_keys.at[peer], kv_recv.at[0, peer])
        arrived(got_values.at[peer], kv_recv.at[1, peer])
    dk = functools.reduce(jnp.add, [got_keys[n] for n in range(chips)])
    dv = functools.reduce(jnp.add, [got_values[n] for n in range(chips)])
    dv_rows = dv.T
    d_normed = (
        d_normed + dot_full(dk.T, w_key[...], NT) + dot_full(dv_rows, w_value[...], NT)
    )
    part[...] = d_normed.reshape(zs, piece, width)
    copies += [
        send(part.at[peer], landed.at[z], part_send.at[n], part_recv.at[z], {"head": peer})
        for n, peer in enumerate(peers)
    ]
    landed[z] = part[z]
    grad_k = dot_halves(halves(dk), normed)
    grad_v = dot_halves(halves(dv), normed)
    grads[...] = jnp.concatenate([grad_q, grad_k, grad_v, grad_o], axis=0).reshape(grads.shape)
    copies.append(send(grads.at[:, other_core], sib_grads, sib_send.at[2], sib_recv.at[2], sibling))
    arrived(sib_grads, sib_recv.at[2])
    go_grads[...] = sib_grads[...] + grads[:, core]
    copies += [
        send(
            go_grads.at[peer], got_grads.at[team], g_send.at[n], g_recv.at[team], team_device(peer, core, chips)
        )
        for n, peer in enumerate(far_teams)
    ]
    got_grads[team] = go_grads[team]
    for peer in peers:
        arrived(landed.at[peer], part_recv.at[peer])
    d_normed = functools.reduce(jnp.add, [landed[n] for n in range(zs)])
    normal, rate = normalize(atoms[mine, :])
    grad_atoms[mine, :] = d_hidden[...] + normalize_back(d_normed, gain[...], normal, rate)
    small_z[z, SMALL_LN1_GAIN : SMALL_LN1_GAIN + 1, :] = column_sum(d_normed * normal)
    small_z[z, SMALL_LN1_BIAS : SMALL_LN1_BIAS + 1, :] = column_sum(d_normed)
    copies += [
        send(small_z.at[z], small_z.at[z], small_z_send.at[n], small_z_recv.at[z], {"head": peer})
        for n, peer in enumerate(peers)
    ]
    copies += [
        send(grad_atoms.at[mine], grad_atoms.at[mine], back_send.at[n], back_recv.at[z], {"head": peer})
        for n, peer in enumerate(peers)
    ]
    for peer in far_teams:
        arrived(got_grads.at[peer], g_recv.at[peer])
    total_grads[team, core] = functools.reduce(jnp.add, [got_grads[n] for n in range(teams)])
    ready = total_grads.at[team, core]
    copies.append(send(ready, ready, t_send.at[0], t_recv.at[team, core], sibling))
    copies += [
        send(ready, ready, t_send.at[n + 1], t_recv.at[team, core], team_device(peer, core, chips))
        for n, peer in enumerate(far_teams)
    ]
    for peer in peers:
        arrived(small_z.at[peer], small_z_recv.at[peer])
    small_all[place, 0:8, :] = functools.reduce(jnp.add, [small_z[n] for n in range(zs)])
    small_all[place, 8:16, :] = small_in[8:16, :]
    small_all[place, SMALL_B_QUERY : SMALL_B_QUERY + 1, 0:feats] = column_sum(dq_rows)
    small_all[place, SMALL_B_VALUE : SMALL_B_VALUE + 1, 0:feats] = column_sum(dv_rows)
    copies += [
        send(small_all.at[place], small_all.at[place], small_send.at[n], small_recv.at[place], target)
        for n, target in enumerate(plane)
    ]
    for n, peer in enumerate(far_teams):
        ready = total_grads.at[peer, core]
        arrived(ready, t_recv.at[peer, core])
        copies.append(send(ready, ready, f_send.at[n], t_recv.at[peer, core], sibling))
    for kind, result in enumerate([grad_up, grad_down]):
        for n in range(teams):
            ready = big_rows(result, n, core)

            @pl.when(lax.div(n, chips) != dp)
            def _(ready=ready, sem=b_recv.at[kind, n, core]):
                arrived(ready, sem)

            copies.append(send(ready, ready, bf_send.at[kind, n], b_recv.at[kind, n, core], sibling))
    for source in far_places:
        arrived(small_all.at[source], small_recv.at[source])
    summed = functools.reduce(jnp.add, [small_all[n] for n in range(2 * teams)])
    small[...] = summed
    ends = summed[SMALL_PENALTY : SMALL_PENALTY + 1, :]
    penalty[...] = ends[:, 0:1] / ends[:, 1:2]
    for peer in [team] + far_teams:
        arrived(total_grads.at[peer, other_core], t_recv.at[peer, other_core])
    total_grads.flush()
    for kind, result in enumerate([grad_up, grad_down]):
        for n in range(teams):
            arrived(big_rows(result, n, other_core), b_recv.at[kind, n, other_core])
        result.flush()
    for peer in peers:
        there = pl.ds(pl.multiple_of(peer * piece, 8), piece)
        arrived(out_atoms.at[there], out_recv.at[peer])
    out_atoms.flush()
    for peer in peers:
        there = pl.ds(pl.multiple_of(peer * piece, 8), piece)
        arrived(grad_atoms.at[there], back_recv.at[peer])
    for copy in copies:
        copy.wait_send()


def finish(zs, dps, units, d_heads, *operands):
    atoms = operands[2]
    chips, feats, rows = lax.axis_size("blk") // 2, d_heads.shape[2] // 2, d_heads.shape[3]
    width = atoms.shape[1]
    piece = rows // zs
    teams = dps * chips
    share = 4 * feats // (2 * teams)
    some = pltpu.VMEM((chips, feats, rows), F32)
    slab = pltpu.VMEM((zs, piece, width), F32)
    one = pltpu.VMEM((teams, share, width), F32)
    dma = pltpu.SemaphoreType.DMA
    return staged_call(
        finish_kernel,
        "finish",
        operands,
        [
            (rows, width),
            (rows, width),
            (teams, 2, share, width),
            (width, units),
            (units, width),
            (SMALL_ROWS, width),
            (1, 1),
        ],
        [some] * 6
        + [slab, slab, pltpu.VMEM((teams, 2, share, width), F32), one, one, one, slab]
        + [
            pltpu.VMEM((zs, 8, width), F32),
            pltpu.VMEM((2 * teams, SMALL_ROWS, width), F32),
            dma((3,)), dma((3,)),
            dma((2, chips)), dma((2, chips)),
            dma((zs,)), dma((zs,)),
            dma((zs,)), dma((zs,)),
            dma((teams,)), dma((teams,)),
            dma((teams,)), dma((teams, 2)), dma((teams,)),
            dma((2, chips, dps)), dma((2, teams, 2)), dma((2, teams)),
            dma((zs,)), dma((zs,)),
            dma((zs,)), dma((zs,)),
            dma((2 * teams,)), dma((2 * teams,)),
            pltpu.VMEM((chips + 1, 2, 2 * feats, rows), F32), dma((1,)),
        ],
        FINISH_MB,
        remote=2,
        near_in=range(10, len(operands)),
        raw=(d_heads,),
        near_out=range(7),
    )


def place_kernel(operands, results, scratch, raw):
    total_grads, small, penalty_in = operands
    penalty, grad_query, grad_key, grad_value, grad_out = results[:5]
    penalty[...] = penalty_in[...]
    feats, width = grad_out.shape
    done = total_grads[...].reshape(4 * feats, width)
    grad_query[...] = done[0:feats].T
    grad_query.flush()
    grad_key[...] = done[feats : 2 * feats].T
    grad_key.flush()
    grad_value[...] = done[2 * feats : 3 * feats].T
    grad_value.flush()
    grad_out[...] = done[3 * feats :]
    grad_out.flush()
    for result, row in zip(results[5:], SMALL_OUTPUTS, strict=True):
        result[...] = small[row : row + 1, 0 : result.shape[1]]


SMALL_OUTPUTS = (
    SMALL_LN1_GAIN, SMALL_LN1_BIAS, SMALL_B_QUERY, SMALL_B_VALUE, SMALL_B_OUT, SMALL_LN2_GAIN, SMALL_LN2_BIAS,
    SMALL_B_UP, SMALL_B_DOWN,
)


def place(feats, units, straight, *operands):
    width = operands[1].shape[1]
    lengths = {SMALL_B_QUERY: feats, SMALL_B_VALUE: feats, SMALL_B_UP: units}
    return staged_call(
        place_kernel,
        "place",
        operands,
        [(1, 1)]
        + [(width, feats)] * 3
        + [(feats, width)]
        + [(1, lengths.get(row, width)) for row in SMALL_OUTPUTS],
        [],
        PLACE_MB,
        straight=straight,
        near_in=(0, 1, 2),
        near_straight=True,
    )


def local(
    zs, dps,
    atoms, pair, mol_ids, ln1_gain, ln1_bias, w_query, b_query, w_key, w_value, b_value, w_out, b_out,
    ln2_gain, ln2_bias, w_up, b_up, w_down, b_down, cot_atoms, cot_pair,
):
    blocks = pair.shape[3] // pair.shape[2]
    inputs, cot = atoms[0], cot_atoms[0]

    def line(value):
        return value.reshape(1, -1)

    (
        queries, kept, id_column, log_sums, mixed, id_row, d_mixed, out_mine, d_hidden, shares, small, *parcels,
    ) = front(
        zs, dps, dps * blocks // 2, pair,
        inputs, mol_ids, line(ln1_gain), line(ln1_bias), w_key, w_value, line(b_value), w_query, line(b_query),
        w_out, cot, w_down, w_up, line(b_out), line(ln2_gain), line(ln2_bias), line(b_up),
        line(b_down),
    )
    parcels = [
        lax.ppermute(parcel, "head", [(source, (source + n + 1) % zs) for source in range(zs)])
        for n, parcel in enumerate(parcels)
    ]
    chips = blocks // 2
    chip_shares = [shares] + [
        lax.ppermute(shares, "blk", [(2 * c + core, 2 * ((c + n) % chips) + core) for c in range(chips) for core in range(2)])
        for n in range(1, chips)
    ]
    out_pair, grad_pair, d_heads = attend_back(
        pair, cot_pair, queries, kept, mixed, d_mixed, log_sums, id_column, id_row
    )
    grad_atoms, out_atoms, total_grads, grad_up, grad_down, small, penalty = finish(
        zs, dps, w_up.shape[1],
        d_heads, out_mine, d_hidden, inputs, line(ln1_gain), line(ln1_bias), w_query, mixed,
        small, w_key, w_value, *parcels, *chip_shares,
    )
    placed = place(
        w_query.shape[1], w_up.shape[1],
        [grad_atoms, out_atoms, grad_up, grad_down],
        total_grads, small, penalty,
    )
    grad_atoms, out_atoms, grad_up, grad_down, penalty, grad_query, grad_key, grad_value, grad_out = placed[:9]
    (
        grad_ln1_gain, grad_ln1_bias, grad_b_query, grad_b_value, grad_b_out, grad_ln2_gain, grad_ln2_bias,
        grad_b_up, grad_b_down,
    ) = [value.reshape(-1) for value in placed[9:]]
    return (
        out_atoms[None],
        out_pair,
        penalty[0, 0],
        grad_atoms[None],
        grad_pair,
        grad_ln1_gain,
        grad_ln1_bias,
        grad_query,
        grad_b_query,
        grad_key,
        grad_value,
        grad_b_value,
        grad_out,
        grad_b_out,
        grad_ln2_gain,
        grad_ln2_bias,
        grad_up,
        grad_b_up,
        grad_down,
        grad_b_down,
    )


def solution(mesh):
    rows, pairs = P("dp", "blk", None), P("dp", "head", "blk", None)
    columns = P(None, "head")
    return jax.shard_map(
        functools.partial(local, mesh.shape["head"], mesh.shape["dp"]),
        mesh=mesh,
        in_specs=(
            rows, pairs, P("dp", "blk"), P(), P(), columns, P("head"), columns, columns, P("head"),
            P("head", None), P(), P(), P(), columns, P("head"), P("head", None), P(), rows, pairs,
        ),
        out_specs=(
            rows, pairs, P(), rows, pairs, P(), P(), columns, P("head"), columns, columns, P("head"),
            P("head", None), P(), P(), P(), columns, P("head"), P("head", None), P(),
        ),
        check_vma=False,
    )
```
